32 devices in a mesh: dp: 16 (over z, y, core), tensor: 2 (over x).
Axes of the slice: x: 2, y: 2, z: 4, core: 2. Of those that a mesh axis runs over, the one named last changes fastest.
Arguments:
- tokens: bfloat16 [16384, 1024], P(('dp', 'tensor')), may hold values from -6 to 6
- cond: bfloat16 [16, 128], P('dp'), may hold values from -6 to 6
- doc_lengths: int32 [16, 4], P('dp'), may hold values from 1 to 512, 1024 in all within a row
- w_ada: bfloat16 [128, 6144], replicated, may hold values from -0.25 to 0.25
- b_ada: float32 [6144], replicated, may hold values from -3 to 3
- gain_one: float32 [1024], replicated, may hold values from 0.5 to 1.5
- w_qkv: bfloat16 [3, 1024, 1024], P(None, None, 'tensor'), may hold values from -0.1875 to 0.1875
- w_out: bfloat16 [1024, 1024], P('tensor'), may hold values from -1.5 to 1.5
- gain_two: float32 [1024], replicated, may hold values from 0.5 to 1.5
- w_up: bfloat16 [1024, 4096], P(None, 'tensor'), may hold values from -0.1875 to 0.1875
- b_up: float32 [4096], P('tensor'), may hold values from -3 to 3
- w_down: bfloat16 [4096, 1024], P('tensor'), may hold values from -0.09375 to 0.09375
- b_down: float32 [1024], replicated, may hold values from -3 to 3
- cotangent: bfloat16 [16384, 1024], P(('dp', 'tensor')), may hold values from -6 to 6
Outputs:
- output: bfloat16 [16384, 1024], P(('dp', 'tensor'))
- grad_tokens: bfloat16 [16384, 1024], P(('dp', 'tensor'))
- grad_cond: float32 [16, 128], P('dp')
- grad_w_ada: float32 [128, 6144], replicated
- grad_b_ada: float32 [6144], replicated
- grad_gain_one: float32 [1024], replicated
- grad_w_qkv: float32 [3, 1024, 1024], P(None, None, 'tensor')
- grad_w_out: float32 [1024, 1024], P('tensor')
- grad_gain_two: float32 [1024], replicated
- grad_w_up: float32 [1024, 4096], P(None, 'tensor')
- grad_b_up: float32 [4096], P('tensor')
- grad_w_down: float32 [4096, 1024], P('tensor')
- grad_b_down: float32 [1024], replicated
The draws below stay inside these ranges and needn't reach their ends.
Inputs may be any that keep to these rules, and one draw needn't show every extreme that they name: `doc_lengths`: each row sums to 1024, and its longest document has exactly half of 1024 tokens.
All inputs are finite; a program needn't handle non-finite values.
Results may differ from the reference program's by a relative error of at most 0.013.
The reference program's roundings to bfloat16 on the way count: a program that leaves them out, or rounds other values in their place, can miss the bound.
Values may be sent and summed in bfloat16 or wider, within the bound.
A program may use at most 192 MiB of HBM per device.

```python
import math
import jax
import jax.numpy as jnp
import numpy as np
from jax import lax

D = 1024
HEADS = 16
HEAD = 64
FF = 4096
COND = 128
SEQ = 1024
SEQS = 16
TOKENS = 16384
BLOCK = 512
NDOC = 4


def block_levels(own_key, shape, cuts, least, high):
    def one(dim, parts):
        steps = jax.random.uniform(jax.random.fold_in(jax.random.fold_in(own_key, 6), dim), (parts,), jnp.float32, least / len(cuts), high / len(cuts))
        return jnp.repeat(jnp.exp(steps), shape[dim] // parts).reshape((-1,) + (1,) * (len(shape) - dim - 1))

    factor_of = one(*cuts[0])
    for cut in cuts[1:]:
        factor_of = factor_of * one(*cut)
    return factor_of


def length_profile(amount, total, limit, slope):
    portions = [(1 << 20) // math.isqrt(rank ** slope) + 1 for rank in range(2, amount + 1)]
    rest, given = total - limit - (amount - 1), [1] * (amount - 1)
    while rest > 0:
        candidates = [i for i in range(amount - 1) if given[i] < limit]
        pool, remaining = sum([portions[i] for i in candidates]), rest
        for i in candidates:
            extra = min(limit - given[i], max(1, remaining * portions[i] // pool), rest)
            given[i] = given[i] + extra
            rest = rest - extra
    return np.array([limit] + given)


def ragged_sizes(rng, number_of, total, most, slope):
    if number_of == 2:
        one = jax.random.randint(rng, (), max(1, total - most), min(most, total - 1) + 1)
        return jnp.stack([one, total - one])
    sizes = jnp.asarray(length_profile(number_of, total, most, slope), jnp.int32)
    twos = (number_of - 1) // 2
    giver, taker = sizes[1:1 + 2 * twos:2], sizes[2:2 + 2 * twos:2]
    slack = jnp.minimum(giver - 1, most - taker)
    shifted = jax.random.randint(jax.random.fold_in(rng, 1), (twos,), 0, 1 << 20) % (slack + 1)
    sizes = sizes.at[1:1 + 2 * twos:2].set(giver - shifted).at[2:2 + 2 * twos:2].set(taker + shifted)
    return sizes[jax.random.permutation(jax.random.fold_in(rng, 2), number_of)]


def centred(rng, shape, scale, most, shards=(), kind=jnp.bfloat16):
    loudness = block_levels(rng, shape, shards, -0.22, 0.18) if shards else 1.0
    drawn = jax.random.normal(rng, shape, jnp.float32) * scale * loudness
    return jnp.minimum(jnp.maximum(drawn, -most), most).astype(kind)


def setup_inputs(seed: int = 0) -> dict:
    seeds = jax.random.split(jax.random.key(seed), 15)
    tokens = centred(seeds[0], (TOKENS, D), 1.0, 6.0, ((0, 32),))
    cond = centred(seeds[1], (SEQS, COND), 1.0, 6.0, ((0, 16),))
    doc_lengths = jax.vmap(lambda own: ragged_sizes(own, NDOC, SEQ, SEQ // 2, 2))(jax.random.split(seeds[2], SEQS)).reshape((SEQS, NDOC)).astype(jnp.int32)
    w_ada = centred(seeds[3], (COND, 6 * D), (4 * COND) ** -0.5, 0.25)
    b_ada = centred(seeds[4], (6 * D,), 0.5, 3.0, (), jnp.float32)
    gain_one = jnp.clip(jax.random.uniform(seeds[5], (D,), jnp.float32, 0.5, 1.5), 0.5, 1.5)
    w_qkv = centred(seeds[6], (3, D, D), D ** -0.5, 0.1875, ((2, 2),))
    w_out = centred(seeds[7], (D, D), (D // 64) ** -0.5, 1.5, ((0, 2),))
    gain_two = jnp.clip(jax.random.uniform(seeds[8], (D,), jnp.float32, 0.5, 1.5), 0.5, 1.5)
    w_up = centred(seeds[9], (D, FF), D ** -0.5, 0.1875, ((1, 2),))
    b_up = centred(seeds[10], (FF,), 0.5, 3.0, ((0, 2),), jnp.float32)
    w_down = centred(seeds[11], (FF, D), FF ** -0.5, 0.09375, ((0, 2),))
    b_down = centred(seeds[12], (D,), 0.6, 3.0, (), jnp.float32)
    cotangent = centred(seeds[13], (TOKENS, D), 1.0, 6.0, ((0, 32),))
    return dict(tokens=tokens, cond=cond, doc_lengths=doc_lengths, w_ada=w_ada, b_ada=b_ada, gain_one=gain_one, w_qkv=w_qkv, w_out=w_out, gain_two=gain_two, w_up=w_up, b_up=b_up, w_down=w_down, b_down=b_down, cotangent=cotangent)


@jax.custom_vjp
def low(v):
    return lax.optimization_barrier(v.astype(jnp.bfloat16)).astype(jnp.float32)

@jax.custom_vjp
def low_back(v):
    return v

def low_keep(v):
    return (low(v), None)

def low_pass(kept, grad):
    return (grad,)

def back_keep(v):
    return (v, None)

def back_low(kept, grad):
    return (low(grad),)
low.defvjp(low_keep, low_pass)
low_back.defvjp(back_keep, back_low)
highest = lax.Precision.HIGHEST
norm_eps = 1e-05
rope_base = 10000.0
masked_score = -1e+30

def layer_norm(values, gain):
    center = values - lax.optimization_barrier(jnp.mean(values, axis=-1, keepdims=True))
    spread = lax.optimization_barrier(jnp.mean(center * center, axis=-1, keepdims=True))
    return center * lax.rsqrt(spread + norm_eps) * gain

def modulate(values, gain, shift, scale):
    return layer_norm(values, gain) * (1.0 + scale) + shift

def rotate(values, cosine, sine):
    half_size = values.shape[-1] // 2
    turned = jnp.concatenate([-values[..., half_size:], values[..., :half_size]], axis=-1)
    return values * cosine + turned * sine

def documents(lengths, length_all):
    doc_ends = jnp.cumsum(lengths).astype(jnp.int32)
    starts = (doc_ends - lengths).astype(jnp.int32)
    places = jnp.arange(length_all, dtype=jnp.int32)
    inside = ((places[:, None] >= starts[None, :]) & (places[:, None] < doc_ends[None, :])).astype(jnp.int32)
    numbers = jnp.arange(lengths.shape[0], dtype=jnp.int32)
    segment = lax.optimization_barrier(jnp.sum(inside * numbers[None, :], axis=1)).astype(jnp.int32)
    doc_first = lax.optimization_barrier(jnp.sum(inside * starts[None, :], axis=1)).astype(jnp.int32)
    doc_last = lax.optimization_barrier(jnp.sum(inside * doc_ends[None, :], axis=1)).astype(jnp.int32)
    return (segment, doc_first, doc_last)

def rope_tables(offsets, head_size):
    exponent = jnp.arange(head_size // 2, dtype=jnp.float32) * (2.0 / head_size)
    frequency = jnp.power(jnp.float32(rope_base), -exponent)
    angles = offsets.astype(jnp.float32)[:, None] * frequency[None, :]
    angles = jnp.concatenate([angles, angles], axis=-1)
    return (jnp.cos(angles)[:, None, :], jnp.sin(angles)[:, None, :])

def attend_block(query_block, query_docs, key_rows, value_rows, key_docs):
    score_scale = query_block.shape[-1] ** (-0.5)
    scores = low_back(jnp.einsum('qhd,khd->hqk', query_block, key_rows, precision=highest) * score_scale)
    scores = jnp.where((query_docs[:, None] == key_docs[None, :])[None], scores, masked_score)
    weights = low(jax.nn.softmax(scores, axis=-1))
    return jnp.einsum('hqk,khd->qhd', weights, value_rows, precision=highest)

def whole_layer(x_seq, cond_seq, w_ada, b_ada, gain_one, w_qkv, w_out, gain_two, w_up, b_up, w_down, b_down, segment, cosine, sine):
    length_all = x_seq.shape[0]
    modulation = jnp.dot(cond_seq, w_ada, precision=highest) + b_ada
    shift_a, scale_a, gate_a, shift_m, scale_m, gate_m = jnp.split(modulation, 6)
    act_one = low(modulate(x_seq, gain_one, shift_a, scale_a))
    projected_qkv = jnp.einsum('sd,tde->tse', act_one, w_qkv, precision=highest).reshape(3, length_all, HEADS, HEAD)
    query_rows = low(rotate(low_back(projected_qkv[0]), cosine, sine))
    key_rows = low(rotate(low_back(projected_qkv[1]), cosine, sine))
    value_rows = low(low_back(projected_qkv[2]))
    block_count = length_all // BLOCK
    attend = jax.checkpoint(attend_block)
    mixed_blocks = lax.map(lambda pieces: attend(pieces[0], pieces[1], key_rows, value_rows, segment), (query_rows.reshape(block_count, BLOCK, HEADS, HEAD), segment.reshape(block_count, BLOCK)))
    mixed_heads = low_back(low(mixed_blocks.reshape(length_all, D)))
    projected = low_back(jnp.dot(mixed_heads, w_out, precision=highest))
    middle = x_seq + gate_a * projected
    act_two = low(modulate(middle, gain_two, shift_m, scale_m))
    pre_act = low_back(jnp.dot(act_two, w_up, precision=highest) + b_up)
    hidden = low(jax.nn.gelu(pre_act, approximate=True))
    branch = low_back(jnp.dot(hidden, w_down, precision=highest) + b_down)
    return middle + gate_m * branch

def reference(tokens, cond, doc_lengths, w_ada, b_ada, gain_one, w_qkv, w_out, gain_two, w_up, b_up, w_down, b_down, cotangent):
    params = tuple((weight_arg.astype(jnp.float32) for weight_arg in (w_ada, b_ada, gain_one, w_qkv, w_out, gain_two, w_up, b_up, w_down, b_down)))
    x_seqs = tokens.astype(jnp.float32).reshape(SEQS, SEQ, D)
    cot_seqs = cotangent.astype(jnp.float32).reshape(SEQS, SEQ, D)
    conds = cond.astype(jnp.float32)

    def one_sequence(sums, inputs):
        x_seq, cond_seq, lengths, cot_seq = inputs
        segment, doc_first, doc_last = documents(lengths, SEQ)
        cosine, sine = rope_tables(jnp.arange(SEQ, dtype=jnp.int32) - doc_first, HEAD)

        def apply_layer(x_in, cond_in, *weights_in):
            return whole_layer(x_in, cond_in, *weights_in, segment, cosine, sine)
        result, pullback = jax.vjp(apply_layer, x_seq, cond_seq, *params)
        grads = pullback(cot_seq)
        sums = tuple((total_part + grad_part for total_part, grad_part in zip(sums, grads[2:])))
        return (sums, (result, grads[0], grads[1]))
    zero_sums = tuple((jnp.zeros_like(weight_arg) for weight_arg in params))
    sums, (results, grad_x, grad_c) = lax.scan(one_sequence, zero_sums, (x_seqs, conds, doc_lengths, cot_seqs))
    return (results.reshape(TOKENS, D).astype(jnp.bfloat16), grad_x.reshape(TOKENS, D).astype(jnp.bfloat16), grad_c, sums[0], sums[1], sums[2], sums[3], sums[4], sums[5], sums[6], sums[7], sums[8], sums[9])
```

```python
import functools

import jax
import jax.numpy as jnp
from jax import lax
from jax.experimental import pallas as pl
from jax.experimental.pallas import tpu as pltpu
from jax.sharding import PartitionSpec as P

HEAD = 64
PAIR = 2 * HEAD
BLOCK = 256
ROWS = 512

norm_eps = 1e-05
rope_base = 10000.0
masked_score = -1e30
f32, bf16 = jnp.float32, jnp.bfloat16


def layer_norm(values, gain):
    center = values - jnp.mean(values, axis=-1, keepdims=True)
    spread = jnp.mean(center * center, axis=-1, keepdims=True)
    return center * lax.rsqrt(spread + norm_eps) * gain


def modulate(values, gain, shift, scale):
    return layer_norm(values, gain) * (1.0 + scale) + shift


def documents(lengths, places):
    numbers = jnp.arange(lengths.shape[0], dtype=jnp.int32)
    earlier = (numbers[None, :] < numbers[:, None]).astype(jnp.int32)
    starts = jnp.sum(earlier * lengths[None, :], axis=1)
    ends = starts + lengths
    inside = ((places[:, None] >= starts[None, :]) & (places[:, None] < ends[None, :])).astype(
        jnp.int32
    )
    segment = jnp.sum(inside * numbers[None, :], axis=1)
    doc_first = jnp.sum(inside * starts[None, :], axis=1)
    return segment, doc_first


def rope_tables(offsets):
    exponent = jnp.arange(HEAD // 2, dtype=f32) * (2.0 / HEAD)
    frequency = jnp.power(jnp.float32(rope_base), -exponent)
    angles = offsets.astype(f32)[:, None] * frequency[None, :]
    cosine, sine = jnp.cos(angles), jnp.sin(angles)
    repeat = PAIR // (HEAD // 2)
    return jnp.concatenate([cosine] * repeat, axis=-1), jnp.concatenate([sine] * repeat, axis=-1)


def turned(values):
    lane = lax.broadcasted_iota(jnp.int32, values.shape, 1)
    half = HEAD // 2
    from_right = pltpu.roll(values, PAIR - half, axis=1)
    from_left = pltpu.roll(values, half, axis=1)
    return jnp.where(lane % HEAD < half, -from_right, from_left)


def mm(a, b, da, db):
    return lax.dot_general(a, b, (((da,), (db,)), ((), ())), preferred_element_type=f32)


def qkv_kernel(x_ref, w_ref, cos_ref, sin_ref, o_ref):
    which = pl.program_id(1)
    y = mm(x_ref[...], w_ref[...], 1, 0)

    @pl.when(which < 2)
    def _():
        factor = jnp.where(which == 0, HEAD**-0.5, 1.0)
        for p in range(y.shape[1] // PAIR):
            u = y[:, p * PAIR : (p + 1) * PAIR]
            r = u * cos_ref[...] + turned(u) * sin_ref[...]
            o_ref[:, p * PAIR : (p + 1) * PAIR] = (r.astype(bf16) * factor.astype(bf16)).astype(bf16)

    @pl.when(which == 2)
    def _():
        o_ref[...] = y.astype(bf16)


def project_qkv(rows, w_qkv, cosine, sine):
    count, depth = rows.shape
    width = w_qkv.shape[2]
    return pl.pallas_call(
        qkv_kernel,
        grid=(count // ROWS, 3),
        in_specs=[
            pl.BlockSpec((ROWS, depth), lambda r, t: (r, 0)),
            pl.BlockSpec((None, depth, width), lambda r, t: (t, 0, 0)),
            pl.BlockSpec((ROWS, PAIR), lambda r, t: (r, 0)),
            pl.BlockSpec((ROWS, PAIR), lambda r, t: (r, 0)),
        ],
        out_specs=pl.BlockSpec((None, ROWS, width), lambda r, t: (t, r, 0)),
        out_shape=jax.ShapeDtypeStruct((3, count, width), bf16),
        compiler_params=pltpu.CompilerParams(vmem_limit_bytes=32 << 20),
        cost_estimate=pl.CostEstimate(
            flops=6 * count * depth * width, bytes_accessed=8 * count * width, transcendentals=0
        ),
        name="qkv",
    )(rows, w_qkv, cosine, sine)


def head_lanes(block, h):
    lane = lax.broadcasted_iota(jnp.int32, block.shape, 1)
    return jnp.where(lane // HEAD == h, block, jnp.zeros_like(block))


def transposed(block):
    return block.astype(f32).T


def forward_kernel(flag_ref, q_ref, k_ref, v_ref, segr_ref, segc_ref, o_ref, lse_ref, vt, m, l, acc):
    blocks = q_ref.shape[0] // BLOCK
    for b in range(blocks):
        vt[b] = transposed(v_ref[b * BLOCK : (b + 1) * BLOCK, :]).astype(bf16)

    @pl.loop(0, blocks)
    def _(qi):
        rows = pl.ds(pl.multiple_of(qi * BLOCK, BLOCK), BLOCK)
        q = q_ref[rows, :]
        m[...] = jnp.full(m.shape, masked_score, f32)
        l[...] = jnp.zeros(l.shape, f32)
        acc[...] = jnp.zeros(acc.shape, f32)

        @pl.loop(0, blocks)
        def _(ki):
            @pl.when(flag_ref[qi * blocks + ki] > 0)
            def _():
                cols = pl.ds(pl.multiple_of(ki * BLOCK, BLOCK), BLOCK)
                k = k_ref[cols, :]
                docs = segc_ref[cols, :]
                same = jnp.concatenate([docs] * (BLOCK // 128), axis=1) == segr_ref[qi]
                for h in range(2):
                    lo, hi = h * HEAD, (h + 1) * HEAD
                    s = jnp.where(same, mm(k, head_lanes(q, h), 1, 1), masked_score)
                    top = jnp.maximum(m[h], jnp.max(s, axis=0, keepdims=True))
                    p = jnp.exp(s - top)
                    shrink = jnp.exp(m[h] - top)
                    m[h] = top
                    l[h] = l[h] * shrink + jnp.sum(p, axis=0, keepdims=True)
                    acc[lo:hi, :] = acc[lo:hi, :] * shrink + mm(vt[ki, lo:hi, :], p.astype(bf16), 1, 0)

        for h in range(2):
            lo, hi = h * HEAD, (h + 1) * HEAD
            lse_ref[h, qi] = m[h] + jnp.log(l[h])
            acc[lo:hi, :] = acc[lo:hi, :] / l[h]
        o_ref[rows, :] = acc[...].T.astype(bf16)


def backward_kernel(
    flag_ref, q_ref, k_ref, v_ref, g_ref, o_ref, lse_ref, segr_ref, segc_ref, cos_ref, sin_ref,
    out_ref, kt, dk, dv, dq,
):
    blocks = q_ref.shape[0] // BLOCK
    for b in range(blocks):
        kt[b] = transposed(k_ref[b * BLOCK : (b + 1) * BLOCK, :]).astype(bf16)
    dk[...] = jnp.zeros(dk.shape, f32)
    dv[...] = jnp.zeros(dv.shape, f32)

    def turn_back(u, rows):
        return (u * cos_ref[rows, :] - turned(u) * sin_ref[rows, :]).astype(bf16)

    @pl.loop(0, blocks)
    def _(qi):
        rows = pl.ds(pl.multiple_of(qi * BLOCK, BLOCK), BLOCK)
        q, g = q_ref[rows, :], g_ref[rows, :]
        both = (g.astype(f32) * o_ref[rows, :].astype(f32)).T
        dq[...] = jnp.zeros(dq.shape, f32)

        @pl.loop(0, blocks)
        def _(ki):
            @pl.when(flag_ref[qi * blocks + ki] > 0)
            def _():
                cols = pl.ds(pl.multiple_of(ki * BLOCK, BLOCK), BLOCK)
                k, v = k_ref[cols, :], v_ref[cols, :]
                docs = segc_ref[cols, :]
                same = jnp.concatenate([docs] * (BLOCK // 128), axis=1) == segr_ref[qi]
                dk_sum, dv_sum = dk[cols, :], dv[cols, :]
                for h in range(2):
                    lo, hi = h * HEAD, (h + 1) * HEAD
                    delta = jnp.sum(both[lo:hi, :], axis=0, keepdims=True)
                    qh, gh = head_lanes(q, h), head_lanes(g, h)
                    s = jnp.where(same, mm(k, qh, 1, 1), masked_score)
                    p = jnp.exp(s - lse_ref[h, qi])
                    ds = (p * (mm(v, gh, 1, 1) - delta)).astype(bf16)
                    dv_sum = dv_sum + mm(p.astype(bf16), gh, 1, 0)
                    dk_sum = dk_sum + mm(ds, qh, 1, 0)
                    dq[lo:hi, :] = dq[lo:hi, :] + mm(kt[ki, lo:hi, :], ds, 1, 0)
                dk[cols, :] = dk_sum
                dv[cols, :] = dv_sum

        out_ref[0, rows, :] = turn_back(dq[...].T * (HEAD**-0.5), rows)

    @pl.loop(0, blocks)
    def _(b):
        rows = pl.ds(pl.multiple_of(b * BLOCK, BLOCK), BLOCK)
        out_ref[1, rows, :] = turn_back(dk[rows, :], rows)
        out_ref[2, rows, :] = dv[rows, :].astype(bf16)


def pieces_of(qkv, length):
    return [pl.BlockSpec((None, length, PAIR), functools.partial(lambda t, p, *_: (t, 0, p), t)) for t in range(3)]


def attend_forward(flags, qkv, seg_rows, seg_cols):
    _, length, width = qkv.shape
    blocks, pairs = length // BLOCK, width // PAIR
    return pl.pallas_call(
        forward_kernel,
        grid_spec=pltpu.PrefetchScalarGridSpec(
            num_scalar_prefetch=1,
            grid=(pairs,),
            in_specs=[
                *pieces_of(qkv, length),
                pl.BlockSpec((blocks, 1, BLOCK), lambda p, *_: (0, 0, 0)),
                pl.BlockSpec((length, 128), lambda p, *_: (0, 0)),
            ],
            out_specs=[
                pl.BlockSpec((length, PAIR), lambda p, *_: (0, p)),
                pl.BlockSpec((2, blocks, 1, BLOCK), lambda p, *_: (p, 0, 0, 0)),
            ],
            scratch_shapes=[
                pltpu.VMEM((blocks, PAIR, BLOCK), bf16),
                pltpu.VMEM((2, 1, BLOCK), f32),
                pltpu.VMEM((2, 1, BLOCK), f32),
                pltpu.VMEM((PAIR, BLOCK), f32),
            ],
        ),
        out_shape=[
            jax.ShapeDtypeStruct((length, width), bf16),
            jax.ShapeDtypeStruct((2 * pairs, blocks, 1, BLOCK), f32),
        ],
        compiler_params=pltpu.CompilerParams(vmem_limit_bytes=48 << 20),
        cost_estimate=pl.CostEstimate(
            flops=4 * length * length * width, bytes_accessed=8 * length * width, transcendentals=length * length * width // HEAD
        ),
        name="attend",
    )(flags, qkv, qkv, qkv, seg_rows, seg_cols)


def attend_backward(flags, qkv, grad, mixed, lse, seg_rows, seg_cols, cosine, sine):
    _, length, width = qkv.shape
    blocks, pairs = length // BLOCK, width // PAIR
    whole = pl.BlockSpec((length, PAIR), lambda p, *_: (0, p))
    table = pl.BlockSpec((length, PAIR), lambda p, *_: (0, 0))
    return pl.pallas_call(
        backward_kernel,
        grid_spec=pltpu.PrefetchScalarGridSpec(
            num_scalar_prefetch=1,
            grid=(pairs,),
            in_specs=[
                *pieces_of(qkv, length),
                whole,
                whole,
                pl.BlockSpec((2, blocks, 1, BLOCK), lambda p, *_: (p, 0, 0, 0)),
                pl.BlockSpec((blocks, 1, BLOCK), lambda p, *_: (0, 0, 0)),
                table,
                table,
                table,
            ],
            out_specs=pl.BlockSpec((3, length, PAIR), lambda p, *_: (0, 0, p)),
            scratch_shapes=[
                pltpu.VMEM((blocks, PAIR, BLOCK), bf16),
                pltpu.VMEM((length, PAIR), f32),
                pltpu.VMEM((length, PAIR), f32),
                pltpu.VMEM((PAIR, BLOCK), f32),
            ],
        ),
        out_shape=jax.ShapeDtypeStruct((3, length, width), bf16),
        compiler_params=pltpu.CompilerParams(vmem_limit_bytes=56 << 20),
        cost_estimate=pl.CostEstimate(
            flops=10 * length * length * width, bytes_accessed=16 * length * width, transcendentals=length * length * width // HEAD
        ),
        name="attend_back",
    )(flags, qkv, qkv, qkv, grad, mixed, lse, seg_rows, seg_cols, cosine, sine)


def body(
    tokens, cond, doc_lengths, w_ada, b_ada, gain_one, w_qkv, w_out, gain_two, w_up, b_up, w_down, b_down, cotangent
):
    tensor_size, dp_size = lax.axis_size("tensor"), lax.axis_size("dp")
    pair = tensor_size == 2
    cube = dp_size & (dp_size - 1) == 0
    own = tokens.shape[0]
    length = own * tensor_size
    me, place = lax.axis_index("tensor"), lax.axis_index("dp")

    def other(values):
        return lax.ppermute(values, "tensor", [(0, 1), (1, 0)])

    def all_rows(values):
        if pair:
            return jnp.concatenate([values, other(values)], axis=0)
        return lax.all_gather(values, "tensor", axis=0, tiled=True)

    def own_sum(values):
        if pair:
            return values[:own] + other(values[own:].astype(bf16)).astype(f32)
        return lax.psum_scatter(values, "tensor", scatter_dimension=0, tiled=True)

    def bit_of(b):
        return (place >> b) & 1

    def across(values, b):
        return lax.ppermute(values, "dp", [(d, d ^ (1 << b)) for d in range(dp_size)])

    def sum_over_dp(part):
        bits = dp_size.bit_length() - 1
        if not cube or part.shape[0] % (16 << bits):
            return lax.psum(part, "dp")
        for b in range(bits):
            half = part.shape[0] // 2
            low, high = part[:half], part[half:]
            first = bit_of(b) == 0
            send = jnp.where(first, high, low).astype(bf16)
            part = jnp.where(first, low, high) + across(send, b).astype(f32)
        part = part.astype(bf16)
        for b in reversed(range(bits)):
            got = across(part, b)
            first = bit_of(b) == 0
            part = jnp.concatenate([jnp.where(first, part, got), jnp.where(first, got, part)], axis=0)
        return part.astype(f32)

    places = jnp.arange(length, dtype=jnp.int32)
    if pair:
        places = (places + me * own) % length
    segment, doc_first = documents(doc_lengths[0], places)
    cosine, sine = rope_tables(places - doc_first)
    blocks = length // BLOCK
    in_blocks = segment.reshape(blocks, BLOCK)
    least, most = jnp.min(in_blocks, axis=1), jnp.max(in_blocks, axis=1)
    meets = (least[:, None] <= most[None, :]) & (least[None, :] <= most[:, None])
    flags = meets.astype(jnp.int32).reshape(-1)
    seg_rows = in_blocks[:, None, :]
    seg_cols = jnp.broadcast_to(segment[:, None], (length, 128))

    modulation = jnp.dot(cond, w_ada, preferred_element_type=f32)[0] + b_ada
    shift_a, scale_a, gate_a, shift_m, scale_m, gate_m = jnp.split(modulation, 6)
    x_rows = tokens.astype(f32)
    grad_out = cotangent.astype(f32)

    act_one = modulate(x_rows, gain_one, shift_a, scale_a).astype(bf16)
    rows_one = all_rows(act_one)
    grad_branch = (grad_out * gate_m).astype(bf16)
    full_branch = all_rows(grad_branch)
    qkv = project_qkv(rows_one, w_qkv, cosine, sine)
    mixed, lse = attend_forward(flags, qkv, seg_rows, seg_cols)
    projected = own_sum(jnp.dot(mixed, w_out, preferred_element_type=f32))
    middle = x_rows + gate_a * projected
    rows_two = all_rows(modulate(middle, gain_two, shift_m, scale_m).astype(bf16))
    pre_act = jnp.dot(rows_two, w_up, preferred_element_type=f32) + b_up
    hidden = jax.nn.gelu(pre_act, approximate=True).astype(bf16)

    grad_hidden = jnp.einsum("sd,fd->sf", full_branch, w_down, preferred_element_type=f32)
    _, gelu_back = jax.vjp(lambda values: jax.nn.gelu(values, approximate=True), pre_act)
    grad_pre = gelu_back(grad_hidden)[0].astype(bf16)
    grad_act_two = own_sum(jnp.einsum("sf,df->sd", grad_pre, w_up, preferred_element_type=f32))
    grad_w_down = sum_over_dp(jnp.einsum("sf,sd->fd", hidden, full_branch, preferred_element_type=f32))
    grad_w_up = sum_over_dp(jnp.einsum("sd,sf->df", rows_two, grad_pre, preferred_element_type=f32))

    branch = own_sum(jnp.dot(hidden, w_down, preferred_element_type=f32)) + b_down
    output = (middle + gate_m * branch).astype(bf16)
    grad_gate_m = jnp.sum(grad_out * branch, axis=0)
    grad_b_down = jnp.sum(grad_branch.astype(f32), axis=0)
    grad_b_up = jnp.sum(grad_pre.astype(f32), axis=0)

    _, second_back = jax.vjp(modulate, middle, gain_two, shift_m, scale_m)
    grad_middle, grad_gain_two, grad_shift_m, grad_scale_m = second_back(grad_act_two)
    grad_middle = grad_middle + grad_out
    full_proj = all_rows((grad_middle * gate_a).astype(bf16))
    grad_gate_a = jnp.sum(grad_middle * projected, axis=0)
    grad_mixed = jnp.einsum("sd,ed->se", full_proj, w_out, preferred_element_type=f32).astype(bf16)
    grad_w_out = sum_over_dp(jnp.einsum("se,sd->ed", mixed, full_proj, preferred_element_type=f32))
    grad_qkv = attend_backward(flags, qkv, grad_mixed, mixed, lse, seg_rows, seg_cols, cosine, sine)
    grad_act_one = own_sum(jnp.einsum("tse,tde->sd", grad_qkv, w_qkv, preferred_element_type=f32))
    grad_w_qkv = jnp.einsum("sd,tse->tde", rows_one, grad_qkv, preferred_element_type=f32)
    grad_w_qkv = sum_over_dp(grad_w_qkv.reshape(-1, grad_w_qkv.shape[2])).reshape(grad_w_qkv.shape)

    _, first_back = jax.vjp(modulate, x_rows, gain_one, shift_a, scale_a)
    grad_x, grad_gain_one, grad_shift_a, grad_scale_a = first_back(grad_act_one)
    grad_x = (grad_x + grad_middle).astype(bf16)

    small = jnp.concatenate(
        [
            grad_shift_a, grad_scale_a, grad_gate_a, grad_shift_m, grad_scale_m, grad_gate_m,
            grad_gain_one, grad_gain_two, grad_b_down,
        ]
    )
    small = lax.psum(small, "tensor")
    mod_size = modulation.shape[0]
    grad_mod = small[:mod_size]
    grad_cond = jnp.dot(w_ada.astype(f32), grad_mod, precision=lax.Precision.HIGHEST)[None, :]
    everyone = lax.all_gather(
        jnp.concatenate([small, grad_b_up, cond[0].astype(f32)])[None, :], "dp", axis=0, tiled=True
    )
    conds = everyone[:, -cond.shape[1] :]
    mods = everyone[:, :mod_size]
    grad_w_ada = jnp.einsum("nc,nm->cm", conds, mods, precision=lax.Precision.HIGHEST, preferred_element_type=f32)
    sums = jnp.sum(everyone, axis=0)
    width = tokens.shape[1]
    grad_b_ada = sums[:mod_size]
    grad_gain_one, grad_gain_two, grad_b_down = jnp.split(sums[mod_size : mod_size + 3 * width], 3)
    grad_b_up = sums[mod_size + 3 * width : -cond.shape[1]]
    return (
        output, grad_x, grad_cond, grad_w_ada, grad_b_ada, grad_gain_one, grad_w_qkv, grad_w_out, grad_gain_two,
        grad_w_up, grad_b_up, grad_w_down, grad_b_down,
    )


def solution(mesh):
    placed = (
        P(("dp", "tensor"), None), P("dp", None), P("dp", None), P(), P(), P(), P(None, None, "tensor"),
        P("tensor", None), P(), P(None, "tensor"), P("tensor"), P("tensor", None), P(), P(("dp", "tensor"), None),
    )
    return jax.shard_map(
        body,
        mesh=mesh,
        in_specs=placed,
        out_specs=(
            P(("dp", "tensor"), None), P(("dp", "tensor"), None), P("dp", None), P(), P(), P(),
            P(None, None, "tensor"), P("tensor", None), P(), P(None, "tensor"), P("tensor"), P("tensor", None), P(),
        ),
        check_vma=False,
    )
```

```python
import functools

import jax
import jax.numpy as jnp
from jax import lax
from jax.experimental import pallas as pl
from jax.experimental.pallas import tpu as pltpu
from jax.sharding import PartitionSpec as P

HEAD = 64
PAIR = 2 * HEAD
BLOCK = 256
ROWS = 512

norm_eps = 1e-05
rope_base = 10000.0
masked_score = -1e30
f32, bf16 = jnp.float32, jnp.bfloat16


def layer_norm(values, gain):
    center = values - jnp.mean(values, axis=-1, keepdims=True)
    spread = jnp.mean(center * center, axis=-1, keepdims=True)
    return center * lax.rsqrt(spread + norm_eps) * gain


def modulate(values, gain, shift, scale):
    return layer_norm(values, gain) * (1.0 + scale) + shift


def documents(lengths, places):
    numbers = jnp.arange(lengths.shape[0], dtype=jnp.int32)
    earlier = (numbers[None, :] < numbers[:, None]).astype(jnp.int32)
    starts = jnp.sum(earlier * lengths[None, :], axis=1)
    ends = starts + lengths
    inside = ((places[:, None] >= starts[None, :]) & (places[:, None] < ends[None, :])).astype(
        jnp.int32
    )
    segment = jnp.sum(inside * numbers[None, :], axis=1)
    doc_first = jnp.sum(inside * starts[None, :], axis=1)
    return segment, doc_first


def rope_tables(offsets):
    exponent = jnp.arange(HEAD // 2, dtype=f32) * (2.0 / HEAD)
    frequency = jnp.power(jnp.float32(rope_base), -exponent)
    angles = offsets.astype(f32)[:, None] * frequency[None, :]
    cosine, sine = jnp.cos(angles), jnp.sin(angles)
    repeat = PAIR // (HEAD // 2)
    return jnp.concatenate([cosine] * repeat, axis=-1), jnp.concatenate([sine] * repeat, axis=-1)


def turned(values):
    lane = lax.broadcasted_iota(jnp.int32, values.shape, 1)
    half = HEAD // 2
    from_right = pltpu.roll(values, PAIR - half, axis=1)
    from_left = pltpu.roll(values, half, axis=1)
    return jnp.where(lane % HEAD < half, -from_right, from_left)


def mm(a, b, da, db):
    return lax.dot_general(a, b, (((da,), (db,)), ((), ())), preferred_element_type=f32)


def qkv_kernel(x_ref, w_ref, cos_ref, sin_ref, o_ref):
    which = pl.program_id(1)
    y = mm(x_ref[...], w_ref[...], 1, 0)

    @pl.when(which < 2)
    def _():
        factor = jnp.where(which == 0, HEAD**-0.5, 1.0)
        for p in range(y.shape[1] // PAIR):
            u = y[:, p * PAIR : (p + 1) * PAIR]
            r = u * cos_ref[...] + turned(u) * sin_ref[...]
            o_ref[:, p * PAIR : (p + 1) * PAIR] = (r.astype(bf16) * factor.astype(bf16)).astype(bf16)

    @pl.when(which == 2)
    def _():
        o_ref[...] = y.astype(bf16)


def project_qkv(rows, w_qkv, cosine, sine):
    count, depth = rows.shape
    width = w_qkv.shape[2]
    return pl.pallas_call(
        qkv_kernel,
        grid=(count // ROWS, 3),
        in_specs=[
            pl.BlockSpec((ROWS, depth), lambda r, t: (r, 0)),
            pl.BlockSpec((None, depth, width), lambda r, t: (t, 0, 0)),
            pl.BlockSpec((ROWS, PAIR), lambda r, t: (r, 0)),
            pl.BlockSpec((ROWS, PAIR), lambda r, t: (r, 0)),
        ],
        out_specs=pl.BlockSpec((None, ROWS, width), lambda r, t: (t, r, 0)),
        out_shape=jax.ShapeDtypeStruct((3, count, width), bf16),
        compiler_params=pltpu.CompilerParams(vmem_limit_bytes=32 << 20),
        cost_estimate=pl.CostEstimate(
            flops=6 * count * depth * width, bytes_accessed=8 * count * width, transcendentals=0
        ),
        name="qkv",
    )(rows, w_qkv, cosine, sine)


def head_lanes(block, h):
    lane = lax.broadcasted_iota(jnp.int32, block.shape, 1)
    return jnp.where(lane // HEAD == h, block, jnp.zeros_like(block))


def transposed(block):
    return block.astype(f32).T


def forward_kernel(flag_ref, q_ref, k_ref, v_ref, segr_ref, segc_ref, o_ref, lse_ref, vt, m, l, acc):
    blocks = q_ref.shape[0] // BLOCK
    for b in range(blocks):
        vt[b] = transposed(v_ref[b * BLOCK : (b + 1) * BLOCK, :]).astype(bf16)

    @pl.loop(0, blocks)
    def _(qi):
        rows = pl.ds(pl.multiple_of(qi * BLOCK, BLOCK), BLOCK)
        q = q_ref[rows, :]
        m[...] = jnp.full(m.shape, masked_score, f32)
        l[...] = jnp.zeros(l.shape, f32)
        acc[...] = jnp.zeros(acc.shape, f32)

        @pl.loop(0, blocks)
        def _(ki):
            @pl.when(flag_ref[qi * blocks + ki] > 0)
            def _():
                cols = pl.ds(pl.multiple_of(ki * BLOCK, BLOCK), BLOCK)
                k = k_ref[cols, :]
                docs = segc_ref[cols, :]
                same = jnp.concatenate([docs] * (BLOCK // 128), axis=1) == segr_ref[qi]
                for h in range(2):
                    lo, hi = h * HEAD, (h + 1) * HEAD
                    s = jnp.where(same, mm(k, head_lanes(q, h), 1, 1), masked_score)
                    top = jnp.maximum(m[h], jnp.max(s, axis=0, keepdims=True))
                    p = jnp.exp(s - top)
                    shrink = jnp.exp(m[h] - top)
                    m[h] = top
                    l[h] = l[h] * shrink + jnp.sum(p, axis=0, keepdims=True)
                    acc[lo:hi, :] = acc[lo:hi, :] * shrink + mm(vt[ki, lo:hi, :], p.astype(bf16), 1, 0)

        for h in range(2):
            lo, hi = h * HEAD, (h + 1) * HEAD
            lse_ref[h, qi] = m[h] + jnp.log(l[h])
            acc[lo:hi, :] = acc[lo:hi, :] / l[h]
        o_ref[rows, :] = acc[...].T.astype(bf16)


def backward_kernel(
    flag_ref, q_ref, k_ref, v_ref, g_ref, o_ref, lse_ref, segr_ref, segc_ref, cos_ref, sin_ref,
    out_ref, kt, dk, dv, dq,
):
    blocks = q_ref.shape[0] // BLOCK
    for b in range(blocks):
        kt[b] = transposed(k_ref[b * BLOCK : (b + 1) * BLOCK, :]).astype(bf16)
    dk[...] = jnp.zeros(dk.shape, f32)
    dv[...] = jnp.zeros(dv.shape, f32)

    def turn_back(u, rows):
        return (u * cos_ref[rows, :] - turned(u) * sin_ref[rows, :]).astype(bf16)

    @pl.loop(0, blocks)
    def _(qi):
        rows = pl.ds(pl.multiple_of(qi * BLOCK, BLOCK), BLOCK)
        q, g = q_ref[rows, :], g_ref[rows, :]
        both = (g.astype(f32) * o_ref[rows, :].astype(f32)).T
        dq[...] = jnp.zeros(dq.shape, f32)

        @pl.loop(0, blocks)
        def _(ki):
            @pl.when(flag_ref[qi * blocks + ki] > 0)
            def _():
                cols = pl.ds(pl.multiple_of(ki * BLOCK, BLOCK), BLOCK)
                k, v = k_ref[cols, :], v_ref[cols, :]
                docs = segc_ref[cols, :]
                same = jnp.concatenate([docs] * (BLOCK // 128), axis=1) == segr_ref[qi]
                dk_sum, dv_sum = dk[cols, :], dv[cols, :]
                for h in range(2):
                    lo, hi = h * HEAD, (h + 1) * HEAD
                    delta = jnp.sum(both[lo:hi, :], axis=0, keepdims=True)
                    qh, gh = head_lanes(q, h), head_lanes(g, h)
                    s = jnp.where(same, mm(k, qh, 1, 1), masked_score)
                    p = jnp.exp(s - lse_ref[h, qi])
                    ds = (p * (mm(v, gh, 1, 1) - delta)).astype(bf16)
                    dv_sum = dv_sum + mm(p.astype(bf16), gh, 1, 0)
                    dk_sum = dk_sum + mm(ds, qh, 1, 0)
                    dq[lo:hi, :] = dq[lo:hi, :] + mm(kt[ki, lo:hi, :], ds, 1, 0)
                dk[cols, :] = dk_sum
                dv[cols, :] = dv_sum

        out_ref[0, rows, :] = turn_back(dq[...].T * (HEAD**-0.5), rows)

    @pl.loop(0, blocks)
    def _(b):
        rows = pl.ds(pl.multiple_of(b * BLOCK, BLOCK), BLOCK)
        out_ref[1, rows, :] = turn_back(dk[rows, :], rows)
        out_ref[2, rows, :] = dv[rows, :].astype(bf16)


def pieces_of(qkv, length):
    return [pl.BlockSpec((None, length, PAIR), functools.partial(lambda t, p, *_: (t, 0, p), t)) for t in range(3)]


def attend_forward(flags, qkv, seg_rows, seg_cols):
    _, length, width = qkv.shape
    blocks, pairs = length // BLOCK, width // PAIR
    return pl.pallas_call(
        forward_kernel,
        grid_spec=pltpu.PrefetchScalarGridSpec(
            num_scalar_prefetch=1,
            grid=(pairs,),
            in_specs=[
                *pieces_of(qkv, length),
                pl.BlockSpec((blocks, 1, BLOCK), lambda p, *_: (0, 0, 0)),
                pl.BlockSpec((length, 128), lambda p, *_: (0, 0)),
            ],
            out_specs=[
                pl.BlockSpec((length, PAIR), lambda p, *_: (0, p)),
                pl.BlockSpec((2, blocks, 1, BLOCK), lambda p, *_: (p, 0, 0, 0)),
            ],
            scratch_shapes=[
                pltpu.VMEM((blocks, PAIR, BLOCK), bf16),
                pltpu.VMEM((2, 1, BLOCK), f32),
                pltpu.VMEM((2, 1, BLOCK), f32),
                pltpu.VMEM((PAIR, BLOCK), f32),
            ],
        ),
        out_shape=[
            jax.ShapeDtypeStruct((length, width), bf16),
            jax.ShapeDtypeStruct((2 * pairs, blocks, 1, BLOCK), f32),
        ],
        compiler_params=pltpu.CompilerParams(vmem_limit_bytes=48 << 20),
        cost_estimate=pl.CostEstimate(
            flops=4 * length * length * width, bytes_accessed=8 * length * width, transcendentals=length * length * width // HEAD
        ),
        name="attend",
    )(flags, qkv, qkv, qkv, seg_rows, seg_cols)


def attend_backward(flags, qkv, grad, mixed, lse, seg_rows, seg_cols, cosine, sine):
    _, length, width = qkv.shape
    blocks, pairs = length // BLOCK, width // PAIR
    whole = pl.BlockSpec((length, PAIR), lambda p, *_: (0, p))
    table = pl.BlockSpec((length, PAIR), lambda p, *_: (0, 0))
    return pl.pallas_call(
        backward_kernel,
        grid_spec=pltpu.PrefetchScalarGridSpec(
            num_scalar_prefetch=1,
            grid=(pairs,),
            in_specs=[
                *pieces_of(qkv, length),
                whole,
                whole,
                pl.BlockSpec((2, blocks, 1, BLOCK), lambda p, *_: (p, 0, 0, 0)),
                pl.BlockSpec((blocks, 1, BLOCK), lambda p, *_: (0, 0, 0)),
                table,
                table,
                table,
            ],
            out_specs=pl.BlockSpec((3, length, PAIR), lambda p, *_: (0, 0, p)),
            scratch_shapes=[
                pltpu.VMEM((blocks, PAIR, BLOCK), bf16),
                pltpu.VMEM((length, PAIR), f32),
                pltpu.VMEM((length, PAIR), f32),
                pltpu.VMEM((PAIR, BLOCK), f32),
            ],
        ),
        out_shape=jax.ShapeDtypeStruct((3, length, width), bf16),
        compiler_params=pltpu.CompilerParams(vmem_limit_bytes=56 << 20),
        cost_estimate=pl.CostEstimate(
            flops=10 * length * length * width, bytes_accessed=16 * length * width, transcendentals=length * length * width // HEAD
        ),
        name="attend_back",
    )(flags, qkv, qkv, qkv, grad, mixed, lse, seg_rows, seg_cols, cosine, sine)


def qkv_pair_kernel(own_ref, got_ref, w_ref, cos_ref, sin_ref, *refs):
    o_ref, rows_ref = refs[-2:]
    which = pl.program_id(0)
    half = own_ref.shape[0]

    @pl.when(which == 0)
    def _():
        rows_ref[:half, :] = own_ref[...]
        rows_ref[half:, :] = got_ref[...]

    y = mm(rows_ref[...], w_ref[...], 1, 0)

    @pl.when(which < 2)
    def _():
        factor = jnp.where(which == 0, HEAD**-0.5, 1.0)
        for p in range(y.shape[1] // PAIR):
            u = y[:, p * PAIR : (p + 1) * PAIR]
            r = u * cos_ref[...] + turned(u) * sin_ref[...]
            o_ref[:, p * PAIR : (p + 1) * PAIR] = (r.astype(bf16) * factor.astype(bf16)).astype(bf16)

    @pl.when(which == 2)
    def _():
        o_ref[...] = y.astype(bf16)


def project_pair(j, own, got, w_qkv, cosine, sine, before, length):
    half, depth = own.shape
    width = w_qkv.shape[2]
    chunk = 2 * half
    table = pl.BlockSpec((chunk, PAIR), lambda t: (j, 0))
    return pl.pallas_call(
        qkv_pair_kernel,
        grid=(3,),
        in_specs=[
            pl.BlockSpec((half, depth), lambda t: (0, 0)),
            pl.BlockSpec((half, depth), lambda t: (0, 0)),
            pl.BlockSpec((None, depth, width), lambda t: (t, 0, 0)),
            table,
            table,
            *[pl.BlockSpec(memory_space=pl.ANY) for _ in before],
        ],
        out_specs=[
            pl.BlockSpec((None, chunk, width), lambda t: (t, j, 0)),
            pl.BlockSpec((chunk, depth), lambda t: (j, 0)),
        ],
        out_shape=[
            jax.ShapeDtypeStruct((3, length, width), bf16),
            jax.ShapeDtypeStruct((length, depth), bf16),
        ],
        input_output_aliases={5 + i: i for i in range(len(before))},
        compiler_params=pltpu.CompilerParams(vmem_limit_bytes=32 << 20),
        cost_estimate=pl.CostEstimate(
            flops=6 * chunk * depth * width, bytes_accessed=8 * depth * width, transcendentals=0
        ),
        name="qkv",
    )(own, got, w_qkv, cosine, sine, *before)


def forward_chunk_kernel(q_ref, k_ref, v_ref, segr_ref, segc_ref, o_ref, lse_ref, vt):
    length, count = k_ref.shape[0], q_ref.shape[0]
    for b in range(0, length, BLOCK):
        vt[:, b : b + BLOCK] = transposed(v_ref[b : b + BLOCK, :]).astype(bf16)
    q = q_ref[...]
    outs = []
    for h in range(2):
        qh = head_lanes(q, h)
        scores = []
        for b in range(0, length, BLOCK):
            same = jnp.concatenate([segc_ref[b : b + BLOCK, :]] * (count // 128), axis=1) == segr_ref[...]
            scores.append(jnp.where(same, mm(k_ref[b : b + BLOCK, :], qh, 1, 1), masked_score))
        top = functools.reduce(jnp.maximum, [jnp.max(s, axis=0, keepdims=True) for s in scores])
        total, summed = 0.0, 0.0
        for i, s in enumerate(scores):
            p = jnp.exp(s - top)
            total = total + jnp.sum(p, axis=0, keepdims=True)
            summed = summed + mm(vt[h * HEAD : (h + 1) * HEAD, i * BLOCK : (i + 1) * BLOCK], p.astype(bf16), 1, 0)
        lse_ref[h] = top + jnp.log(total)
        outs.append(summed / total)
    o_ref[...] = jnp.concatenate(outs, axis=0).T.astype(bf16)


def pair_pieces(j, length, chunk):
    return [
        pl.BlockSpec((None, chunk, PAIR), lambda p: (0, j, p)),
        pl.BlockSpec((None, length, PAIR), lambda p: (1, 0, p)),
        pl.BlockSpec((None, length, PAIR), lambda p: (2, 0, p)),
    ]


def attend_forward_pair(j, chunk, qkv, seg_rows, seg_cols):
    _, length, width = qkv.shape
    pairs = width // PAIR
    return pl.pallas_call(
        forward_chunk_kernel,
        grid=(pairs,),
        in_specs=[
            *pair_pieces(j, length, chunk),
            pl.BlockSpec((1, chunk), lambda p: (0, j)),
            pl.BlockSpec((length, 128), lambda p: (0, 0)),
        ],
        out_specs=[
            pl.BlockSpec((chunk, PAIR), lambda p: (0, p)),
            pl.BlockSpec((2, 1, chunk), lambda p: (p, 0, 0)),
        ],
        out_shape=[
            jax.ShapeDtypeStruct((chunk, width), bf16),
            jax.ShapeDtypeStruct((2 * pairs, 1, chunk), f32),
        ],
        scratch_shapes=[pltpu.VMEM((PAIR, length), bf16)],
        compiler_params=pltpu.CompilerParams(vmem_limit_bytes=48 << 20),
        cost_estimate=pl.CostEstimate(
            flops=16 * chunk * length * width,
            bytes_accessed=8 * length * width,
            transcendentals=chunk * length * width // HEAD,
        ),
        name="attend",
    )(qkv, qkv, qkv, seg_rows, seg_cols)


def backward_chunk_kernel(
    last, q_ref, k_ref, v_ref, g_ref, o_ref, lse_ref, segr_ref, segc_ref, cos_ref, sin_ref, cos_all, sin_all, *refs
):
    if last:
        dk_in, dv_in, _, dq_ref, dk_ref, dv_ref, kt, dk, dv = refs
        dk[...] = dk_in[...]
        dv[...] = dv_in[...]
    else:
        dq_ref, dk, dv, kt = refs
        dk[...] = jnp.zeros(dk.shape, f32)
        dv[...] = jnp.zeros(dv.shape, f32)
    length, count = k_ref.shape[0], q_ref.shape[0]
    for b in range(0, length, BLOCK):
        kt[:, b : b + BLOCK] = transposed(k_ref[b : b + BLOCK, :]).astype(bf16)
    q, g = q_ref[...], g_ref[...]
    both = (g.astype(f32) * o_ref[...].astype(f32)).T
    qh = [head_lanes(q, h) for h in range(2)]
    gh = [head_lanes(g, h) for h in range(2)]
    delta = [jnp.sum(both[h * HEAD : (h + 1) * HEAD, :], axis=0, keepdims=True) for h in range(2)]
    q_two, g_two = jnp.concatenate(qh, axis=0), jnp.concatenate(gh, axis=0)
    dq = [0.0, 0.0]
    for b in range(0, length, BLOCK):
        cols = slice(b, b + BLOCK)
        k, v = k_ref[cols, :], v_ref[cols, :]
        same = jnp.concatenate([segc_ref[cols, :]] * (count // 128), axis=1) == segr_ref[...]
        ps, ds = [], []
        for h in range(2):
            s = jnp.where(same, mm(k, qh[h], 1, 1), masked_score)
            p = jnp.exp(s - lse_ref[h])
            d = (p * (mm(v, gh[h], 1, 1) - delta[h])).astype(bf16)
            ps.append(p.astype(bf16))
            ds.append(d)
            dq[h] = dq[h] + mm(kt[h * HEAD : (h + 1) * HEAD, cols], d, 1, 0)
        dv[cols, :] += mm(jnp.concatenate(ps, axis=1), g_two, 1, 0)
        dk[cols, :] += mm(jnp.concatenate(ds, axis=1), q_two, 1, 0)

    def turn_back(u, cosine, sine):
        return (u * cosine - turned(u) * sine).astype(bf16)

    dq_ref[...] = turn_back(jnp.concatenate(dq, axis=0).T * (HEAD**-0.5), cos_ref[...], sin_ref[...])
    if last:
        for b in range(0, length, BLOCK):
            rows = slice(b, b + BLOCK)
            dk_ref[rows, :] = turn_back(dk[rows, :], cos_all[rows, :], sin_all[rows, :])
            dv_ref[rows, :] = dv[rows, :].astype(bf16)


def attend_backward_pair(j, chunk, qkv, grad, mixed, lse, seg_rows, seg_cols, cosine, sine, before):
    _, length, width = qkv.shape
    pairs = width // PAIR
    last = bool(before)
    whole = pl.BlockSpec((length, PAIR), lambda p: (0, p))
    part = pl.BlockSpec((chunk, PAIR), lambda p: (0, p))
    table = pl.BlockSpec((chunk, PAIR), lambda p: (j, 0))
    table_all = pl.BlockSpec((length, PAIR), lambda p: (0, 0))
    dq_before = before[:1]
    return pl.pallas_call(
        functools.partial(backward_chunk_kernel, last),
        grid=(pairs,),
        in_specs=[
            *pair_pieces(j, length, chunk),
            part,
            part,
            pl.BlockSpec((2, 1, chunk), lambda p: (p, 0, 0)),
            pl.BlockSpec((1, chunk), lambda p: (0, j)),
            table_all,
            table,
            table,
            table_all,
            table_all,
            *([whole, whole, pl.BlockSpec(memory_space=pl.ANY)] if last else []),
        ],
        out_specs=[pl.BlockSpec((chunk, PAIR), lambda p: (j, p)), whole, whole],
        out_shape=[
            jax.ShapeDtypeStruct((length, width), bf16),
            jax.ShapeDtypeStruct((length, width), bf16 if last else f32),
            jax.ShapeDtypeStruct((length, width), bf16 if last else f32),
        ],
        scratch_shapes=[
            pltpu.VMEM((PAIR, length), bf16),
            *([pltpu.VMEM((length, PAIR), f32)] * 2 if last else []),
        ],
        input_output_aliases={14: 0} if last else {},
        compiler_params=pltpu.CompilerParams(vmem_limit_bytes=56 << 20),
        cost_estimate=pl.CostEstimate(
            flops=40 * chunk * length * width,
            bytes_accessed=16 * length * width,
            transcendentals=chunk * length * width // HEAD,
        ),
        name="attend_back",
    )(
        qkv, qkv, qkv, grad, mixed, lse, seg_rows, seg_cols, cosine, sine, cosine, sine,
        *((*before[1:], *dq_before) if last else ()),
    )


def mlp_kernel(own_ref, got_ref, b_own_ref, b_got_ref, up_ref, bias_ref, down_ref, *refs):
    rows_ref, hidden_ref, pre_ref, own_grad, got_grad, own_branch, got_branch, bias_grad, grads, branch = refs[-10:]
    tile, tiles = pl.program_id(0), pl.num_programs(0)
    half = own_ref.shape[0]

    @pl.when(tile == 0)
    def _():
        rows_ref[:half, :] = own_ref[...]
        rows_ref[half:, :] = got_ref[...]

    up, down = up_ref[...], down_ref[...]
    cubic, root = 0.044715, (2.0 / jnp.pi) ** 0.5
    for part in range(2):
        rows = slice(part * half, (part + 1) * half)
        back = (b_own_ref, b_got_ref)[part]
        u = mm((own_ref, got_ref)[part][...], up, 1, 0) + bias_ref[...]
        square = u * u
        t = jnp.tanh(root * u * (1.0 + cubic * square))
        hidden = (0.5 * u * (1.0 + t)).astype(bf16)
        slope = 0.5 * (1.0 + t) + 0.5 * u * (1.0 - t * t) * (root * (1.0 + 3.0 * cubic * square))
        grad = mm(back[...], down, 1, 1) * slope
        grad_low = grad.astype(bf16)
        hidden_ref[rows, :] = hidden
        pre_ref[rows, :] = grad_low
        total = jnp.sum(grad_low.astype(f32), axis=0, keepdims=True)
        more, more_branch = mm(grad_low, up, 1, 1), mm(hidden, down, 1, 0)

        @pl.when(tile == 0)
        def _():
            grads[rows, :] = more
            branch[rows, :] = more_branch

        @pl.when(tile > 0)
        def _():
            grads[rows, :] += more
            branch[rows, :] += more_branch

        if part == 0:
            bias_grad[...] = total
        else:
            bias_grad[...] += total

    @pl.when(tile == tiles - 1)
    def _():
        own_grad[...] = grads[:half, :]
        got_grad[...] = grads[half:, :].astype(bf16)
        own_branch[...] = branch[:half, :]
        got_branch[...] = branch[half:, :].astype(bf16)


def mlp_pair(j, own, got, back_own, back_got, w_up, b_up, w_down, before, length):
    half, depth = own.shape
    width = w_up.shape[1]
    chunk, tile = 2 * half, 512
    small = pl.BlockSpec((half, depth), lambda t: (0, 0))
    wide = pl.BlockSpec((chunk, tile), lambda t: (j, t))
    return pl.pallas_call(
        mlp_kernel,
        grid=(width // tile,),
        in_specs=[
            small, small, small, small,
            pl.BlockSpec((depth, tile), lambda t: (0, t)),
            pl.BlockSpec((1, tile), lambda t: (0, t)),
            pl.BlockSpec((tile, depth), lambda t: (t, 0)),
            *[pl.BlockSpec(memory_space=pl.ANY) for _ in before],
        ],
        out_specs=[
            pl.BlockSpec((chunk, depth), lambda t: (j, 0)), wide, wide,
            small, small, small, small,
            pl.BlockSpec((1, tile), lambda t: (0, t)),
        ],
        out_shape=[
            jax.ShapeDtypeStruct((length, depth), bf16),
            jax.ShapeDtypeStruct((length, width), bf16),
            jax.ShapeDtypeStruct((length, width), bf16),
            jax.ShapeDtypeStruct((half, depth), f32),
            jax.ShapeDtypeStruct((half, depth), bf16),
            jax.ShapeDtypeStruct((half, depth), f32),
            jax.ShapeDtypeStruct((half, depth), bf16),
            jax.ShapeDtypeStruct((1, width), f32),
        ],
        scratch_shapes=[pltpu.VMEM((chunk, depth), f32), pltpu.VMEM((chunk, depth), f32)],
        input_output_aliases={7 + i: i for i in range(len(before))},
        compiler_params=pltpu.CompilerParams(vmem_limit_bytes=56 << 20),
        cost_estimate=pl.CostEstimate(
            flops=12 * chunk * depth * width, bytes_accessed=12 * depth * width, transcendentals=chunk * width
        ),
        name="mlp",
    )(own, got, back_own, back_got, w_up, b_up[None, :], w_down, *before)


def qkv_back_kernel(q_ref, k_ref, v_ref, w_ref, o_ref):
    total = mm(q_ref[...], w_ref[0], 1, 1) + mm(k_ref[...], w_ref[1], 1, 1) + mm(v_ref[...], w_ref[2], 1, 1)
    o_ref[...] = total.astype(o_ref.dtype)


def project_back_pair(part, half, dq, dk, dv, w_qkv, kind):
    length, width = dq.shape
    depth = w_qkv.shape[1]
    block = pl.BlockSpec((half, width), lambda c: (2 * c + part, 0))
    return pl.pallas_call(
        qkv_back_kernel,
        grid=(length // (2 * half),),
        in_specs=[block, block, block, pl.BlockSpec((3, depth, width), lambda c: (0, 0, 0))],
        out_specs=pl.BlockSpec((half, depth), lambda c: (c, 0)),
        out_shape=jax.ShapeDtypeStruct((length // 2, depth), kind),
        compiler_params=pltpu.CompilerParams(vmem_limit_bytes=32 << 20),
        cost_estimate=pl.CostEstimate(
            flops=3 * length * depth * width, bytes_accessed=6 * depth * width, transcendentals=0
        ),
        name="qkv_back",
    )(dq, dk, dv, w_qkv)


MESH = pl.DeviceIdType.MESH
ADD_ROWS = 32


def add_low(out, out_at, a, a_at, b, rows):
    @pl.loop(0, rows // ADD_ROWS)
    def _(i):
        at = pl.multiple_of(i * ADD_ROWS, ADD_ROWS)
        total = a[pl.ds(pl.multiple_of(a_at + at, ADD_ROWS), ADD_ROWS), :].astype(f32)
        total = total + b[pl.ds(at, ADD_ROWS), :].astype(f32)
        out[pl.ds(pl.multiple_of(out_at + at, ADD_ROWS), ADD_ROWS), :] = total.astype(bf16)


class Unit:
    def __init__(self, part, out, row, rows, held, got, send, recv, local, place):
        self.part, self.out, self.row, self.rows = part, out, row, rows
        self.held, self.got, self.send, self.recv, self.local = held, got, send, recv, local
        self.bit = [(place // (1 << b)) % 2 for b in range(4)]
        self.partner = [place + (1 - 2 * self.bit[b]) * (1 << b) for b in range(4)]
        self.base = [row]
        for b in range(4):
            self.base.append(self.base[-1] + self.bit[b] * (rows >> (b + 1)))

    def remote(self, src, dst, stage, b):
        return pltpu.make_async_remote_copy(
            src_ref=src,
            dst_ref=dst,
            send_sem=self.send.at[stage],
            recv_sem=self.recv.at[stage],
            device_id={"dp": self.partner[b]},
            device_id_type=MESH,
        )

    def at(self, start, rows):
        return pl.ds(pl.multiple_of(start, ADD_ROWS), rows)

    def halving(self, b):
        half = self.rows >> (b + 1)
        if b == 0:
            src = self.part.at[self.at(self.row + (1 - self.bit[0]) * half, half)]
        else:
            src = self.held[b - 1].at[self.at((1 - self.bit[b]) * half, half)]
        return self.remote(src, self.got[b], b, b)

    def keep(self):
        half = self.rows // 2
        return pltpu.make_async_copy(
            self.part.at[self.at(self.row + self.bit[0] * half, half)], self.held[0], self.local.at[0]
        )

    def own(self):
        return pltpu.make_async_copy(
            self.held[3], self.out.at[self.at(self.base[4], self.rows >> 4)], self.local.at[1]
        )

    def gathering(self, b):
        size = self.rows >> (b + 1)
        spot = self.out.at[self.at(self.base[b + 1], size)]
        return self.remote(self.held[3] if b == 3 else spot, spot, 7 - b, b)

    def step(self, k):
        if k == 0:
            self.halving(0).start()
            self.keep().start()
        elif k == 1:
            self.halving(0).wait()
            self.keep().wait()
            add_low(self.held[0], 0, self.held[0], 0, self.got[0], self.rows // 2)
            self.halving(1).start()
        elif k < 5:
            b = k - 1
            self.halving(b).wait()
            half = self.rows >> (b + 1)
            add_low(self.held[b], 0, self.held[b - 1], self.bit[b] * half, self.got[b], half)
            if b < 3:
                self.halving(b + 1).start()
            else:
                self.own().start()
                self.gathering(3).start()
        elif k == 5:
            self.own().wait()
            self.gathering(3).wait()
            self.gathering(2).start()
        elif k < 8:
            self.gathering(8 - k).wait()
            self.gathering(7 - k).start()
        else:
            self.gathering(0).wait()


STEPS = 9


def greet(targets):
    barrier = pltpu.get_barrier_semaphore()
    for target in targets:
        pl.semaphore_signal(barrier, inc=1, device_id=target, device_id_type=MESH)
    pl.semaphore_wait(barrier, len(targets))


def reduce_kernel(cuts, arrays, *refs):
    parts, outs, scratch = refs[:arrays], refs[arrays : 2 * arrays], refs[2 * arrays :]
    place = lax.axis_index("dp")
    units = []
    for i, (which, row, rows) in enumerate(cuts):
        mine = scratch[11 * i : 11 * (i + 1)]
        units.append(Unit(parts[which], outs[which], row, rows, mine[:4], mine[4:8], *mine[8:], place))
    greet([{"dp": partner} for partner in units[0].partner])
    late = [0, 1, 3, 5, 7, 8, 9, 11, 13]
    order = sorted((late[k] + 2 * i, k, i) for i in range(len(units)) for k in range(STEPS))
    for _, k, i in order:
        units[i].step(k)


def unit_scratch(rows, columns):
    return [
        *[pltpu.VMEM((rows >> (b + 1), columns), bf16) for b in range(4)],
        *[pltpu.VMEM((rows >> (b + 1), columns), bf16) for b in range(4)],
        pltpu.SemaphoreType.DMA((8,)),
        pltpu.SemaphoreType.DMA((8,)),
        pltpu.SemaphoreType.DMA((2,)),
    ]


def reduce_over_dp(parts, cuts):
    scratch = []
    for which, _, rows in cuts:
        scratch += unit_scratch(rows, parts[which].shape[1])
    anywhere = pl.BlockSpec(memory_space=pl.ANY)
    return pl.pallas_call(
        functools.partial(reduce_kernel, cuts, len(parts)),
        in_specs=[anywhere] * len(parts),
        out_specs=[anywhere] * len(parts),
        out_shape=[jax.ShapeDtypeStruct(p.shape, p.dtype) for p in parts],
        scratch_shapes=scratch,
        compiler_params=pltpu.CompilerParams(collective_id=1, has_side_effects=True, vmem_limit_bytes=40 << 20),
        name="reduce",
    )(*parts)


def body_pair(
    tokens, cond, doc_lengths, w_ada, b_ada, gain_one, w_qkv, w_out, gain_two, w_up, b_up, w_down, b_down, cotangent
):
    dp_size = lax.axis_size("dp")
    bits = dp_size.bit_length() - 1
    own, width = tokens.shape
    length = 2 * own
    chunks = 2
    half, chunk = own // chunks, length // chunks
    me = lax.axis_index("tensor")

    def swap(values):
        return lax.ppermute(values, "tensor", [(0, 1), (1, 0)])

    def across(values, b):
        return lax.ppermute(values, "dp", [(d, d ^ (1 << b)) for d in range(dp_size)])

    def gathered(row):
        for b in reversed(range(bits)):
            row = jnp.concatenate([row, across(row, b)], axis=0)
        return row

    step = jnp.arange(length, dtype=jnp.int32)
    in_chunk = step % chunk
    places = jnp.where(in_chunk < half, me, 1 - me) * own + (step // chunk) * half + in_chunk % half
    segment, doc_first = documents(doc_lengths[0], places)
    cosine, sine = rope_tables(places - doc_first)
    seg_rows = segment[None, :]
    seg_cols = jnp.broadcast_to(segment[:, None], (length, 128))

    modulation = jnp.dot(cond, w_ada, preferred_element_type=f32)[0] + b_ada
    shift_a, scale_a, gate_a, shift_m, scale_m, gate_m = jnp.split(modulation, 6)
    cuts = [slice(c * half, (c + 1) * half) for c in range(chunks)]
    x_rows = [tokens[cut].astype(f32) for cut in cuts]
    grad_out = [cotangent[cut].astype(f32) for cut in cuts]
    each = range(chunks)

    act_one = [modulate(x_rows[c], gain_one, shift_a, scale_a).astype(bf16) for c in each]
    got_one = [swap(act_one[c]) for c in each]
    back = [(grad_out[c] * gate_m).astype(bf16) for c in each]
    state = ()
    for c in each:
        state = project_pair(c, act_one[c], got_one[c], w_qkv, cosine, sine, state, length)
    qkv, rows_one = state
    got_back = [swap(back[c]) for c in each]
    full_back = jnp.concatenate([piece for c in each for piece in (back[c], got_back[c])], axis=0)

    mixed, lse, projected, middle, act_two, got_two = [], [], [], [], [], []
    for c in each:
        m, l = attend_forward_pair(c, chunk, qkv, seg_rows, seg_cols)
        mixed.append(m)
        lse.append(l)
    sums = [swap(jnp.dot(mixed[c][half:], w_out, preferred_element_type=f32).astype(bf16)) for c in each]
    for c in each:
        projected.append(jnp.dot(mixed[c][:half], w_out, preferred_element_type=f32) + sums[c].astype(f32))
        middle.append(x_rows[c] + gate_a * projected[c])
        act_two.append(modulate(middle[c], gain_two, shift_m, scale_m).astype(bf16))
        got_two.append(swap(act_two[c]))
    state, pieces = (), []
    for c in each:
        out = mlp_pair(c, act_two[c], got_two[c], back[c], got_back[c], w_up, b_up, w_down, state, length)
        state, rest = out[:3], out[3:]
        pieces.append(rest)
    rows_two, hidden, grad_pre = state
    grad_b_up = sum(pieces[c][4] for c in each)[0]
    grad_act_two = [pieces[c][0] + swap(pieces[c][1]).astype(f32) for c in each]
    grad_w_down = mm(hidden, full_back, 0, 0).astype(bf16)
    grad_w_up = mm(rows_two, grad_pre, 0, 0).astype(bf16)

    vectors, grad_middle, full_proj, grad_mixed = [], [], [], []
    for c in each:
        _, second_back = jax.vjp(modulate, middle[c], gain_two, shift_m, scale_m)
        grad, grad_gain_two, grad_shift_m, grad_scale_m = second_back(grad_act_two[c])
        grad_middle.append(grad + grad_out[c])
        vectors.append([grad_gain_two, grad_shift_m, grad_scale_m])
        proj = (grad_middle[c] * gate_a).astype(bf16)
        full_proj.append(jnp.concatenate([proj, swap(proj)], axis=0))
        grad_mixed.append(mm(full_proj[c], w_out, 1, 1).astype(bf16))
    grad_gain_two, grad_shift_m, grad_scale_m = [sum(parts) for parts in zip(*vectors)]
    branch = [pieces[c][2] + swap(pieces[c][3]).astype(f32) + b_down for c in each]
    output = jnp.concatenate([(middle[c] + gate_m * branch[c]).astype(bf16) for c in each], axis=0)
    grad_gate_m = sum(jnp.sum(grad_out[c] * branch[c], axis=0) for c in each)
    grad_b_down = sum(jnp.sum(back[c].astype(f32), axis=0) for c in each)
    grad_gate_a = sum(jnp.sum(grad_middle[c] * projected[c], axis=0) for c in each)

    grads = ()
    for c in each:
        grads = attend_backward_pair(
            c, chunk, qkv, grad_mixed[c], mixed[c], lse[c], seg_rows, seg_cols, cosine, sine, grads
        )
    grad_w_out = sum(mm(mixed[c], full_proj[c], 0, 0) for c in each).astype(bf16)
    for_other = swap(project_back_pair(1, half, *grads, w_qkv, bf16))
    grad_act_one = project_back_pair(0, half, *grads, w_qkv, f32) + for_other.astype(f32)
    grad_w_qkv = [mm(rows_one, grads[t], 0, 0).astype(bf16) for t in range(3)]
    depth, wide = w_up.shape
    cuts = (
        (0, 0, wide // 2), (0, wide // 2, wide // 2), (1, 0, depth // 2), (1, depth // 2, depth // 2),
        (2, 0, w_out.shape[0]), (3, 0, depth), (4, 0, depth), (5, 0, depth),
    )
    reduced = reduce_over_dp((grad_w_down, grad_w_up, grad_w_out, *grad_w_qkv), cuts)
    grad_w_down, grad_w_up, grad_w_out, *grad_w_qkv = [r.astype(f32) for r in reduced]
    grad_w_qkv = jnp.stack(grad_w_qkv)

    x_all = tokens.astype(f32)
    _, first_back = jax.vjp(modulate, x_all, gain_one, shift_a, scale_a)
    grad_x, grad_gain_one, grad_shift_a, grad_scale_a = first_back(grad_act_one)
    grad_x = (grad_x + jnp.concatenate(grad_middle, axis=0)).astype(bf16)

    small = jnp.concatenate(
        [
            grad_shift_a, grad_scale_a, grad_gate_a, grad_shift_m, grad_scale_m, grad_gate_m,
            grad_gain_one, grad_gain_two, grad_b_down,
        ]
    )[None, :]
    small = small + swap(small)
    mod_size = modulation.shape[0]
    grad_mod = small[0, :mod_size]
    grad_cond = jnp.dot(w_ada.astype(f32), grad_mod, precision=lax.Precision.HIGHEST)[None, :]
    everyone = gathered(jnp.concatenate([small, grad_b_up[None, :], cond.astype(f32)], axis=1))
    conds = everyone[:, -cond.shape[1] :]
    mods = everyone[:, :mod_size]
    grad_w_ada = jnp.einsum("nc,nm->cm", conds, mods, precision=lax.Precision.HIGHEST, preferred_element_type=f32)
    sums = jnp.sum(everyone, axis=0)
    grad_b_ada = sums[:mod_size]
    grad_gain_one, grad_gain_two, grad_b_down = jnp.split(sums[mod_size : mod_size + 3 * width], 3)
    grad_b_up = sums[mod_size + 3 * width : -cond.shape[1]]
    return (
        output, grad_x, grad_cond, grad_w_ada, grad_b_ada, grad_gain_one, grad_w_qkv, grad_w_out, grad_gain_two,
        grad_w_up, grad_b_up, grad_w_down, grad_b_down,
    )


def body_any(
    tokens, cond, doc_lengths, w_ada, b_ada, gain_one, w_qkv, w_out, gain_two, w_up, b_up, w_down, b_down, cotangent
):
    tensor_size = lax.axis_size("tensor")
    own = tokens.shape[0]
    length = own * tensor_size

    def all_rows(values):
        return lax.all_gather(values, "tensor", axis=0, tiled=True)

    def own_sum(values):
        return lax.psum_scatter(values, "tensor", scatter_dimension=0, tiled=True)

    def sum_over_dp(part):
        return lax.psum(part, "dp")

    places = jnp.arange(length, dtype=jnp.int32)
    segment, doc_first = documents(doc_lengths[0], places)
    cosine, sine = rope_tables(places - doc_first)
    blocks = length // BLOCK
    in_blocks = segment.reshape(blocks, BLOCK)
    least, most = jnp.min(in_blocks, axis=1), jnp.max(in_blocks, axis=1)
    meets = (least[:, None] <= most[None, :]) & (least[None, :] <= most[:, None])
    flags = meets.astype(jnp.int32).reshape(-1)
    seg_rows = in_blocks[:, None, :]
    seg_cols = jnp.broadcast_to(segment[:, None], (length, 128))

    modulation = jnp.dot(cond, w_ada, preferred_element_type=f32)[0] + b_ada
    shift_a, scale_a, gate_a, shift_m, scale_m, gate_m = jnp.split(modulation, 6)
    x_rows = tokens.astype(f32)
    grad_out = cotangent.astype(f32)

    act_one = modulate(x_rows, gain_one, shift_a, scale_a).astype(bf16)
    rows_one = all_rows(act_one)
    grad_branch = (grad_out * gate_m).astype(bf16)
    full_branch = all_rows(grad_branch)
    qkv = project_qkv(rows_one, w_qkv, cosine, sine)
    mixed, lse = attend_forward(flags, qkv, seg_rows, seg_cols)
    projected = own_sum(jnp.dot(mixed, w_out, preferred_element_type=f32))
    middle = x_rows + gate_a * projected
    rows_two = all_rows(modulate(middle, gain_two, shift_m, scale_m).astype(bf16))
    pre_act = jnp.dot(rows_two, w_up, preferred_element_type=f32) + b_up
    hidden = jax.nn.gelu(pre_act, approximate=True).astype(bf16)

    grad_hidden = jnp.einsum("sd,fd->sf", full_branch, w_down, preferred_element_type=f32)
    _, gelu_back = jax.vjp(lambda values: jax.nn.gelu(values, approximate=True), pre_act)
    grad_pre = gelu_back(grad_hidden)[0].astype(bf16)
    grad_act_two = own_sum(jnp.einsum("sf,df->sd", grad_pre, w_up, preferred_element_type=f32))
    grad_w_down = sum_over_dp(jnp.einsum("sf,sd->fd", hidden, full_branch, preferred_element_type=f32))
    grad_w_up = sum_over_dp(jnp.einsum("sd,sf->df", rows_two, grad_pre, preferred_element_type=f32))

    branch = own_sum(jnp.dot(hidden, w_down, preferred_element_type=f32)) + b_down
    output = (middle + gate_m * branch).astype(bf16)
    grad_gate_m = jnp.sum(grad_out * branch, axis=0)
    grad_b_down = jnp.sum(grad_branch.astype(f32), axis=0)
    grad_b_up = jnp.sum(grad_pre.astype(f32), axis=0)

    _, second_back = jax.vjp(modulate, middle, gain_two, shift_m, scale_m)
    grad_middle, grad_gain_two, grad_shift_m, grad_scale_m = second_back(grad_act_two)
    grad_middle = grad_middle + grad_out
    full_proj = all_rows((grad_middle * gate_a).astype(bf16))
    grad_gate_a = jnp.sum(grad_middle * projected, axis=0)
    grad_mixed = jnp.einsum("sd,ed->se", full_proj, w_out, preferred_element_type=f32).astype(bf16)
    grad_w_out = sum_over_dp(jnp.einsum("se,sd->ed", mixed, full_proj, preferred_element_type=f32))
    grad_qkv = attend_backward(flags, qkv, grad_mixed, mixed, lse, seg_rows, seg_cols, cosine, sine)
    grad_act_one = own_sum(jnp.einsum("tse,tde->sd", grad_qkv, w_qkv, preferred_element_type=f32))
    grad_w_qkv = jnp.einsum("sd,tse->tde", rows_one, grad_qkv, preferred_element_type=f32)
    grad_w_qkv = sum_over_dp(grad_w_qkv.reshape(-1, grad_w_qkv.shape[2])).reshape(grad_w_qkv.shape)

    _, first_back = jax.vjp(modulate, x_rows, gain_one, shift_a, scale_a)
    grad_x, grad_gain_one, grad_shift_a, grad_scale_a = first_back(grad_act_one)
    grad_x = (grad_x + grad_middle).astype(bf16)

    small = jnp.concatenate(
        [
            grad_shift_a, grad_scale_a, grad_gate_a, grad_shift_m, grad_scale_m, grad_gate_m,
            grad_gain_one, grad_gain_two, grad_b_down,
        ]
    )
    small = lax.psum(small, "tensor")
    mod_size = modulation.shape[0]
    grad_mod = small[:mod_size]
    grad_cond = jnp.dot(w_ada.astype(f32), grad_mod, precision=lax.Precision.HIGHEST)[None, :]
    everyone = lax.all_gather(
        jnp.concatenate([small, grad_b_up, cond[0].astype(f32)])[None, :], "dp", axis=0, tiled=True
    )
    conds = everyone[:, -cond.shape[1] :]
    mods = everyone[:, :mod_size]
    grad_w_ada = jnp.einsum("nc,nm->cm", conds, mods, precision=lax.Precision.HIGHEST, preferred_element_type=f32)
    sums = jnp.sum(everyone, axis=0)
    width = tokens.shape[1]
    grad_b_ada = sums[:mod_size]
    grad_gain_one, grad_gain_two, grad_b_down = jnp.split(sums[mod_size : mod_size + 3 * width], 3)
    grad_b_up = sums[mod_size + 3 * width : -cond.shape[1]]
    return (
        output, grad_x, grad_cond, grad_w_ada, grad_b_ada, grad_gain_one, grad_w_qkv, grad_w_out, grad_gain_two,
        grad_w_up, grad_b_up, grad_w_down, grad_b_down,
    )


def solution(mesh):
    swaps = mesh.shape["tensor"] == 2 and mesh.shape["dp"] == 16
    placed = (
        P(("dp", "tensor"), None), P("dp", None), P("dp", None), P(), P(), P(), P(None, None, "tensor"),
        P("tensor", None), P(), P(None, "tensor"), P("tensor"), P("tensor", None), P(), P(("dp", "tensor"), None),
    )
    return jax.shard_map(
        body_pair if swaps else body_any,
        mesh=mesh,
        in_specs=placed,
        out_specs=(
            P(("dp", "tensor"), None), P(("dp", "tensor"), None), P("dp", None), P(), P(), P(),
            P(None, None, "tensor"), P("tensor", None), P(), P(None, "tensor"), P("tensor"), P("tensor", None), P(),
        ),
        check_vma=False,
    )
```

```python
import functools

import jax
import jax.numpy as jnp
from jax import lax
from jax.experimental import pallas as pl
from jax.experimental.pallas import tpu as pltpu
from jax.sharding import PartitionSpec as P

HEAD = 64
PAIR = 2 * HEAD
BLOCK = 256
ROWS = 512

norm_eps = 1e-05
rope_base = 10000.0
masked_score = -1e30
f32, bf16 = jnp.float32, jnp.bfloat16


def layer_norm(values, gain):
    center = values - jnp.mean(values, axis=-1, keepdims=True)
    spread = jnp.mean(center * center, axis=-1, keepdims=True)
    return center * lax.rsqrt(spread + norm_eps) * gain


def modulate(values, gain, shift, scale):
    return layer_norm(values, gain) * (1.0 + scale) + shift


def documents(lengths, places):
    numbers = jnp.arange(lengths.shape[0], dtype=jnp.int32)
    earlier = (numbers[None, :] < numbers[:, None]).astype(jnp.int32)
    starts = jnp.sum(earlier * lengths[None, :], axis=1)
    ends = starts + lengths
    inside = ((places[:, None] >= starts[None, :]) & (places[:, None] < ends[None, :])).astype(
        jnp.int32
    )
    segment = jnp.sum(inside * numbers[None, :], axis=1)
    doc_first = jnp.sum(inside * starts[None, :], axis=1)
    return segment, doc_first


def rope_tables(offsets):
    exponent = jnp.arange(HEAD // 2, dtype=f32) * (2.0 / HEAD)
    frequency = jnp.power(jnp.float32(rope_base), -exponent)
    angles = offsets.astype(f32)[:, None] * frequency[None, :]
    cosine, sine = jnp.cos(angles), jnp.sin(angles)
    repeat = PAIR // (HEAD // 2)
    return jnp.concatenate([cosine] * repeat, axis=-1), jnp.concatenate([sine] * repeat, axis=-1)


def turned(values):
    lane = lax.broadcasted_iota(jnp.int32, values.shape, 1)
    half = HEAD // 2
    from_right = pltpu.roll(values, PAIR - half, axis=1)
    from_left = pltpu.roll(values, half, axis=1)
    return jnp.where(lane % HEAD < half, -from_right, from_left)


def mm(a, b, da, db):
    return lax.dot_general(a, b, (((da,), (db,)), ((), ())), preferred_element_type=f32)


def qkv_kernel(x_ref, w_ref, cos_ref, sin_ref, o_ref):
    which = pl.program_id(1)
    y = mm(x_ref[...], w_ref[...], 1, 0)

    @pl.when(which < 2)
    def _():
        factor = jnp.where(which == 0, HEAD**-0.5, 1.0)
        for p in range(y.shape[1] // PAIR):
            u = y[:, p * PAIR : (p + 1) * PAIR]
            r = u * cos_ref[...] + turned(u) * sin_ref[...]
            o_ref[:, p * PAIR : (p + 1) * PAIR] = (r.astype(bf16) * factor.astype(bf16)).astype(bf16)

    @pl.when(which == 2)
    def _():
        o_ref[...] = y.astype(bf16)


def project_qkv(rows, w_qkv, cosine, sine):
    count, depth = rows.shape
    width = w_qkv.shape[2]
    return pl.pallas_call(
        qkv_kernel,
        grid=(count // ROWS, 3),
        in_specs=[
            pl.BlockSpec((ROWS, depth), lambda r, t: (r, 0)),
            pl.BlockSpec((None, depth, width), lambda r, t: (t, 0, 0)),
            pl.BlockSpec((ROWS, PAIR), lambda r, t: (r, 0)),
            pl.BlockSpec((ROWS, PAIR), lambda r, t: (r, 0)),
        ],
        out_specs=pl.BlockSpec((None, ROWS, width), lambda r, t: (t, r, 0)),
        out_shape=jax.ShapeDtypeStruct((3, count, width), bf16),
        compiler_params=pltpu.CompilerParams(vmem_limit_bytes=32 << 20),
        cost_estimate=pl.CostEstimate(
            flops=6 * count * depth * width, bytes_accessed=8 * count * width, transcendentals=0
        ),
        name="qkv",
    )(rows, w_qkv, cosine, sine)


def head_lanes(block, h):
    lane = lax.broadcasted_iota(jnp.int32, block.shape, 1)
    return jnp.where(lane // HEAD == h, block, jnp.zeros_like(block))


def transposed(block):
    return block.astype(f32).T


def forward_kernel(flag_ref, q_ref, k_ref, v_ref, segr_ref, segc_ref, o_ref, lse_ref, vt, m, l, acc):
    blocks = q_ref.shape[0] // BLOCK
    for b in range(blocks):
        vt[b] = transposed(v_ref[b * BLOCK : (b + 1) * BLOCK, :]).astype(bf16)

    @pl.loop(0, blocks)
    def _(qi):
        rows = pl.ds(pl.multiple_of(qi * BLOCK, BLOCK), BLOCK)
        q = q_ref[rows, :]
        m[...] = jnp.full(m.shape, masked_score, f32)
        l[...] = jnp.zeros(l.shape, f32)
        acc[...] = jnp.zeros(acc.shape, f32)

        @pl.loop(0, blocks)
        def _(ki):
            @pl.when(flag_ref[qi * blocks + ki] > 0)
            def _():
                cols = pl.ds(pl.multiple_of(ki * BLOCK, BLOCK), BLOCK)
                k = k_ref[cols, :]
                docs = segc_ref[cols, :]
                same = jnp.concatenate([docs] * (BLOCK // 128), axis=1) == segr_ref[qi]
                for h in range(2):
                    lo, hi = h * HEAD, (h + 1) * HEAD
                    s = jnp.where(same, mm(k, head_lanes(q, h), 1, 1), masked_score)
                    top = jnp.maximum(m[h], jnp.max(s, axis=0, keepdims=True))
                    p = jnp.exp(s - top)
                    shrink = jnp.exp(m[h] - top)
                    m[h] = top
                    l[h] = l[h] * shrink + jnp.sum(p, axis=0, keepdims=True)
                    acc[lo:hi, :] = acc[lo:hi, :] * shrink + mm(vt[ki, lo:hi, :], p.astype(bf16), 1, 0)

        for h in range(2):
            lo, hi = h * HEAD, (h + 1) * HEAD
            lse_ref[h, qi] = m[h] + jnp.log(l[h])
            acc[lo:hi, :] = acc[lo:hi, :] / l[h]
        o_ref[rows, :] = acc[...].T.astype(bf16)


def backward_kernel(
    flag_ref, q_ref, k_ref, v_ref, g_ref, o_ref, lse_ref, segr_ref, segc_ref, cos_ref, sin_ref,
    out_ref, kt, dk, dv, dq,
):
    blocks = q_ref.shape[0] // BLOCK
    for b in range(blocks):
        kt[b] = transposed(k_ref[b * BLOCK : (b + 1) * BLOCK, :]).astype(bf16)
    dk[...] = jnp.zeros(dk.shape, f32)
    dv[...] = jnp.zeros(dv.shape, f32)

    def turn_back(u, rows):
        return (u * cos_ref[rows, :] - turned(u) * sin_ref[rows, :]).astype(bf16)

    @pl.loop(0, blocks)
    def _(qi):
        rows = pl.ds(pl.multiple_of(qi * BLOCK, BLOCK), BLOCK)
        q, g = q_ref[rows, :], g_ref[rows, :]
        both = (g.astype(f32) * o_ref[rows, :].astype(f32)).T
        dq[...] = jnp.zeros(dq.shape, f32)

        @pl.loop(0, blocks)
        def _(ki):
            @pl.when(flag_ref[qi * blocks + ki] > 0)
            def _():
                cols = pl.ds(pl.multiple_of(ki * BLOCK, BLOCK), BLOCK)
                k, v = k_ref[cols, :], v_ref[cols, :]
                docs = segc_ref[cols, :]
                same = jnp.concatenate([docs] * (BLOCK // 128), axis=1) == segr_ref[qi]
                dk_sum, dv_sum = dk[cols, :], dv[cols, :]
                for h in range(2):
                    lo, hi = h * HEAD, (h + 1) * HEAD
                    delta = jnp.sum(both[lo:hi, :], axis=0, keepdims=True)
                    qh, gh = head_lanes(q, h), head_lanes(g, h)
                    s = jnp.where(same, mm(k, qh, 1, 1), masked_score)
                    p = jnp.exp(s - lse_ref[h, qi])
                    ds = (p * (mm(v, gh, 1, 1) - delta)).astype(bf16)
                    dv_sum = dv_sum + mm(p.astype(bf16), gh, 1, 0)
                    dk_sum = dk_sum + mm(ds, qh, 1, 0)
                    dq[lo:hi, :] = dq[lo:hi, :] + mm(kt[ki, lo:hi, :], ds, 1, 0)
                dk[cols, :] = dk_sum
                dv[cols, :] = dv_sum

        out_ref[0, rows, :] = turn_back(dq[...].T * (HEAD**-0.5), rows)

    @pl.loop(0, blocks)
    def _(b):
        rows = pl.ds(pl.multiple_of(b * BLOCK, BLOCK), BLOCK)
        out_ref[1, rows, :] = turn_back(dk[rows, :], rows)
        out_ref[2, rows, :] = dv[rows, :].astype(bf16)


def pieces_of(qkv, length):
    return [pl.BlockSpec((None, length, PAIR), functools.partial(lambda t, p, *_: (t, 0, p), t)) for t in range(3)]


def attend_forward(flags, qkv, seg_rows, seg_cols):
    _, length, width = qkv.shape
    blocks, pairs = length // BLOCK, width // PAIR
    return pl.pallas_call(
        forward_kernel,
        grid_spec=pltpu.PrefetchScalarGridSpec(
            num_scalar_prefetch=1,
            grid=(pairs,),
            in_specs=[
                *pieces_of(qkv, length),
                pl.BlockSpec((blocks, 1, BLOCK), lambda p, *_: (0, 0, 0)),
                pl.BlockSpec((length, 128), lambda p, *_: (0, 0)),
            ],
            out_specs=[
                pl.BlockSpec((length, PAIR), lambda p, *_: (0, p)),
                pl.BlockSpec((2, blocks, 1, BLOCK), lambda p, *_: (p, 0, 0, 0)),
            ],
            scratch_shapes=[
                pltpu.VMEM((blocks, PAIR, BLOCK), bf16),
                pltpu.VMEM((2, 1, BLOCK), f32),
                pltpu.VMEM((2, 1, BLOCK), f32),
                pltpu.VMEM((PAIR, BLOCK), f32),
            ],
        ),
        out_shape=[
            jax.ShapeDtypeStruct((length, width), bf16),
            jax.ShapeDtypeStruct((2 * pairs, blocks, 1, BLOCK), f32),
        ],
        compiler_params=pltpu.CompilerParams(vmem_limit_bytes=48 << 20),
        cost_estimate=pl.CostEstimate(
            flops=4 * length * length * width, bytes_accessed=8 * length * width, transcendentals=length * length * width // HEAD
        ),
        name="attend",
    )(flags, qkv, qkv, qkv, seg_rows, seg_cols)


def attend_backward(flags, qkv, grad, mixed, lse, seg_rows, seg_cols, cosine, sine):
    _, length, width = qkv.shape
    blocks, pairs = length // BLOCK, width // PAIR
    whole = pl.BlockSpec((length, PAIR), lambda p, *_: (0, p))
    table = pl.BlockSpec((length, PAIR), lambda p, *_: (0, 0))
    return pl.pallas_call(
        backward_kernel,
        grid_spec=pltpu.PrefetchScalarGridSpec(
            num_scalar_prefetch=1,
            grid=(pairs,),
            in_specs=[
                *pieces_of(qkv, length),
                whole,
                whole,
                pl.BlockSpec((2, blocks, 1, BLOCK), lambda p, *_: (p, 0, 0, 0)),
                pl.BlockSpec((blocks, 1, BLOCK), lambda p, *_: (0, 0, 0)),
                table,
                table,
                table,
            ],
            out_specs=pl.BlockSpec((3, length, PAIR), lambda p, *_: (0, 0, p)),
            scratch_shapes=[
                pltpu.VMEM((blocks, PAIR, BLOCK), bf16),
                pltpu.VMEM((length, PAIR), f32),
                pltpu.VMEM((length, PAIR), f32),
                pltpu.VMEM((PAIR, BLOCK), f32),
            ],
        ),
        out_shape=jax.ShapeDtypeStruct((3, length, width), bf16),
        compiler_params=pltpu.CompilerParams(vmem_limit_bytes=56 << 20),
        cost_estimate=pl.CostEstimate(
            flops=10 * length * length * width, bytes_accessed=16 * length * width, transcendentals=length * length * width // HEAD
        ),
        name="attend_back",
    )(flags, qkv, qkv, qkv, grad, mixed, lse, seg_rows, seg_cols, cosine, sine)


def qkv_pair_kernel(own_ref, got_ref, w_ref, cos_ref, sin_ref, *refs):
    o_ref, rows_ref = refs[-2:]
    which = pl.program_id(0)
    half = own_ref.shape[0]

    @pl.when(which == 0)
    def _():
        rows_ref[:half, :] = own_ref[...]
        rows_ref[half:, :] = got_ref[...]

    y = mm(rows_ref[...], w_ref[...], 1, 0)

    @pl.when(which < 2)
    def _():
        factor = jnp.where(which == 0, HEAD**-0.5, 1.0)
        for p in range(y.shape[1] // PAIR):
            u = y[:, p * PAIR : (p + 1) * PAIR]
            r = u * cos_ref[...] + turned(u) * sin_ref[...]
            o_ref[:, p * PAIR : (p + 1) * PAIR] = (r.astype(bf16) * factor.astype(bf16)).astype(bf16)

    @pl.when(which == 2)
    def _():
        o_ref[...] = y.astype(bf16)


def project_pair(j, own, got, w_qkv, cosine, sine, before, length):
    half, depth = own.shape
    width = w_qkv.shape[2]
    chunk = 2 * half
    table = pl.BlockSpec((chunk, PAIR), lambda t: (j, 0))
    return pl.pallas_call(
        qkv_pair_kernel,
        grid=(3,),
        in_specs=[
            pl.BlockSpec((half, depth), lambda t: (0, 0)),
            pl.BlockSpec((half, depth), lambda t: (0, 0)),
            pl.BlockSpec((None, depth, width), lambda t: (t, 0, 0)),
            table,
            table,
            *[pl.BlockSpec(memory_space=pl.ANY) for _ in before],
        ],
        out_specs=[
            pl.BlockSpec((None, chunk, width), lambda t: (t, j, 0)),
            pl.BlockSpec((chunk, depth), lambda t: (j, 0)),
        ],
        out_shape=[
            jax.ShapeDtypeStruct((3, length, width), bf16),
            jax.ShapeDtypeStruct((length, depth), bf16),
        ],
        input_output_aliases={5 + i: i for i in range(len(before))},
        compiler_params=pltpu.CompilerParams(vmem_limit_bytes=32 << 20),
        cost_estimate=pl.CostEstimate(
            flops=6 * chunk * depth * width, bytes_accessed=8 * depth * width, transcendentals=0
        ),
        name="qkv",
    )(own, got, w_qkv, cosine, sine, *before)


def forward_chunk_kernel(q_ref, k_ref, v_ref, segr_ref, segc_ref, o_ref, lse_ref, vt):
    length, count = k_ref.shape[0], q_ref.shape[0]
    for b in range(0, length, BLOCK):
        vt[:, b : b + BLOCK] = transposed(v_ref[b : b + BLOCK, :]).astype(bf16)
    q = q_ref[...]
    outs = []
    for h in range(2):
        qh = head_lanes(q, h)
        scores = []
        for b in range(0, length, BLOCK):
            same = jnp.concatenate([segc_ref[b : b + BLOCK, :]] * (count // 128), axis=1) == segr_ref[...]
            scores.append(jnp.where(same, mm(k_ref[b : b + BLOCK, :], qh, 1, 1), masked_score))
        top = functools.reduce(jnp.maximum, [jnp.max(s, axis=0, keepdims=True) for s in scores])
        total, summed = 0.0, 0.0
        for i, s in enumerate(scores):
            p = jnp.exp(s - top)
            total = total + jnp.sum(p, axis=0, keepdims=True)
            summed = summed + mm(vt[h * HEAD : (h + 1) * HEAD, i * BLOCK : (i + 1) * BLOCK], p.astype(bf16), 1, 0)
        lse_ref[h] = top + jnp.log(total)
        outs.append(summed / total)
    o_ref[...] = jnp.concatenate(outs, axis=0).T.astype(bf16)


def pair_pieces(j, length, chunk):
    return [
        pl.BlockSpec((None, chunk, PAIR), lambda p: (0, j, p)),
        pl.BlockSpec((None, length, PAIR), lambda p: (1, 0, p)),
        pl.BlockSpec((None, length, PAIR), lambda p: (2, 0, p)),
    ]


def attend_forward_pair(j, chunk, qkv, seg_rows, seg_cols):
    _, length, width = qkv.shape
    pairs = width // PAIR
    return pl.pallas_call(
        forward_chunk_kernel,
        grid=(pairs,),
        in_specs=[
            *pair_pieces(j, length, chunk),
            pl.BlockSpec((1, chunk), lambda p: (0, j)),
            pl.BlockSpec((length, 128), lambda p: (0, 0)),
        ],
        out_specs=[
            pl.BlockSpec((chunk, PAIR), lambda p: (0, p)),
            pl.BlockSpec((2, 1, chunk), lambda p: (p, 0, 0)),
        ],
        out_shape=[
            jax.ShapeDtypeStruct((chunk, width), bf16),
            jax.ShapeDtypeStruct((2 * pairs, 1, chunk), f32),
        ],
        scratch_shapes=[pltpu.VMEM((PAIR, length), bf16)],
        compiler_params=pltpu.CompilerParams(vmem_limit_bytes=48 << 20),
        cost_estimate=pl.CostEstimate(
            flops=16 * chunk * length * width,
            bytes_accessed=8 * length * width,
            transcendentals=chunk * length * width // HEAD,
        ),
        name="attend",
    )(qkv, qkv, qkv, seg_rows, seg_cols)


def mlp_kernel(own_ref, got_ref, b_own_ref, b_got_ref, up_ref, bias_ref, down_ref, *refs):
    rows_ref, hidden_ref, pre_ref, own_grad, got_grad, own_branch, got_branch, bias_grad, back, grads, branch = refs[-11:]
    tile, tiles = pl.program_id(0), pl.num_programs(0)
    half = own_ref.shape[0]

    @pl.when(tile == 0)
    def _():
        rows_ref[:half, :] = own_ref[...]
        rows_ref[half:, :] = got_ref[...]
        back[:half, :] = b_own_ref[...]
        back[half:, :] = b_got_ref[...]

    cubic, root = 0.044715, (2.0 / jnp.pi) ** 0.5
    u = mm(rows_ref[...], up_ref[...], 1, 0) + bias_ref[...]
    square = u * u
    t = jnp.tanh(u * (root + (root * cubic) * square))
    rising = 0.5 * (1.0 + t)
    hidden = (u * rising).astype(bf16)
    slope = rising + (0.5 * u) * (1.0 - t * t) * (root + (3.0 * cubic * root) * square)
    grad = (mm(back[...], down_ref[...], 1, 1) * slope).astype(bf16)
    hidden_ref[...] = hidden
    pre_ref[...] = grad
    bias_grad[...] = jnp.sum(grad.astype(f32), axis=0, keepdims=True)
    more, more_branch = mm(grad, up_ref[...], 1, 1), mm(hidden, down_ref[...], 1, 0)

    @pl.when(tile == 0)
    def _():
        grads[...] = more
        branch[...] = more_branch

    @pl.when(tile > 0)
    def _():
        grads[...] += more
        branch[...] += more_branch

    @pl.when(tile == tiles - 1)
    def _():
        own_grad[...] = grads[:half, :]
        got_grad[...] = grads[half:, :].astype(bf16)
        own_branch[...] = branch[:half, :]
        got_branch[...] = branch[half:, :].astype(bf16)


def mlp_pair(j, own, got, back_own, back_got, w_up, b_up, w_down, before, length):
    half, depth = own.shape
    width = w_up.shape[1]
    chunk, tile = 2 * half, min(width, 1024)
    small = pl.BlockSpec((half, depth), lambda t: (0, 0))
    wide = pl.BlockSpec((chunk, tile), lambda t: (j, t))
    return pl.pallas_call(
        mlp_kernel,
        grid=(width // tile,),
        in_specs=[
            small, small, small, small,
            pl.BlockSpec((depth, tile), lambda t: (0, t)),
            pl.BlockSpec((1, tile), lambda t: (0, t)),
            pl.BlockSpec((tile, depth), lambda t: (t, 0)),
            *[pl.BlockSpec(memory_space=pl.ANY) for _ in before],
        ],
        out_specs=[
            pl.BlockSpec((chunk, depth), lambda t: (j, 0)), wide, wide,
            small, small, small, small,
            pl.BlockSpec((1, tile), lambda t: (0, t)),
        ],
        out_shape=[
            jax.ShapeDtypeStruct((length, depth), bf16),
            jax.ShapeDtypeStruct((length, width), bf16),
            jax.ShapeDtypeStruct((length, width), bf16),
            jax.ShapeDtypeStruct((half, depth), f32),
            jax.ShapeDtypeStruct((half, depth), bf16),
            jax.ShapeDtypeStruct((half, depth), f32),
            jax.ShapeDtypeStruct((half, depth), bf16),
            jax.ShapeDtypeStruct((1, width), f32),
        ],
        scratch_shapes=[
            pltpu.VMEM((chunk, depth), bf16),
            pltpu.VMEM((chunk, depth), f32),
            pltpu.VMEM((chunk, depth), f32),
        ],
        input_output_aliases={7 + i: i for i in range(len(before))},
        compiler_params=pltpu.CompilerParams(vmem_limit_bytes=56 << 20),
        cost_estimate=pl.CostEstimate(
            flops=12 * chunk * depth * width, bytes_accessed=12 * depth * width, transcendentals=chunk * width
        ),
        name="mlp",
    )(own, got, back_own, back_got, w_up, b_up[None, :], w_down, *before)


MESH = pl.DeviceIdType.MESH
ADD_ROWS = 32
STEPS = 9
EDGES = 4


def add_low(a, a_at, b, rows):
    @pl.loop(0, rows // ADD_ROWS)
    def _(i):
        at = pl.ds(pl.multiple_of(i * ADD_ROWS, ADD_ROWS), ADD_ROWS)
        kept = a[pl.ds(pl.multiple_of(a_at + i * ADD_ROWS, ADD_ROWS), ADD_ROWS), :].astype(f32)
        b[at, :] = (kept + b[at, :].astype(f32)).astype(bf16)


class Unit:
    def __init__(self, part, out, row, rows, held, got, send, recv, local, place):
        self.part, self.out, self.row, self.rows = part, out, row, rows
        self.held, self.got, self.send, self.recv, self.local = held, got, send, recv, local
        self.bit = [(place // (1 << b)) % 2 for b in range(EDGES)]
        self.partner = [place + (1 - 2 * self.bit[b]) * (1 << b) for b in range(EDGES)]
        self.base = [row]
        for b in range(EDGES):
            self.base.append(self.base[-1] + self.bit[b] * (rows >> (b + 1)))

    def remote(self, src, dst, stage, b):
        return pltpu.make_async_remote_copy(
            src_ref=src,
            dst_ref=dst,
            send_sem=self.send.at[stage],
            recv_sem=self.recv.at[stage],
            device_id={"dp": self.partner[b]},
            device_id_type=MESH,
        )

    def at(self, start, rows):
        return pl.ds(pl.multiple_of(start, ADD_ROWS), rows)

    def halving(self, b):
        half = self.rows >> (b + 1)
        if b == 0:
            first = self.row if self.held is not None else 0
            src = self.part.at[self.at(first + (1 - self.bit[0]) * half, half)]
        else:
            src = self.got[b - 1].at[self.at((1 - self.bit[b]) * half, half)]
        return self.remote(src, self.got[b], b, b)

    def keep(self):
        half = self.rows // 2
        return pltpu.make_async_copy(
            self.part.at[self.at(self.row + self.bit[0] * half, half)], self.held, self.local.at[0]
        )

    def own(self):
        return pltpu.make_async_copy(
            self.got[3], self.out.at[self.at(self.base[4], self.rows >> 4)], self.local.at[1]
        )

    def gathering(self, b):
        size = self.rows >> (b + 1)
        spot = self.out.at[self.at(self.base[b + 1], size)]
        return self.remote(self.got[3] if b == 3 else spot, spot, 7 - b, b)

    def step(self, k):
        if k == 0:
            self.halving(0).start()
            if self.held is not None:
                self.keep().start()
        elif k < 5:
            b = k - 1
            self.halving(b).wait()
            half = self.rows >> (b + 1)
            if b == 0 and self.held is not None:
                self.keep().wait()
                add_low(self.held, 0, self.got[0], half)
            else:
                add_low(self.part if b == 0 else self.got[b - 1], self.bit[b] * half, self.got[b], half)
            if b < 3:
                self.halving(b + 1).start()
            else:
                self.own().start()
                self.gathering(3).start()
        elif k == 5:
            self.own().wait()
            self.gathering(3).wait()
            self.gathering(2).start()
        elif k < 8:
            self.gathering(8 - k).wait()
            self.gathering(7 - k).start()
        else:
            self.gathering(0).wait()


def unit_scratch(rows, columns, kept):
    return [
        pltpu.VMEM((rows // 2 if kept else rows, columns), bf16),
        *[pltpu.VMEM((rows >> (b + 1), columns), bf16) for b in range(EDGES)],
        pltpu.SemaphoreType.DMA((2 * EDGES,)),
        pltpu.SemaphoreType.DMA((2 * EDGES,)),
        pltpu.SemaphoreType.DMA((2,)),
    ]


def greet(targets):
    barrier = pltpu.get_barrier_semaphore()
    for target in targets:
        pl.semaphore_signal(barrier, inc=1, device_id=target, device_id_type=MESH)
    pl.semaphore_wait(barrier, len(targets))


def tail_kernel(
    down_part, up_part, qkv_hbm, mixed_hbm, rows_hbm, w_qkv_hbm, w_out_hbm,
    own_grad, got_grad, middle, out_grad, rows_of, lse, segr, segc, cosine, sine,
    down_sum, up_sum, out_sum, q_sum, k_sum, v_sum, mid_grad, one_grad, col_sums,
    qkv, mixed, rows_one, w_qkv, w_out, proj, mix_grad, d_qkv, dk, dv, kt, from_x, send_one, got_one,
    load, x_send, x_recv, *more,
):
    place, me = lax.axis_index("dp"), lax.axis_index("tensor")
    length = rows_one.shape[0]
    chunks, half, depth = got_grad.shape
    chunk = 2 * half
    width = mixed.shape[1]
    pairs = width // PAIR
    across = {"tensor": 1 - me}

    wide, deep = up_part.shape[0], down_part.shape[0]
    specs = [
        (down_part, down_sum, 0, deep // 2), (down_part, down_sum, deep // 2, deep // 2),
        (up_part, up_sum, 0, wide // 2), (up_part, up_sum, wide // 2, wide // 2),
        (None, out_sum, 0, width), (None, v_sum, 0, depth), (None, k_sum, 0, depth), (None, q_sum, 0, depth),
    ]
    units = []
    for i, (part, out, row, rows) in enumerate(specs):
        own, *got, send, recv, local = more[8 * i : 8 * (i + 1)]
        units.append(Unit(own if part is None else part, out, row, rows, None if part is None else own, got, send, recv, local, place))

    def x_copy(src, dst, i):
        return pltpu.make_async_remote_copy(
            src_ref=src, dst_ref=dst, send_sem=x_send.at[i], recv_sem=x_recv.at[i],
            device_id=across, device_id_type=MESH,
        )

    grads_in = [x_copy(got_grad.at[c], from_x.at[c], c) for c in range(chunks)]
    projs = [x_copy(proj.at[c, :half], proj.at[c, half:], chunks + c) for c in range(chunks)]
    ones = [x_copy(send_one.at[c], got_one.at[c], 2 * chunks + c) for c in range(chunks)]
    loads = [
        pltpu.make_async_copy(src, dst, load.at[i])
        for i, (src, dst) in enumerate(
            [(w_out_hbm, w_out), (mixed_hbm, mixed), (qkv_hbm, qkv), (rows_hbm, rows_one), (w_qkv_hbm, w_qkv)]
        )
    ]

    late = [0, 5, 17, 24, 31, 38, 45, 65, 68]
    turns = [(late[k] + (12 if k > 1 else 2) * i, k, i) for i in range(4) for k in range(STEPS)]
    turns += [(t, k, 4) for k, t in enumerate([None, 47, 60, 66, 72, 78, 84, 104, 107]) if k]
    for i in range(3):
        turns += [(t + (6 if k > 1 else 3) * i, k, 5 + i) for k, t in enumerate([None, 88, 100, 106, 112, 118, 124, 134, 138]) if k]
    turns = sorted(turns)
    done = [0]

    def until(time):
        while done[0] < len(turns) and turns[done[0]][0] <= time:
            _, k, i = turns[done[0]]
            units[i].step(k)
            done[0] += 1

    greet([*[{"dp": partner} for partner in units[0].partner], across])
    for c in range(chunks):
        grads_in[c].start()
    until(4)
    for copy in loads:
        copy.start()

    gain, scale, gate = rows_of[0:1, :], rows_of[1:2, :], rows_of[2:3, :]
    step_rows = 64

    def norm_back(c):
        grads_in[c].wait()

        @pl.loop(0, half // step_rows)
        def _(i):
            at = pl.ds(pl.multiple_of(i * step_rows, step_rows), step_rows)
            grad = own_grad[c, at, :] + from_x[c, at, :].astype(f32)
            values = middle[c, at, :]
            center = values - jnp.mean(values, axis=1, keepdims=True)
            root = lax.rsqrt(jnp.mean(center * center, axis=1, keepdims=True) + norm_eps)
            normal = center * root
            inner = grad * (gain * (1.0 + scale))
            back = root * (
                inner - jnp.mean(inner, axis=1, keepdims=True) - normal * jnp.mean(inner * normal, axis=1, keepdims=True)
            )
            total = back + out_grad[c, at, :].astype(f32)
            mid_grad[c, at, :] = total
            proj[c, at, :] = (total * gate).astype(bf16)
            shifted = jnp.sum(grad, axis=0, keepdims=True)
            scaled = jnp.sum(grad * normal, axis=0, keepdims=True)
            both = jnp.concatenate([shifted, scaled, jnp.zeros((6, depth), f32)], axis=0)
            if c == 0:
                fresh = jnp.where(i == 0, jnp.zeros_like(both), col_sums[...])
                col_sums[...] = fresh + both
            else:
                col_sums[...] += both

        projs[c].start()

    norm_back(0)
    until(20)
    norm_back(1)
    until(28)
    loads[0].wait()
    for c in range(chunks):
        projs[c].wait()
        mix_grad[c * chunk : (c + 1) * chunk, :] = mm(proj[c], w_out[...], 1, 1).astype(bf16)
        until(32 + 10 * c)

    loads[1].wait()
    out_part = units[4].part
    for r in range(0, width, 256):
        out_part[r : r + 256, :] = (
            mm(mixed[:chunk, r : r + 256], proj[0], 0, 0) + mm(mixed[chunk:, r : r + 256], proj[1], 0, 0)
        ).astype(bf16)
    units[4].step(0)
    until(46)

    loads[2].wait()

    def turn_back(u, rows):
        return (u * cosine[rows, :] - turned(u) * sine[rows, :]).astype(bf16)

    def attend_back(p, c):
        lanes = pl.ds(pl.multiple_of(p * PAIR, PAIR), PAIR)
        rows = pl.ds(pl.multiple_of(c * chunk, chunk), chunk)
        q, g = qkv[0, rows, lanes], mix_grad[rows, lanes]
        both = (g.astype(f32) * mixed[rows, lanes].astype(f32)).T
        qh = [head_lanes(q, h) for h in range(2)]
        gh = [head_lanes(g, h) for h in range(2)]
        delta = [jnp.sum(both[h * HEAD : (h + 1) * HEAD, :], axis=0, keepdims=True) for h in range(2)]
        q_two, g_two = jnp.concatenate(qh, axis=0), jnp.concatenate(gh, axis=0)
        docs = segr[:, rows]
        dq = [0.0, 0.0]
        for b in range(0, length, BLOCK):
            cols = slice(b, b + BLOCK)
            k, v = qkv[1, cols, lanes], qkv[2, cols, lanes]
            turned_k = transposed(k).astype(bf16)
            same = jnp.concatenate([segc[cols, :]] * (chunk // 128), axis=1) == docs
            ps, ds = [], []
            for h in range(2):
                s = jnp.where(same, mm(k, qh[h], 1, 1), masked_score)
                pr = jnp.exp(s - lse[c, 2 * p + h])
                d = (pr * (mm(v, gh[h], 1, 1) - delta[h])).astype(bf16)
                ps.append(pr.astype(bf16))
                ds.append(d)
                dq[h] = dq[h] + mm(turned_k[h * HEAD : (h + 1) * HEAD, :], d, 1, 0)
            add_v = mm(jnp.concatenate(ps, axis=1), g_two, 1, 0)
            add_k = mm(jnp.concatenate(ds, axis=1), q_two, 1, 0)
            dv[cols, :] = jnp.where(c == 0, 0.0, dv[cols, :]) + add_v
            dk[cols, :] = jnp.where(c == 0, 0.0, dk[cols, :]) + add_k
        d_qkv[0, rows, lanes] = turn_back(jnp.concatenate(dq, axis=0).T * (HEAD**-0.5), rows)

        @pl.when(c == chunks - 1)
        def _():
            @pl.loop(0, length // BLOCK)
            def _(b):
                at = pl.ds(pl.multiple_of(b * BLOCK, BLOCK), BLOCK)
                d_qkv[1, at, lanes] = turn_back(dk[at, :], at)
                d_qkv[2, at, lanes] = dv[at, :].astype(bf16)

    @pl.loop(0, pairs * chunks)
    def _(i):
        attend_back(i // chunks, i % chunks)
        for n in range(pairs * chunks):

            @pl.when(i == n)
            def _():
                until(50 + 4.5 * n)

    loads[4].wait()

    def rows_back(start):
        at = slice(start, start + half)
        return (
            mm(d_qkv[0, at, :], w_qkv[0], 1, 1) + mm(d_qkv[1, at, :], w_qkv[1], 1, 1) + mm(d_qkv[2, at, :], w_qkv[2], 1, 1)
        )

    for c in range(chunks):
        send_one[c] = rows_back(c * chunk + half).astype(bf16)
        ones[c].start()
    until(83)
    loads[3].wait()
    for i in range(3):
        part = units[5 + i].part

        @pl.loop(0, depth // 256)
        def _(r):
            at = pl.ds(pl.multiple_of(r * 256, 256), 256)
            part[at, :] = mm(rows_one[:, at], d_qkv[2 - i], 0, 0).astype(bf16)

        units[5 + i].step(0)
        until(87 + 3 * i)
    for c in range(chunks):
        one_grad[c] = rows_back(c * chunk)
        until(97 + 3 * c)
    for c in range(chunks):
        ones[c].wait()
        one_grad[c] = one_grad[c] + got_one[c].astype(f32)
        until(108 + 3 * c)
    until(1000)


def tail(down_part, up_part, qkv, mixed, rows_one, w_qkv, w_out, own_grad, got_grad, middle, out_grad, rows_of, lse, segr, segc, cosine, sine):
    _, length, width = qkv.shape
    chunks, half, depth = got_grad.shape
    anywhere, near = pl.BlockSpec(memory_space=pl.ANY), pl.BlockSpec(memory_space=pltpu.VMEM)
    shaped = jax.ShapeDtypeStruct
    (deep, _), (_, wide) = down_part.shape, up_part.shape
    scratch = [
        pltpu.VMEM(qkv.shape, bf16),
        pltpu.VMEM(mixed.shape, bf16),
        pltpu.VMEM(rows_one.shape, bf16),
        pltpu.VMEM(w_qkv.shape, bf16),
        pltpu.VMEM(w_out.shape, bf16),
        pltpu.VMEM((chunks, 2 * half, depth), bf16),
        pltpu.VMEM((length, width), bf16),
        pltpu.VMEM((3, length, width), bf16),
        pltpu.VMEM((length, PAIR), f32),
        pltpu.VMEM((length, PAIR), f32),
        pltpu.VMEM((8, 128), f32),
        pltpu.VMEM(got_grad.shape, bf16),
        pltpu.VMEM(got_grad.shape, bf16),
        pltpu.VMEM(got_grad.shape, bf16),
        pltpu.SemaphoreType.DMA((5,)),
        pltpu.SemaphoreType.DMA((3 * chunks,)),
        pltpu.SemaphoreType.DMA((3 * chunks,)),
        *unit_scratch(deep // 2, depth, True) * 2,
        *unit_scratch(depth // 2, wide, True) * 2,
        *unit_scratch(width, depth, False),
        *unit_scratch(depth, width, False) * 3,
    ]
    return pl.pallas_call(
        tail_kernel,
        in_specs=[anywhere] * 7 + [near] * 10,
        out_specs=[anywhere] * 6 + [near] * 3,
        out_shape=[
            shaped(down_part.shape, bf16), shaped(up_part.shape, bf16), shaped((width, depth), bf16),
            *[shaped((depth, width), bf16)] * 3,
            shaped(got_grad.shape, f32), shaped(got_grad.shape, f32), shaped((8, depth), f32),
        ],
        scratch_shapes=scratch,
        compiler_params=pltpu.CompilerParams(collective_id=1, has_side_effects=True, vmem_limit_bytes=61 << 20),
        name="tail",
    )(down_part, up_part, qkv, mixed, rows_one, w_qkv, w_out, own_grad, got_grad, middle, out_grad, rows_of, lse, segr, segc, cosine, sine)


def body_pair(
    tokens, cond, doc_lengths, w_ada, b_ada, gain_one, w_qkv, w_out, gain_two, w_up, b_up, w_down, b_down, cotangent
):
    dp_size = lax.axis_size("dp")
    bits = dp_size.bit_length() - 1
    own, width = tokens.shape
    length = 2 * own
    chunks = 2
    half, chunk = own // chunks, length // chunks
    me = lax.axis_index("tensor")

    def swap(values):
        return lax.ppermute(values, "tensor", [(0, 1), (1, 0)])

    def across(values, b):
        return lax.ppermute(values, "dp", [(d, d ^ (1 << b)) for d in range(dp_size)])

    def gathered(row):
        for b in reversed(range(bits)):
            row = jnp.concatenate([row, across(row, b)], axis=0)
        return row

    step = jnp.arange(length, dtype=jnp.int32)
    in_chunk = step % chunk
    places = jnp.where(in_chunk < half, me, 1 - me) * own + (step // chunk) * half + in_chunk % half
    segment, doc_first = documents(doc_lengths[0], places)
    cosine, sine = rope_tables(places - doc_first)
    seg_rows = segment[None, :]
    seg_cols = jnp.broadcast_to(segment[:, None], (length, 128))

    modulation = jnp.dot(cond, w_ada, preferred_element_type=f32)[0] + b_ada
    shift_a, scale_a, gate_a, shift_m, scale_m, gate_m = jnp.split(modulation, 6)
    cuts = [slice(c * half, (c + 1) * half) for c in range(chunks)]
    x_rows = [tokens[cut].astype(f32) for cut in cuts]
    grad_out = [cotangent[cut].astype(f32) for cut in cuts]
    each = range(chunks)

    act_one = [modulate(x_rows[c], gain_one, shift_a, scale_a).astype(bf16) for c in each]
    got_one = [swap(act_one[c]) for c in each]
    back = [(grad_out[c] * gate_m).astype(bf16) for c in each]
    state = ()
    for c in each:
        state = project_pair(c, act_one[c], got_one[c], w_qkv, cosine, sine, state, length)
    qkv, rows_one = state
    got_back = [swap(back[c]) for c in each]
    full_back = jnp.concatenate([piece for c in each for piece in (back[c], got_back[c])], axis=0)

    mixed, lse, projected, middle, act_two, got_two = [], [], [], [], [], []
    for c in each:
        m, l = attend_forward_pair(c, chunk, qkv, seg_rows, seg_cols)
        mixed.append(m)
        lse.append(l)
    sums = [swap(jnp.dot(mixed[c][half:], w_out, preferred_element_type=f32).astype(bf16)) for c in each]
    for c in each:
        projected.append(jnp.dot(mixed[c][:half], w_out, preferred_element_type=f32) + sums[c].astype(f32))
        middle.append(x_rows[c] + gate_a * projected[c])
        act_two.append(modulate(middle[c], gain_two, shift_m, scale_m).astype(bf16))
        got_two.append(swap(act_two[c]))
    state, pieces = (), []
    for c in each:
        out = mlp_pair(c, act_two[c], got_two[c], back[c], got_back[c], w_up, b_up, w_down, state, length)
        state, rest = out[:3], out[3:]
        pieces.append(rest)
    rows_two, hidden, grad_pre = state
    grad_b_up = sum(pieces[c][4] for c in each)[0]
    grad_w_down = mm(hidden, full_back, 0, 0).astype(bf16)
    grad_w_up = mm(rows_two, grad_pre, 0, 0).astype(bf16)
    branch = [pieces[c][2] + swap(pieces[c][3]).astype(f32) + b_down for c in each]
    output = jnp.concatenate([(middle[c] + gate_m * branch[c]).astype(bf16) for c in each], axis=0)
    grad_gate_m = sum(jnp.sum(grad_out[c] * branch[c], axis=0) for c in each)
    grad_b_down = sum(jnp.sum(back[c].astype(f32), axis=0) for c in each)

    in_chunks = (chunks, half, width)
    *sums, grad_middle, grad_act_one, columns = tail(
        grad_w_down, grad_w_up, qkv, jnp.concatenate(mixed, axis=0), rows_one, w_qkv, w_out,
        jnp.stack([pieces[c][0] for c in each]), jnp.stack([pieces[c][1] for c in each]),
        jnp.stack(middle), cotangent.reshape(in_chunks), jnp.stack([gain_two, scale_m, gate_a] + [gate_a] * 5),
        jnp.stack(lse), seg_rows, seg_cols, cosine, sine,
    )
    grad_w_down, grad_w_up, grad_w_out, grad_q, grad_k, grad_v = [s.astype(f32) for s in sums]
    grad_w_qkv = jnp.stack([grad_q, grad_k, grad_v])
    grad_middle, grad_act_one = grad_middle.reshape(own, width), grad_act_one.reshape(own, width)
    grad_shift_m, grad_scale_m, grad_gain_two = columns[0], columns[1] * gain_two, columns[1] * (1.0 + scale_m)
    grad_gate_a = jnp.sum(grad_middle * jnp.concatenate(projected, axis=0), axis=0)

    x_all = tokens.astype(f32)
    _, first_back = jax.vjp(modulate, x_all, gain_one, shift_a, scale_a)
    grad_x, grad_gain_one, grad_shift_a, grad_scale_a = first_back(grad_act_one)
    grad_x = (grad_x + grad_middle).astype(bf16)

    small = jnp.concatenate(
        [
            grad_shift_a, grad_scale_a, grad_gate_a, grad_shift_m, grad_scale_m, grad_gate_m,
            grad_gain_one, grad_gain_two, grad_b_down,
        ]
    )[None, :]
    small = small + swap(small)
    mod_size = modulation.shape[0]
    grad_mod = small[0, :mod_size]
    grad_cond = jnp.dot(w_ada.astype(f32), grad_mod, precision=lax.Precision.HIGHEST)[None, :]
    everyone = gathered(jnp.concatenate([small, grad_b_up[None, :], cond.astype(f32)], axis=1))
    conds = everyone[:, -cond.shape[1] :]
    mods = everyone[:, :mod_size]
    grad_w_ada = jnp.einsum("nc,nm->cm", conds, mods, precision=lax.Precision.HIGHEST, preferred_element_type=f32)
    sums = jnp.sum(everyone, axis=0)
    grad_b_ada = sums[:mod_size]
    grad_gain_one, grad_gain_two, grad_b_down = jnp.split(sums[mod_size : mod_size + 3 * width], 3)
    grad_b_up = sums[mod_size + 3 * width : -cond.shape[1]]
    return (
        output, grad_x, grad_cond, grad_w_ada, grad_b_ada, grad_gain_one, grad_w_qkv, grad_w_out, grad_gain_two,
        grad_w_up, grad_b_up, grad_w_down, grad_b_down,
    )


def body_any(
    tokens, cond, doc_lengths, w_ada, b_ada, gain_one, w_qkv, w_out, gain_two, w_up, b_up, w_down, b_down, cotangent
):
    tensor_size = lax.axis_size("tensor")
    own = tokens.shape[0]
    length = own * tensor_size

    def all_rows(values):
        return lax.all_gather(values, "tensor", axis=0, tiled=True)

    def own_sum(values):
        return lax.psum_scatter(values, "tensor", scatter_dimension=0, tiled=True)

    def sum_over_dp(part):
        return lax.psum(part, "dp")

    places = jnp.arange(length, dtype=jnp.int32)
    segment, doc_first = documents(doc_lengths[0], places)
    cosine, sine = rope_tables(places - doc_first)
    blocks = length // BLOCK
    in_blocks = segment.reshape(blocks, BLOCK)
    least, most = jnp.min(in_blocks, axis=1), jnp.max(in_blocks, axis=1)
    meets = (least[:, None] <= most[None, :]) & (least[None, :] <= most[:, None])
    flags = meets.astype(jnp.int32).reshape(-1)
    seg_rows = in_blocks[:, None, :]
    seg_cols = jnp.broadcast_to(segment[:, None], (length, 128))

    modulation = jnp.dot(cond, w_ada, preferred_element_type=f32)[0] + b_ada
    shift_a, scale_a, gate_a, shift_m, scale_m, gate_m = jnp.split(modulation, 6)
    x_rows = tokens.astype(f32)
    grad_out = cotangent.astype(f32)

    act_one = modulate(x_rows, gain_one, shift_a, scale_a).astype(bf16)
    rows_one = all_rows(act_one)
    grad_branch = (grad_out * gate_m).astype(bf16)
    full_branch = all_rows(grad_branch)
    qkv = project_qkv(rows_one, w_qkv, cosine, sine)
    mixed, lse = attend_forward(flags, qkv, seg_rows, seg_cols)
    projected = own_sum(jnp.dot(mixed, w_out, preferred_element_type=f32))
    middle = x_rows + gate_a * projected
    rows_two = all_rows(modulate(middle, gain_two, shift_m, scale_m).astype(bf16))
    pre_act = jnp.dot(rows_two, w_up, preferred_element_type=f32) + b_up
    hidden = jax.nn.gelu(pre_act, approximate=True).astype(bf16)

    grad_hidden = jnp.einsum("sd,fd->sf", full_branch, w_down, preferred_element_type=f32)
    _, gelu_back = jax.vjp(lambda values: jax.nn.gelu(values, approximate=True), pre_act)
    grad_pre = gelu_back(grad_hidden)[0].astype(bf16)
    grad_act_two = own_sum(jnp.einsum("sf,df->sd", grad_pre, w_up, preferred_element_type=f32))
    grad_w_down = sum_over_dp(jnp.einsum("sf,sd->fd", hidden, full_branch, preferred_element_type=f32))
    grad_w_up = sum_over_dp(jnp.einsum("sd,sf->df", rows_two, grad_pre, preferred_element_type=f32))

    branch = own_sum(jnp.dot(hidden, w_down, preferred_element_type=f32)) + b_down
    output = (middle + gate_m * branch).astype(bf16)
    grad_gate_m = jnp.sum(grad_out * branch, axis=0)
    grad_b_down = jnp.sum(grad_branch.astype(f32), axis=0)
    grad_b_up = jnp.sum(grad_pre.astype(f32), axis=0)

    _, second_back = jax.vjp(modulate, middle, gain_two, shift_m, scale_m)
    grad_middle, grad_gain_two, grad_shift_m, grad_scale_m = second_back(grad_act_two)
    grad_middle = grad_middle + grad_out
    full_proj = all_rows((grad_middle * gate_a).astype(bf16))
    grad_gate_a = jnp.sum(grad_middle * projected, axis=0)
    grad_mixed = jnp.einsum("sd,ed->se", full_proj, w_out, preferred_element_type=f32).astype(bf16)
    grad_w_out = sum_over_dp(jnp.einsum("se,sd->ed", mixed, full_proj, preferred_element_type=f32))
    grad_qkv = attend_backward(flags, qkv, grad_mixed, mixed, lse, seg_rows, seg_cols, cosine, sine)
    grad_act_one = own_sum(jnp.einsum("tse,tde->sd", grad_qkv, w_qkv, preferred_element_type=f32))
    grad_w_qkv = jnp.einsum("sd,tse->tde", rows_one, grad_qkv, preferred_element_type=f32)
    grad_w_qkv = sum_over_dp(grad_w_qkv.reshape(-1, grad_w_qkv.shape[2])).reshape(grad_w_qkv.shape)

    _, first_back = jax.vjp(modulate, x_rows, gain_one, shift_a, scale_a)
    grad_x, grad_gain_one, grad_shift_a, grad_scale_a = first_back(grad_act_one)
    grad_x = (grad_x + grad_middle).astype(bf16)

    small = jnp.concatenate(
        [
            grad_shift_a, grad_scale_a, grad_gate_a, grad_shift_m, grad_scale_m, grad_gate_m,
            grad_gain_one, grad_gain_two, grad_b_down,
        ]
    )
    small = lax.psum(small, "tensor")
    mod_size = modulation.shape[0]
    grad_mod = small[:mod_size]
    grad_cond = jnp.dot(w_ada.astype(f32), grad_mod, precision=lax.Precision.HIGHEST)[None, :]
    everyone = lax.all_gather(
        jnp.concatenate([small, grad_b_up, cond[0].astype(f32)])[None, :], "dp", axis=0, tiled=True
    )
    conds = everyone[:, -cond.shape[1] :]
    mods = everyone[:, :mod_size]
    grad_w_ada = jnp.einsum("nc,nm->cm", conds, mods, precision=lax.Precision.HIGHEST, preferred_element_type=f32)
    sums = jnp.sum(everyone, axis=0)
    width = tokens.shape[1]
    grad_b_ada = sums[:mod_size]
    grad_gain_one, grad_gain_two, grad_b_down = jnp.split(sums[mod_size : mod_size + 3 * width], 3)
    grad_b_up = sums[mod_size + 3 * width : -cond.shape[1]]
    return (
        output, grad_x, grad_cond, grad_w_ada, grad_b_ada, grad_gain_one, grad_w_qkv, grad_w_out, grad_gain_two,
        grad_w_up, grad_b_up, grad_w_down, grad_b_down,
    )


def solution(mesh):
    swaps = mesh.shape["tensor"] == 2 and mesh.shape["dp"] == 16
    placed = (
        P(("dp", "tensor"), None), P("dp", None), P("dp", None), P(), P(), P(), P(None, None, "tensor"),
        P("tensor", None), P(), P(None, "tensor"), P("tensor"), P("tensor", None), P(), P(("dp", "tensor"), None),
    )
    return jax.shard_map(
        body_pair if swaps else body_any,
        mesh=mesh,
        in_specs=placed,
        out_specs=(
            P(("dp", "tensor"), None), P(("dp", "tensor"), None), P("dp", None), P(), P(), P(),
            P(None, None, "tensor"), P("tensor", None), P(), P(None, "tensor"), P("tensor"), P("tensor", None), P(),
        ),
        check_vma=False,
    )
```

```python
import functools

import jax
import jax.numpy as jnp
from jax import lax
from jax.experimental import pallas as pl
from jax.experimental.pallas import tpu as pltpu
from jax.sharding import PartitionSpec as P

HEAD = 64
PAIR = 2 * HEAD
BLOCK = 256
ROWS = 512

norm_eps = 1e-05
rope_base = 10000.0
masked_score = -1e30
f32, bf16 = jnp.float32, jnp.bfloat16


def layer_norm(values, gain):
    center = values - jnp.mean(values, axis=-1, keepdims=True)
    spread = jnp.mean(center * center, axis=-1, keepdims=True)
    return center * lax.rsqrt(spread + norm_eps) * gain


def modulate(values, gain, shift, scale):
    return layer_norm(values, gain) * (1.0 + scale) + shift


def documents(lengths, places):
    numbers = jnp.arange(lengths.shape[0], dtype=jnp.int32)
    earlier = (numbers[None, :] < numbers[:, None]).astype(jnp.int32)
    starts = jnp.sum(earlier * lengths[None, :], axis=1)
    ends = starts + lengths
    inside = ((places[:, None] >= starts[None, :]) & (places[:, None] < ends[None, :])).astype(
        jnp.int32
    )
    segment = jnp.sum(inside * numbers[None, :], axis=1)
    doc_first = jnp.sum(inside * starts[None, :], axis=1)
    return segment, doc_first


def rope_tables(offsets):
    exponent = jnp.arange(HEAD // 2, dtype=f32) * (2.0 / HEAD)
    frequency = jnp.power(jnp.float32(rope_base), -exponent)
    angles = offsets.astype(f32)[:, None] * frequency[None, :]
    cosine, sine = jnp.cos(angles), jnp.sin(angles)
    repeat = PAIR // (HEAD // 2)
    return jnp.concatenate([cosine] * repeat, axis=-1), jnp.concatenate([sine] * repeat, axis=-1)


def turned(values):
    lane = lax.broadcasted_iota(jnp.int32, values.shape, 1)
    half = HEAD // 2
    from_right = pltpu.roll(values, PAIR - half, axis=1)
    from_left = pltpu.roll(values, half, axis=1)
    return jnp.where(lane % HEAD < half, -from_right, from_left)


def mm(a, b, da, db):
    return lax.dot_general(a, b, (((da,), (db,)), ((), ())), preferred_element_type=f32)


def qkv_kernel(x_ref, w_ref, cos_ref, sin_ref, o_ref):
    which = pl.program_id(1)
    y = mm(x_ref[...], w_ref[...], 1, 0)

    @pl.when(which < 2)
    def _():
        factor = jnp.where(which == 0, HEAD**-0.5, 1.0)
        for p in range(y.shape[1] // PAIR):
            u = y[:, p * PAIR : (p + 1) * PAIR]
            r = u * cos_ref[...] + turned(u) * sin_ref[...]
            o_ref[:, p * PAIR : (p + 1) * PAIR] = (r.astype(bf16) * factor.astype(bf16)).astype(bf16)

    @pl.when(which == 2)
    def _():
        o_ref[...] = y.astype(bf16)


def project_qkv(rows, w_qkv, cosine, sine):
    count, depth = rows.shape
    width = w_qkv.shape[2]
    return pl.pallas_call(
        qkv_kernel,
        grid=(count // ROWS, 3),
        in_specs=[
            pl.BlockSpec((ROWS, depth), lambda r, t: (r, 0)),
            pl.BlockSpec((None, depth, width), lambda r, t: (t, 0, 0)),
            pl.BlockSpec((ROWS, PAIR), lambda r, t: (r, 0)),
            pl.BlockSpec((ROWS, PAIR), lambda r, t: (r, 0)),
        ],
        out_specs=pl.BlockSpec((None, ROWS, width), lambda r, t: (t, r, 0)),
        out_shape=jax.ShapeDtypeStruct((3, count, width), bf16),
        compiler_params=pltpu.CompilerParams(vmem_limit_bytes=32 << 20),
        cost_estimate=pl.CostEstimate(
            flops=6 * count * depth * width, bytes_accessed=8 * count * width, transcendentals=0
        ),
        name="qkv",
    )(rows, w_qkv, cosine, sine)


def head_lanes(block, h):
    lane = lax.broadcasted_iota(jnp.int32, block.shape, 1)
    return jnp.where(lane // HEAD == h, block, jnp.zeros_like(block))


def transposed(block):
    return block.astype(f32).T


def forward_kernel(flag_ref, q_ref, k_ref, v_ref, segr_ref, segc_ref, o_ref, lse_ref, vt, m, l, acc):
    blocks = q_ref.shape[0] // BLOCK
    for b in range(blocks):
        vt[b] = transposed(v_ref[b * BLOCK : (b + 1) * BLOCK, :]).astype(bf16)

    @pl.loop(0, blocks)
    def _(qi):
        rows = pl.ds(pl.multiple_of(qi * BLOCK, BLOCK), BLOCK)
        q = q_ref[rows, :]
        m[...] = jnp.full(m.shape, masked_score, f32)
        l[...] = jnp.zeros(l.shape, f32)
        acc[...] = jnp.zeros(acc.shape, f32)

        @pl.loop(0, blocks)
        def _(ki):
            @pl.when(flag_ref[qi * blocks + ki] > 0)
            def _():
                cols = pl.ds(pl.multiple_of(ki * BLOCK, BLOCK), BLOCK)
                k = k_ref[cols, :]
                docs = segc_ref[cols, :]
                same = jnp.concatenate([docs] * (BLOCK // 128), axis=1) == segr_ref[qi]
                for h in range(2):
                    lo, hi = h * HEAD, (h + 1) * HEAD
                    s = jnp.where(same, mm(k, head_lanes(q, h), 1, 1), masked_score)
                    top = jnp.maximum(m[h], jnp.max(s, axis=0, keepdims=True))
                    p = jnp.exp(s - top)
                    shrink = jnp.exp(m[h] - top)
                    m[h] = top
                    l[h] = l[h] * shrink + jnp.sum(p, axis=0, keepdims=True)
                    acc[lo:hi, :] = acc[lo:hi, :] * shrink + mm(vt[ki, lo:hi, :], p.astype(bf16), 1, 0)

        for h in range(2):
            lo, hi = h * HEAD, (h + 1) * HEAD
            lse_ref[h, qi] = m[h] + jnp.log(l[h])
            acc[lo:hi, :] = acc[lo:hi, :] / l[h]
        o_ref[rows, :] = acc[...].T.astype(bf16)


def backward_kernel(
    flag_ref, q_ref, k_ref, v_ref, g_ref, o_ref, lse_ref, segr_ref, segc_ref, cos_ref, sin_ref,
    out_ref, kt, dk, dv, dq,
):
    blocks = q_ref.shape[0] // BLOCK
    for b in range(blocks):
        kt[b] = transposed(k_ref[b * BLOCK : (b + 1) * BLOCK, :]).astype(bf16)
    dk[...] = jnp.zeros(dk.shape, f32)
    dv[...] = jnp.zeros(dv.shape, f32)

    def turn_back(u, rows):
        return (u * cos_ref[rows, :] - turned(u) * sin_ref[rows, :]).astype(bf16)

    @pl.loop(0, blocks)
    def _(qi):
        rows = pl.ds(pl.multiple_of(qi * BLOCK, BLOCK), BLOCK)
        q, g = q_ref[rows, :], g_ref[rows, :]
        both = (g.astype(f32) * o_ref[rows, :].astype(f32)).T
        dq[...] = jnp.zeros(dq.shape, f32)

        @pl.loop(0, blocks)
        def _(ki):
            @pl.when(flag_ref[qi * blocks + ki] > 0)
            def _():
                cols = pl.ds(pl.multiple_of(ki * BLOCK, BLOCK), BLOCK)
                k, v = k_ref[cols, :], v_ref[cols, :]
                docs = segc_ref[cols, :]
                same = jnp.concatenate([docs] * (BLOCK // 128), axis=1) == segr_ref[qi]
                dk_sum, dv_sum = dk[cols, :], dv[cols, :]
                for h in range(2):
                    lo, hi = h * HEAD, (h + 1) * HEAD
                    delta = jnp.sum(both[lo:hi, :], axis=0, keepdims=True)
                    qh, gh = head_lanes(q, h), head_lanes(g, h)
                    s = jnp.where(same, mm(k, qh, 1, 1), masked_score)
                    p = jnp.exp(s - lse_ref[h, qi])
                    ds = (p * (mm(v, gh, 1, 1) - delta)).astype(bf16)
                    dv_sum = dv_sum + mm(p.astype(bf16), gh, 1, 0)
                    dk_sum = dk_sum + mm(ds, qh, 1, 0)
                    dq[lo:hi, :] = dq[lo:hi, :] + mm(kt[ki, lo:hi, :], ds, 1, 0)
                dk[cols, :] = dk_sum
                dv[cols, :] = dv_sum

        out_ref[0, rows, :] = turn_back(dq[...].T * (HEAD**-0.5), rows)

    @pl.loop(0, blocks)
    def _(b):
        rows = pl.ds(pl.multiple_of(b * BLOCK, BLOCK), BLOCK)
        out_ref[1, rows, :] = turn_back(dk[rows, :], rows)
        out_ref[2, rows, :] = dv[rows, :].astype(bf16)


def pieces_of(qkv, length):
    return [pl.BlockSpec((None, length, PAIR), functools.partial(lambda t, p, *_: (t, 0, p), t)) for t in range(3)]


def attend_forward(flags, qkv, seg_rows, seg_cols):
    _, length, width = qkv.shape
    blocks, pairs = length // BLOCK, width // PAIR
    return pl.pallas_call(
        forward_kernel,
        grid_spec=pltpu.PrefetchScalarGridSpec(
            num_scalar_prefetch=1,
            grid=(pairs,),
            in_specs=[
                *pieces_of(qkv, length),
                pl.BlockSpec((blocks, 1, BLOCK), lambda p, *_: (0, 0, 0)),
                pl.BlockSpec((length, 128), lambda p, *_: (0, 0)),
            ],
            out_specs=[
                pl.BlockSpec((length, PAIR), lambda p, *_: (0, p)),
                pl.BlockSpec((2, blocks, 1, BLOCK), lambda p, *_: (p, 0, 0, 0)),
            ],
            scratch_shapes=[
                pltpu.VMEM((blocks, PAIR, BLOCK), bf16),
                pltpu.VMEM((2, 1, BLOCK), f32),
                pltpu.VMEM((2, 1, BLOCK), f32),
                pltpu.VMEM((PAIR, BLOCK), f32),
            ],
        ),
        out_shape=[
            jax.ShapeDtypeStruct((length, width), bf16),
            jax.ShapeDtypeStruct((2 * pairs, blocks, 1, BLOCK), f32),
        ],
        compiler_params=pltpu.CompilerParams(vmem_limit_bytes=48 << 20),
        cost_estimate=pl.CostEstimate(
            flops=4 * length * length * width, bytes_accessed=8 * length * width, transcendentals=length * length * width // HEAD
        ),
        name="attend",
    )(flags, qkv, qkv, qkv, seg_rows, seg_cols)


def attend_backward(flags, qkv, grad, mixed, lse, seg_rows, seg_cols, cosine, sine):
    _, length, width = qkv.shape
    blocks, pairs = length // BLOCK, width // PAIR
    whole = pl.BlockSpec((length, PAIR), lambda p, *_: (0, p))
    table = pl.BlockSpec((length, PAIR), lambda p, *_: (0, 0))
    return pl.pallas_call(
        backward_kernel,
        grid_spec=pltpu.PrefetchScalarGridSpec(
            num_scalar_prefetch=1,
            grid=(pairs,),
            in_specs=[
                *pieces_of(qkv, length),
                whole,
                whole,
                pl.BlockSpec((2, blocks, 1, BLOCK), lambda p, *_: (p, 0, 0, 0)),
                pl.BlockSpec((blocks, 1, BLOCK), lambda p, *_: (0, 0, 0)),
                table,
                table,
                table,
            ],
            out_specs=pl.BlockSpec((3, length, PAIR), lambda p, *_: (0, 0, p)),
            scratch_shapes=[
                pltpu.VMEM((blocks, PAIR, BLOCK), bf16),
                pltpu.VMEM((length, PAIR), f32),
                pltpu.VMEM((length, PAIR), f32),
                pltpu.VMEM((PAIR, BLOCK), f32),
            ],
        ),
        out_shape=jax.ShapeDtypeStruct((3, length, width), bf16),
        compiler_params=pltpu.CompilerParams(vmem_limit_bytes=56 << 20),
        cost_estimate=pl.CostEstimate(
            flops=10 * length * length * width, bytes_accessed=16 * length * width, transcendentals=length * length * width // HEAD
        ),
        name="attend_back",
    )(flags, qkv, qkv, qkv, grad, mixed, lse, seg_rows, seg_cols, cosine, sine)


def qkv_pair_kernel(own_ref, got_ref, w_ref, cos_ref, sin_ref, *refs):
    o_ref, rows_ref = refs[-2:]
    which = pl.program_id(0)
    half = own_ref.shape[0]

    @pl.when(which == 0)
    def _():
        rows_ref[:half, :] = own_ref[...]
        rows_ref[half:, :] = got_ref[...]

    y = mm(rows_ref[...], w_ref[...], 1, 0)

    @pl.when(which < 2)
    def _():
        factor = jnp.where(which == 0, HEAD**-0.5, 1.0)
        for p in range(y.shape[1] // PAIR):
            u = y[:, p * PAIR : (p + 1) * PAIR]
            r = u * cos_ref[...] + turned(u) * sin_ref[...]
            o_ref[:, p * PAIR : (p + 1) * PAIR] = (r.astype(bf16) * factor.astype(bf16)).astype(bf16)

    @pl.when(which == 2)
    def _():
        o_ref[...] = y.astype(bf16)


def project_pair(j, own, got, w_qkv, cosine, sine, before, length):
    half, depth = own.shape
    width = w_qkv.shape[2]
    chunk = 2 * half
    table = pl.BlockSpec((chunk, PAIR), lambda t: (j, 0))
    return pl.pallas_call(
        qkv_pair_kernel,
        grid=(3,),
        in_specs=[
            pl.BlockSpec((half, depth), lambda t: (0, 0)),
            pl.BlockSpec((half, depth), lambda t: (0, 0)),
            pl.BlockSpec((None, depth, width), lambda t: (t, 0, 0)),
            table,
            table,
            *[pl.BlockSpec(memory_space=pl.ANY) for _ in before],
        ],
        out_specs=[
            pl.BlockSpec((None, chunk, width), lambda t: (t, j, 0)),
            pl.BlockSpec((chunk, depth), lambda t: (j, 0)),
        ],
        out_shape=[
            jax.ShapeDtypeStruct((3, length, width), bf16),
            jax.ShapeDtypeStruct((length, depth), bf16),
        ],
        input_output_aliases={5 + i: i for i in range(len(before))},
        compiler_params=pltpu.CompilerParams(vmem_limit_bytes=32 << 20),
        cost_estimate=pl.CostEstimate(
            flops=6 * chunk * depth * width, bytes_accessed=8 * depth * width, transcendentals=0
        ),
        name="qkv",
    )(own, got, w_qkv, cosine, sine, *before)


def forward_chunk_kernel(q_ref, k_ref, v_ref, segr_ref, segc_ref, o_ref, lse_ref, vt):
    length, count = k_ref.shape[0], q_ref.shape[0]
    for b in range(0, length, BLOCK):
        vt[:, b : b + BLOCK] = transposed(v_ref[b : b + BLOCK, :]).astype(bf16)
    q = q_ref[...]
    outs = []
    for h in range(2):
        qh = head_lanes(q, h)
        scores = []
        for b in range(0, length, BLOCK):
            same = jnp.concatenate([segc_ref[b : b + BLOCK, :]] * (count // 128), axis=1) == segr_ref[...]
            scores.append(jnp.where(same, mm(k_ref[b : b + BLOCK, :], qh, 1, 1), masked_score))
        top = functools.reduce(jnp.maximum, [jnp.max(s, axis=0, keepdims=True) for s in scores])
        total, summed = 0.0, 0.0
        for i, s in enumerate(scores):
            p = jnp.exp(s - top)
            total = total + jnp.sum(p, axis=0, keepdims=True)
            summed = summed + mm(vt[h * HEAD : (h + 1) * HEAD, i * BLOCK : (i + 1) * BLOCK], p.astype(bf16), 1, 0)
        lse_ref[h] = top + jnp.log(total)
        outs.append(summed / total)
    o_ref[...] = jnp.concatenate(outs, axis=0).T.astype(bf16)


def pair_pieces(j, length, chunk):
    return [
        pl.BlockSpec((None, chunk, PAIR), lambda p: (0, j, p)),
        pl.BlockSpec((None, length, PAIR), lambda p: (1, 0, p)),
        pl.BlockSpec((None, length, PAIR), lambda p: (2, 0, p)),
    ]


def attend_forward_pair(j, chunk, qkv, seg_rows, seg_cols):
    _, length, width = qkv.shape
    pairs = width // PAIR
    return pl.pallas_call(
        forward_chunk_kernel,
        grid=(pairs,),
        in_specs=[
            *pair_pieces(j, length, chunk),
            pl.BlockSpec((1, chunk), lambda p: (0, j)),
            pl.BlockSpec((length, 128), lambda p: (0, 0)),
        ],
        out_specs=[
            pl.BlockSpec((chunk, PAIR), lambda p: (0, p)),
            pl.BlockSpec((2, 1, chunk), lambda p: (p, 0, 0)),
        ],
        out_shape=[
            jax.ShapeDtypeStruct((chunk, width), bf16),
            jax.ShapeDtypeStruct((2 * pairs, 1, chunk), f32),
        ],
        scratch_shapes=[pltpu.VMEM((PAIR, length), bf16)],
        compiler_params=pltpu.CompilerParams(vmem_limit_bytes=48 << 20),
        cost_estimate=pl.CostEstimate(
            flops=16 * chunk * length * width,
            bytes_accessed=8 * length * width,
            transcendentals=chunk * length * width // HEAD,
        ),
        name="attend",
    )(qkv, qkv, qkv, seg_rows, seg_cols)


def mlp_kernel(own_ref, got_ref, b_own_ref, b_got_ref, up_ref, bias_ref, down_ref, *refs):
    rows_ref, hidden_ref, pre_ref, own_grad, got_grad, own_branch, got_branch, bias_grad, back, grads, branch = refs[-11:]
    tile, tiles = pl.program_id(0), pl.num_programs(0)
    half = own_ref.shape[0]

    @pl.when(tile == 0)
    def _():
        rows_ref[:half, :] = own_ref[...]
        rows_ref[half:, :] = got_ref[...]
        back[:half, :] = b_own_ref[...]
        back[half:, :] = b_got_ref[...]

    cubic, root = 0.044715, (2.0 / jnp.pi) ** 0.5
    u = mm(rows_ref[...], up_ref[...], 1, 0) + bias_ref[...]
    square = u * u
    t = jnp.tanh(u * (root + (root * cubic) * square))
    rising = 0.5 * (1.0 + t)
    hidden = (u * rising).astype(bf16)
    slope = rising + (0.5 * u) * (1.0 - t * t) * (root + (3.0 * cubic * root) * square)
    grad = (mm(back[...], down_ref[...], 1, 1) * slope).astype(bf16)
    hidden_ref[...] = hidden
    pre_ref[...] = grad
    bias_grad[...] = jnp.sum(grad.astype(f32), axis=0, keepdims=True)
    more, more_branch = mm(grad, up_ref[...], 1, 1), mm(hidden, down_ref[...], 1, 0)

    @pl.when(tile == 0)
    def _():
        grads[...] = more
        branch[...] = more_branch

    @pl.when(tile > 0)
    def _():
        grads[...] += more
        branch[...] += more_branch

    @pl.when(tile == tiles - 1)
    def _():
        own_grad[...] = grads[:half, :]
        got_grad[...] = grads[half:, :].astype(bf16)
        own_branch[...] = branch[:half, :]
        got_branch[...] = branch[half:, :].astype(bf16)


def mlp_pair(j, own, got, back_own, back_got, w_up, b_up, w_down, before, length):
    half, depth = own.shape
    width = w_up.shape[1]
    chunk, tile = 2 * half, min(width, 1024)
    small = pl.BlockSpec((half, depth), lambda t: (0, 0))
    wide = pl.BlockSpec((chunk, tile), lambda t: (j, t))
    return pl.pallas_call(
        mlp_kernel,
        grid=(width // tile,),
        in_specs=[
            small, small, small, small,
            pl.BlockSpec((depth, tile), lambda t: (0, t)),
            pl.BlockSpec((1, tile), lambda t: (0, t)),
            pl.BlockSpec((tile, depth), lambda t: (t, 0)),
            *[pl.BlockSpec(memory_space=pl.ANY) for _ in before],
        ],
        out_specs=[
            pl.BlockSpec((chunk, depth), lambda t: (j, 0)), wide, wide,
            small, small, small, small,
            pl.BlockSpec((1, tile), lambda t: (0, t)),
        ],
        out_shape=[
            jax.ShapeDtypeStruct((length, depth), bf16),
            jax.ShapeDtypeStruct((length, width), bf16),
            jax.ShapeDtypeStruct((length, width), bf16),
            jax.ShapeDtypeStruct((half, depth), f32),
            jax.ShapeDtypeStruct((half, depth), bf16),
            jax.ShapeDtypeStruct((half, depth), f32),
            jax.ShapeDtypeStruct((half, depth), bf16),
            jax.ShapeDtypeStruct((1, width), f32),
        ],
        scratch_shapes=[
            pltpu.VMEM((chunk, depth), bf16),
            pltpu.VMEM((chunk, depth), f32),
            pltpu.VMEM((chunk, depth), f32),
        ],
        input_output_aliases={7 + i: i for i in range(len(before))},
        compiler_params=pltpu.CompilerParams(vmem_limit_bytes=56 << 20),
        cost_estimate=pl.CostEstimate(
            flops=12 * chunk * depth * width, bytes_accessed=12 * depth * width, transcendentals=chunk * width
        ),
        name="mlp",
    )(own, got, back_own, back_got, w_up, b_up[None, :], w_down, *before)


MESH = pl.DeviceIdType.MESH
ADD_ROWS = 32
STEPS = 9
EDGES = 4


def add_low(a, a_at, b, rows):
    @pl.loop(0, rows // ADD_ROWS)
    def _(i):
        at = pl.ds(pl.multiple_of(i * ADD_ROWS, ADD_ROWS), ADD_ROWS)
        kept = a[pl.ds(pl.multiple_of(a_at + i * ADD_ROWS, ADD_ROWS), ADD_ROWS), :].astype(f32)
        b[at, :] = (kept + b[at, :].astype(f32)).astype(bf16)


class Unit:
    def __init__(self, part, out, column, got, send, recv, local, place):
        self.part, self.out, self.got = part, out, got
        self.send, self.recv, self.local = send, recv, local
        self.rows, columns = 2 * got[0].shape[0], got[0].shape[1]
        self.columns = pl.ds(column, columns)
        self.bit = [(place // (1 << b)) % 2 for b in range(EDGES)]
        self.partner = [place + (1 - 2 * self.bit[b]) * (1 << b) for b in range(EDGES)]
        self.base = [0]
        for b in range(EDGES):
            self.base.append(self.base[-1] + self.bit[b] * (self.rows >> (b + 1)))

    def remote(self, src, dst, stage, b):
        return pltpu.make_async_remote_copy(
            src_ref=src,
            dst_ref=dst,
            send_sem=self.send.at[stage],
            recv_sem=self.recv.at[stage],
            device_id={"dp": self.partner[b]},
            device_id_type=MESH,
        )

    def halving(self, b):
        half = self.rows >> (b + 1)
        source = self.part if b == 0 else self.got[b - 1]
        away = pl.ds(pl.multiple_of((1 - self.bit[b]) * half, ADD_ROWS), half)
        return self.remote(source.at[away], self.got[b], b, b)

    def spot(self, b):
        size = self.rows >> (b + 1)
        return self.out.at[pl.ds(pl.multiple_of(self.base[b + 1], ADD_ROWS), size), self.columns]

    def own(self):
        return pltpu.make_async_copy(self.got[3], self.spot(3), self.local.at[0])

    def gathering(self, b):
        return self.remote(self.got[3] if b == 3 else self.spot(b), self.spot(b), 7 - b, b)

    def step(self, k):
        if k == 0:
            self.halving(0).start()
        elif k < 5:
            b = k - 1
            self.halving(b).wait()
            half = self.rows >> (b + 1)
            add_low(self.part if b == 0 else self.got[b - 1], self.bit[b] * half, self.got[b], half)
            if b < 3:
                self.halving(b + 1).start()
            else:
                self.own().start()
                self.gathering(3).start()
        elif k == 5:
            self.own().wait()
            self.gathering(3).wait()
            self.gathering(2).start()
        elif k < 8:
            self.gathering(8 - k).wait()
            self.gathering(7 - k).start()
        else:
            self.gathering(0).wait()


def unit_scratch(rows, columns):
    return [
        *[pltpu.VMEM((rows >> (b + 1), columns), bf16) for b in range(EDGES)],
        pltpu.SemaphoreType.DMA((2 * EDGES,)),
        pltpu.SemaphoreType.DMA((2 * EDGES,)),
        pltpu.SemaphoreType.DMA((1,)),
    ]


def greet(targets):
    barrier = pltpu.get_barrier_semaphore()
    for target in targets:
        pl.semaphore_signal(barrier, inc=1, device_id=target, device_id_type=MESH)
    pl.semaphore_wait(barrier, len(targets))


TURNS = (
    (None, 7, 19, 26, 33, 40, 47, 62, 66),
    (None, 11, 31, 38, 45, 52, 59, 76, 80),
    (None, 16, 42, 49, 56, 63, 72, 92, 96),
    (None, 23, 54, 61, 68, 75, 98, 114, 118),
    (None, 59, 66, 71, 76, 81, 86, 104, 108),
    (None, 84, 96, 101, 106, 111, 116, 134, 138),
    (None, 86, 101, 106, 111, 116, 121, 140, 144),
    (None, 88, 106, 111, 116, 121, 126, 146, 150),
)
WIDE = 512
STEP_ROWS = 64


def tail_kernel(
    hidden, full_back, rows_two, grad_pre, qkv_hbm, mixed_a, mixed_b, rows_hbm, w_qkv_hbm, w_out_hbm,
    grad_a, grad_b, got_a, got_b, mid_a, mid_b, proj_a, proj_b, tokens_hbm, cot_hbm,
    rows_of, known, lse_a, lse_b, segr, segc, cosine, sine,
    down_sum, up_sum, out_sum, q_sum, k_sum, v_sum, grad_x, everyone,
    qkv, mixed, rows_one, w_qkv, w_out, proj, mix_grad, d_qkv, dk, dv, from_x, grads, middle, projected, tokens, cot,
    part_a, part_b, part_c, part_d, part_e, col_sums, small, small_got,
    load, x_send, x_recv, all_send, all_recv, *more,
):
    place, me = lax.axis_index("dp"), lax.axis_index("tensor")
    length, depth = rows_one.shape
    chunks, half, _ = from_x.shape
    chunk = 2 * half
    width = mixed.shape[1]
    pairs = width // PAIR
    across = {"tensor": 1 - me}

    specs = [
        (part_a, down_sum.at[pl.ds(0, depth)], 0), (part_b, down_sum.at[pl.ds(depth, depth)], 0),
        (part_c, up_sum, 0), (part_d, up_sum, depth), (part_e, out_sum, 0),
        (qkv.at[2], v_sum, 0), (qkv.at[1], k_sum, 0), (qkv.at[0], q_sum, 0),
    ]
    units = []
    for i, (part, out, column) in enumerate(specs):
        *got, send, recv, local = more[7 * i : 7 * (i + 1)]
        units.append(Unit(part, out, column, got, send, recv, local, place))

    def x_copy(src, dst, i):
        return pltpu.make_async_remote_copy(
            src_ref=src, dst_ref=dst, send_sem=x_send.at[i], recv_sem=x_recv.at[i],
            device_id=across, device_id_type=MESH,
        )

    each = range(chunks)
    grads_in = [x_copy((got_a, got_b)[c], from_x.at[c], c) for c in each]
    projs = [x_copy(proj.at[c, :half], proj.at[c, half:], chunks + c) for c in each]
    ones = [x_copy(proj.at[c, :half], from_x.at[c], 2 * chunks + c) for c in each]
    smalls = x_copy(small, small_got, 3 * chunks)
    partner = units[0].partner

    loads = []

    def fetch(src, dst):
        copy = pltpu.make_async_copy(src, dst, load.at[len(loads)])
        copy.start()
        loads.append(copy)
        return copy

    turns = sorted((t, k, i) for i, times in enumerate(TURNS) for k, t in enumerate(times) if k)
    done = [0]

    def until(time):
        while done[0] < len(turns) and turns[done[0]][0] <= time:
            _, k, i = turns[done[0]]
            units[i].step(k)
            done[0] += 1

    greet([*[{"dp": p} for p in partner], across])
    grads_in[0].start()
    slots = [w_qkv.at[0], w_qkv.at[1], w_qkv.at[2], d_qkv.at[2]]
    cut = lambda t: slice(t * WIDE, (t + 1) * WIDE)
    backs = fetch(full_back, rows_one)
    hiddens = [fetch(hidden.at[:, cut(t)], slots[t]) for t in range(4)]
    norms = [
        [fetch(src, dst.at[c]) for src, dst in (
            ((grad_a, grad_b)[c], grads), ((mid_a, mid_b)[c], middle), ((proj_a, proj_b)[c], projected),
            (tokens_hbm.at[c * half : (c + 1) * half], tokens), (cot_hbm.at[c * half : (c + 1) * half], cot),
        )]
        for c in each
    ]
    twos = [fetch(rows_two.at[:, cut(t)], d_qkv.at[t]) for t in range(2)]
    col_sums[...] = jnp.zeros(col_sums.shape, f32)

    backs.wait()
    pres = []
    for t in range(4):
        hiddens[t].wait()
        part = (part_a, part_b)[t // 2]

        @pl.loop(0, WIDE // 256)
        def _(r):
            at = pl.ds(pl.multiple_of(r * 256, 256), 256)
            to = pl.ds(pl.multiple_of((t % 2) * WIDE + r * 256, 256), 256)
            part[to, :] = mm(slots[t][:, at], rows_one[...], 0, 0).astype(bf16)

        pres.append(fetch(grad_pre.at[:, cut(t)], slots[t]))
        if t % 2:
            units[t // 2].step(0)
            until(4 + 4 * (t // 2))
    main = [
        fetch(w_out_hbm, w_out), fetch(mixed_a, mixed.at[:chunk]), fetch(mixed_b, mixed.at[chunk:]),
        fetch(qkv_hbm, qkv), fetch(rows_hbm, rows_one),
    ]

    def up_part(t):
        pres[t].wait()
        part = (part_c, part_d)[t // 2]

        @pl.loop(0, depth // 256)
        def _(r):
            to = pl.ds(pl.multiple_of(r * 256, 256), 256)
            at = pl.ds(pl.multiple_of((r % 2) * 256, 256), 256)
            part[to, cut(t % 2)] = mm(d_qkv[r // 2, :, at], slots[t][...], 0, 0).astype(bf16)

    def fold(row, values):
        col_sums[row : row + 1, :] += jnp.sum(values, axis=0, keepdims=True)

    def norm_back(grad, values, weight):
        center = values - jnp.mean(values, axis=1, keepdims=True)
        root = lax.rsqrt(jnp.mean(center * center, axis=1, keepdims=True) + norm_eps)
        normal = center * root
        inner = grad * weight
        back = inner - jnp.mean(inner, axis=1, keepdims=True) - normal * jnp.mean(inner * normal, axis=1, keepdims=True)
        return root * back, normal

    gain_two, scale_m, gate_a, gain_one, scale_a = [rows_of[r : r + 1, :] for r in range(5)]

    def second_norm(c):
        for copy in norms[c]:
            copy.wait()

        @pl.loop(0, half // STEP_ROWS)
        def _(i):
            at = pl.ds(pl.multiple_of(i * STEP_ROWS, STEP_ROWS), STEP_ROWS)
            grad = grads[c, at, :] + from_x[c, at, :].astype(f32)
            back, normal = norm_back(grad, middle[c, at, :], gain_two * (1.0 + scale_m))
            total = back + cot[c, at, :].astype(f32)
            grads[c, at, :] = total
            proj[c, at, :] = (total * gate_a).astype(bf16)
            fold(0, grad)
            fold(1, grad * normal)
            fold(2, total * projected[c, at, :])

        projs[c].start()

    for copy in twos:
        copy.wait()
    up_part(0)
    up_part(1)
    units[2].step(0)
    grads_in[0].wait()
    grads_in[1].start()
    second_norm(0)
    until(16)
    up_part(2)
    up_part(3)
    units[3].step(0)
    weights = fetch(w_qkv_hbm, w_qkv)
    until(23)
    grads_in[1].wait()
    second_norm(1)
    until(32)

    def turn_back(u, rows):
        return (u * cosine[rows, :] - turned(u) * sine[rows, :]).astype(bf16)

    def attend_back(p, c):
        lanes = pl.ds(pl.multiple_of(p * PAIR, PAIR), PAIR)
        rows = slice(c * chunk, (c + 1) * chunk)
        q, g = qkv[0, rows, lanes], mix_grad[rows, lanes]
        both = (g.astype(f32) * mixed[rows, lanes].astype(f32)).T
        qh = [head_lanes(q, h) for h in range(2)]
        gh = [head_lanes(g, h) for h in range(2)]
        delta = [jnp.sum(both[h * HEAD : (h + 1) * HEAD, :], axis=0, keepdims=True) for h in range(2)]
        q_two, g_two = jnp.concatenate(qh, axis=0), jnp.concatenate(gh, axis=0)
        docs = segr[:, rows]
        dq = [0.0, 0.0]
        for b in range(0, length, BLOCK):
            cols = slice(b, b + BLOCK)
            k, v = qkv[1, cols, lanes], qkv[2, cols, lanes]
            turned_k = transposed(k).astype(bf16)
            same = jnp.concatenate([segc[cols, :]] * (chunk // 128), axis=1) == docs
            ps, ds = [], []
            for h in range(2):
                s = jnp.where(same, mm(k, qh[h], 1, 1), masked_score)
                pr = jnp.exp(s - (lse_a, lse_b)[c][2 * p + h])
                d = (pr * (mm(v, gh[h], 1, 1) - delta[h])).astype(bf16)
                ps.append(pr.astype(bf16))
                ds.append(d)
                dq[h] = dq[h] + mm(turned_k[h * HEAD : (h + 1) * HEAD, :], d, 1, 0)
            add_v = mm(jnp.concatenate(ps, axis=1), g_two, 1, 0)
            add_k = mm(jnp.concatenate(ds, axis=1), q_two, 1, 0)
            if c < chunks - 1:
                dv[cols, lanes] = add_v if c == 0 else dv[cols, lanes] + add_v
                dk[cols, lanes] = add_k if c == 0 else dk[cols, lanes] + add_k
            else:
                d_qkv[1, cols, lanes] = turn_back(dk[cols, lanes] + add_k, cols)
                d_qkv[2, cols, lanes] = (dv[cols, lanes] + add_v).astype(bf16)
        d_qkv[0, rows, lanes] = turn_back(jnp.concatenate(dq, axis=0).T * (HEAD**-0.5), rows)

    for copy in main:
        copy.wait()
    clock = 36
    for c in each:
        projs[c].wait()
        mix_grad[c * chunk : (c + 1) * chunk, :] = mm(proj[c], w_out[...], 1, 1).astype(bf16)
        if c == chunks - 1:

            @pl.loop(0, width // 256)
            def _(r):
                at = pl.ds(pl.multiple_of(r * 256, 256), 256)
                part_e[at, :] = sum(
                    mm(mixed[n * chunk : (n + 1) * chunk, at], proj[n], 0, 0) for n in each
                ).astype(bf16)

            units[4].step(0)
            clock += 3
        until(clock)

        @pl.loop(0, pairs)
        def _(p):
            attend_back(p, c)
            for n in range(pairs):

                @pl.when(p == n)
                def _():
                    until(clock + 4.4 * (n + 1))

        clock += 19

    def rows_back(start):
        at = slice(start, start + half)
        return sum(mm(d_qkv[t, at, :], w_qkv[t], 1, 1) for t in range(3))

    weights.wait()
    for c in each:
        proj[c, :half] = rows_back(c * chunk + half).astype(bf16)
        if c == 0:
            ones[c].start()
        until(clock + 2 * (c + 1))
    for i in range(3):

        @pl.loop(0, depth // 256)
        def _(r):
            at = pl.ds(pl.multiple_of(r * 256, 256), 256)
            qkv[2 - i, at, :] = mm(rows_one[:, at], d_qkv[2 - i], 0, 0).astype(bf16)

        units[5 + i].step(0)
        until(clock + 6 + 2 * i)
    for c in each:
        middle[c] = rows_back(c * chunk)

    for c in each:
        ones[c].wait()
        if c < chunks - 1:
            ones[c + 1].start()

        @pl.loop(0, half // STEP_ROWS)
        def _(i):
            at = pl.ds(pl.multiple_of(i * STEP_ROWS, STEP_ROWS), STEP_ROWS)
            grad = middle[c, at, :] + from_x[c, at, :].astype(f32)
            back, normal = norm_back(grad, tokens[c, at, :].astype(f32), gain_one * (1.0 + scale_a))
            grad_x[c, at, :] = (back + grads[c, at, :]).astype(bf16)
            fold(3, grad)
            fold(4, grad * normal)

        until(100 + 10 * c)

    shift, scaled, gated, shift_one, scaled_one = [col_sums[r : r + 1, :] for r in range(5)]
    small[...] = known[...] + jnp.concatenate(
        [
            shift_one, gain_one * scaled_one, gated, shift, gain_two * scaled, jnp.zeros_like(shift),
            (1.0 + scale_a) * scaled_one, (1.0 + scale_m) * scaled, jnp.zeros((8, depth), f32),
        ],
        axis=0,
    )
    smalls.start()
    until(112)
    smalls.wait()
    number = lax.broadcasted_iota(jnp.int32, small.shape, 0)
    everyone[0] = small[...] + jnp.where(number < 9, small_got[...], 0.0)
    for n, b in enumerate(reversed(range(EDGES))):
        copy = pltpu.make_async_remote_copy(
            src_ref=everyone.at[pl.ds(0, 1 << n)], dst_ref=everyone.at[pl.ds(1 << n, 1 << n)],
            send_sem=all_send.at[n], recv_sem=all_recv.at[n],
            device_id={"dp": partner[b]}, device_id_type=MESH,
        )
        copy.start()
        until(117 + 6 * n)
        copy.wait()
    until(1000)


def tail(
    hidden, full_back, rows_two, grad_pre, qkv, mixed, rows_one, w_qkv, w_out, own_grad, got_grad, middle, projected,
    tokens, cot, rows_of, known, lse, segr, segc, cosine, sine,
):
    _, length, width = qkv.shape
    chunks = len(mixed)
    half, depth = got_grad[0].shape
    anywhere, near = pl.BlockSpec(memory_space=pl.ANY), pl.BlockSpec(memory_space=pltpu.VMEM)
    shaped, kept = jax.ShapeDtypeStruct, pltpu.VMEM
    in_chunks = (chunks, half, depth)
    scratch = [
        kept(qkv.shape, bf16), kept((length, width), bf16), kept(rows_one.shape, bf16), kept(w_qkv.shape, bf16),
        kept(w_out.shape, bf16), kept((chunks, 2 * half, depth), bf16), kept((length, width), bf16),
        kept((3, length, width), bf16), kept((length, width), f32), kept((length, width), f32),
        kept(in_chunks, bf16), kept(in_chunks, f32), kept(in_chunks, f32), kept(in_chunks, f32),
        kept(in_chunks, bf16), kept(in_chunks, bf16),
        *[kept((depth, depth), bf16)] * 4, kept((width, depth), bf16),
        kept((8, depth), f32), kept(known.shape, f32), kept(known.shape, f32),
        pltpu.SemaphoreType.DMA((27,)),
        pltpu.SemaphoreType.DMA((3 * chunks + 1,)), pltpu.SemaphoreType.DMA((3 * chunks + 1,)),
        pltpu.SemaphoreType.DMA((EDGES,)), pltpu.SemaphoreType.DMA((EDGES,)),
        *unit_scratch(depth, depth) * 4, *unit_scratch(width, depth), *unit_scratch(depth, width) * 3,
    ]
    return pl.pallas_call(
        tail_kernel,
        in_specs=[anywhere] * 20 + [near] * 8,
        out_specs=[anywhere] * 6 + [near] * 2,
        out_shape=[
            shaped((hidden.shape[1], depth), bf16), shaped((depth, hidden.shape[1]), bf16), shaped((width, depth), bf16),
            *[shaped((depth, width), bf16)] * 3,
            shaped(in_chunks, bf16), shaped((1 << EDGES, *known.shape), f32),
        ],
        scratch_shapes=scratch,
        compiler_params=pltpu.CompilerParams(collective_id=1, has_side_effects=True, vmem_limit_bytes=61 << 20),
        name="tail",
    )(
        hidden, full_back, rows_two, grad_pre, qkv, *mixed, rows_one, w_qkv, w_out, *own_grad, *got_grad, *middle,
        *projected, tokens, cot, rows_of, known, *lse, segr, segc, cosine, sine,
    )


def body_pair(
    tokens, cond, doc_lengths, w_ada, b_ada, gain_one, w_qkv, w_out, gain_two, w_up, b_up, w_down, b_down, cotangent
):
    own, width = tokens.shape
    length = 2 * own
    chunks = 2
    half, chunk = own // chunks, length // chunks
    me = lax.axis_index("tensor")

    def swap(values):
        return lax.ppermute(values, "tensor", [(0, 1), (1, 0)])

    step = jnp.arange(length, dtype=jnp.int32)
    in_chunk = step % chunk
    places = jnp.where(in_chunk < half, me, 1 - me) * own + (step // chunk) * half + in_chunk % half
    segment, doc_first = documents(doc_lengths[0], places)
    cosine, sine = rope_tables(places - doc_first)
    seg_rows = segment[None, :]
    seg_cols = jnp.broadcast_to(segment[:, None], (length, 128))

    modulation = jnp.dot(cond, w_ada, preferred_element_type=f32)[0] + b_ada
    shift_a, scale_a, gate_a, shift_m, scale_m, gate_m = jnp.split(modulation, 6)
    cuts = [slice(c * half, (c + 1) * half) for c in range(chunks)]
    x_rows = [tokens[cut].astype(f32) for cut in cuts]
    grad_out = [cotangent[cut].astype(f32) for cut in cuts]
    each = range(chunks)

    act_one = [modulate(x_rows[c], gain_one, shift_a, scale_a).astype(bf16) for c in each]
    got_one = [swap(act_one[c]) for c in each]
    back = [(grad_out[c] * gate_m).astype(bf16) for c in each]
    state = ()
    for c in each:
        state = project_pair(c, act_one[c], got_one[c], w_qkv, cosine, sine, state, length)
    qkv, rows_one = state
    got_back = [swap(back[c]) for c in each]
    full_back = jnp.concatenate([piece for c in each for piece in (back[c], got_back[c])], axis=0)

    mixed, lse, projected, middle, act_two, got_two = [], [], [], [], [], []
    for c in each:
        m, l = attend_forward_pair(c, chunk, qkv, seg_rows, seg_cols)
        mixed.append(m)
        lse.append(l)
    sums = [swap(jnp.dot(mixed[c][half:], w_out, preferred_element_type=f32).astype(bf16)) for c in each]
    for c in each:
        projected.append(jnp.dot(mixed[c][:half], w_out, preferred_element_type=f32) + sums[c].astype(f32))
        middle.append(x_rows[c] + gate_a * projected[c])
        act_two.append(modulate(middle[c], gain_two, shift_m, scale_m).astype(bf16))
        got_two.append(swap(act_two[c]))
    state, pieces = (), []
    for c in each:
        out = mlp_pair(c, act_two[c], got_two[c], back[c], got_back[c], w_up, b_up, w_down, state, length)
        state, rest = out[:3], out[3:]
        pieces.append(rest)
    rows_two, hidden, grad_pre = state
    grad_b_up = sum(pieces[c][4] for c in each)[0]
    branch = [pieces[c][2] + swap(pieces[c][3]).astype(f32) + b_down for c in each]
    output = jnp.concatenate([(middle[c] + gate_m * branch[c]).astype(bf16) for c in each], axis=0)
    grad_gate_m = sum(jnp.sum(grad_out[c] * branch[c], axis=0) for c in each)
    grad_b_down = sum(jnp.sum(back[c].astype(f32), axis=0) for c in each)

    none = jnp.zeros((width,), f32)
    known = jnp.stack(
        [
            none, none, none, none, none, grad_gate_m, none, none, grad_b_down,
            grad_b_up[:width], grad_b_up[width:],
            jnp.pad(cond[0].astype(f32), (0, width - cond.shape[1])), none, none, none, none,
        ]
    )
    *sums, grad_x, everyone = tail(
        hidden, full_back, rows_two, grad_pre, qkv, mixed, rows_one, w_qkv, w_out,
        [pieces[c][0] for c in each], [pieces[c][1] for c in each], middle, projected, tokens, cotangent,
        jnp.stack([gain_two, scale_m, gate_a, gain_one, scale_a, none, none, none]), known,
        lse, seg_rows, seg_cols, cosine, sine,
    )
    grad_w_down, grad_w_up, grad_w_out, grad_q, grad_k, grad_v = [s.astype(f32) for s in sums]
    grad_w_qkv = jnp.stack([grad_q, grad_k, grad_v])
    grad_x = grad_x.reshape(own, width)
    mods = everyone[:, :6].reshape(-1, 6 * width)
    conds = everyone[:, 11, : cond.shape[1]]
    grad_cond = jnp.dot(w_ada.astype(f32), mods[0], precision=lax.Precision.HIGHEST)[None, :]
    grad_w_ada = jnp.einsum("nc,nm->cm", conds, mods, precision=lax.Precision.HIGHEST, preferred_element_type=f32)
    total = jnp.sum(everyone, axis=0)
    grad_b_ada = total[:6].reshape(-1)
    grad_gain_one, grad_gain_two, grad_b_down = total[6], total[7], total[8]
    grad_b_up = total[9:11].reshape(-1)
    return (
        output, grad_x, grad_cond, grad_w_ada, grad_b_ada, grad_gain_one, grad_w_qkv, grad_w_out, grad_gain_two,
        grad_w_up, grad_b_up, grad_w_down, grad_b_down,
    )


def body_any(
    tokens, cond, doc_lengths, w_ada, b_ada, gain_one, w_qkv, w_out, gain_two, w_up, b_up, w_down, b_down, cotangent
):
    tensor_size = lax.axis_size("tensor")
    own = tokens.shape[0]
    length = own * tensor_size

    def all_rows(values):
        return lax.all_gather(values, "tensor", axis=0, tiled=True)

    def own_sum(values):
        return lax.psum_scatter(values, "tensor", scatter_dimension=0, tiled=True)

    def sum_over_dp(part):
        return lax.psum(part, "dp")

    places = jnp.arange(length, dtype=jnp.int32)
    segment, doc_first = documents(doc_lengths[0], places)
    cosine, sine = rope_tables(places - doc_first)
    blocks = length // BLOCK
    in_blocks = segment.reshape(blocks, BLOCK)
    least, most = jnp.min(in_blocks, axis=1), jnp.max(in_blocks, axis=1)
    meets = (least[:, None] <= most[None, :]) & (least[None, :] <= most[:, None])
    flags = meets.astype(jnp.int32).reshape(-1)
    seg_rows = in_blocks[:, None, :]
    seg_cols = jnp.broadcast_to(segment[:, None], (length, 128))

    modulation = jnp.dot(cond, w_ada, preferred_element_type=f32)[0] + b_ada
    shift_a, scale_a, gate_a, shift_m, scale_m, gate_m = jnp.split(modulation, 6)
    x_rows = tokens.astype(f32)
    grad_out = cotangent.astype(f32)

    act_one = modulate(x_rows, gain_one, shift_a, scale_a).astype(bf16)
    rows_one = all_rows(act_one)
    grad_branch = (grad_out * gate_m).astype(bf16)
    full_branch = all_rows(grad_branch)
    qkv = project_qkv(rows_one, w_qkv, cosine, sine)
    mixed, lse = attend_forward(flags, qkv, seg_rows, seg_cols)
    projected = own_sum(jnp.dot(mixed, w_out, preferred_element_type=f32))
    middle = x_rows + gate_a * projected
    rows_two = all_rows(modulate(middle, gain_two, shift_m, scale_m).astype(bf16))
    pre_act = jnp.dot(rows_two, w_up, preferred_element_type=f32) + b_up
    hidden = jax.nn.gelu(pre_act, approximate=True).astype(bf16)

    grad_hidden = jnp.einsum("sd,fd->sf", full_branch, w_down, preferred_element_type=f32)
    _, gelu_back = jax.vjp(lambda values: jax.nn.gelu(values, approximate=True), pre_act)
    grad_pre = gelu_back(grad_hidden)[0].astype(bf16)
    grad_act_two = own_sum(jnp.einsum("sf,df->sd", grad_pre, w_up, preferred_element_type=f32))
    grad_w_down = sum_over_dp(jnp.einsum("sf,sd->fd", hidden, full_branch, preferred_element_type=f32))
    grad_w_up = sum_over_dp(jnp.einsum("sd,sf->df", rows_two, grad_pre, preferred_element_type=f32))

    branch = own_sum(jnp.dot(hidden, w_down, preferred_element_type=f32)) + b_down
    output = (middle + gate_m * branch).astype(bf16)
    grad_gate_m = jnp.sum(grad_out * branch, axis=0)
    grad_b_down = jnp.sum(grad_branch.astype(f32), axis=0)
    grad_b_up = jnp.sum(grad_pre.astype(f32), axis=0)

    _, second_back = jax.vjp(modulate, middle, gain_two, shift_m, scale_m)
    grad_middle, grad_gain_two, grad_shift_m, grad_scale_m = second_back(grad_act_two)
    grad_middle = grad_middle + grad_out
    full_proj = all_rows((grad_middle * gate_a).astype(bf16))
    grad_gate_a = jnp.sum(grad_middle * projected, axis=0)
    grad_mixed = jnp.einsum("sd,ed->se", full_proj, w_out, preferred_element_type=f32).astype(bf16)
    grad_w_out = sum_over_dp(jnp.einsum("se,sd->ed", mixed, full_proj, preferred_element_type=f32))
    grad_qkv = attend_backward(flags, qkv, grad_mixed, mixed, lse, seg_rows, seg_cols, cosine, sine)
    grad_act_one = own_sum(jnp.einsum("tse,tde->sd", grad_qkv, w_qkv, preferred_element_type=f32))
    grad_w_qkv = jnp.einsum("sd,tse->tde", rows_one, grad_qkv, preferred_element_type=f32)
    grad_w_qkv = sum_over_dp(grad_w_qkv.reshape(-1, grad_w_qkv.shape[2])).reshape(grad_w_qkv.shape)

    _, first_back = jax.vjp(modulate, x_rows, gain_one, shift_a, scale_a)
    grad_x, grad_gain_one, grad_shift_a, grad_scale_a = first_back(grad_act_one)
    grad_x = (grad_x + grad_middle).astype(bf16)

    small = jnp.concatenate(
        [
            grad_shift_a, grad_scale_a, grad_gate_a, grad_shift_m, grad_scale_m, grad_gate_m,
            grad_gain_one, grad_gain_two, grad_b_down,
        ]
    )
    small = lax.psum(small, "tensor")
    mod_size = modulation.shape[0]
    grad_mod = small[:mod_size]
    grad_cond = jnp.dot(w_ada.astype(f32), grad_mod, precision=lax.Precision.HIGHEST)[None, :]
    everyone = lax.all_gather(
        jnp.concatenate([small, grad_b_up, cond[0].astype(f32)])[None, :], "dp", axis=0, tiled=True
    )
    conds = everyone[:, -cond.shape[1] :]
    mods = everyone[:, :mod_size]
    grad_w_ada = jnp.einsum("nc,nm->cm", conds, mods, precision=lax.Precision.HIGHEST, preferred_element_type=f32)
    sums = jnp.sum(everyone, axis=0)
    width = tokens.shape[1]
    grad_b_ada = sums[:mod_size]
    grad_gain_one, grad_gain_two, grad_b_down = jnp.split(sums[mod_size : mod_size + 3 * width], 3)
    grad_b_up = sums[mod_size + 3 * width : -cond.shape[1]]
    return (
        output, grad_x, grad_cond, grad_w_ada, grad_b_ada, grad_gain_one, grad_w_qkv, grad_w_out, grad_gain_two,
        grad_w_up, grad_b_up, grad_w_down, grad_b_down,
    )


def solution(mesh):
    swaps = mesh.shape["tensor"] == 2 and mesh.shape["dp"] == 16
    placed = (
        P(("dp", "tensor"), None), P("dp", None), P("dp", None), P(), P(), P(), P(None, None, "tensor"),
        P("tensor", None), P(), P(None, "tensor"), P("tensor"), P("tensor", None), P(), P(("dp", "tensor"), None),
    )
    return jax.shard_map(
        body_pair if swaps else body_any,
        mesh=mesh,
        in_specs=placed,
        out_specs=(
            P(("dp", "tensor"), None), P(("dp", "tensor"), None), P("dp", None), P(), P(), P(),
            P(None, None, "tensor"), P("tensor", None), P(), P(None, "tensor"), P("tensor"), P("tensor", None), P(),
        ),
        check_vma=False,
    )
```

```python
import functools

import jax
import jax.numpy as jnp
from jax import lax
from jax.experimental import pallas as pl
from jax.experimental.pallas import tpu as pltpu
from jax.sharding import PartitionSpec as P

HEAD = 64
PAIR = 2 * HEAD
BLOCK = 256
ROWS = 512

norm_eps = 1e-05
rope_base = 10000.0
masked_score = -1e30
f32, bf16 = jnp.float32, jnp.bfloat16


def layer_norm(values, gain):
    center = values - jnp.mean(values, axis=-1, keepdims=True)
    spread = jnp.mean(center * center, axis=-1, keepdims=True)
    return center * lax.rsqrt(spread + norm_eps) * gain


def modulate(values, gain, shift, scale):
    return layer_norm(values, gain) * (1.0 + scale) + shift


def documents(lengths, places):
    numbers = jnp.arange(lengths.shape[0], dtype=jnp.int32)
    earlier = (numbers[None, :] < numbers[:, None]).astype(jnp.int32)
    starts = jnp.sum(earlier * lengths[None, :], axis=1)
    ends = starts + lengths
    inside = ((places[:, None] >= starts[None, :]) & (places[:, None] < ends[None, :])).astype(
        jnp.int32
    )
    segment = jnp.sum(inside * numbers[None, :], axis=1)
    doc_first = jnp.sum(inside * starts[None, :], axis=1)
    return segment, doc_first


def rope_tables(offsets):
    exponent = jnp.arange(HEAD // 2, dtype=f32) * (2.0 / HEAD)
    frequency = jnp.power(jnp.float32(rope_base), -exponent)
    angles = offsets.astype(f32)[:, None] * frequency[None, :]
    cosine, sine = jnp.cos(angles), jnp.sin(angles)
    repeat = PAIR // (HEAD // 2)
    return jnp.concatenate([cosine] * repeat, axis=-1), jnp.concatenate([sine] * repeat, axis=-1)


def turned(values):
    lane = lax.broadcasted_iota(jnp.int32, values.shape, 1)
    half = HEAD // 2
    from_right = pltpu.roll(values, PAIR - half, axis=1)
    from_left = pltpu.roll(values, half, axis=1)
    return jnp.where(lane % HEAD < half, -from_right, from_left)


def mm(a, b, da, db):
    return lax.dot_general(a, b, (((da,), (db,)), ((), ())), preferred_element_type=f32)


def qkv_kernel(x_ref, w_ref, cos_ref, sin_ref, o_ref):
    which = pl.program_id(1)
    y = mm(x_ref[...], w_ref[...], 1, 0)

    @pl.when(which < 2)
    def _():
        factor = jnp.where(which == 0, HEAD**-0.5, 1.0)
        for p in range(y.shape[1] // PAIR):
            u = y[:, p * PAIR : (p + 1) * PAIR]
            r = u * cos_ref[...] + turned(u) * sin_ref[...]
            o_ref[:, p * PAIR : (p + 1) * PAIR] = (r.astype(bf16) * factor.astype(bf16)).astype(bf16)

    @pl.when(which == 2)
    def _():
        o_ref[...] = y.astype(bf16)


def project_qkv(rows, w_qkv, cosine, sine):
    count, depth = rows.shape
    width = w_qkv.shape[2]
    return pl.pallas_call(
        qkv_kernel,
        grid=(count // ROWS, 3),
        in_specs=[
            pl.BlockSpec((ROWS, depth), lambda r, t: (r, 0)),
            pl.BlockSpec((None, depth, width), lambda r, t: (t, 0, 0)),
            pl.BlockSpec((ROWS, PAIR), lambda r, t: (r, 0)),
            pl.BlockSpec((ROWS, PAIR), lambda r, t: (r, 0)),
        ],
        out_specs=pl.BlockSpec((None, ROWS, width), lambda r, t: (t, r, 0)),
        out_shape=jax.ShapeDtypeStruct((3, count, width), bf16),
        compiler_params=pltpu.CompilerParams(vmem_limit_bytes=32 << 20),
        cost_estimate=pl.CostEstimate(
            flops=6 * count * depth * width, bytes_accessed=8 * count * width, transcendentals=0
        ),
        name="qkv",
    )(rows, w_qkv, cosine, sine)


def head_lanes(block, h):
    lane = lax.broadcasted_iota(jnp.int32, block.shape, 1)
    return jnp.where(lane // HEAD == h, block, jnp.zeros_like(block))


def transposed(block):
    return block.astype(f32).T


def forward_kernel(flag_ref, q_ref, k_ref, v_ref, segr_ref, segc_ref, o_ref, lse_ref, vt, m, l, acc):
    blocks = q_ref.shape[0] // BLOCK
    for b in range(blocks):
        vt[b] = transposed(v_ref[b * BLOCK : (b + 1) * BLOCK, :]).astype(bf16)

    @pl.loop(0, blocks)
    def _(qi):
        rows = pl.ds(pl.multiple_of(qi * BLOCK, BLOCK), BLOCK)
        q = q_ref[rows, :]
        m[...] = jnp.full(m.shape, masked_score, f32)
        l[...] = jnp.zeros(l.shape, f32)
        acc[...] = jnp.zeros(acc.shape, f32)

        @pl.loop(0, blocks)
        def _(ki):
            @pl.when(flag_ref[qi * blocks + ki] > 0)
            def _():
                cols = pl.ds(pl.multiple_of(ki * BLOCK, BLOCK), BLOCK)
                k = k_ref[cols, :]
                docs = segc_ref[cols, :]
                same = jnp.concatenate([docs] * (BLOCK // 128), axis=1) == segr_ref[qi]
                for h in range(2):
                    lo, hi = h * HEAD, (h + 1) * HEAD
                    s = jnp.where(same, mm(k, head_lanes(q, h), 1, 1), masked_score)
                    top = jnp.maximum(m[h], jnp.max(s, axis=0, keepdims=True))
                    p = jnp.exp(s - top)
                    shrink = jnp.exp(m[h] - top)
                    m[h] = top
                    l[h] = l[h] * shrink + jnp.sum(p, axis=0, keepdims=True)
                    acc[lo:hi, :] = acc[lo:hi, :] * shrink + mm(vt[ki, lo:hi, :], p.astype(bf16), 1, 0)

        for h in range(2):
            lo, hi = h * HEAD, (h + 1) * HEAD
            lse_ref[h, qi] = m[h] + jnp.log(l[h])
            acc[lo:hi, :] = acc[lo:hi, :] / l[h]
        o_ref[rows, :] = acc[...].T.astype(bf16)


def backward_kernel(
    flag_ref, q_ref, k_ref, v_ref, g_ref, o_ref, lse_ref, segr_ref, segc_ref, cos_ref, sin_ref,
    out_ref, kt, dk, dv, dq,
):
    blocks = q_ref.shape[0] // BLOCK
    for b in range(blocks):
        kt[b] = transposed(k_ref[b * BLOCK : (b + 1) * BLOCK, :]).astype(bf16)
    dk[...] = jnp.zeros(dk.shape, f32)
    dv[...] = jnp.zeros(dv.shape, f32)

    def turn_back(u, rows):
        return (u * cos_ref[rows, :] - turned(u) * sin_ref[rows, :]).astype(bf16)

    @pl.loop(0, blocks)
    def _(qi):
        rows = pl.ds(pl.multiple_of(qi * BLOCK, BLOCK), BLOCK)
        q, g = q_ref[rows, :], g_ref[rows, :]
        both = (g.astype(f32) * o_ref[rows, :].astype(f32)).T
        dq[...] = jnp.zeros(dq.shape, f32)

        @pl.loop(0, blocks)
        def _(ki):
            @pl.when(flag_ref[qi * blocks + ki] > 0)
            def _():
                cols = pl.ds(pl.multiple_of(ki * BLOCK, BLOCK), BLOCK)
                k, v = k_ref[cols, :], v_ref[cols, :]
                docs = segc_ref[cols, :]
                same = jnp.concatenate([docs] * (BLOCK // 128), axis=1) == segr_ref[qi]
                dk_sum, dv_sum = dk[cols, :], dv[cols, :]
                for h in range(2):
                    lo, hi = h * HEAD, (h + 1) * HEAD
                    delta = jnp.sum(both[lo:hi, :], axis=0, keepdims=True)
                    qh, gh = head_lanes(q, h), head_lanes(g, h)
                    s = jnp.where(same, mm(k, qh, 1, 1), masked_score)
                    p = jnp.exp(s - lse_ref[h, qi])
                    ds = (p * (mm(v, gh, 1, 1) - delta)).astype(bf16)
                    dv_sum = dv_sum + mm(p.astype(bf16), gh, 1, 0)
                    dk_sum = dk_sum + mm(ds, qh, 1, 0)
                    dq[lo:hi, :] = dq[lo:hi, :] + mm(kt[ki, lo:hi, :], ds, 1, 0)
                dk[cols, :] = dk_sum
                dv[cols, :] = dv_sum

        out_ref[0, rows, :] = turn_back(dq[...].T * (HEAD**-0.5), rows)

    @pl.loop(0, blocks)
    def _(b):
        rows = pl.ds(pl.multiple_of(b * BLOCK, BLOCK), BLOCK)
        out_ref[1, rows, :] = turn_back(dk[rows, :], rows)
        out_ref[2, rows, :] = dv[rows, :].astype(bf16)


def pieces_of(qkv, length):
    return [pl.BlockSpec((None, length, PAIR), functools.partial(lambda t, p, *_: (t, 0, p), t)) for t in range(3)]


def attend_forward(flags, qkv, seg_rows, seg_cols):
    _, length, width = qkv.shape
    blocks, pairs = length // BLOCK, width // PAIR
    return pl.pallas_call(
        forward_kernel,
        grid_spec=pltpu.PrefetchScalarGridSpec(
            num_scalar_prefetch=1,
            grid=(pairs,),
            in_specs=[
                *pieces_of(qkv, length),
                pl.BlockSpec((blocks, 1, BLOCK), lambda p, *_: (0, 0, 0)),
                pl.BlockSpec((length, 128), lambda p, *_: (0, 0)),
            ],
            out_specs=[
                pl.BlockSpec((length, PAIR), lambda p, *_: (0, p)),
                pl.BlockSpec((2, blocks, 1, BLOCK), lambda p, *_: (p, 0, 0, 0)),
            ],
            scratch_shapes=[
                pltpu.VMEM((blocks, PAIR, BLOCK), bf16),
                pltpu.VMEM((2, 1, BLOCK), f32),
                pltpu.VMEM((2, 1, BLOCK), f32),
                pltpu.VMEM((PAIR, BLOCK), f32),
            ],
        ),
        out_shape=[
            jax.ShapeDtypeStruct((length, width), bf16),
            jax.ShapeDtypeStruct((2 * pairs, blocks, 1, BLOCK), f32),
        ],
        compiler_params=pltpu.CompilerParams(vmem_limit_bytes=48 << 20),
        cost_estimate=pl.CostEstimate(
            flops=4 * length * length * width, bytes_accessed=8 * length * width, transcendentals=length * length * width // HEAD
        ),
        name="attend",
    )(flags, qkv, qkv, qkv, seg_rows, seg_cols)


def attend_backward(flags, qkv, grad, mixed, lse, seg_rows, seg_cols, cosine, sine):
    _, length, width = qkv.shape
    blocks, pairs = length // BLOCK, width // PAIR
    whole = pl.BlockSpec((length, PAIR), lambda p, *_: (0, p))
    table = pl.BlockSpec((length, PAIR), lambda p, *_: (0, 0))
    return pl.pallas_call(
        backward_kernel,
        grid_spec=pltpu.PrefetchScalarGridSpec(
            num_scalar_prefetch=1,
            grid=(pairs,),
            in_specs=[
                *pieces_of(qkv, length),
                whole,
                whole,
                pl.BlockSpec((2, blocks, 1, BLOCK), lambda p, *_: (p, 0, 0, 0)),
                pl.BlockSpec((blocks, 1, BLOCK), lambda p, *_: (0, 0, 0)),
                table,
                table,
                table,
            ],
            out_specs=pl.BlockSpec((3, length, PAIR), lambda p, *_: (0, 0, p)),
            scratch_shapes=[
                pltpu.VMEM((blocks, PAIR, BLOCK), bf16),
                pltpu.VMEM((length, PAIR), f32),
                pltpu.VMEM((length, PAIR), f32),
                pltpu.VMEM((PAIR, BLOCK), f32),
            ],
        ),
        out_shape=jax.ShapeDtypeStruct((3, length, width), bf16),
        compiler_params=pltpu.CompilerParams(vmem_limit_bytes=56 << 20),
        cost_estimate=pl.CostEstimate(
            flops=10 * length * length * width, bytes_accessed=16 * length * width, transcendentals=length * length * width // HEAD
        ),
        name="attend_back",
    )(flags, qkv, qkv, qkv, grad, mixed, lse, seg_rows, seg_cols, cosine, sine)


def qkv_pair_kernel(own_ref, got_ref, w_ref, cos_ref, sin_ref, *refs):
    o_ref, rows_ref = refs[-2:]
    which = pl.program_id(0)
    half = own_ref.shape[0]

    @pl.when(which == 0)
    def _():
        rows_ref[:half, :] = own_ref[...]
        rows_ref[half:, :] = got_ref[...]

    y = mm(rows_ref[...], w_ref[...], 1, 0)

    @pl.when(which < 2)
    def _():
        factor = jnp.where(which == 0, HEAD**-0.5, 1.0)
        for p in range(y.shape[1] // PAIR):
            u = y[:, p * PAIR : (p + 1) * PAIR]
            r = u * cos_ref[...] + turned(u) * sin_ref[...]
            o_ref[:, p * PAIR : (p + 1) * PAIR] = (r.astype(bf16) * factor.astype(bf16)).astype(bf16)

    @pl.when(which == 2)
    def _():
        o_ref[...] = y.astype(bf16)


def project_pair(j, own, got, w_qkv, cosine, sine, before, length):
    half, depth = own.shape
    width = w_qkv.shape[2]
    chunk = 2 * half
    table = pl.BlockSpec((chunk, PAIR), lambda t: (j, 0))
    return pl.pallas_call(
        qkv_pair_kernel,
        grid=(3,),
        in_specs=[
            pl.BlockSpec((half, depth), lambda t: (0, 0)),
            pl.BlockSpec((half, depth), lambda t: (0, 0)),
            pl.BlockSpec((None, depth, width), lambda t: (t, 0, 0)),
            table,
            table,
            *[pl.BlockSpec(memory_space=pl.ANY) for _ in before],
        ],
        out_specs=[
            pl.BlockSpec((None, chunk, width), lambda t: (t, j, 0)),
            pl.BlockSpec((chunk, depth), lambda t: (j, 0)),
        ],
        out_shape=[
            jax.ShapeDtypeStruct((3, length, width), bf16),
            jax.ShapeDtypeStruct((length, depth), bf16),
        ],
        input_output_aliases={5 + i: i for i in range(len(before))},
        compiler_params=pltpu.CompilerParams(vmem_limit_bytes=32 << 20),
        cost_estimate=pl.CostEstimate(
            flops=6 * chunk * depth * width, bytes_accessed=8 * depth * width, transcendentals=0
        ),
        name="qkv",
    )(own, got, w_qkv, cosine, sine, *before)


def forward_chunk_kernel(q_ref, k_ref, v_ref, segr_ref, segc_ref, o_ref, lse_ref, vt):
    length, count = k_ref.shape[0], q_ref.shape[0]
    for b in range(0, length, BLOCK):
        vt[:, b : b + BLOCK] = transposed(v_ref[b : b + BLOCK, :]).astype(bf16)
    q = q_ref[...]
    outs = []
    for h in range(2):
        qh = head_lanes(q, h)
        scores = []
        for b in range(0, length, BLOCK):
            same = jnp.concatenate([segc_ref[b : b + BLOCK, :]] * (count // 128), axis=1) == segr_ref[...]
            scores.append(jnp.where(same, mm(k_ref[b : b + BLOCK, :], qh, 1, 1), masked_score))
        top = functools.reduce(jnp.maximum, [jnp.max(s, axis=0, keepdims=True) for s in scores])
        total, summed = 0.0, 0.0
        for i, s in enumerate(scores):
            p = jnp.exp(s - top)
            total = total + jnp.sum(p, axis=0, keepdims=True)
            summed = summed + mm(vt[h * HEAD : (h + 1) * HEAD, i * BLOCK : (i + 1) * BLOCK], p.astype(bf16), 1, 0)
        lse_ref[h] = top + jnp.log(total)
        outs.append(summed / total)
    o_ref[...] = jnp.concatenate(outs, axis=0).T.astype(bf16)


def pair_pieces(j, length, chunk):
    return [
        pl.BlockSpec((None, chunk, PAIR), lambda p: (0, j, p)),
        pl.BlockSpec((None, length, PAIR), lambda p: (1, 0, p)),
        pl.BlockSpec((None, length, PAIR), lambda p: (2, 0, p)),
    ]


def attend_forward_pair(j, chunk, qkv, seg_rows, seg_cols):
    _, length, width = qkv.shape
    pairs = width // PAIR
    return pl.pallas_call(
        forward_chunk_kernel,
        grid=(pairs,),
        in_specs=[
            *pair_pieces(j, length, chunk),
            pl.BlockSpec((1, chunk), lambda p: (0, j)),
            pl.BlockSpec((length, 128), lambda p: (0, 0)),
        ],
        out_specs=[
            pl.BlockSpec((chunk, PAIR), lambda p: (0, p)),
            pl.BlockSpec((2, 1, chunk), lambda p: (p, 0, 0)),
        ],
        out_shape=[
            jax.ShapeDtypeStruct((chunk, width), bf16),
            jax.ShapeDtypeStruct((2 * pairs, 1, chunk), f32),
        ],
        scratch_shapes=[pltpu.VMEM((PAIR, length), bf16)],
        compiler_params=pltpu.CompilerParams(vmem_limit_bytes=48 << 20),
        cost_estimate=pl.CostEstimate(
            flops=16 * chunk * length * width,
            bytes_accessed=8 * length * width,
            transcendentals=chunk * length * width // HEAD,
        ),
        name="attend",
    )(qkv, qkv, qkv, seg_rows, seg_cols)


def mlp_kernel(own_ref, got_ref, b_own_ref, b_got_ref, up_ref, bias_ref, down_ref, *refs):
    rows_ref, back, hidden_ref, pre_ref, own_grad, got_grad, own_branch, got_branch, bias_grad, grads, branch = refs[-11:]
    tile, tiles = pl.program_id(0), pl.num_programs(0)
    half = own_ref.shape[0]

    @pl.when(tile == 0)
    def _():
        rows_ref[:half, :] = own_ref[...]
        rows_ref[half:, :] = got_ref[...]
        back[:half, :] = b_own_ref[...]
        back[half:, :] = b_got_ref[...]

    cubic, root = 0.044715, (2.0 / jnp.pi) ** 0.5
    u = mm(rows_ref[...], up_ref[...], 1, 0) + bias_ref[...]
    square = u * u
    t = jnp.tanh(u * (root + (root * cubic) * square))
    rising = 0.5 * (1.0 + t)
    hidden = (u * rising).astype(bf16)
    slope = rising + (0.5 * u) * (1.0 - t * t) * (root + (3.0 * cubic * root) * square)
    grad = (mm(back[...], down_ref[...], 1, 1) * slope).astype(bf16)
    hidden_ref[...] = hidden
    pre_ref[...] = grad
    bias_grad[...] = jnp.sum(grad.astype(f32), axis=0, keepdims=True)
    more, more_branch = mm(grad, up_ref[...], 1, 1), mm(hidden, down_ref[...], 1, 0)

    @pl.when(tile == 0)
    def _():
        grads[...] = more
        branch[...] = more_branch

    @pl.when(tile > 0)
    def _():
        grads[...] += more
        branch[...] += more_branch

    @pl.when(tile == tiles - 1)
    def _():
        own_grad[...] = grads[:half, :]
        got_grad[...] = grads[half:, :].astype(bf16)
        own_branch[...] = branch[:half, :]
        got_branch[...] = branch[half:, :].astype(bf16)


def mlp_pair(j, own, got, back_own, back_got, w_up, b_up, w_down, before, length):
    half, depth = own.shape
    width = w_up.shape[1]
    chunk, tile = 2 * half, min(width, 1024)
    small = pl.BlockSpec((half, depth), lambda t: (0, 0))
    wide = pl.BlockSpec((chunk, tile), lambda t: (j, t))
    return pl.pallas_call(
        mlp_kernel,
        grid=(width // tile,),
        in_specs=[
            small, small, small, small,
            pl.BlockSpec((depth, tile), lambda t: (0, t)),
            pl.BlockSpec((1, tile), lambda t: (0, t)),
            pl.BlockSpec((tile, depth), lambda t: (t, 0)),
            *[pl.BlockSpec(memory_space=pl.ANY) for _ in before],
        ],
        out_specs=[
            pl.BlockSpec((chunk, depth), lambda t: (j, 0)), pl.BlockSpec((chunk, depth), lambda t: (j, 0)), wide, wide,
            small, small, small, small,
            pl.BlockSpec((1, tile), lambda t: (0, t)),
        ],
        out_shape=[
            jax.ShapeDtypeStruct((length, depth), bf16),
            jax.ShapeDtypeStruct((length, depth), bf16),
            jax.ShapeDtypeStruct((length, width), bf16),
            jax.ShapeDtypeStruct((length, width), bf16),
            jax.ShapeDtypeStruct((half, depth), f32),
            jax.ShapeDtypeStruct((half, depth), bf16),
            jax.ShapeDtypeStruct((half, depth), f32),
            jax.ShapeDtypeStruct((half, depth), bf16),
            jax.ShapeDtypeStruct((1, width), f32),
        ],
        scratch_shapes=[
            pltpu.VMEM((chunk, depth), f32),
            pltpu.VMEM((chunk, depth), f32),
        ],
        input_output_aliases={7 + i: i for i in range(len(before))},
        compiler_params=pltpu.CompilerParams(vmem_limit_bytes=56 << 20),
        cost_estimate=pl.CostEstimate(
            flops=12 * chunk * depth * width, bytes_accessed=12 * depth * width, transcendentals=chunk * width
        ),
        name="mlp",
    )(own, got, back_own, back_got, w_up, b_up[None, :], w_down, *before)


MESH = pl.DeviceIdType.MESH
ADD_ROWS = 32
STEPS = 9
EDGES = 4


def add_low(a, a_at, b, rows):
    @pl.loop(0, rows // ADD_ROWS)
    def _(i):
        at = pl.ds(pl.multiple_of(i * ADD_ROWS, ADD_ROWS), ADD_ROWS)
        kept = a[pl.ds(pl.multiple_of(a_at + i * ADD_ROWS, ADD_ROWS), ADD_ROWS), :].astype(f32)
        b[at, :] = (kept + b[at, :].astype(f32)).astype(bf16)


class Unit:
    def __init__(self, part, out, column, got, send, recv, local, place):
        self.part, self.out, self.got = part, out, got
        self.send, self.recv, self.local = send, recv, local
        self.rows, columns = 2 * got[0].shape[0], got[0].shape[1]
        self.columns = pl.ds(column, columns)
        self.bit = [(place // (1 << b)) % 2 for b in range(EDGES)]
        self.partner = [place + (1 - 2 * self.bit[b]) * (1 << b) for b in range(EDGES)]
        self.base = [0]
        for b in range(EDGES):
            self.base.append(self.base[-1] + self.bit[b] * (self.rows >> (b + 1)))

    def remote(self, src, dst, stage, b):
        return pltpu.make_async_remote_copy(
            src_ref=src,
            dst_ref=dst,
            send_sem=self.send.at[stage],
            recv_sem=self.recv.at[stage],
            device_id={"dp": self.partner[b]},
            device_id_type=MESH,
        )

    def halving(self, b):
        half = self.rows >> (b + 1)
        source = self.part if b == 0 else self.got[b - 1]
        away = pl.ds(pl.multiple_of((1 - self.bit[b]) * half, ADD_ROWS), half)
        return self.remote(source.at[away], self.got[b], b, b)

    def spot(self, b):
        size = self.rows >> (b + 1)
        return self.out.at[pl.ds(pl.multiple_of(self.base[b + 1], ADD_ROWS), size), self.columns]

    def own(self):
        return pltpu.make_async_copy(self.got[3], self.spot(3), self.local.at[0])

    def gathering(self, b):
        return self.remote(self.got[3] if b == 3 else self.spot(b), self.spot(b), 7 - b, b)

    def step(self, k):
        if k == 0:
            self.halving(0).start()
        elif k < 5:
            b = k - 1
            self.halving(b).wait()
            half = self.rows >> (b + 1)
            add_low(self.part if b == 0 else self.got[b - 1], self.bit[b] * half, self.got[b], half)
            if b < 3:
                self.halving(b + 1).start()
            else:
                self.own().start()
                self.gathering(3).start()
        elif k == 5:
            self.own().wait()
            self.gathering(3).wait()
            self.gathering(2).start()
        elif k < 8:
            self.gathering(8 - k).wait()
            self.gathering(7 - k).start()
        else:
            self.gathering(0).wait()


def unit_scratch(rows, columns):
    return [
        *[pltpu.VMEM((rows >> (b + 1), columns), bf16) for b in range(EDGES)],
        pltpu.SemaphoreType.DMA((2 * EDGES,)),
        pltpu.SemaphoreType.DMA((2 * EDGES,)),
        pltpu.SemaphoreType.DMA((1,)),
    ]


def greet(targets):
    barrier = pltpu.get_barrier_semaphore()
    for target in targets:
        pl.semaphore_signal(barrier, inc=1, device_id=target, device_id_type=MESH)
    pl.semaphore_wait(barrier, len(targets))


ORDER = (
    (6.5, 1, 1), (10, 3, 1), (10, 1, 2), (10, 1, 3), (10.5, 2, 1), (10.5, 3, 2), (10.5, 0, 1), (11.5, 1, 4),
    (13.5, 1, 5), (13.5, 3, 3), (15.5, 3, 4), (16.5, 1, 6), (16.5, 2, 2), (18.5, 4, 1), (18.5, 3, 5), (19.5, 0, 2),
    (19.5, 2, 3), (20.5, 3, 6), (21.5, 4, 2), (21.5, 2, 4), (22.5, 0, 3), (23.5, 5, 1), (24.5, 6, 1), (25.5, 4, 3),
    (25.5, 3, 7), (25.5, 7, 1), (25.5, 2, 5), (27.5, 3, 8), (29.5, 4, 4), (30.5, 1, 7), (30.5, 0, 4), (31, 5, 2),
    (31, 2, 6), (31, 1, 8), (31, 4, 5), (32, 0, 5), (32, 5, 3), (32, 4, 6), (32, 5, 4), (32.5, 5, 5), (33, 0, 6),
    (34, 7, 2), (34, 2, 7), (34, 5, 6), (34, 4, 7), (35, 2, 8), (35, 4, 8), (35, 7, 3), (35, 6, 2), (36, 7, 4),
    (36, 6, 3), (36, 7, 5), (36, 5, 7), (36, 6, 4), (36, 5, 8), (36, 7, 6), (36, 6, 5), (37, 6, 6), (37, 0, 7),
    (99, 0, 8), (99, 7, 7), (99, 7, 8), (99, 6, 7), (99, 6, 8),
)
WIDE = 512
STEP_ROWS = 64


def tail_kernel(
    hidden, full_back, rows_two, grad_pre, qkv_hbm, mixed_a, mixed_b, rows_hbm, w_qkv_hbm, w_out_hbm,
    grad_a, grad_b, got_a, got_b, mid_a, mid_b, proj_a, proj_b, branch_a, branch_b, send_a, send_b, tokens_hbm, cot_hbm,
    rows_of, known, lse_a, lse_b, segr, segc, cosine, sine,
    down_sum, up_sum, out_sum, q_sum, k_sum, v_sum, output, grad_x, everyone,
    qkv, mixed, rows_one, w_qkv, w_out, proj, mix_grad, d_qkv, dk, dv, from_x, grads, middle, projected, tokens, cot,
    part_a, part_b, part_c, part_d, part_e, branch_got, col_sums, small, small_got,
    load, store, x_send, x_recv, all_send, all_recv, *more,
):
    place, me = lax.axis_index("dp"), lax.axis_index("tensor")
    length, depth = rows_one.shape
    chunks, half, _ = from_x.shape
    chunk = 2 * half
    width = mixed.shape[1]
    pairs = width // PAIR
    across = {"tensor": 1 - me}

    specs = [
        (part_a, down_sum.at[pl.ds(0, depth)], 0), (part_b, down_sum.at[pl.ds(depth, depth)], 0),
        (part_c, up_sum, 0), (part_d, up_sum, depth), (part_e, out_sum, 0),
        (qkv.at[2], v_sum, 0), (qkv.at[1], k_sum, 0), (qkv.at[0], q_sum, 0),
    ]
    units = []
    for i, (part, out, column) in enumerate(specs):
        *got, send, recv, local = more[7 * i : 7 * (i + 1)]
        units.append(Unit(part, out, column, got, send, recv, local, place))

    def x_copy(src, dst, i):
        return pltpu.make_async_remote_copy(
            src_ref=src, dst_ref=dst, send_sem=x_send.at[i], recv_sem=x_recv.at[i],
            device_id=across, device_id_type=MESH,
        )

    each = range(chunks)
    grads_in = [x_copy((got_a, got_b)[c], from_x.at[c], c) for c in each]
    projs = [x_copy(proj.at[c, :half], proj.at[c, half:], chunks + c) for c in each]
    ones = [x_copy(proj.at[c, :half], from_x.at[c], 2 * chunks + c) for c in each]
    branches = [x_copy((send_a, send_b)[c], branch_got.at[c], 3 * chunks + c) for c in each]
    smalls = x_copy(small, small_got, 4 * chunks)
    outputs = [
        pltpu.make_async_copy(branch_got.at[c], output.at[c * half : (c + 1) * half], store.at[c]) for c in each
    ]
    partner = units[0].partner

    loads = []

    def fetch(src, dst):
        copy = pltpu.make_async_copy(src, dst, load.at[len(loads)])
        copy.start()
        loads.append(copy)
        return copy

    done = [0]

    def until(place_now):
        while done[0] < len(ORDER) and ORDER[done[0]][0] <= place_now:
            _, i, k = ORDER[done[0]]
            units[i].step(k)
            done[0] += 1

    greet([*[{"dp": p} for p in partner], across])
    grads_in[0].start()
    slots = [w_qkv.at[0], w_qkv.at[1], w_qkv.at[2], d_qkv.at[2]]
    cut = lambda t: slice(t * WIDE, (t + 1) * WIDE)
    backs = fetch(full_back, rows_one)
    hiddens = [fetch(hidden.at[:, cut(t)], slots[t]) for t in range(4)]
    norms = [
        [fetch(src, dst.at[c]) for src, dst in (
            ((grad_a, grad_b)[c], grads), ((mid_a, mid_b)[c], middle), ((proj_a, proj_b)[c], projected),
            (tokens_hbm.at[c * half : (c + 1) * half], tokens), (cot_hbm.at[c * half : (c + 1) * half], cot),
        )]
        for c in each
    ]
    twos = [fetch(rows_two.at[:, cut(t)], d_qkv.at[t]) for t in range(2)]
    col_sums[...] = jnp.zeros(col_sums.shape, f32)

    backs.wait()
    pres = []
    for t in range(4):
        until(1 + t)
        hiddens[t].wait()
        part = (part_a, part_b)[t // 2]

        @pl.loop(0, WIDE // 256)
        def _(r):
            at = pl.ds(pl.multiple_of(r * 256, 256), 256)
            to = pl.ds(pl.multiple_of((t % 2) * WIDE + r * 256, 256), 256)
            part[to, :] = mm(slots[t][:, at], rows_one[...], 0, 0).astype(bf16)

        pres.append(fetch(grad_pre.at[:, cut(t)], slots[t]))
        if t % 2:
            units[t // 2].step(0)
    main = [
        fetch(w_out_hbm, w_out), fetch(mixed_a, mixed.at[:chunk]), fetch(mixed_b, mixed.at[chunk:]),
        fetch(qkv_hbm, qkv), fetch(rows_hbm, rows_one),
    ]

    def up_part(t):
        pres[t].wait()
        part = (part_c, part_d)[t // 2]

        @pl.loop(0, depth // 256)
        def _(r):
            to = pl.ds(pl.multiple_of(r * 256, 256), 256)
            at = pl.ds(pl.multiple_of((r % 2) * 256, 256), 256)
            part[to, cut(t % 2)] = mm(d_qkv[r // 2, :, at], slots[t][...], 0, 0).astype(bf16)

    def fold(row, values):
        col_sums[row : row + 1, :] += jnp.sum(values, axis=0, keepdims=True)

    def norm_back(grad, values, weight):
        center = values - jnp.mean(values, axis=1, keepdims=True)
        root = lax.rsqrt(jnp.mean(center * center, axis=1, keepdims=True) + norm_eps)
        normal = center * root
        inner = grad * weight
        back = inner - jnp.mean(inner, axis=1, keepdims=True) - normal * jnp.mean(inner * normal, axis=1, keepdims=True)
        return root * back, normal

    gain_two, scale_m, gate_a, gain_one, scale_a, gate_m, b_down = [rows_of[r : r + 1, :] for r in range(7)]

    def second_norm(c):
        for copy in norms[c]:
            copy.wait()

        @pl.loop(0, half // STEP_ROWS)
        def _(i):
            at = pl.ds(pl.multiple_of(i * STEP_ROWS, STEP_ROWS), STEP_ROWS)
            grad = grads[c, at, :] + from_x[c, at, :].astype(f32)
            back, normal = norm_back(grad, middle[c, at, :], gain_two * (1.0 + scale_m))
            total = back + cot[c, at, :].astype(f32)
            grads[c, at, :] = total
            proj[c, at, :] = (total * gate_a).astype(bf16)
            fold(0, grad)
            fold(1, grad * normal)
            fold(2, total * projected[c, at, :])

        projs[c].start()

    for copy in twos:
        copy.wait()
    until(5)
    up_part(0)
    until(6)
    up_part(1)
    units[2].step(0)
    until(7)
    grads_in[0].wait()
    grads_in[1].start()
    second_norm(0)
    owns = [fetch(branch_a, projected.at[0])]
    until(8)
    up_part(2)
    until(9)
    up_part(3)
    units[3].step(0)
    weights = fetch(w_qkv_hbm, w_qkv)
    until(10)
    grads_in[1].wait()
    second_norm(1)
    owns.append(fetch(branch_b, projected.at[1]))

    def turn_back(u, rows):
        return (u * cosine[rows, :] - turned(u) * sine[rows, :]).astype(bf16)

    def attend_back(p, c):
        lanes = pl.ds(pl.multiple_of(p * PAIR, PAIR), PAIR)
        rows = slice(c * chunk, (c + 1) * chunk)
        q, g = qkv[0, rows, lanes], mix_grad[rows, lanes]
        both = (g.astype(f32) * mixed[rows, lanes].astype(f32)).T
        qh = [head_lanes(q, h) for h in range(2)]
        gh = [head_lanes(g, h) for h in range(2)]
        delta = [jnp.sum(both[h * HEAD : (h + 1) * HEAD, :], axis=0, keepdims=True) for h in range(2)]
        q_two, g_two = jnp.concatenate(qh, axis=0), jnp.concatenate(gh, axis=0)
        docs = segr[:, rows]
        dq = [0.0, 0.0]
        for b in range(0, length, BLOCK):
            cols = slice(b, b + BLOCK)
            k, v = qkv[1, cols, lanes], qkv[2, cols, lanes]
            turned_k = transposed(k).astype(bf16)
            same = jnp.concatenate([segc[cols, :]] * (chunk // 128), axis=1) == docs
            ps, ds = [], []
            for h in range(2):
                s = jnp.where(same, mm(k, qh[h], 1, 1), masked_score)
                pr = jnp.exp(s - (lse_a, lse_b)[c][2 * p + h])
                d = (pr * (mm(v, gh[h], 1, 1) - delta[h])).astype(bf16)
                ps.append(pr.astype(bf16))
                ds.append(d)
                dq[h] = dq[h] + mm(turned_k[h * HEAD : (h + 1) * HEAD, :], d, 1, 0)
            add_v = mm(jnp.concatenate(ps, axis=1), g_two, 1, 0)
            add_k = mm(jnp.concatenate(ds, axis=1), q_two, 1, 0)
            if c < chunks - 1:
                dv[cols, lanes] = add_v if c == 0 else dv[cols, lanes] + add_v
                dk[cols, lanes] = add_k if c == 0 else dk[cols, lanes] + add_k
            else:
                d_qkv[1, cols, lanes] = turn_back(dk[cols, lanes] + add_k, cols)
                d_qkv[2, cols, lanes] = (dv[cols, lanes] + add_v).astype(bf16)
        d_qkv[0, rows, lanes] = turn_back(jnp.concatenate(dq, axis=0).T * (HEAD**-0.5), rows)

    for copy in main:
        copy.wait()
    now = 11
    for c in each:
        until(now)
        projs[c].wait()
        if c == chunks - 1:
            for copy in branches:
                copy.start()
        mix_grad[c * chunk : (c + 1) * chunk, :] = mm(proj[c], w_out[...], 1, 1).astype(bf16)
        now += 1
        if c == chunks - 1:
            until(now)

            @pl.loop(0, width // 256)
            def _(r):
                at = pl.ds(pl.multiple_of(r * 256, 256), 256)
                part_e[at, :] = sum(
                    mm(mixed[n * chunk : (n + 1) * chunk, at], proj[n], 0, 0) for n in each
                ).astype(bf16)

            units[4].step(0)
            now += 1

        @pl.loop(0, pairs)
        def _(p):
            for n in range(pairs):

                @pl.when(p == n)
                def _():
                    until(now + n)

            attend_back(p, c)

        now += pairs

    def rows_back(start):
        at = slice(start, start + half)
        return sum(mm(d_qkv[t, at, :], w_qkv[t], 1, 1) for t in range(3))

    for i in range(3):
        until(now + i)

        @pl.loop(0, depth // 256)
        def _(r):
            at = pl.ds(pl.multiple_of(r * 256, 256), 256)
            qkv[2 - i, at, :] = mm(rows_one[:, at], d_qkv[2 - i], 0, 0).astype(bf16)

        units[5 + i].step(0)
    now += 3
    weights.wait()
    for c in each:
        until(now + c)
        proj[c, :half] = rows_back(c * chunk + half).astype(bf16)
        if c == 0:
            ones[c].start()
    now += chunks
    for c in each:
        until(now + c)
        branches[c].wait()
        owns[c].wait()

        @pl.loop(0, half // STEP_ROWS)
        def _(i):
            at = pl.ds(pl.multiple_of(i * STEP_ROWS, STEP_ROWS), STEP_ROWS)
            branch = projected[c, at, :] + branch_got[c, at, :].astype(f32) + b_down
            branch_got[c, at, :] = (middle[c, at, :] + gate_m * branch).astype(bf16)
            fold(5, cot[c, at, :].astype(f32) * branch)

        outputs[c].start()
    now += chunks
    for c in each:
        until(now + c)
        projected[c] = rows_back(c * chunk)
    now += chunks
    for c in each:
        until(now + c)
        ones[c].wait()
        if c < chunks - 1:
            ones[c + 1].start()

        @pl.loop(0, half // STEP_ROWS)
        def _(i):
            at = pl.ds(pl.multiple_of(i * STEP_ROWS, STEP_ROWS), STEP_ROWS)
            grad = projected[c, at, :] + from_x[c, at, :].astype(f32)
            back, normal = norm_back(grad, tokens[c, at, :].astype(f32), gain_one * (1.0 + scale_a))
            grad_x[c, at, :] = (back + grads[c, at, :]).astype(bf16)
            fold(3, grad)
            fold(4, grad * normal)

    now += chunks
    shift, scaled, gated, shift_one, scaled_one, gated_m = [col_sums[r : r + 1, :] for r in range(6)]
    small[...] = known[...] + jnp.concatenate(
        [
            shift_one, gain_one * scaled_one, gated, shift, gain_two * scaled, gated_m,
            (1.0 + scale_a) * scaled_one, (1.0 + scale_m) * scaled, jnp.zeros((8, depth), f32),
        ],
        axis=0,
    )
    smalls.start()
    until(now)
    smalls.wait()
    number = lax.broadcasted_iota(jnp.int32, small.shape, 0)
    everyone[0] = small[...] + jnp.where(number < 9, small_got[...], 0.0)
    for n, b in enumerate(reversed(range(EDGES))):
        copy = pltpu.make_async_remote_copy(
            src_ref=everyone.at[pl.ds(0, 1 << n)], dst_ref=everyone.at[pl.ds(1 << n, 1 << n)],
            send_sem=all_send.at[n], recv_sem=all_recv.at[n],
            device_id={"dp": partner[b]}, device_id_type=MESH,
        )
        copy.start()
        until(now + 1 + n)
        copy.wait()
    until(1000)
    for copy in outputs:
        copy.wait()


def tail(
    hidden, full_back, rows_two, grad_pre, qkv, mixed, rows_one, w_qkv, w_out, own_grad, got_grad, middle, projected,
    own_branch, got_branch, tokens, cot, rows_of, known, lse, segr, segc, cosine, sine,
):
    _, length, width = qkv.shape
    chunks = len(mixed)
    half, depth = got_grad[0].shape
    anywhere, near = pl.BlockSpec(memory_space=pl.ANY), pl.BlockSpec(memory_space=pltpu.VMEM)
    shaped, kept = jax.ShapeDtypeStruct, pltpu.VMEM
    in_chunks = (chunks, half, depth)
    scratch = [
        kept(qkv.shape, bf16), kept((length, width), bf16), kept(rows_one.shape, bf16), kept(w_qkv.shape, bf16),
        kept(w_out.shape, bf16), kept((chunks, 2 * half, depth), bf16), kept((length, width), bf16),
        kept((3, length, width), bf16), kept((length, width), f32), kept((length, width), f32),
        kept(in_chunks, bf16), kept(in_chunks, f32), kept(in_chunks, f32), kept(in_chunks, f32),
        kept(in_chunks, bf16), kept(in_chunks, bf16),
        *[kept((depth, depth), bf16)] * 4, kept((width, depth), bf16), kept(in_chunks, bf16),
        kept((8, depth), f32), kept(known.shape, f32), kept(known.shape, f32),
        pltpu.SemaphoreType.DMA((29,)), pltpu.SemaphoreType.DMA((chunks,)),
        pltpu.SemaphoreType.DMA((4 * chunks + 1,)), pltpu.SemaphoreType.DMA((4 * chunks + 1,)),
        pltpu.SemaphoreType.DMA((EDGES,)), pltpu.SemaphoreType.DMA((EDGES,)),
        *unit_scratch(depth, depth) * 4, *unit_scratch(width, depth), *unit_scratch(depth, width) * 3,
    ]
    return pl.pallas_call(
        tail_kernel,
        in_specs=[anywhere] * 24 + [near] * 8,
        out_specs=[anywhere] * 7 + [near] * 2,
        out_shape=[
            shaped((hidden.shape[1], depth), bf16), shaped((depth, hidden.shape[1]), bf16), shaped((width, depth), bf16),
            *[shaped((depth, width), bf16)] * 3, shaped(tokens.shape, bf16),
            shaped(in_chunks, bf16), shaped((1 << EDGES, *known.shape), f32),
        ],
        scratch_shapes=scratch,
        compiler_params=pltpu.CompilerParams(collective_id=1, has_side_effects=True, vmem_limit_bytes=61 << 20),
        name="tail",
    )(
        hidden, full_back, rows_two, grad_pre, qkv, *mixed, rows_one, w_qkv, w_out, *own_grad, *got_grad, *middle,
        *projected, *own_branch, *got_branch, tokens, cot, rows_of, known, *lse, segr, segc, cosine, sine,
    )


def body_pair(
    tokens, cond, doc_lengths, w_ada, b_ada, gain_one, w_qkv, w_out, gain_two, w_up, b_up, w_down, b_down, cotangent
):
    own, width = tokens.shape
    length = 2 * own
    chunks = 2
    half, chunk = own // chunks, length // chunks
    me = lax.axis_index("tensor")

    def swap(values):
        return lax.ppermute(values, "tensor", [(0, 1), (1, 0)])

    step = jnp.arange(length, dtype=jnp.int32)
    in_chunk = step % chunk
    places = jnp.where(in_chunk < half, me, 1 - me) * own + (step // chunk) * half + in_chunk % half
    segment, doc_first = documents(doc_lengths[0], places)
    cosine, sine = rope_tables(places - doc_first)
    seg_rows = segment[None, :]
    seg_cols = jnp.broadcast_to(segment[:, None], (length, 128))

    modulation = jnp.dot(cond, w_ada, preferred_element_type=f32)[0] + b_ada
    shift_a, scale_a, gate_a, shift_m, scale_m, gate_m = jnp.split(modulation, 6)
    cuts = [slice(c * half, (c + 1) * half) for c in range(chunks)]
    x_rows = [tokens[cut].astype(f32) for cut in cuts]
    grad_out = [cotangent[cut].astype(f32) for cut in cuts]
    each = range(chunks)

    def after(value, *others):
        return lax.optimization_barrier((value, *others))[0]

    act_one = [modulate(x_rows[c], gain_one, shift_a, scale_a).astype(bf16) for c in each]
    back = [(grad_out[c] * gate_m).astype(bf16) for c in each]
    got_one = [swap(act_one[0])]
    got_one.append(swap(after(act_one[1], got_one[0])))
    got_back = [swap(after(back[0], got_one[1]))]
    got_back.append(swap(after(back[1], got_back[0])))
    state = ()
    for c in each:
        state = project_pair(c, act_one[c], got_one[c], w_qkv, cosine, sine, state, length)
    qkv, rows_one = state

    mixed, lse, sums, projected, middle, act_two, got_two = [], [], [], [], [], [], []
    for c in each:
        waits = () if c == 0 else (got_back[0], sums[0])
        m, l = attend_forward_pair(c, chunk, after(qkv, *waits) if c else qkv, seg_rows, seg_cols)
        if c:
            m = after(m, arrived[0])
        mixed.append(m)
        lse.append(l)
        sums.append(jnp.dot(m[half:], w_out, preferred_element_type=f32).astype(bf16))
        arrived = [swap(sums[0])] if c == 0 else [arrived[0], swap(sums[1])]
    for c in each:
        projected.append(jnp.dot(mixed[c][:half], w_out, preferred_element_type=f32) + arrived[c].astype(f32))
        middle.append(x_rows[c] + gate_a * projected[c])
        act_two.append(modulate(middle[c], gain_two, shift_m, scale_m).astype(bf16))
        got_two.append(swap(act_two[c]))
    got_two[0] = after(got_two[0], act_two[1])
    state, pieces = (), []
    for c in each:
        out = mlp_pair(c, act_two[c], got_two[c], back[c], got_back[c], w_up, b_up, w_down, state, length)
        state, rest = out[:4], out[4:]
        pieces.append(rest)
    rows_two, full_back, hidden, grad_pre = state
    grad_b_up = sum(pieces[c][4] for c in each)[0]
    grad_b_down = sum(jnp.sum(back[c].astype(f32), axis=0) for c in each)

    none = jnp.zeros((width,), f32)
    known = jnp.stack(
        [
            none, none, none, none, none, none, none, none, grad_b_down,
            grad_b_up[:width], grad_b_up[width:],
            jnp.pad(cond[0].astype(f32), (0, width - cond.shape[1])), none, none, none, none,
        ]
    )
    *sums, output, grad_x, everyone = tail(
        hidden, full_back, rows_two, grad_pre, qkv, mixed, rows_one, w_qkv, w_out,
        *[[pieces[c][n] for c in each] for n in range(2)], middle, projected,
        *[[pieces[c][n] for c in each] for n in range(2, 4)], tokens, cotangent,
        jnp.stack([gain_two, scale_m, gate_a, gain_one, scale_a, gate_m, b_down, none]), known,
        lse, seg_rows, seg_cols, cosine, sine,
    )
    grad_w_down, grad_w_up, grad_w_out, grad_q, grad_k, grad_v = [s.astype(f32) for s in sums]
    grad_w_qkv = jnp.stack([grad_q, grad_k, grad_v])
    grad_x = grad_x.reshape(own, width)
    mods = everyone[:, :6].reshape(-1, 6 * width)
    conds = everyone[:, 11, : cond.shape[1]]
    grad_cond = jnp.dot(w_ada.astype(f32), mods[0], precision=lax.Precision.HIGHEST)[None, :]
    grad_w_ada = jnp.einsum("nc,nm->cm", conds, mods, precision=lax.Precision.HIGHEST, preferred_element_type=f32)
    total = jnp.sum(everyone, axis=0)
    grad_b_ada = total[:6].reshape(-1)
    grad_gain_one, grad_gain_two, grad_b_down = total[6], total[7], total[8]
    grad_b_up = total[9:11].reshape(-1)
    return (
        output, grad_x, grad_cond, grad_w_ada, grad_b_ada, grad_gain_one, grad_w_qkv, grad_w_out, grad_gain_two,
        grad_w_up, grad_b_up, grad_w_down, grad_b_down,
    )


def body_any(
    tokens, cond, doc_lengths, w_ada, b_ada, gain_one, w_qkv, w_out, gain_two, w_up, b_up, w_down, b_down, cotangent
):
    tensor_size = lax.axis_size("tensor")
    own = tokens.shape[0]
    length = own * tensor_size

    def all_rows(values):
        return lax.all_gather(values, "tensor", axis=0, tiled=True)

    def own_sum(values):
        return lax.psum_scatter(values, "tensor", scatter_dimension=0, tiled=True)

    def sum_over_dp(part):
        return lax.psum(part, "dp")

    places = jnp.arange(length, dtype=jnp.int32)
    segment, doc_first = documents(doc_lengths[0], places)
    cosine, sine = rope_tables(places - doc_first)
    blocks = length // BLOCK
    in_blocks = segment.reshape(blocks, BLOCK)
    least, most = jnp.min(in_blocks, axis=1), jnp.max(in_blocks, axis=1)
    meets = (least[:, None] <= most[None, :]) & (least[None, :] <= most[:, None])
    flags = meets.astype(jnp.int32).reshape(-1)
    seg_rows = in_blocks[:, None, :]
    seg_cols = jnp.broadcast_to(segment[:, None], (length, 128))

    modulation = jnp.dot(cond, w_ada, preferred_element_type=f32)[0] + b_ada
    shift_a, scale_a, gate_a, shift_m, scale_m, gate_m = jnp.split(modulation, 6)
    x_rows = tokens.astype(f32)
    grad_out = cotangent.astype(f32)

    act_one = modulate(x_rows, gain_one, shift_a, scale_a).astype(bf16)
    rows_one = all_rows(act_one)
    grad_branch = (grad_out * gate_m).astype(bf16)
    full_branch = all_rows(grad_branch)
    qkv = project_qkv(rows_one, w_qkv, cosine, sine)
    mixed, lse = attend_forward(flags, qkv, seg_rows, seg_cols)
    projected = own_sum(jnp.dot(mixed, w_out, preferred_element_type=f32))
    middle = x_rows + gate_a * projected
    rows_two = all_rows(modulate(middle, gain_two, shift_m, scale_m).astype(bf16))
    pre_act = jnp.dot(rows_two, w_up, preferred_element_type=f32) + b_up
    hidden = jax.nn.gelu(pre_act, approximate=True).astype(bf16)

    grad_hidden = jnp.einsum("sd,fd->sf", full_branch, w_down, preferred_element_type=f32)
    _, gelu_back = jax.vjp(lambda values: jax.nn.gelu(values, approximate=True), pre_act)
    grad_pre = gelu_back(grad_hidden)[0].astype(bf16)
    grad_act_two = own_sum(jnp.einsum("sf,df->sd", grad_pre, w_up, preferred_element_type=f32))
    grad_w_down = sum_over_dp(jnp.einsum("sf,sd->fd", hidden, full_branch, preferred_element_type=f32))
    grad_w_up = sum_over_dp(jnp.einsum("sd,sf->df", rows_two, grad_pre, preferred_element_type=f32))

    branch = own_sum(jnp.dot(hidden, w_down, preferred_element_type=f32)) + b_down
    output = (middle + gate_m * branch).astype(bf16)
    grad_gate_m = jnp.sum(grad_out * branch, axis=0)
    grad_b_down = jnp.sum(grad_branch.astype(f32), axis=0)
    grad_b_up = jnp.sum(grad_pre.astype(f32), axis=0)

    _, second_back = jax.vjp(modulate, middle, gain_two, shift_m, scale_m)
    grad_middle, grad_gain_two, grad_shift_m, grad_scale_m = second_back(grad_act_two)
    grad_middle = grad_middle + grad_out
    full_proj = all_rows((grad_middle * gate_a).astype(bf16))
    grad_gate_a = jnp.sum(grad_middle * projected, axis=0)
    grad_mixed = jnp.einsum("sd,ed->se", full_proj, w_out, preferred_element_type=f32).astype(bf16)
    grad_w_out = sum_over_dp(jnp.einsum("se,sd->ed", mixed, full_proj, preferred_element_type=f32))
    grad_qkv = attend_backward(flags, qkv, grad_mixed, mixed, lse, seg_rows, seg_cols, cosine, sine)
    grad_act_one = own_sum(jnp.einsum("tse,tde->sd", grad_qkv, w_qkv, preferred_element_type=f32))
    grad_w_qkv = jnp.einsum("sd,tse->tde", rows_one, grad_qkv, preferred_element_type=f32)
    grad_w_qkv = sum_over_dp(grad_w_qkv.reshape(-1, grad_w_qkv.shape[2])).reshape(grad_w_qkv.shape)

    _, first_back = jax.vjp(modulate, x_rows, gain_one, shift_a, scale_a)
    grad_x, grad_gain_one, grad_shift_a, grad_scale_a = first_back(grad_act_one)
    grad_x = (grad_x + grad_middle).astype(bf16)

    small = jnp.concatenate(
        [
            grad_shift_a, grad_scale_a, grad_gate_a, grad_shift_m, grad_scale_m, grad_gate_m,
            grad_gain_one, grad_gain_two, grad_b_down,
        ]
    )
    small = lax.psum(small, "tensor")
    mod_size = modulation.shape[0]
    grad_mod = small[:mod_size]
    grad_cond = jnp.dot(w_ada.astype(f32), grad_mod, precision=lax.Precision.HIGHEST)[None, :]
    everyone = lax.all_gather(
        jnp.concatenate([small, grad_b_up, cond[0].astype(f32)])[None, :], "dp", axis=0, tiled=True
    )
    conds = everyone[:, -cond.shape[1] :]
    mods = everyone[:, :mod_size]
    grad_w_ada = jnp.einsum("nc,nm->cm", conds, mods, precision=lax.Precision.HIGHEST, preferred_element_type=f32)
    sums = jnp.sum(everyone, axis=0)
    width = tokens.shape[1]
    grad_b_ada = sums[:mod_size]
    grad_gain_one, grad_gain_two, grad_b_down = jnp.split(sums[mod_size : mod_size + 3 * width], 3)
    grad_b_up = sums[mod_size + 3 * width : -cond.shape[1]]
    return (
        output, grad_x, grad_cond, grad_w_ada, grad_b_ada, grad_gain_one, grad_w_qkv, grad_w_out, grad_gain_two,
        grad_w_up, grad_b_up, grad_w_down, grad_b_down,
    )


def solution(mesh):
    swaps = mesh.shape["tensor"] == 2 and mesh.shape["dp"] == 16
    placed = (
        P(("dp", "tensor"), None), P("dp", None), P("dp", None), P(), P(), P(), P(None, None, "tensor"),
        P("tensor", None), P(), P(None, "tensor"), P("tensor"), P("tensor", None), P(), P(("dp", "tensor"), None),
    )
    return jax.shard_map(
        body_pair if swaps else body_any,
        mesh=mesh,
        in_specs=placed,
        out_specs=(
            P(("dp", "tensor"), None), P(("dp", "tensor"), None), P("dp", None), P(), P(), P(),
            P(None, None, "tensor"), P("tensor", None), P(), P(None, "tensor"), P("tensor"), P("tensor", None), P(),
        ),
        check_vma=False,
    )
```

```python
import functools

import jax
import jax.numpy as jnp
from jax import lax
from jax.experimental import pallas as pl
from jax.experimental.pallas import tpu as pltpu
from jax.sharding import PartitionSpec as P

HEAD = 64
PAIR = 2 * HEAD
BLOCK = 256
ROWS = 512

norm_eps = 1e-05
rope_base = 10000.0
masked_score = -1e30
f32, bf16 = jnp.float32, jnp.bfloat16


def layer_norm(values, gain):
    center = values - jnp.mean(values, axis=-1, keepdims=True)
    spread = jnp.mean(center * center, axis=-1, keepdims=True)
    return center * lax.rsqrt(spread + norm_eps) * gain


def modulate(values, gain, shift, scale):
    return layer_norm(values, gain) * (1.0 + scale) + shift


def documents(lengths, places):
    numbers = jnp.arange(lengths.shape[0], dtype=jnp.int32)
    earlier = (numbers[None, :] < numbers[:, None]).astype(jnp.int32)
    starts = jnp.sum(earlier * lengths[None, :], axis=1)
    ends = starts + lengths
    inside = ((places[:, None] >= starts[None, :]) & (places[:, None] < ends[None, :])).astype(
        jnp.int32
    )
    segment = jnp.sum(inside * numbers[None, :], axis=1)
    doc_first = jnp.sum(inside * starts[None, :], axis=1)
    return segment, doc_first


def rope_tables(offsets):
    exponent = jnp.arange(HEAD // 2, dtype=f32) * (2.0 / HEAD)
    frequency = jnp.power(jnp.float32(rope_base), -exponent)
    angles = offsets.astype(f32)[:, None] * frequency[None, :]
    cosine, sine = jnp.cos(angles), jnp.sin(angles)
    repeat = PAIR // (HEAD // 2)
    return jnp.concatenate([cosine] * repeat, axis=-1), jnp.concatenate([sine] * repeat, axis=-1)


def turned(values):
    lane = lax.broadcasted_iota(jnp.int32, values.shape, 1)
    half = HEAD // 2
    from_right = pltpu.roll(values, PAIR - half, axis=1)
    from_left = pltpu.roll(values, half, axis=1)
    return jnp.where(lane % HEAD < half, -from_right, from_left)


def mm(a, b, da, db):
    return lax.dot_general(a, b, (((da,), (db,)), ((), ())), preferred_element_type=f32)


def qkv_kernel(x_ref, w_ref, cos_ref, sin_ref, o_ref):
    which = pl.program_id(1)
    y = mm(x_ref[...], w_ref[...], 1, 0)

    @pl.when(which < 2)
    def _():
        factor = jnp.where(which == 0, HEAD**-0.5, 1.0)
        for p in range(y.shape[1] // PAIR):
            u = y[:, p * PAIR : (p + 1) * PAIR]
            r = u * cos_ref[...] + turned(u) * sin_ref[...]
            o_ref[:, p * PAIR : (p + 1) * PAIR] = (r.astype(bf16) * factor.astype(bf16)).astype(bf16)

    @pl.when(which == 2)
    def _():
        o_ref[...] = y.astype(bf16)


def project_qkv(rows, w_qkv, cosine, sine):
    count, depth = rows.shape
    width = w_qkv.shape[2]
    return pl.pallas_call(
        qkv_kernel,
        grid=(count // ROWS, 3),
        in_specs=[
            pl.BlockSpec((ROWS, depth), lambda r, t: (r, 0)),
            pl.BlockSpec((None, depth, width), lambda r, t: (t, 0, 0)),
            pl.BlockSpec((ROWS, PAIR), lambda r, t: (r, 0)),
            pl.BlockSpec((ROWS, PAIR), lambda r, t: (r, 0)),
        ],
        out_specs=pl.BlockSpec((None, ROWS, width), lambda r, t: (t, r, 0)),
        out_shape=jax.ShapeDtypeStruct((3, count, width), bf16),
        compiler_params=pltpu.CompilerParams(vmem_limit_bytes=32 << 20),
        cost_estimate=pl.CostEstimate(
            flops=6 * count * depth * width, bytes_accessed=8 * count * width, transcendentals=0
        ),
        name="qkv",
    )(rows, w_qkv, cosine, sine)


def head_lanes(block, h):
    lane = lax.broadcasted_iota(jnp.int32, block.shape, 1)
    return jnp.where(lane // HEAD == h, block, jnp.zeros_like(block))


def transposed(block):
    return block.astype(f32).T


def forward_kernel(flag_ref, q_ref, k_ref, v_ref, segr_ref, segc_ref, o_ref, lse_ref, vt, m, l, acc):
    blocks = q_ref.shape[0] // BLOCK
    for b in range(blocks):
        vt[b] = transposed(v_ref[b * BLOCK : (b + 1) * BLOCK, :]).astype(bf16)

    @pl.loop(0, blocks)
    def _(qi):
        rows = pl.ds(pl.multiple_of(qi * BLOCK, BLOCK), BLOCK)
        q = q_ref[rows, :]
        m[...] = jnp.full(m.shape, masked_score, f32)
        l[...] = jnp.zeros(l.shape, f32)
        acc[...] = jnp.zeros(acc.shape, f32)

        @pl.loop(0, blocks)
        def _(ki):
            @pl.when(flag_ref[qi * blocks + ki] > 0)
            def _():
                cols = pl.ds(pl.multiple_of(ki * BLOCK, BLOCK), BLOCK)
                k = k_ref[cols, :]
                docs = segc_ref[cols, :]
                same = jnp.concatenate([docs] * (BLOCK // 128), axis=1) == segr_ref[qi]
                for h in range(2):
                    lo, hi = h * HEAD, (h + 1) * HEAD
                    s = jnp.where(same, mm(k, head_lanes(q, h), 1, 1), masked_score)
                    top = jnp.maximum(m[h], jnp.max(s, axis=0, keepdims=True))
                    p = jnp.exp(s - top)
                    shrink = jnp.exp(m[h] - top)
                    m[h] = top
                    l[h] = l[h] * shrink + jnp.sum(p, axis=0, keepdims=True)
                    acc[lo:hi, :] = acc[lo:hi, :] * shrink + mm(vt[ki, lo:hi, :], p.astype(bf16), 1, 0)

        for h in range(2):
            lo, hi = h * HEAD, (h + 1) * HEAD
            lse_ref[h, qi] = m[h] + jnp.log(l[h])
            acc[lo:hi, :] = acc[lo:hi, :] / l[h]
        o_ref[rows, :] = acc[...].T.astype(bf16)


def backward_kernel(
    flag_ref, q_ref, k_ref, v_ref, g_ref, o_ref, lse_ref, segr_ref, segc_ref, cos_ref, sin_ref,
    out_ref, kt, dk, dv, dq,
):
    blocks = q_ref.shape[0] // BLOCK
    for b in range(blocks):
        kt[b] = transposed(k_ref[b * BLOCK : (b + 1) * BLOCK, :]).astype(bf16)
    dk[...] = jnp.zeros(dk.shape, f32)
    dv[...] = jnp.zeros(dv.shape, f32)

    def turn_back(u, rows):
        return (u * cos_ref[rows, :] - turned(u) * sin_ref[rows, :]).astype(bf16)

    @pl.loop(0, blocks)
    def _(qi):
        rows = pl.ds(pl.multiple_of(qi * BLOCK, BLOCK), BLOCK)
        q, g = q_ref[rows, :], g_ref[rows, :]
        both = (g.astype(f32) * o_ref[rows, :].astype(f32)).T
        dq[...] = jnp.zeros(dq.shape, f32)

        @pl.loop(0, blocks)
        def _(ki):
            @pl.when(flag_ref[qi * blocks + ki] > 0)
            def _():
                cols = pl.ds(pl.multiple_of(ki * BLOCK, BLOCK), BLOCK)
                k, v = k_ref[cols, :], v_ref[cols, :]
                docs = segc_ref[cols, :]
                same = jnp.concatenate([docs] * (BLOCK // 128), axis=1) == segr_ref[qi]
                dk_sum, dv_sum = dk[cols, :], dv[cols, :]
                for h in range(2):
                    lo, hi = h * HEAD, (h + 1) * HEAD
                    delta = jnp.sum(both[lo:hi, :], axis=0, keepdims=True)
                    qh, gh = head_lanes(q, h), head_lanes(g, h)
                    s = jnp.where(same, mm(k, qh, 1, 1), masked_score)
                    p = jnp.exp(s - lse_ref[h, qi])
                    ds = (p * (mm(v, gh, 1, 1) - delta)).astype(bf16)
                    dv_sum = dv_sum + mm(p.astype(bf16), gh, 1, 0)
                    dk_sum = dk_sum + mm(ds, qh, 1, 0)
                    dq[lo:hi, :] = dq[lo:hi, :] + mm(kt[ki, lo:hi, :], ds, 1, 0)
                dk[cols, :] = dk_sum
                dv[cols, :] = dv_sum

        out_ref[0, rows, :] = turn_back(dq[...].T * (HEAD**-0.5), rows)

    @pl.loop(0, blocks)
    def _(b):
        rows = pl.ds(pl.multiple_of(b * BLOCK, BLOCK), BLOCK)
        out_ref[1, rows, :] = turn_back(dk[rows, :], rows)
        out_ref[2, rows, :] = dv[rows, :].astype(bf16)


def pieces_of(qkv, length):
    return [pl.BlockSpec((None, length, PAIR), functools.partial(lambda t, p, *_: (t, 0, p), t)) for t in range(3)]


def attend_forward(flags, qkv, seg_rows, seg_cols):
    _, length, width = qkv.shape
    blocks, pairs = length // BLOCK, width // PAIR
    return pl.pallas_call(
        forward_kernel,
        grid_spec=pltpu.PrefetchScalarGridSpec(
            num_scalar_prefetch=1,
            grid=(pairs,),
            in_specs=[
                *pieces_of(qkv, length),
                pl.BlockSpec((blocks, 1, BLOCK), lambda p, *_: (0, 0, 0)),
                pl.BlockSpec((length, 128), lambda p, *_: (0, 0)),
            ],
            out_specs=[
                pl.BlockSpec((length, PAIR), lambda p, *_: (0, p)),
                pl.BlockSpec((2, blocks, 1, BLOCK), lambda p, *_: (p, 0, 0, 0)),
            ],
            scratch_shapes=[
                pltpu.VMEM((blocks, PAIR, BLOCK), bf16),
                pltpu.VMEM((2, 1, BLOCK), f32),
                pltpu.VMEM((2, 1, BLOCK), f32),
                pltpu.VMEM((PAIR, BLOCK), f32),
            ],
        ),
        out_shape=[
            jax.ShapeDtypeStruct((length, width), bf16),
            jax.ShapeDtypeStruct((2 * pairs, blocks, 1, BLOCK), f32),
        ],
        compiler_params=pltpu.CompilerParams(vmem_limit_bytes=48 << 20),
        cost_estimate=pl.CostEstimate(
            flops=4 * length * length * width, bytes_accessed=8 * length * width, transcendentals=length * length * width // HEAD
        ),
        name="attend",
    )(flags, qkv, qkv, qkv, seg_rows, seg_cols)


def attend_backward(flags, qkv, grad, mixed, lse, seg_rows, seg_cols, cosine, sine):
    _, length, width = qkv.shape
    blocks, pairs = length // BLOCK, width // PAIR
    whole = pl.BlockSpec((length, PAIR), lambda p, *_: (0, p))
    table = pl.BlockSpec((length, PAIR), lambda p, *_: (0, 0))
    return pl.pallas_call(
        backward_kernel,
        grid_spec=pltpu.PrefetchScalarGridSpec(
            num_scalar_prefetch=1,
            grid=(pairs,),
            in_specs=[
                *pieces_of(qkv, length),
                whole,
                whole,
                pl.BlockSpec((2, blocks, 1, BLOCK), lambda p, *_: (p, 0, 0, 0)),
                pl.BlockSpec((blocks, 1, BLOCK), lambda p, *_: (0, 0, 0)),
                table,
                table,
                table,
            ],
            out_specs=pl.BlockSpec((3, length, PAIR), lambda p, *_: (0, 0, p)),
            scratch_shapes=[
                pltpu.VMEM((blocks, PAIR, BLOCK), bf16),
                pltpu.VMEM((length, PAIR), f32),
                pltpu.VMEM((length, PAIR), f32),
                pltpu.VMEM((PAIR, BLOCK), f32),
            ],
        ),
        out_shape=jax.ShapeDtypeStruct((3, length, width), bf16),
        compiler_params=pltpu.CompilerParams(vmem_limit_bytes=56 << 20),
        cost_estimate=pl.CostEstimate(
            flops=10 * length * length * width, bytes_accessed=16 * length * width, transcendentals=length * length * width // HEAD
        ),
        name="attend_back",
    )(flags, qkv, qkv, qkv, grad, mixed, lse, seg_rows, seg_cols, cosine, sine)


MESH = pl.DeviceIdType.MESH
ADD_ROWS = 32
STEPS = 9
EDGES = 4


def add_low(a, a_at, b, rows):
    @pl.loop(0, rows // ADD_ROWS)
    def _(i):
        at = pl.ds(pl.multiple_of(i * ADD_ROWS, ADD_ROWS), ADD_ROWS)
        kept = a[pl.ds(pl.multiple_of(a_at + i * ADD_ROWS, ADD_ROWS), ADD_ROWS), :].astype(f32)
        b[at, :] = (kept + b[at, :].astype(f32)).astype(bf16)


class Unit:
    def __init__(self, part, out, column, got, send, recv, local, place, bits=(0, 1, 2, 3)):
        self.part, self.out, self.got = part, out, got
        self.send, self.recv, self.local = send, recv, local
        self.rows, columns = 2 * got[0].shape[0], got[0].shape[1]
        self.columns = pl.ds(column, columns)
        self.bit = [(place // (1 << b)) % 2 for b in bits]
        self.partner = [place + (1 - 2 * bit) * (1 << b) for bit, b in zip(self.bit, bits, strict=True)]
        self.base = [0]
        for b in range(EDGES):
            self.base.append(self.base[-1] + self.bit[b] * (self.rows >> (b + 1)))

    def remote(self, src, dst, stage, b):
        return pltpu.make_async_remote_copy(
            src_ref=src,
            dst_ref=dst,
            send_sem=self.send.at[stage],
            recv_sem=self.recv.at[stage],
            device_id={"dp": self.partner[b]},
            device_id_type=MESH,
        )

    def halving(self, b):
        half = self.rows >> (b + 1)
        source = self.part if b == 0 else self.got[b - 1]
        away = pl.ds(pl.multiple_of((1 - self.bit[b]) * half, ADD_ROWS), half)
        return self.remote(source.at[away], self.got[b], b, b)

    def spot(self, b):
        size = self.rows >> (b + 1)
        return self.out.at[pl.ds(pl.multiple_of(self.base[b + 1], ADD_ROWS), size), self.columns]

    def own(self):
        return pltpu.make_async_copy(self.got[3], self.spot(3), self.local.at[0])

    def gathering(self, b):
        return self.remote(self.got[3] if b == 3 else self.spot(b), self.spot(b), 7 - b, b)

    def step(self, k):
        if k == 0:
            self.halving(0).start()
        elif k < 5:
            b = k - 1
            self.halving(b).wait()
            half = self.rows >> (b + 1)
            add_low(self.part if b == 0 else self.got[b - 1], self.bit[b] * half, self.got[b], half)
            if b < 3:
                self.halving(b + 1).start()
            else:
                self.own().start()
                self.gathering(3).start()
        elif k == 5:
            self.own().wait()
            self.gathering(3).wait()
            self.gathering(2).start()
        elif k < 8:
            self.gathering(8 - k).wait()
            self.gathering(7 - k).start()
        else:
            self.gathering(0).wait()


def unit_scratch(rows, columns):
    return [
        *[pltpu.VMEM((rows >> (b + 1), columns), bf16) for b in range(EDGES)],
        pltpu.SemaphoreType.DMA((2 * EDGES,)),
        pltpu.SemaphoreType.DMA((2 * EDGES,)),
        pltpu.SemaphoreType.DMA((1,)),
    ]


def greet(targets):
    barrier = pltpu.get_barrier_semaphore()
    for target in targets:
        pl.semaphore_signal(barrier, inc=1, device_id=target, device_id_type=MESH)
    pl.semaphore_wait(barrier, len(targets))


ORDER = (
    (3.5, 0, 1), (5.5, 1, 1), (7.5, 2, 1), (7.5, 0, 2), (9.5, 1, 2), (9.5, 0, 3), (10, 3, 1), (10, 0, 4), (10, 1, 3),
    (10, 2, 2), (10.5, 4, 1), (10.5, 1, 4), (10.5, 0, 5), (12.5, 1, 5), (12.5, 2, 3), (13.5, 3, 2), (13.5, 0, 6),
    (14.5, 2, 4), (15.5, 1, 6), (15.5, 4, 2), (15.5, 3, 3), (15.5, 0, 7), (17.5, 0, 8), (17.5, 2, 5), (18.5, 5, 1),
    (18.5, 1, 7), (19.5, 1, 8), (19.5, 3, 4), (20.5, 5, 2), (20.5, 4, 3), (20.5, 2, 6), (21.5, 3, 5), (23.5, 5, 3),
    (23.5, 4, 4), (23.5, 6, 1), (26.5, 7, 1), (26.5, 5, 4), (26.5, 2, 7), (29.5, 6, 2), (29.5, 8, 1), (29.5, 5, 5),
    (29.5, 2, 8), (30.5, 4, 5), (31, 7, 2), (31, 3, 6), (32, 6, 3), (32, 8, 2), (32, 6, 4), (32, 7, 3), (32, 5, 6),
    (33, 4, 6), (33, 3, 7), (33, 8, 3), (33, 6, 5), (33, 7, 4), (34, 3, 8), (34, 8, 4), (34, 5, 7), (34, 7, 5),
    (35, 5, 8), (35, 6, 6), (35, 8, 5), (36, 7, 6), (36, 4, 7), (36, 4, 8), (36, 6, 7), (36, 8, 6), (37, 6, 8),
    (99, 7, 7), (99, 7, 8), (99, 8, 7), (99, 8, 8),
)
WIDE = 512
STEP_ROWS = 64


def fetcher(sems):
    count = [0]

    def fetch(src, dst):
        copy = pltpu.make_async_copy(src, dst, sems.at[count[0]])
        copy.start()
        count[0] += 1
        return copy

    return fetch


def head_kernel(
    tokens_hbm, cot_hbm, w_qkv_hbm, w_out_hbm, w_up_hbm, w_down_hbm,
    mods, gain_one, gain_two, sequence, b_up, segr, segc, cosine, sine,
    qkv_out, mixed_out, one_out, back_out, two_out, hidden_out, pre_out, own_grad, send_grad, middle_out,
    projected_out, own_branch, send_branch, lse, known,
    tokens, cot, w_qkv, w_out, w_up, w_down, rows_one, full_back, rows_two, qkv, mixed, from_sum, send_sum, projected,
    middle, hidden, pre, grads, branch, low_grads, low_branch, bias, bias_down, load, x_send, x_recv,
):
    me = lax.axis_index("tensor")
    length, depth = rows_one.shape
    chunks, half, _ = from_sum.shape
    chunk = 2 * half
    width = mixed.shape[1]
    pairs = width // PAIR
    across = {"tensor": 1 - me}
    each = range(chunks)
    own = [slice(c * chunk, c * chunk + half) for c in each]
    got = [slice(c * chunk + half, (c + 1) * chunk) for c in each]
    whole = [slice(c * chunk, (c + 1) * chunk) for c in each]
    fetch = fetcher(load)

    def x_copy(src, dst, i):
        return pltpu.make_async_remote_copy(
            src_ref=src, dst_ref=dst, send_sem=x_send.at[i], recv_sem=x_recv.at[i],
            device_id=across, device_id_type=MESH,
        )

    ones = [x_copy(rows_one.at[own[c]], rows_one.at[got[c]], c) for c in each]
    backs = [x_copy(full_back.at[own[c]], full_back.at[got[c]], chunks + c) for c in each]
    shares = [x_copy(send_sum.at[c], from_sum.at[c], 2 * chunks + c) for c in each]
    twos = [x_copy(rows_two.at[own[c]], rows_two.at[got[c]], 3 * chunks + c) for c in each]

    shift_a, scale_a, gate_a, shift_m, scale_m, gate_m = [mods[r : r + 1, :] for r in range(6)]
    gain_one, gain_two = gain_one[...], gain_two[...]
    reads = [fetch(tokens_hbm, tokens), fetch(w_qkv_hbm, w_qkv), fetch(cot_hbm, cot)]
    reads += [fetch(w_out_hbm, w_out), fetch(w_up_hbm, w_up), fetch(w_down_hbm, w_down)]
    writes = []
    greet([across])

    def normal_of(values):
        center = values - jnp.mean(values, axis=1, keepdims=True)
        return center * lax.rsqrt(jnp.mean(center * center, axis=1, keepdims=True) + norm_eps)

    def by_rows(work):
        @pl.loop(0, half // STEP_ROWS)
        def _(i):
            work(pl.multiple_of(i * STEP_ROWS, STEP_ROWS))

    reads[0].wait()
    for c in each:

        def first_norm(at, c=c):
            values = tokens[pl.ds(c * half + at, STEP_ROWS), :].astype(f32)
            out = normal_of(values) * gain_one * (1.0 + scale_a) + shift_a
            rows_one[pl.ds(c * chunk + at, STEP_ROWS), :] = out.astype(bf16)

        by_rows(first_norm)
        if c == 0:
            ones[c].start()
    reads[2].wait()
    bias_down[...] = jnp.zeros(bias_down.shape, f32)
    for c in each:

        def weigh(at, c=c):
            low = (cot[pl.ds(c * half + at, STEP_ROWS), :].astype(f32) * gate_m).astype(bf16)
            full_back[pl.ds(c * chunk + at, STEP_ROWS), :] = low
            bias_down[...] += jnp.sum(low.astype(f32), axis=0, keepdims=True)

        by_rows(weigh)
    reads[1].wait()

    def project(c):
        rows = whole[c]
        for t in range(3):
            y = mm(rows_one[rows, :], w_qkv[t], 1, 0)
            if t == 2:
                qkv[t, rows, :] = y.astype(bf16)
                continue
            for p in range(pairs):
                lanes = slice(p * PAIR, (p + 1) * PAIR)
                u = y[:, lanes]
                low = (u * cosine[rows, :] + turned(u) * sine[rows, :]).astype(bf16)
                qkv[t, rows, lanes] = low * jnp.asarray(HEAD**-0.5 if t == 0 else 1.0, bf16)

    ones[0].wait()
    ones[1].start()
    project(0)
    ones[1].wait()
    backs[0].start()
    project(1)
    writes.append(fetch(rows_one, one_out))
    writes.append(fetch(qkv, qkv_out))

    def attend(p, c):
        lanes = pl.ds(pl.multiple_of(p * PAIR, PAIR), PAIR)
        q = qkv[0, whole[c], lanes]
        docs = segr[:, whole[c]]
        outs = []
        for h in range(2):
            qh = head_lanes(q, h)
            scores = []
            for b in range(0, length, BLOCK):
                same = jnp.concatenate([segc[b : b + BLOCK, :]] * (chunk // 128), axis=1) == docs
                scores.append(jnp.where(same, mm(qkv[1, b : b + BLOCK, lanes], qh, 1, 1), masked_score))
            top = functools.reduce(jnp.maximum, [jnp.max(s, axis=0, keepdims=True) for s in scores])
            total, summed = 0.0, 0.0
            for i, s in enumerate(scores):
                pr = jnp.exp(s - top)
                total = total + jnp.sum(pr, axis=0, keepdims=True)
                v = transposed(qkv[2, i * BLOCK : (i + 1) * BLOCK, lanes]).astype(bf16)
                summed = summed + mm(v[h * HEAD : (h + 1) * HEAD, :], pr.astype(bf16), 1, 0)
            lse[c, 2 * p + h] = top + jnp.log(total)
            outs.append(summed / total)
        mixed[whole[c], lanes] = jnp.concatenate(outs, axis=0).T.astype(bf16)

    for c in each:

        @pl.loop(0, pairs)
        def _(p):
            attend(p, c)

        if c == 0:
            reads[3].wait()
        send_sum[c] = mm(mixed[got[c], :], w_out[...], 1, 0).astype(bf16)
        shares[c].start()
        projected[c] = mm(mixed[own[c], :], w_out[...], 1, 0)
    writes.append(fetch(mixed, mixed_out))

    def second_norm(c):
        shares[c].wait()

        def work(at):
            rows = pl.ds(at, STEP_ROWS)
            share = projected[c, rows, :] + from_sum[c, rows, :].astype(f32)
            projected[c, rows, :] = share
            values = tokens[pl.ds(c * half + at, STEP_ROWS), :].astype(f32) + gate_a * share
            middle[c, rows, :] = values
            out = normal_of(values) * gain_two * (1.0 + scale_m) + shift_m
            rows_two[pl.ds(c * chunk + at, STEP_ROWS), :] = out.astype(bf16)

        by_rows(work)
        twos[c].start()

    cubic, root = 0.044715, (2.0 / jnp.pi) ** 0.5
    tile = 2 * WIDE
    bias[...] = jnp.zeros(bias.shape, f32)
    held = [[], []]

    def feed_forward(slot, rows):
        for copy in held[slot]:
            copy.wait()

        @pl.loop(0, w_up.shape[1] // tile)
        def _(t):
            at = pl.ds(pl.multiple_of(t * tile, tile), tile)
            u = mm(rows_two[rows, :], w_up[:, at], 1, 0) + b_up[:, at]
            square = u * u
            t_h = jnp.tanh(u * (root + (root * cubic) * square))
            rising = 0.5 * (1.0 + t_h)
            low_hidden = (u * rising).astype(bf16)
            slope = rising + (0.5 * u) * (1.0 - t_h * t_h) * (root + (3.0 * cubic * root) * square)
            low = (mm(full_back[rows, :], w_down[at, :], 1, 1) * slope).astype(bf16)
            hidden[slot, :, at] = low_hidden
            pre[slot, :, at] = low
            bias[:, at] += jnp.sum(low.astype(f32), axis=0, keepdims=True)
            more, more_branch = mm(low, w_up[:, at], 1, 1), mm(low_hidden, w_down[at, :], 1, 0)

            @pl.when(t == 0)
            def _():
                grads[slot] = more
                branch[slot] = more_branch

            @pl.when(t > 0)
            def _():
                grads[slot] += more
                branch[slot] += more_branch

        held[slot] = [fetch(hidden.at[slot], hidden_out.at[rows]), fetch(pre.at[slot], pre_out.at[rows])]

    second_norm(0)
    for read in reads[4:]:
        read.wait()
    for c in each:
        if c:
            second_norm(c)
        feed_forward(c, own[c])
        held[c] += [fetch(grads.at[c], own_grad.at[c]), fetch(branch.at[c], own_branch.at[c])]
    writes.append(fetch(middle, middle_out))
    writes.append(fetch(projected, projected_out))
    for c in each:
        twos[c].wait()
        backs[c].wait()
        if c == 0:
            backs[1].start()
        feed_forward(c, got[c])
        low_grads[c] = grads[c].astype(bf16)
        low_branch[c] = branch[c].astype(bf16)
        writes += [fetch(low_grads.at[c], send_grad.at[c]), fetch(low_branch.at[c], send_branch.at[c]), *held[c]]
    writes += [fetch(full_back, back_out), fetch(rows_two, two_out)]
    known[...] = jnp.concatenate(
        [
            jnp.zeros((8, depth), f32), bias_down[...], bias[:, :depth], bias[:, depth:], sequence[...],
            jnp.zeros((4, depth), f32),
        ],
        axis=0,
    )
    for copy in writes:
        copy.wait()


def head(tokens, cot, w_qkv, w_out, w_up, w_down, *near_args, chunks):
    own, depth = tokens.shape
    length, width, wide = 2 * own, w_qkv.shape[2], w_up.shape[1]
    half = own // chunks
    anywhere, near = pl.BlockSpec(memory_space=pl.ANY), pl.BlockSpec(memory_space=pltpu.VMEM)
    shaped, kept = jax.ShapeDtypeStruct, pltpu.VMEM
    parts, rows = (chunks, half, depth), (length, depth)
    return pl.pallas_call(
        head_kernel,
        in_specs=[anywhere] * 6 + [near] * len(near_args),
        out_specs=[anywhere] * 13 + [near] * 2,
        out_shape=[
            shaped((3, length, width), bf16), shaped((length, width), bf16), *[shaped(rows, bf16)] * 3,
            *[shaped((length, wide), bf16)] * 2, shaped(parts, f32), shaped(parts, bf16),
            shaped(parts, f32), shaped(parts, f32), shaped(parts, f32), shaped(parts, bf16),
            shaped((chunks, width // HEAD, 1, length // chunks), f32), shaped((16, depth), f32),
        ],
        scratch_shapes=[
            kept(tokens.shape, bf16), kept(tokens.shape, bf16), kept(w_qkv.shape, bf16), kept(w_out.shape, bf16),
            kept(w_up.shape, bf16), kept(w_down.shape, bf16), *[kept(rows, bf16)] * 3, kept((3, length, width), bf16),
            kept((length, width), bf16), kept(parts, bf16), kept(parts, bf16), kept(parts, f32), kept(parts, f32),
            *[kept((chunks, half, wide), bf16)] * 2, *[kept(parts, f32)] * 2,
            kept(parts, bf16), kept(parts, bf16), kept((1, wide), f32), kept((1, depth), f32),
            pltpu.SemaphoreType.DMA((32,)),
            pltpu.SemaphoreType.DMA((4 * chunks,)), pltpu.SemaphoreType.DMA((4 * chunks,)),
        ],
        compiler_params=pltpu.CompilerParams(collective_id=2, has_side_effects=True, vmem_limit_bytes=61 << 20),
        name="head",
    )(tokens, cot, w_qkv, w_out, w_up, w_down, *near_args)


def tail_kernel(
    hidden, full_back, rows_two, grad_pre, qkv_hbm, mixed_hbm, rows_hbm, w_qkv_hbm, w_out_hbm,
    own_grad, send_grad, mid_hbm, proj_hbm, own_branch, send_branch, tokens_hbm, cot_hbm,
    mods, gain_one, gain_two, b_down, known, lse, segr, segc, cosine, sine,
    down_sum, up_sum, out_sum, q_sum, k_sum, v_sum, output, ada, grad_x, mine, total,
    qkv, mixed, rows_one, w_qkv, w_out, proj, mix_grad, d_qkv, dk, dv, from_x, grads, middle, projected, tokens, cot,
    part_a, part_b, part_c, part_d, part_e, branch_got, col_sums, small, small_got, everyone,
    load, store, x_send, x_recv, all_send, all_recv, *more,
):
    place, me = lax.axis_index("dp"), lax.axis_index("tensor")
    length, depth = rows_one.shape
    chunks, half, _ = from_x.shape
    chunk = 2 * half
    width = mixed.shape[1]
    pairs = width // PAIR
    across = {"tensor": 1 - me}

    specs = [
        (part_a.at[pl.ds(0, WIDE)], down_sum.at[pl.ds(0, WIDE)], 0),
        (part_a.at[pl.ds(WIDE, WIDE)], down_sum.at[pl.ds(WIDE, WIDE)], 0),
        (part_b, down_sum.at[pl.ds(depth, depth)], 0),
        (part_c, up_sum, 0), (part_d, up_sum, depth), (part_e, out_sum, 0),
        (qkv.at[2], v_sum, 0), (qkv.at[1], k_sum, 0), (qkv.at[0], q_sum, 0),
    ]
    units = []
    for i, (part, out, column) in enumerate(specs):
        *got, send, recv, local = more[7 * i : 7 * (i + 1)]
        units.append(Unit(part, out, column, got, send, recv, local, place))

    def x_copy(src, dst, i):
        return pltpu.make_async_remote_copy(
            src_ref=src, dst_ref=dst, send_sem=x_send.at[i], recv_sem=x_recv.at[i],
            device_id=across, device_id_type=MESH,
        )

    each = range(chunks)
    grads_in = [x_copy(send_grad.at[c], from_x.at[c], c) for c in each]
    projs = [x_copy(proj.at[c, :half], proj.at[c, half:], chunks + c) for c in each]
    ones = [x_copy(proj.at[c, :half], from_x.at[c], 2 * chunks + c) for c in each]
    branches = [x_copy(send_branch.at[c], branch_got.at[c], 3 * chunks + c) for c in each]
    smalls = x_copy(small, small_got, 4 * chunks)
    outputs = [
        pltpu.make_async_copy(branch_got.at[c], output.at[c * half : (c + 1) * half], store.at[c]) for c in each
    ]
    partner = units[0].partner

    fetch = fetcher(load)
    done = [0]

    def until(place_now):
        while done[0] < len(ORDER) and ORDER[done[0]][0] <= place_now:
            _, i, k = ORDER[done[0]]
            units[i].step(k)
            done[0] += 1

    greet([*[{"dp": p} for p in partner], across])
    grads_in[0].start()
    slots = [w_qkv.at[0], w_qkv.at[1], w_qkv.at[2], d_qkv.at[2]]
    cut = lambda t: slice(t * WIDE, (t + 1) * WIDE)
    backs = fetch(full_back, rows_one)
    hiddens = [fetch(hidden.at[:, cut(t)], slots[t]) for t in range(4)]
    norms = [
        [fetch(src, dst.at[c]) for src, dst in (
            (own_grad.at[c], grads), (mid_hbm.at[c], middle), (proj_hbm.at[c], projected),
            (tokens_hbm.at[c * half : (c + 1) * half], tokens), (cot_hbm.at[c * half : (c + 1) * half], cot),
        )]
        for c in each
    ]
    twos = [fetch(rows_two.at[:, cut(t)], d_qkv.at[t]) for t in range(2)]
    col_sums[...] = jnp.zeros(col_sums.shape, f32)

    backs.wait()
    pres = []
    for t in range(4):
        until(1 + t)
        hiddens[t].wait()
        part = (part_a, part_b)[t // 2]

        @pl.loop(0, WIDE // 256)
        def _(r):
            at = pl.ds(pl.multiple_of(r * 256, 256), 256)
            to = pl.ds(pl.multiple_of((t % 2) * WIDE + r * 256, 256), 256)
            part[to, :] = mm(slots[t][:, at], rows_one[...], 0, 0).astype(bf16)

        pres.append(fetch(grad_pre.at[:, cut(t)], slots[t]))
        if t != 2:
            units[min(t, 2)].step(0)
    main = [
        fetch(w_out_hbm, w_out), fetch(mixed_hbm, mixed), fetch(qkv_hbm, qkv), fetch(rows_hbm, rows_one),
    ]

    def up_part(t):
        pres[t].wait()
        part = (part_c, part_d)[t // 2]

        @pl.loop(0, depth // 256)
        def _(r):
            to = pl.ds(pl.multiple_of(r * 256, 256), 256)
            at = pl.ds(pl.multiple_of((r % 2) * 256, 256), 256)
            part[to, cut(t % 2)] = mm(d_qkv[r // 2, :, at], slots[t][...], 0, 0).astype(bf16)

    def fold(row, values):
        col_sums[row : row + 1, :] += jnp.sum(values, axis=0, keepdims=True)

    def norm_back(grad, values, weight):
        center = values - jnp.mean(values, axis=1, keepdims=True)
        root = lax.rsqrt(jnp.mean(center * center, axis=1, keepdims=True) + norm_eps)
        normal = center * root
        inner = grad * weight
        back = inner - jnp.mean(inner, axis=1, keepdims=True) - normal * jnp.mean(inner * normal, axis=1, keepdims=True)
        return root * back, normal

    scale_a, gate_a, scale_m, gate_m = [mods[r : r + 1, :] for r in (1, 2, 4, 5)]
    gain_one, gain_two, b_down = gain_one[...], gain_two[...], b_down[...]

    def second_norm(c):
        for copy in norms[c]:
            copy.wait()

        @pl.loop(0, half // STEP_ROWS)
        def _(i):
            at = pl.ds(pl.multiple_of(i * STEP_ROWS, STEP_ROWS), STEP_ROWS)
            grad = grads[c, at, :] + from_x[c, at, :].astype(f32)
            back, normal = norm_back(grad, middle[c, at, :], gain_two * (1.0 + scale_m))
            total = back + cot[c, at, :].astype(f32)
            grads[c, at, :] = total
            proj[c, at, :] = (total * gate_a).astype(bf16)
            fold(0, grad)
            fold(1, grad * normal)
            fold(2, total * projected[c, at, :])

        projs[c].start()

    for copy in twos:
        copy.wait()
    until(5)
    up_part(0)
    until(6)
    up_part(1)
    units[3].step(0)
    until(7)
    grads_in[0].wait()
    grads_in[1].start()
    second_norm(0)
    owns = [fetch(own_branch.at[0], projected.at[0])]
    until(8)
    up_part(2)
    until(9)
    up_part(3)
    units[4].step(0)
    weights = fetch(w_qkv_hbm, w_qkv)
    until(10)
    grads_in[1].wait()
    second_norm(1)
    owns.append(fetch(own_branch.at[1], projected.at[1]))

    def turn_back(u, rows):
        return (u * cosine[rows, :] - turned(u) * sine[rows, :]).astype(bf16)

    def attend_back(p, c):
        lanes = pl.ds(pl.multiple_of(p * PAIR, PAIR), PAIR)
        rows = slice(c * chunk, (c + 1) * chunk)
        q, g = qkv[0, rows, lanes], mix_grad[rows, lanes]
        both = (g.astype(f32) * mixed[rows, lanes].astype(f32)).T
        qh = [head_lanes(q, h) for h in range(2)]
        gh = [head_lanes(g, h) for h in range(2)]
        delta = [jnp.sum(both[h * HEAD : (h + 1) * HEAD, :], axis=0, keepdims=True) for h in range(2)]
        q_two, g_two = jnp.concatenate(qh, axis=0), jnp.concatenate(gh, axis=0)
        docs = segr[:, rows]
        dq = [0.0, 0.0]
        for b in range(0, length, BLOCK):
            cols = slice(b, b + BLOCK)
            k, v = qkv[1, cols, lanes], qkv[2, cols, lanes]
            turned_k = transposed(k).astype(bf16)
            same = jnp.concatenate([segc[cols, :]] * (chunk // 128), axis=1) == docs
            ps, ds = [], []
            for h in range(2):
                s = jnp.where(same, mm(k, qh[h], 1, 1), masked_score)
                pr = jnp.exp(s - lse[c, 2 * p + h])
                d = (pr * (mm(v, gh[h], 1, 1) - delta[h])).astype(bf16)
                ps.append(pr.astype(bf16))
                ds.append(d)
                dq[h] = dq[h] + mm(turned_k[h * HEAD : (h + 1) * HEAD, :], d, 1, 0)
            add_v = mm(jnp.concatenate(ps, axis=1), g_two, 1, 0)
            add_k = mm(jnp.concatenate(ds, axis=1), q_two, 1, 0)
            if c < chunks - 1:
                dv[cols, lanes] = add_v if c == 0 else dv[cols, lanes] + add_v
                dk[cols, lanes] = add_k if c == 0 else dk[cols, lanes] + add_k
            else:
                d_qkv[1, cols, lanes] = turn_back(dk[cols, lanes] + add_k, cols)
                d_qkv[2, cols, lanes] = (dv[cols, lanes] + add_v).astype(bf16)
        d_qkv[0, rows, lanes] = turn_back(jnp.concatenate(dq, axis=0).T * (HEAD**-0.5), rows)

    for copy in main:
        copy.wait()
    now = 11
    for c in each:
        until(now)
        projs[c].wait()
        if c == chunks - 1:
            for copy in branches:
                copy.start()
        mix_grad[c * chunk : (c + 1) * chunk, :] = mm(proj[c], w_out[...], 1, 1).astype(bf16)
        now += 1
        if c == chunks - 1:
            until(now)

            @pl.loop(0, width // 256)
            def _(r):
                at = pl.ds(pl.multiple_of(r * 256, 256), 256)
                part_e[at, :] = sum(
                    mm(mixed[n * chunk : (n + 1) * chunk, at], proj[n], 0, 0) for n in each
                ).astype(bf16)

            units[5].step(0)
            now += 1

        @pl.loop(0, pairs)
        def _(p):
            for n in range(pairs):

                @pl.when(p == n)
                def _():
                    until(now + n)

            attend_back(p, c)

        now += pairs

    def rows_back(start):
        at = slice(start, start + half)
        return sum(mm(d_qkv[t, at, :], w_qkv[t], 1, 1) for t in range(3))

    for i in range(3):
        until(now + i)

        @pl.loop(0, depth // 256)
        def _(r):
            at = pl.ds(pl.multiple_of(r * 256, 256), 256)
            qkv[2 - i, at, :] = mm(rows_one[:, at], d_qkv[2 - i], 0, 0).astype(bf16)

        units[6 + i].step(0)
    now += 3
    weights.wait()
    for c in each:
        until(now + c)
        proj[c, :half] = rows_back(c * chunk + half).astype(bf16)
        if c == 0:
            ones[c].start()
    now += chunks
    for c in each:
        until(now + c)
        branches[c].wait()
        owns[c].wait()

        @pl.loop(0, half // STEP_ROWS)
        def _(i):
            at = pl.ds(pl.multiple_of(i * STEP_ROWS, STEP_ROWS), STEP_ROWS)
            branch = projected[c, at, :] + branch_got[c, at, :].astype(f32) + b_down
            branch_got[c, at, :] = (middle[c, at, :] + gate_m * branch).astype(bf16)
            fold(5, cot[c, at, :].astype(f32) * branch)

        outputs[c].start()
    now += chunks
    for c in each:
        until(now + c)
        projected[c] = rows_back(c * chunk)
    now += chunks
    for c in each:
        until(now + c)
        ones[c].wait()
        if c < chunks - 1:
            ones[c + 1].start()

        @pl.loop(0, half // STEP_ROWS)
        def _(i):
            at = pl.ds(pl.multiple_of(i * STEP_ROWS, STEP_ROWS), STEP_ROWS)
            grad = projected[c, at, :] + from_x[c, at, :].astype(f32)
            back, normal = norm_back(grad, tokens[c, at, :].astype(f32), gain_one * (1.0 + scale_a))
            grad_x[c, at, :] = (back + grads[c, at, :]).astype(bf16)
            fold(3, grad)
            fold(4, grad * normal)

    now += chunks
    shift, scaled, gated, shift_one, scaled_one, gated_m = [col_sums[r : r + 1, :] for r in range(6)]
    small[...] = known[...] + jnp.concatenate(
        [
            shift_one, gain_one * scaled_one, gated, shift, gain_two * scaled, gated_m,
            (1.0 + scale_a) * scaled_one, (1.0 + scale_m) * scaled, jnp.zeros((8, depth), f32),
        ],
        axis=0,
    )
    smalls.start()
    until(now)
    smalls.wait()
    number = lax.broadcasted_iota(jnp.int32, small.shape, 0)
    everyone[0] = small[...] + jnp.where(number < 9, small_got[...], 0.0)
    for n, b in enumerate((1, 3, 2, 0)):
        copy = pltpu.make_async_remote_copy(
            src_ref=everyone.at[pl.ds(0, 1 << n)], dst_ref=everyone.at[pl.ds(1 << n, 1 << n)],
            send_sem=all_send.at[n], recv_sem=all_recv.at[n],
            device_id={"dp": partner[b]}, device_id_type=MESH,
        )
        copy.start()
        until(now + 1 + n)
        copy.wait()
    mine[...] = everyone[0]
    total[...] = sum(everyone[n] for n in range(1 << EDGES))
    conds = jnp.concatenate([everyone[n, 11:12, : ada.shape[0]] for n in range(1 << EDGES)], axis=0)
    spans = []
    for j in range(ada.shape[1] // width):
        vector, side = divmod(j * width, depth)
        mods = jnp.concatenate([everyone[n, vector : vector + 1, side : side + width] for n in range(1 << EDGES)], axis=0)
        rows = slice(j // 2 * ada.shape[0], (j // 2 + 1) * ada.shape[0])
        spot = (dk, dv)[j % 2].at[rows]
        spot[...] = lax.dot_general(
            conds, mods, (((0,), (0,)), ((), ())), precision=lax.Precision.HIGHEST, preferred_element_type=f32
        )
        spans.append(pltpu.make_async_copy(spot, ada.at[:, j * width : (j + 1) * width], store.at[chunks + j]))
        spans[-1].start()
    until(1000)
    for copy in (*outputs, *spans):
        copy.wait()


def tail(*args, ada_shape):
    hidden, qkv, rows_one, w_qkv, w_out, own_grad, tokens = (args[n] for n in (0, 4, 6, 7, 8, 9, 15))
    known = args[21]
    _, length, width = qkv.shape
    chunks, half, depth = own_grad.shape
    anywhere, near = pl.BlockSpec(memory_space=pl.ANY), pl.BlockSpec(memory_space=pltpu.VMEM)
    shaped, kept = jax.ShapeDtypeStruct, pltpu.VMEM
    in_chunks = (chunks, half, depth)
    scratch = [
        kept(qkv.shape, bf16), kept((length, width), bf16), kept(rows_one.shape, bf16), kept(w_qkv.shape, bf16),
        kept(w_out.shape, bf16), kept((chunks, 2 * half, depth), bf16), kept((length, width), bf16),
        kept((3, length, width), bf16), kept((length, width), f32), kept((length, width), f32),
        kept(in_chunks, bf16), kept(in_chunks, f32), kept(in_chunks, f32), kept(in_chunks, f32),
        kept(in_chunks, bf16), kept(in_chunks, bf16),
        *[kept((depth, depth), bf16)] * 4, kept((width, depth), bf16), kept(in_chunks, bf16),
        kept((8, depth), f32), kept(known.shape, f32), kept(known.shape, f32), kept((1 << EDGES, *known.shape), f32),
        pltpu.SemaphoreType.DMA((30,)), pltpu.SemaphoreType.DMA((chunks + ada_shape[1] // width,)),
        pltpu.SemaphoreType.DMA((4 * chunks + 1,)), pltpu.SemaphoreType.DMA((4 * chunks + 1,)),
        pltpu.SemaphoreType.DMA((EDGES,)), pltpu.SemaphoreType.DMA((EDGES,)),
        *unit_scratch(WIDE, depth) * 2, *unit_scratch(depth, depth) * 3, *unit_scratch(width, depth), *unit_scratch(depth, width) * 3,
    ]
    return pl.pallas_call(
        tail_kernel,
        in_specs=[anywhere] * 17 + [near] * 10,
        out_specs=[anywhere] * 8 + [near] * 3,
        out_shape=[
            shaped((hidden.shape[1], depth), bf16), shaped((depth, hidden.shape[1]), bf16), shaped((width, depth), bf16),
            *[shaped((depth, width), bf16)] * 3, shaped(tokens.shape, bf16),
            shaped(ada_shape, f32), shaped(in_chunks, bf16), shaped(known.shape, f32), shaped(known.shape, f32),
        ],
        scratch_shapes=scratch,
        compiler_params=pltpu.CompilerParams(collective_id=1, has_side_effects=True, vmem_limit_bytes=61 << 20),
        name="tail",
    )(*args)


def body_pair(
    tokens, cond, doc_lengths, w_ada, b_ada, gain_one, w_qkv, w_out, gain_two, w_up, b_up, w_down, b_down, cotangent
):
    own, width = tokens.shape
    length = 2 * own
    chunks = 2
    half, chunk = own // chunks, length // chunks
    me = lax.axis_index("tensor")

    step = jnp.arange(length, dtype=jnp.int32)
    in_chunk = step % chunk
    places = jnp.where(in_chunk < half, me, 1 - me) * own + (step // chunk) * half + in_chunk % half
    segment, doc_first = documents(doc_lengths[0], places)
    cosine, sine = rope_tables(places - doc_first)
    seg_rows = segment[None, :]
    seg_cols = jnp.broadcast_to(segment[:, None], (length, 128))

    modulation = jnp.dot(cond, w_ada, preferred_element_type=f32)[0] + b_ada
    sequence = jnp.pad(cond.astype(f32), ((0, 0), (0, width - cond.shape[1])))
    mods = modulation.reshape(6, width)
    (
        qkv, mixed, rows_one, full_back, rows_two, hidden, grad_pre, own_grad, send_grad, middle, projected,
        own_branch, send_branch, lse, known,
    ) = head(
        tokens, cotangent, w_qkv, w_out, w_up, w_down, mods, gain_one[None, :], gain_two[None, :], sequence,
        b_up[None, :], seg_rows, seg_cols, cosine, sine, chunks=chunks,
    )
    *sums, output, grad_w_ada, grad_x, mine, total = tail(
        hidden, full_back, rows_two, grad_pre, qkv, mixed, rows_one, w_qkv, w_out, own_grad, send_grad,
        middle, projected, own_branch, send_branch, tokens, cotangent,
        mods, gain_one[None, :], gain_two[None, :], b_down[None, :], known,
        lse, seg_rows, seg_cols, cosine, sine, ada_shape=w_ada.shape,
    )
    grad_w_down, grad_w_up, grad_w_out, grad_q, grad_k, grad_v = [s.astype(f32) for s in sums]
    grad_w_qkv = jnp.stack([grad_q, grad_k, grad_v])
    grad_x = grad_x.reshape(own, width)
    grad_cond = jnp.dot(w_ada.astype(f32), mine[:6].reshape(-1), precision=lax.Precision.HIGHEST)[None, :]
    grad_b_ada = total[:6].reshape(-1)
    grad_gain_one, grad_gain_two, grad_b_down = total[6], total[7], total[8]
    grad_b_up = total[9:11].reshape(-1)
    return (
        output, grad_x, grad_cond, grad_w_ada, grad_b_ada, grad_gain_one, grad_w_qkv, grad_w_out, grad_gain_two,
        grad_w_up, grad_b_up, grad_w_down, grad_b_down,
    )


def body_any(
    tokens, cond, doc_lengths, w_ada, b_ada, gain_one, w_qkv, w_out, gain_two, w_up, b_up, w_down, b_down, cotangent
):
    tensor_size = lax.axis_size("tensor")
    own = tokens.shape[0]
    length = own * tensor_size

    def all_rows(values):
        return lax.all_gather(values, "tensor", axis=0, tiled=True)

    def own_sum(values):
        return lax.psum_scatter(values, "tensor", scatter_dimension=0, tiled=True)

    def sum_over_dp(part):
        return lax.psum(part, "dp")

    places = jnp.arange(length, dtype=jnp.int32)
    segment, doc_first = documents(doc_lengths[0], places)
    cosine, sine = rope_tables(places - doc_first)
    blocks = length // BLOCK
    in_blocks = segment.reshape(blocks, BLOCK)
    least, most = jnp.min(in_blocks, axis=1), jnp.max(in_blocks, axis=1)
    meets = (least[:, None] <= most[None, :]) & (least[None, :] <= most[:, None])
    flags = meets.astype(jnp.int32).reshape(-1)
    seg_rows = in_blocks[:, None, :]
    seg_cols = jnp.broadcast_to(segment[:, None], (length, 128))

    modulation = jnp.dot(cond, w_ada, preferred_element_type=f32)[0] + b_ada
    shift_a, scale_a, gate_a, shift_m, scale_m, gate_m = jnp.split(modulation, 6)
    x_rows = tokens.astype(f32)
    grad_out = cotangent.astype(f32)

    act_one = modulate(x_rows, gain_one, shift_a, scale_a).astype(bf16)
    rows_one = all_rows(act_one)
    grad_branch = (grad_out * gate_m).astype(bf16)
    full_branch = all_rows(grad_branch)
    qkv = project_qkv(rows_one, w_qkv, cosine, sine)
    mixed, lse = attend_forward(flags, qkv, seg_rows, seg_cols)
    projected = own_sum(jnp.dot(mixed, w_out, preferred_element_type=f32))
    middle = x_rows + gate_a * projected
    rows_two = all_rows(modulate(middle, gain_two, shift_m, scale_m).astype(bf16))
    pre_act = jnp.dot(rows_two, w_up, preferred_element_type=f32) + b_up
    hidden = jax.nn.gelu(pre_act, approximate=True).astype(bf16)

    grad_hidden = jnp.einsum("sd,fd->sf", full_branch, w_down, preferred_element_type=f32)
    _, gelu_back = jax.vjp(lambda values: jax.nn.gelu(values, approximate=True), pre_act)
    grad_pre = gelu_back(grad_hidden)[0].astype(bf16)
    grad_act_two = own_sum(jnp.einsum("sf,df->sd", grad_pre, w_up, preferred_element_type=f32))
    grad_w_down = sum_over_dp(jnp.einsum("sf,sd->fd", hidden, full_branch, preferred_element_type=f32))
    grad_w_up = sum_over_dp(jnp.einsum("sd,sf->df", rows_two, grad_pre, preferred_element_type=f32))

    branch = own_sum(jnp.dot(hidden, w_down, preferred_element_type=f32)) + b_down
    output = (middle + gate_m * branch).astype(bf16)
    grad_gate_m = jnp.sum(grad_out * branch, axis=0)
    grad_b_down = jnp.sum(grad_branch.astype(f32), axis=0)
    grad_b_up = jnp.sum(grad_pre.astype(f32), axis=0)

    _, second_back = jax.vjp(modulate, middle, gain_two, shift_m, scale_m)
    grad_middle, grad_gain_two, grad_shift_m, grad_scale_m = second_back(grad_act_two)
    grad_middle = grad_middle + grad_out
    full_proj = all_rows((grad_middle * gate_a).astype(bf16))
    grad_gate_a = jnp.sum(grad_middle * projected, axis=0)
    grad_mixed = jnp.einsum("sd,ed->se", full_proj, w_out, preferred_element_type=f32).astype(bf16)
    grad_w_out = sum_over_dp(jnp.einsum("se,sd->ed", mixed, full_proj, preferred_element_type=f32))
    grad_qkv = attend_backward(flags, qkv, grad_mixed, mixed, lse, seg_rows, seg_cols, cosine, sine)
    grad_act_one = own_sum(jnp.einsum("tse,tde->sd", grad_qkv, w_qkv, preferred_element_type=f32))
    grad_w_qkv = jnp.einsum("sd,tse->tde", rows_one, grad_qkv, preferred_element_type=f32)
    grad_w_qkv = sum_over_dp(grad_w_qkv.reshape(-1, grad_w_qkv.shape[2])).reshape(grad_w_qkv.shape)

    _, first_back = jax.vjp(modulate, x_rows, gain_one, shift_a, scale_a)
    grad_x, grad_gain_one, grad_shift_a, grad_scale_a = first_back(grad_act_one)
    grad_x = (grad_x + grad_middle).astype(bf16)

    small = jnp.concatenate(
        [
            grad_shift_a, grad_scale_a, grad_gate_a, grad_shift_m, grad_scale_m, grad_gate_m,
            grad_gain_one, grad_gain_two, grad_b_down,
        ]
    )
    small = lax.psum(small, "tensor")
    mod_size = modulation.shape[0]
    grad_mod = small[:mod_size]
    grad_cond = jnp.dot(w_ada.astype(f32), grad_mod, precision=lax.Precision.HIGHEST)[None, :]
    everyone = lax.all_gather(
        jnp.concatenate([small, grad_b_up, cond[0].astype(f32)])[None, :], "dp", axis=0, tiled=True
    )
    conds = everyone[:, -cond.shape[1] :]
    mods = everyone[:, :mod_size]
    grad_w_ada = jnp.einsum("nc,nm->cm", conds, mods, precision=lax.Precision.HIGHEST, preferred_element_type=f32)
    sums = jnp.sum(everyone, axis=0)
    width = tokens.shape[1]
    grad_b_ada = sums[:mod_size]
    grad_gain_one, grad_gain_two, grad_b_down = jnp.split(sums[mod_size : mod_size + 3 * width], 3)
    grad_b_up = sums[mod_size + 3 * width : -cond.shape[1]]
    return (
        output, grad_x, grad_cond, grad_w_ada, grad_b_ada, grad_gain_one, grad_w_qkv, grad_w_out, grad_gain_two,
        grad_w_up, grad_b_up, grad_w_down, grad_b_down,
    )


def solution(mesh):
    swaps = mesh.shape["tensor"] == 2 and mesh.shape["dp"] == 16
    placed = (
        P(("dp", "tensor"), None), P("dp", None), P("dp", None), P(), P(), P(), P(None, None, "tensor"),
        P("tensor", None), P(), P(None, "tensor"), P("tensor"), P("tensor", None), P(), P(("dp", "tensor"), None),
    )
    return jax.shard_map(
        body_pair if swaps else body_any,
        mesh=mesh,
        in_specs=placed,
        out_specs=(
            P(("dp", "tensor"), None), P(("dp", "tensor"), None), P("dp", None), P(), P(), P(),
            P(None, None, "tensor"), P("tensor", None), P(), P(None, "tensor"), P("tensor"), P("tensor", None), P(),
        ),
        check_vma=False,
    )
```

```python
import functools

import jax
import jax.numpy as jnp
from jax import lax
from jax.experimental import pallas as pl
from jax.experimental.pallas import tpu as pltpu
from jax.sharding import PartitionSpec as P

HEAD = 64
PAIR = 2 * HEAD
BLOCK = 256
ROWS = 512

norm_eps = 1e-05
rope_base = 10000.0
masked_score = -1e30
f32, bf16 = jnp.float32, jnp.bfloat16


def layer_norm(values, gain):
    center = values - jnp.mean(values, axis=-1, keepdims=True)
    spread = jnp.mean(center * center, axis=-1, keepdims=True)
    return center * lax.rsqrt(spread + norm_eps) * gain


def modulate(values, gain, shift, scale):
    return layer_norm(values, gain) * (1.0 + scale) + shift


def documents(lengths, places):
    numbers = jnp.arange(lengths.shape[0], dtype=jnp.int32)
    earlier = (numbers[None, :] < numbers[:, None]).astype(jnp.int32)
    starts = jnp.sum(earlier * lengths[None, :], axis=1)
    ends = starts + lengths
    inside = ((places[:, None] >= starts[None, :]) & (places[:, None] < ends[None, :])).astype(
        jnp.int32
    )
    segment = jnp.sum(inside * numbers[None, :], axis=1)
    doc_first = jnp.sum(inside * starts[None, :], axis=1)
    return segment, doc_first


def rope_tables(offsets):
    exponent = jnp.arange(HEAD // 2, dtype=f32) * (2.0 / HEAD)
    frequency = jnp.power(jnp.float32(rope_base), -exponent)
    angles = offsets.astype(f32)[:, None] * frequency[None, :]
    cosine, sine = jnp.cos(angles), jnp.sin(angles)
    repeat = PAIR // (HEAD // 2)
    return jnp.concatenate([cosine] * repeat, axis=-1), jnp.concatenate([sine] * repeat, axis=-1)


def turned(values):
    lane = lax.broadcasted_iota(jnp.int32, values.shape, 1)
    half = HEAD // 2
    from_right = pltpu.roll(values, PAIR - half, axis=1)
    from_left = pltpu.roll(values, half, axis=1)
    return jnp.where(lane % HEAD < half, -from_right, from_left)


def mm(a, b, da, db):
    return lax.dot_general(a, b, (((da,), (db,)), ((), ())), preferred_element_type=f32)


def qkv_kernel(x_ref, w_ref, cos_ref, sin_ref, o_ref):
    which = pl.program_id(1)
    y = mm(x_ref[...], w_ref[...], 1, 0)

    @pl.when(which < 2)
    def _():
        factor = jnp.where(which == 0, HEAD**-0.5, 1.0)
        for p in range(y.shape[1] // PAIR):
            u = y[:, p * PAIR : (p + 1) * PAIR]
            r = u * cos_ref[...] + turned(u) * sin_ref[...]
            o_ref[:, p * PAIR : (p + 1) * PAIR] = (r.astype(bf16) * factor.astype(bf16)).astype(bf16)

    @pl.when(which == 2)
    def _():
        o_ref[...] = y.astype(bf16)


def project_qkv(rows, w_qkv, cosine, sine):
    count, depth = rows.shape
    width = w_qkv.shape[2]
    return pl.pallas_call(
        qkv_kernel,
        grid=(count // ROWS, 3),
        in_specs=[
            pl.BlockSpec((ROWS, depth), lambda r, t: (r, 0)),
            pl.BlockSpec((None, depth, width), lambda r, t: (t, 0, 0)),
            pl.BlockSpec((ROWS, PAIR), lambda r, t: (r, 0)),
            pl.BlockSpec((ROWS, PAIR), lambda r, t: (r, 0)),
        ],
        out_specs=pl.BlockSpec((None, ROWS, width), lambda r, t: (t, r, 0)),
        out_shape=jax.ShapeDtypeStruct((3, count, width), bf16),
        compiler_params=pltpu.CompilerParams(vmem_limit_bytes=32 << 20),
        cost_estimate=pl.CostEstimate(
            flops=6 * count * depth * width, bytes_accessed=8 * count * width, transcendentals=0
        ),
        name="qkv",
    )(rows, w_qkv, cosine, sine)


def head_lanes(block, h):
    lane = lax.broadcasted_iota(jnp.int32, block.shape, 1)
    return jnp.where(lane // HEAD == h, block, jnp.zeros_like(block))


def transposed(block):
    return block.astype(f32).T


def forward_kernel(flag_ref, q_ref, k_ref, v_ref, segr_ref, segc_ref, o_ref, lse_ref, vt, m, l, acc):
    blocks = q_ref.shape[0] // BLOCK
    for b in range(blocks):
        vt[b] = transposed(v_ref[b * BLOCK : (b + 1) * BLOCK, :]).astype(bf16)

    @pl.loop(0, blocks)
    def _(qi):
        rows = pl.ds(pl.multiple_of(qi * BLOCK, BLOCK), BLOCK)
        q = q_ref[rows, :]
        m[...] = jnp.full(m.shape, masked_score, f32)
        l[...] = jnp.zeros(l.shape, f32)
        acc[...] = jnp.zeros(acc.shape, f32)

        @pl.loop(0, blocks)
        def _(ki):
            @pl.when(flag_ref[qi * blocks + ki] > 0)
            def _():
                cols = pl.ds(pl.multiple_of(ki * BLOCK, BLOCK), BLOCK)
                k = k_ref[cols, :]
                docs = segc_ref[cols, :]
                same = jnp.concatenate([docs] * (BLOCK // 128), axis=1) == segr_ref[qi]
                for h in range(2):
                    lo, hi = h * HEAD, (h + 1) * HEAD
                    s = jnp.where(same, mm(k, head_lanes(q, h), 1, 1), masked_score)
                    top = jnp.maximum(m[h], jnp.max(s, axis=0, keepdims=True))
                    p = jnp.exp(s - top)
                    shrink = jnp.exp(m[h] - top)
                    m[h] = top
                    l[h] = l[h] * shrink + jnp.sum(p, axis=0, keepdims=True)
                    acc[lo:hi, :] = acc[lo:hi, :] * shrink + mm(vt[ki, lo:hi, :], p.astype(bf16), 1, 0)

        for h in range(2):
            lo, hi = h * HEAD, (h + 1) * HEAD
            lse_ref[h, qi] = m[h] + jnp.log(l[h])
            acc[lo:hi, :] = acc[lo:hi, :] / l[h]
        o_ref[rows, :] = acc[...].T.astype(bf16)


def backward_kernel(
    flag_ref, q_ref, k_ref, v_ref, g_ref, o_ref, lse_ref, segr_ref, segc_ref, cos_ref, sin_ref,
    out_ref, kt, dk, dv, dq,
):
    blocks = q_ref.shape[0] // BLOCK
    for b in range(blocks):
        kt[b] = transposed(k_ref[b * BLOCK : (b + 1) * BLOCK, :]).astype(bf16)
    dk[...] = jnp.zeros(dk.shape, f32)
    dv[...] = jnp.zeros(dv.shape, f32)

    def turn_back(u, rows):
        return (u * cos_ref[rows, :] - turned(u) * sin_ref[rows, :]).astype(bf16)

    @pl.loop(0, blocks)
    def _(qi):
        rows = pl.ds(pl.multiple_of(qi * BLOCK, BLOCK), BLOCK)
        q, g = q_ref[rows, :], g_ref[rows, :]
        both = (g.astype(f32) * o_ref[rows, :].astype(f32)).T
        dq[...] = jnp.zeros(dq.shape, f32)

        @pl.loop(0, blocks)
        def _(ki):
            @pl.when(flag_ref[qi * blocks + ki] > 0)
            def _():
                cols = pl.ds(pl.multiple_of(ki * BLOCK, BLOCK), BLOCK)
                k, v = k_ref[cols, :], v_ref[cols, :]
                docs = segc_ref[cols, :]
                same = jnp.concatenate([docs] * (BLOCK // 128), axis=1) == segr_ref[qi]
                dk_sum, dv_sum = dk[cols, :], dv[cols, :]
                for h in range(2):
                    lo, hi = h * HEAD, (h + 1) * HEAD
                    delta = jnp.sum(both[lo:hi, :], axis=0, keepdims=True)
                    qh, gh = head_lanes(q, h), head_lanes(g, h)
                    s = jnp.where(same, mm(k, qh, 1, 1), masked_score)
                    p = jnp.exp(s - lse_ref[h, qi])
                    ds = (p * (mm(v, gh, 1, 1) - delta)).astype(bf16)
                    dv_sum = dv_sum + mm(p.astype(bf16), gh, 1, 0)
                    dk_sum = dk_sum + mm(ds, qh, 1, 0)
                    dq[lo:hi, :] = dq[lo:hi, :] + mm(kt[ki, lo:hi, :], ds, 1, 0)
                dk[cols, :] = dk_sum
                dv[cols, :] = dv_sum

        out_ref[0, rows, :] = turn_back(dq[...].T * (HEAD**-0.5), rows)

    @pl.loop(0, blocks)
    def _(b):
        rows = pl.ds(pl.multiple_of(b * BLOCK, BLOCK), BLOCK)
        out_ref[1, rows, :] = turn_back(dk[rows, :], rows)
        out_ref[2, rows, :] = dv[rows, :].astype(bf16)


def pieces_of(qkv, length):
    return [pl.BlockSpec((None, length, PAIR), functools.partial(lambda t, p, *_: (t, 0, p), t)) for t in range(3)]


def attend_forward(flags, qkv, seg_rows, seg_cols):
    _, length, width = qkv.shape
    blocks, pairs = length // BLOCK, width // PAIR
    return pl.pallas_call(
        forward_kernel,
        grid_spec=pltpu.PrefetchScalarGridSpec(
            num_scalar_prefetch=1,
            grid=(pairs,),
            in_specs=[
                *pieces_of(qkv, length),
                pl.BlockSpec((blocks, 1, BLOCK), lambda p, *_: (0, 0, 0)),
                pl.BlockSpec((length, 128), lambda p, *_: (0, 0)),
            ],
            out_specs=[
                pl.BlockSpec((length, PAIR), lambda p, *_: (0, p)),
                pl.BlockSpec((2, blocks, 1, BLOCK), lambda p, *_: (p, 0, 0, 0)),
            ],
            scratch_shapes=[
                pltpu.VMEM((blocks, PAIR, BLOCK), bf16),
                pltpu.VMEM((2, 1, BLOCK), f32),
                pltpu.VMEM((2, 1, BLOCK), f32),
                pltpu.VMEM((PAIR, BLOCK), f32),
            ],
        ),
        out_shape=[
            jax.ShapeDtypeStruct((length, width), bf16),
            jax.ShapeDtypeStruct((2 * pairs, blocks, 1, BLOCK), f32),
        ],
        compiler_params=pltpu.CompilerParams(vmem_limit_bytes=48 << 20),
        cost_estimate=pl.CostEstimate(
            flops=4 * length * length * width, bytes_accessed=8 * length * width, transcendentals=length * length * width // HEAD
        ),
        name="attend",
    )(flags, qkv, qkv, qkv, seg_rows, seg_cols)


def attend_backward(flags, qkv, grad, mixed, lse, seg_rows, seg_cols, cosine, sine):
    _, length, width = qkv.shape
    blocks, pairs = length // BLOCK, width // PAIR
    whole = pl.BlockSpec((length, PAIR), lambda p, *_: (0, p))
    table = pl.BlockSpec((length, PAIR), lambda p, *_: (0, 0))
    return pl.pallas_call(
        backward_kernel,
        grid_spec=pltpu.PrefetchScalarGridSpec(
            num_scalar_prefetch=1,
            grid=(pairs,),
            in_specs=[
                *pieces_of(qkv, length),
                whole,
                whole,
                pl.BlockSpec((2, blocks, 1, BLOCK), lambda p, *_: (p, 0, 0, 0)),
                pl.BlockSpec((blocks, 1, BLOCK), lambda p, *_: (0, 0, 0)),
                table,
                table,
                table,
            ],
            out_specs=pl.BlockSpec((3, length, PAIR), lambda p, *_: (0, 0, p)),
            scratch_shapes=[
                pltpu.VMEM((blocks, PAIR, BLOCK), bf16),
                pltpu.VMEM((length, PAIR), f32),
                pltpu.VMEM((length, PAIR), f32),
                pltpu.VMEM((PAIR, BLOCK), f32),
            ],
        ),
        out_shape=jax.ShapeDtypeStruct((3, length, width), bf16),
        compiler_params=pltpu.CompilerParams(vmem_limit_bytes=56 << 20),
        cost_estimate=pl.CostEstimate(
            flops=10 * length * length * width, bytes_accessed=16 * length * width, transcendentals=length * length * width // HEAD
        ),
        name="attend_back",
    )(flags, qkv, qkv, qkv, grad, mixed, lse, seg_rows, seg_cols, cosine, sine)


MESH = pl.DeviceIdType.MESH
ADD_ROWS = 32
STEPS = 9
EDGES = 4


def add_low(a, a_at, b, rows):
    @pl.loop(0, rows // ADD_ROWS)
    def _(i):
        at = pl.ds(pl.multiple_of(i * ADD_ROWS, ADD_ROWS), ADD_ROWS)
        kept = a[pl.ds(pl.multiple_of(a_at + i * ADD_ROWS, ADD_ROWS), ADD_ROWS), :].astype(f32)
        b[at, :] = (kept + b[at, :].astype(f32)).astype(bf16)


class Unit:
    def __init__(self, part, out, column, got, send, recv, local, place, bits=(0, 1, 2, 3)):
        self.part, self.out, self.got = part, out, got
        self.send, self.recv, self.local = send, recv, local
        self.rows, columns = 2 * got[0].shape[0], got[0].shape[1]
        self.columns = pl.ds(column, columns)
        self.bit = [(place // (1 << b)) % 2 for b in bits]
        self.partner = [place + (1 - 2 * bit) * (1 << b) for bit, b in zip(self.bit, bits, strict=True)]
        self.base = [0]
        for b in range(EDGES):
            self.base.append(self.base[-1] + self.bit[b] * (self.rows >> (b + 1)))

    def remote(self, src, dst, stage, b):
        return pltpu.make_async_remote_copy(
            src_ref=src,
            dst_ref=dst,
            send_sem=self.send.at[stage],
            recv_sem=self.recv.at[stage],
            device_id={"dp": self.partner[b]},
            device_id_type=MESH,
        )

    def halving(self, b):
        half = self.rows >> (b + 1)
        source = self.part if b == 0 else self.got[b - 1]
        away = pl.ds(pl.multiple_of((1 - self.bit[b]) * half, ADD_ROWS), half)
        return self.remote(source.at[away], self.got[b], b, b)

    def spot(self, b):
        size = self.rows >> (b + 1)
        return self.out.at[pl.ds(pl.multiple_of(self.base[b + 1], ADD_ROWS), size), self.columns]

    def own(self):
        return pltpu.make_async_copy(self.got[3], self.spot(3), self.local.at[0])

    def gathering(self, b):
        return self.remote(self.got[3] if b == 3 else self.spot(b), self.spot(b), 7 - b, b)

    def step(self, k):
        if k == 0:
            self.halving(0).start()
        elif k < 5:
            b = k - 1
            self.halving(b).wait()
            half = self.rows >> (b + 1)
            add_low(self.part if b == 0 else self.got[b - 1], self.bit[b] * half, self.got[b], half)
            if b < 3:
                self.halving(b + 1).start()
            else:
                self.own().start()
                self.gathering(3).start()
        elif k == 5:
            self.own().wait()
            self.gathering(3).wait()
            self.gathering(2).start()
        elif k < 8:
            self.gathering(8 - k).wait()
            self.gathering(7 - k).start()
        else:
            self.gathering(0).wait()


def unit_scratch(rows, columns):
    return [
        *[pltpu.VMEM((rows >> (b + 1), columns), bf16) for b in range(EDGES)],
        pltpu.SemaphoreType.DMA((2 * EDGES,)),
        pltpu.SemaphoreType.DMA((2 * EDGES,)),
        pltpu.SemaphoreType.DMA((1,)),
    ]


def greet(targets):
    barrier = pltpu.get_barrier_semaphore()
    for target in targets:
        pl.semaphore_signal(barrier, inc=1, device_id=target, device_id_type=MESH)
    pl.semaphore_wait(barrier, len(targets))


ORDER = (
    (3, 0, 1), (6, 1, 1), (7, 0, 2), (8, 2, 1), (8, 0, 3), (8, 1, 2), (9, 1, 3), (10, 0, 4), (10, 3, 1), (10, 1, 4),
    (10, 2, 2), (10, 4, 1), (11, 0, 5), (13, 1, 5), (13, 2, 3), (15, 2, 4), (15, 0, 6), (15, 3, 2), (15, 1, 6),
    (18, 2, 5), (19, 5, 1), (19, 3, 3), (20, 4, 2), (20, 2, 6), (21, 3, 4), (22, 4, 3), (23, 5, 2), (24, 6, 1),
    (24, 3, 5), (26, 7, 1), (26, 2, 7), (26, 4, 4), (28, 6, 2), (28, 8, 1), (28, 1, 7), (29, 5, 3), (29, 2, 8),
    (29, 4, 5), (29, 3, 6), (29, 6, 3), (29, 0, 7), (29, 1, 8), (30, 7, 2), (32, 5, 4), (32, 8, 2), (32, 4, 6),
    (32, 7, 3), (32, 5, 5), (32, 6, 4), (32, 7, 4), (33, 8, 3), (33, 3, 7), (33, 5, 6), (33, 6, 5), (34, 4, 7),
    (34, 7, 5), (34, 0, 8), (34, 8, 4), (35, 4, 8), (35, 6, 6), (35, 8, 5), (35, 7, 6), (36, 8, 6), (36, 6, 7),
    (36, 5, 7), (37, 8, 7), (38, 7, 7), (99, 6, 8), (99, 5, 8), (99, 7, 8), (99, 3, 8), (99, 8, 8),
)
WIDE = 512
STEP_ROWS = 64


def vectors_of(product, bias, depth):
    return [product[:, r * depth : (r + 1) * depth] + bias[:, r * depth : (r + 1) * depth] for r in range(6)]


def fetcher(sems):
    count = [0]

    def fetch(src, dst):
        copy = pltpu.make_async_copy(src, dst, sems.at[count[0]])
        copy.start()
        count[0] += 1
        return copy

    return fetch


def head_kernel(
    tokens_hbm, cot_hbm, w_qkv_hbm, w_out_hbm, w_up_hbm, w_down_hbm,
    mods, b_ada, gain_one, gain_two, cond, b_up, frequency, lengths,
    qkv_out, mixed_out, one_out, back_out, two_out, hidden_out, pre_out, own_grad, send_grad, middle_out,
    projected_out, own_branch, send_branch, lse, known, segr, segc, cosine, sine,
    tokens, cot, w_qkv, w_out, w_up, w_down, rows_one, full_back, rows_two, qkv, mixed, from_sum, send_sum, projected,
    middle, hidden, pre, grads, branch, low_grads, low_branch, bias, bias_down, load, x_send, x_recv,
):
    me = lax.axis_index("tensor")
    length, depth = rows_one.shape
    chunks, half, _ = from_sum.shape
    chunk = 2 * half
    width = mixed.shape[1]
    pairs = width // PAIR
    across = {"tensor": 1 - me}
    each = range(chunks)
    own = [slice(c * chunk, c * chunk + half) for c in each]
    got = [slice(c * chunk + half, (c + 1) * chunk) for c in each]
    whole = [slice(c * chunk, (c + 1) * chunk) for c in each]
    fetch = fetcher(load)

    def x_copy(src, dst, i):
        return pltpu.make_async_remote_copy(
            src_ref=src, dst_ref=dst, send_sem=x_send.at[i], recv_sem=x_recv.at[i],
            device_id=across, device_id_type=MESH,
        )

    ones = [x_copy(rows_one.at[own[c]], rows_one.at[got[c]], c) for c in each]
    backs = [x_copy(full_back.at[own[c]], full_back.at[got[c]], chunks + c) for c in each]
    shares = [x_copy(send_sum.at[c], from_sum.at[c], 2 * chunks + c) for c in each]
    twos = [x_copy(rows_two.at[own[c]], rows_two.at[got[c]], 3 * chunks + c) for c in each]

    shift_a, scale_a, gate_a, shift_m, scale_m, gate_m = vectors_of(mods, b_ada, depth)
    gain_one, gain_two = gain_one[...], gain_two[...]
    reads = [fetch(tokens_hbm, tokens), fetch(w_qkv_hbm, w_qkv), fetch(cot_hbm, cot)]
    reads += [fetch(w_out_hbm, w_out), fetch(w_up_hbm, w_up), fetch(w_down_hbm, w_down)]
    writes = []
    greet([across])

    def normal_of(values):
        center = values - jnp.mean(values, axis=1, keepdims=True)
        return center * lax.rsqrt(jnp.mean(center * center, axis=1, keepdims=True) + norm_eps)

    def by_rows(work):
        @pl.loop(0, half // STEP_ROWS)
        def _(i):
            work(pl.multiple_of(i * STEP_ROWS, STEP_ROWS))

    reads[0].wait()
    for c in each:

        def first_norm(at, c=c):
            values = tokens[pl.ds(c * half + at, STEP_ROWS), :].astype(f32)
            out = normal_of(values) * gain_one * (1.0 + scale_a) + shift_a
            rows_one[pl.ds(c * chunk + at, STEP_ROWS), :] = out.astype(bf16)

        by_rows(first_norm)
        if c == 0:
            ones[c].start()
    reads[2].wait()
    bias_down[...] = jnp.zeros(bias_down.shape, f32)
    for c in each:

        def weigh(at, c=c):
            low = (cot[pl.ds(c * half + at, STEP_ROWS), :].astype(f32) * gate_m).astype(bf16)
            full_back[pl.ds(c * chunk + at, STEP_ROWS), :] = low
            bias_down[...] += jnp.sum(low.astype(f32), axis=0, keepdims=True)

        by_rows(weigh)

    starts = [0]
    for n in range(lengths.shape[1] - 1):
        starts.append(starts[-1] + lengths[0, n])

    def place_of(step):
        at = step % chunk
        return jnp.where(at < half, me, 1 - me) * (chunks * half) + (step // chunk) * half + at % half

    def document_of(place):
        return sum((place >= start).astype(jnp.int32) for start in starts[1:])

    segr[...] = document_of(place_of(lax.broadcasted_iota(jnp.int32, segr.shape, 1)))

    @pl.loop(0, length // STEP_ROWS)
    def _(i):
        at = pl.multiple_of(i * STEP_ROWS, STEP_ROWS)
        place = place_of(at + lax.broadcasted_iota(jnp.int32, (STEP_ROWS, PAIR), 0))
        first = functools.reduce(jnp.maximum, [jnp.where(place >= start, start, 0) for start in starts])
        angles = (place - first).astype(f32) * frequency[...]
        rows = pl.ds(at, STEP_ROWS)
        segc[rows, :] = document_of(place)
        cosine[rows, :] = jnp.cos(angles)
        sine[rows, :] = jnp.sin(angles)

    reads[1].wait()

    def project(c):
        rows = whole[c]
        for t in range(3):
            y = mm(rows_one[rows, :], w_qkv[t], 1, 0)
            if t == 2:
                qkv[t, rows, :] = y.astype(bf16)
                continue
            for p in range(pairs):
                lanes = slice(p * PAIR, (p + 1) * PAIR)
                u = y[:, lanes]
                low = (u * cosine[rows, :] + turned(u) * sine[rows, :]).astype(bf16)
                qkv[t, rows, lanes] = low * jnp.asarray(HEAD**-0.5 if t == 0 else 1.0, bf16)

    ones[0].wait()
    ones[1].start()
    project(0)
    ones[1].wait()
    backs[0].start()
    project(1)
    writes.append(fetch(rows_one, one_out))
    writes.append(fetch(qkv, qkv_out))

    def attend(p, c):
        lanes = pl.ds(pl.multiple_of(p * PAIR, PAIR), PAIR)
        q = qkv[0, whole[c], lanes]
        docs = segr[:, whole[c]]
        outs = []
        for h in range(2):
            qh = head_lanes(q, h)
            scores = []
            for b in range(0, length, BLOCK):
                same = jnp.concatenate([segc[b : b + BLOCK, :]] * (chunk // 128), axis=1) == docs
                scores.append(jnp.where(same, mm(qkv[1, b : b + BLOCK, lanes], qh, 1, 1), masked_score))
            top = functools.reduce(jnp.maximum, [jnp.max(s, axis=0, keepdims=True) for s in scores])
            total, summed = 0.0, 0.0
            for i, s in enumerate(scores):
                pr = jnp.exp(s - top)
                total = total + jnp.sum(pr, axis=0, keepdims=True)
                v = transposed(qkv[2, i * BLOCK : (i + 1) * BLOCK, lanes]).astype(bf16)
                summed = summed + mm(v[h * HEAD : (h + 1) * HEAD, :], pr.astype(bf16), 1, 0)
            lse[c, 2 * p + h] = top + jnp.log(total)
            outs.append(summed / total)
        mixed[whole[c], lanes] = jnp.concatenate(outs, axis=0).T.astype(bf16)

    for c in each:

        @pl.loop(0, pairs)
        def _(p):
            attend(p, c)

        if c == 0:
            reads[3].wait()
        send_sum[c] = mm(mixed[got[c], :], w_out[...], 1, 0).astype(bf16)
        shares[c].start()
        projected[c] = mm(mixed[own[c], :], w_out[...], 1, 0)
    writes.append(fetch(mixed, mixed_out))

    def second_norm(c):
        shares[c].wait()

        def work(at):
            rows = pl.ds(at, STEP_ROWS)
            share = projected[c, rows, :] + from_sum[c, rows, :].astype(f32)
            projected[c, rows, :] = share
            values = tokens[pl.ds(c * half + at, STEP_ROWS), :].astype(f32) + gate_a * share
            middle[c, rows, :] = values
            out = normal_of(values) * gain_two * (1.0 + scale_m) + shift_m
            rows_two[pl.ds(c * chunk + at, STEP_ROWS), :] = out.astype(bf16)

        by_rows(work)
        twos[c].start()

    cubic, root = 0.044715, (2.0 / jnp.pi) ** 0.5
    tile = 2 * WIDE
    bias[...] = jnp.zeros(bias.shape, f32)
    held = [[], []]

    def feed_forward(slot, rows):
        for copy in held[slot]:
            copy.wait()

        @pl.loop(0, w_up.shape[1] // tile)
        def _(t):
            at = pl.ds(pl.multiple_of(t * tile, tile), tile)
            u = mm(rows_two[rows, :], w_up[:, at], 1, 0) + b_up[:, at]
            square = u * u
            t_h = jnp.tanh(u * (root + (root * cubic) * square))
            rising = 0.5 * (1.0 + t_h)
            low_hidden = (u * rising).astype(bf16)
            slope = rising + (0.5 * u) * (1.0 - t_h * t_h) * (root + (3.0 * cubic * root) * square)
            low = (mm(full_back[rows, :], w_down[at, :], 1, 1) * slope).astype(bf16)
            hidden[slot, :, at] = low_hidden
            pre[slot, :, at] = low
            bias[:, at] += jnp.sum(low.astype(f32), axis=0, keepdims=True)
            more, more_branch = mm(low, w_up[:, at], 1, 1), mm(low_hidden, w_down[at, :], 1, 0)

            @pl.when(t == 0)
            def _():
                grads[slot] = more
                branch[slot] = more_branch

            @pl.when(t > 0)
            def _():
                grads[slot] += more
                branch[slot] += more_branch

        held[slot] = [fetch(hidden.at[slot], hidden_out.at[rows]), fetch(pre.at[slot], pre_out.at[rows])]

    second_norm(0)
    for read in reads[4:]:
        read.wait()
    for c in each:
        if c:
            second_norm(c)
        feed_forward(c, own[c])
        held[c] += [fetch(grads.at[c], own_grad.at[c]), fetch(branch.at[c], own_branch.at[c])]
    writes.append(fetch(middle, middle_out))
    writes.append(fetch(projected, projected_out))
    for c in each:
        twos[c].wait()
        backs[c].wait()
        if c == 0:
            backs[1].start()
        feed_forward(c, got[c])
        low_grads[c] = grads[c].astype(bf16)
        low_branch[c] = branch[c].astype(bf16)
        writes += [fetch(low_grads.at[c], send_grad.at[c]), fetch(low_branch.at[c], send_branch.at[c]), *held[c]]
    writes += [fetch(full_back, back_out), fetch(rows_two, two_out)]
    known[...] = jnp.concatenate(
        [
            jnp.zeros((8, depth), f32), bias_down[...], bias[:, :depth], bias[:, depth:],
            jnp.concatenate([cond[...].astype(f32), jnp.zeros((1, depth - cond.shape[1]), f32)], axis=1),
            jnp.zeros((4, depth), f32),
        ],
        axis=0,
    )
    for copy in writes:
        copy.wait()


def head(tokens, cot, w_qkv, w_out, w_up, w_down, *near_args, chunks):
    own, depth = tokens.shape
    length, width, wide = 2 * own, w_qkv.shape[2], w_up.shape[1]
    half = own // chunks
    anywhere, near = pl.BlockSpec(memory_space=pl.ANY), pl.BlockSpec(memory_space=pltpu.VMEM)
    shaped, kept = jax.ShapeDtypeStruct, pltpu.VMEM
    parts, rows = (chunks, half, depth), (length, depth)
    return pl.pallas_call(
        head_kernel,
        in_specs=[anywhere] * 6 + [near] * (len(near_args) - 1) + [pl.BlockSpec(memory_space=pltpu.SMEM)],
        out_specs=[anywhere] * 13 + [near] * 6,
        out_shape=[
            shaped((3, length, width), bf16), shaped((length, width), bf16), *[shaped(rows, bf16)] * 3,
            *[shaped((length, wide), bf16)] * 2, shaped(parts, f32), shaped(parts, bf16),
            shaped(parts, f32), shaped(parts, f32), shaped(parts, f32), shaped(parts, bf16),
            shaped((chunks, width // HEAD, 1, length // chunks), f32), shaped((16, depth), f32),
            shaped((1, length), jnp.int32), shaped((length, PAIR), jnp.int32), *[shaped((length, PAIR), f32)] * 2,
        ],
        scratch_shapes=[
            kept(tokens.shape, bf16), kept(tokens.shape, bf16), kept(w_qkv.shape, bf16), kept(w_out.shape, bf16),
            kept(w_up.shape, bf16), kept(w_down.shape, bf16), *[kept(rows, bf16)] * 3, kept((3, length, width), bf16),
            kept((length, width), bf16), kept(parts, bf16), kept(parts, bf16), kept(parts, f32), kept(parts, f32),
            *[kept((chunks, half, wide), bf16)] * 2, *[kept(parts, f32)] * 2,
            kept(parts, bf16), kept(parts, bf16), kept((1, wide), f32), kept((1, depth), f32),
            pltpu.SemaphoreType.DMA((32,)),
            pltpu.SemaphoreType.DMA((4 * chunks,)), pltpu.SemaphoreType.DMA((4 * chunks,)),
        ],
        compiler_params=pltpu.CompilerParams(collective_id=2, has_side_effects=True, vmem_limit_bytes=61 << 20),
        name="head",
    )(tokens, cot, w_qkv, w_out, w_up, w_down, *near_args)


def tail_kernel(
    hidden, full_back, rows_two, grad_pre, qkv_hbm, mixed_hbm, rows_hbm, w_qkv_hbm, w_out_hbm,
    own_grad, send_grad, mid_hbm, proj_hbm, own_branch, send_branch, tokens_hbm, cot_hbm,
    mods, b_ada, gain_one, gain_two, b_down, known, lse, segr, segc, cosine, sine, w_ada,
    down_sum, up_sum, out_sum, q_sum, k_sum, v_sum, output, ada, grad_x, cond_grad, ada_bias, one_gain, two_gain, down_bias, up_bias,
    qkv, mixed, rows_one, w_qkv, w_out, proj, mix_grad, d_qkv, dk, dv, from_x, grads, middle, projected, tokens, cot,
    part_a, part_b, part_c, part_d, part_e, branch_got, col_sums, small, small_got, everyone,
    load, store, x_send, x_recv, all_send, all_recv, *more,
):
    place, me = lax.axis_index("dp"), lax.axis_index("tensor")
    length, depth = rows_one.shape
    chunks, half, _ = from_x.shape
    chunk = 2 * half
    width = mixed.shape[1]
    pairs = width // PAIR
    across = {"tensor": 1 - me}

    specs = [
        (part_a.at[pl.ds(0, WIDE)], down_sum.at[pl.ds(0, WIDE)], 0),
        (part_a.at[pl.ds(WIDE, WIDE)], down_sum.at[pl.ds(WIDE, WIDE)], 0),
        (part_b, down_sum.at[pl.ds(depth, depth)], 0),
        (part_c, up_sum, 0), (part_d, up_sum, depth), (part_e, out_sum, 0),
        (qkv.at[2], v_sum, 0), (qkv.at[1], k_sum, 0), (qkv.at[0], q_sum, 0),
    ]
    units = []
    for i, (part, out, column) in enumerate(specs):
        *got, send, recv, local = more[7 * i : 7 * (i + 1)]
        units.append(Unit(part, out, column, got, send, recv, local, place))

    def x_copy(src, dst, i):
        return pltpu.make_async_remote_copy(
            src_ref=src, dst_ref=dst, send_sem=x_send.at[i], recv_sem=x_recv.at[i],
            device_id=across, device_id_type=MESH,
        )

    each = range(chunks)
    grads_in = [x_copy(send_grad.at[c], from_x.at[c], c) for c in each]
    projs = [x_copy(proj.at[c, :half], proj.at[c, half:], chunks + c) for c in each]
    ones = [x_copy(proj.at[c, :half], from_x.at[c], 2 * chunks + c) for c in each]
    branches = [x_copy(send_branch.at[c], branch_got.at[c], 3 * chunks + c) for c in each]
    smalls = x_copy(small, small_got, 4 * chunks)
    outputs = [
        pltpu.make_async_copy(branch_got.at[c], output.at[c * half : (c + 1) * half], store.at[c]) for c in each
    ]
    partner = units[0].partner

    fetch = fetcher(load)
    done = [0]

    def until(place_now):
        while done[0] < len(ORDER) and ORDER[done[0]][0] <= place_now:
            _, i, k = ORDER[done[0]]
            units[i].step(k)
            done[0] += 1

    greet([*[{"dp": p} for p in partner], across])
    grads_in[0].start()
    slots = [w_qkv.at[0], w_qkv.at[1], w_qkv.at[2], d_qkv.at[2]]
    cut = lambda t: slice(t * WIDE, (t + 1) * WIDE)
    backs = fetch(full_back, rows_one)
    hiddens = [fetch(hidden.at[:, cut(t)], slots[t]) for t in range(4)]
    norms = [
        [fetch(src, dst.at[c]) for src, dst in (
            (own_grad.at[c], grads), (mid_hbm.at[c], middle), (proj_hbm.at[c], projected),
            (tokens_hbm.at[c * half : (c + 1) * half], tokens), (cot_hbm.at[c * half : (c + 1) * half], cot),
        )]
        for c in each
    ]
    twos = [fetch(rows_two.at[:, cut(t)], d_qkv.at[t]) for t in range(2)]
    col_sums[...] = jnp.zeros(col_sums.shape, f32)

    backs.wait()
    pres = []
    for t in range(4):
        until(1 + t)
        hiddens[t].wait()
        part = (part_a, part_b)[t // 2]

        @pl.loop(0, WIDE // 256)
        def _(r):
            at = pl.ds(pl.multiple_of(r * 256, 256), 256)
            to = pl.ds(pl.multiple_of((t % 2) * WIDE + r * 256, 256), 256)
            part[to, :] = mm(slots[t][:, at], rows_one[...], 0, 0).astype(bf16)

        pres.append(fetch(grad_pre.at[:, cut(t)], slots[t]))
        if t != 2:
            units[min(t, 2)].step(0)
    main = [
        fetch(w_out_hbm, w_out), fetch(mixed_hbm, mixed), fetch(qkv_hbm, qkv), fetch(rows_hbm, rows_one),
    ]

    def up_part(t):
        pres[t].wait()
        part = (part_c, part_d)[t // 2]

        @pl.loop(0, depth // 256)
        def _(r):
            to = pl.ds(pl.multiple_of(r * 256, 256), 256)
            at = pl.ds(pl.multiple_of((r % 2) * 256, 256), 256)
            part[to, cut(t % 2)] = mm(d_qkv[r // 2, :, at], slots[t][...], 0, 0).astype(bf16)

    def fold(row, values):
        col_sums[row : row + 1, :] += jnp.sum(values, axis=0, keepdims=True)

    def norm_back(grad, values, weight):
        center = values - jnp.mean(values, axis=1, keepdims=True)
        root = lax.rsqrt(jnp.mean(center * center, axis=1, keepdims=True) + norm_eps)
        normal = center * root
        inner = grad * weight
        back = inner - jnp.mean(inner, axis=1, keepdims=True) - normal * jnp.mean(inner * normal, axis=1, keepdims=True)
        return root * back, normal

    _, scale_a, gate_a, _, scale_m, gate_m = vectors_of(mods, b_ada, depth)
    gain_one, gain_two, b_down = gain_one[...], gain_two[...], b_down[...]

    def second_norm(c):
        for copy in norms[c]:
            copy.wait()

        @pl.loop(0, half // STEP_ROWS)
        def _(i):
            at = pl.ds(pl.multiple_of(i * STEP_ROWS, STEP_ROWS), STEP_ROWS)
            grad = grads[c, at, :] + from_x[c, at, :].astype(f32)
            back, normal = norm_back(grad, middle[c, at, :], gain_two * (1.0 + scale_m))
            total = back + cot[c, at, :].astype(f32)
            grads[c, at, :] = total
            proj[c, at, :] = (total * gate_a).astype(bf16)
            fold(0, grad)
            fold(1, grad * normal)
            fold(2, total * projected[c, at, :])

        projs[c].start()

    for copy in twos:
        copy.wait()
    until(5)
    up_part(0)
    until(6)
    up_part(1)
    units[3].step(0)
    until(7)
    grads_in[0].wait()
    grads_in[1].start()
    second_norm(0)
    owns = [fetch(own_branch.at[0], projected.at[0])]
    until(8)
    up_part(2)
    until(9)
    up_part(3)
    units[4].step(0)
    weights = fetch(w_qkv_hbm, w_qkv)
    until(10)
    grads_in[1].wait()
    second_norm(1)
    owns.append(fetch(own_branch.at[1], projected.at[1]))

    def turn_back(u, rows):
        return (u * cosine[rows, :] - turned(u) * sine[rows, :]).astype(bf16)

    def attend_back(p, c):
        lanes = pl.ds(pl.multiple_of(p * PAIR, PAIR), PAIR)
        rows = slice(c * chunk, (c + 1) * chunk)
        q, g = qkv[0, rows, lanes], mix_grad[rows, lanes]
        both = (g.astype(f32) * mixed[rows, lanes].astype(f32)).T
        qh = [head_lanes(q, h) for h in range(2)]
        gh = [head_lanes(g, h) for h in range(2)]
        delta = [jnp.sum(both[h * HEAD : (h + 1) * HEAD, :], axis=0, keepdims=True) for h in range(2)]
        q_two, g_two = jnp.concatenate(qh, axis=0), jnp.concatenate(gh, axis=0)
        docs = segr[:, rows]
        dq = [0.0, 0.0]
        for b in range(0, length, BLOCK):
            cols = slice(b, b + BLOCK)
            k, v = qkv[1, cols, lanes], qkv[2, cols, lanes]
            turned_k = transposed(k).astype(bf16)
            same = jnp.concatenate([segc[cols, :]] * (chunk // 128), axis=1) == docs
            ps, ds = [], []
            for h in range(2):
                s = jnp.where(same, mm(k, qh[h], 1, 1), masked_score)
                pr = jnp.exp(s - lse[c, 2 * p + h])
                d = (pr * (mm(v, gh[h], 1, 1) - delta[h])).astype(bf16)
                ps.append(pr.astype(bf16))
                ds.append(d)
                dq[h] = dq[h] + mm(turned_k[h * HEAD : (h + 1) * HEAD, :], d, 1, 0)
            add_v = mm(jnp.concatenate(ps, axis=1), g_two, 1, 0)
            add_k = mm(jnp.concatenate(ds, axis=1), q_two, 1, 0)
            if c < chunks - 1:
                dv[cols, lanes] = add_v if c == 0 else dv[cols, lanes] + add_v
                dk[cols, lanes] = add_k if c == 0 else dk[cols, lanes] + add_k
            else:
                d_qkv[1, cols, lanes] = turn_back(dk[cols, lanes] + add_k, cols)
                d_qkv[2, cols, lanes] = (dv[cols, lanes] + add_v).astype(bf16)
        d_qkv[0, rows, lanes] = turn_back(jnp.concatenate(dq, axis=0).T * (HEAD**-0.5), rows)

    for copy in main:
        copy.wait()
    now = 11
    for c in each:
        until(now)
        projs[c].wait()
        if c == chunks - 1:
            for copy in branches:
                copy.start()
        mix_grad[c * chunk : (c + 1) * chunk, :] = mm(proj[c], w_out[...], 1, 1).astype(bf16)
        now += 1
        if c == chunks - 1:
            until(now)

            @pl.loop(0, width // 256)
            def _(r):
                at = pl.ds(pl.multiple_of(r * 256, 256), 256)
                part_e[at, :] = sum(
                    mm(mixed[n * chunk : (n + 1) * chunk, at], proj[n], 0, 0) for n in each
                ).astype(bf16)

            units[5].step(0)
            now += 1

        @pl.loop(0, pairs)
        def _(p):
            for n in range(pairs):

                @pl.when(p == n)
                def _():
                    until(now + n)

            attend_back(p, c)

        now += pairs

    def rows_back(start):
        at = slice(start, start + half)
        return sum(mm(d_qkv[t, at, :], w_qkv[t], 1, 1) for t in range(3))

    for i in range(3):
        until(now + i)

        @pl.loop(0, depth // 256)
        def _(r):
            at = pl.ds(pl.multiple_of(r * 256, 256), 256)
            qkv[2 - i, at, :] = mm(rows_one[:, at], d_qkv[2 - i], 0, 0).astype(bf16)

        units[6 + i].step(0)
    now += 3
    weights.wait()
    for c in each:
        until(now + c)
        proj[c, :half] = rows_back(c * chunk + half).astype(bf16)
        if c == 0:
            ones[c].start()
    now += chunks
    for c in each:
        until(now + c)
        branches[c].wait()
        owns[c].wait()

        @pl.loop(0, half // STEP_ROWS)
        def _(i):
            at = pl.ds(pl.multiple_of(i * STEP_ROWS, STEP_ROWS), STEP_ROWS)
            branch = projected[c, at, :] + branch_got[c, at, :].astype(f32) + b_down
            branch_got[c, at, :] = (middle[c, at, :] + gate_m * branch).astype(bf16)
            fold(5, cot[c, at, :].astype(f32) * branch)

        outputs[c].start()
    now += chunks
    for c in each:
        until(now + c)
        projected[c] = rows_back(c * chunk)
    now += chunks
    for c in each:
        until(now + c)
        ones[c].wait()
        if c < chunks - 1:
            ones[c + 1].start()

        @pl.loop(0, half // STEP_ROWS)
        def _(i):
            at = pl.ds(pl.multiple_of(i * STEP_ROWS, STEP_ROWS), STEP_ROWS)
            grad = projected[c, at, :] + from_x[c, at, :].astype(f32)
            back, normal = norm_back(grad, tokens[c, at, :].astype(f32), gain_one * (1.0 + scale_a))
            grad_x[c, at, :] = (back + grads[c, at, :]).astype(bf16)
            fold(3, grad)
            fold(4, grad * normal)

    now += chunks
    shift, scaled, gated, shift_one, scaled_one, gated_m = [col_sums[r : r + 1, :] for r in range(6)]
    small[...] = known[...] + jnp.concatenate(
        [
            shift_one, gain_one * scaled_one, gated, shift, gain_two * scaled, gated_m,
            (1.0 + scale_a) * scaled_one, (1.0 + scale_m) * scaled, jnp.zeros((8, depth), f32),
        ],
        axis=0,
    )
    smalls.start()
    until(now)
    smalls.wait()
    number = lax.broadcasted_iota(jnp.int32, small.shape, 0)
    everyone[0] = small[...] + jnp.where(number < 9, small_got[...], 0.0)
    for n, b in enumerate((1, 3, 2, 0)):
        copy = pltpu.make_async_remote_copy(
            src_ref=everyone.at[pl.ds(0, 1 << n)], dst_ref=everyone.at[pl.ds(1 << n, 1 << n)],
            send_sem=all_send.at[n], recv_sem=all_recv.at[n],
            device_id={"dp": partner[b]}, device_id_type=MESH,
        )
        copy.start()
        until(now + 1 + n)
        copy.wait()
    total = sum(everyone[n] for n in range(1 << EDGES))
    for r in range(6):
        ada_bias[:, r * depth : (r + 1) * depth] = total[r : r + 1, :]
    lanes = 0.0
    for r in range(6):
        for t in range(0, depth, 128):
            at = r * depth + t
            lanes = lanes + w_ada[:, at : at + 128].astype(f32) * everyone[0, r : r + 1, t : t + 128]
    cond_grad[...] = jnp.sum(lanes.T, axis=0, keepdims=True)
    one_gain[...], two_gain[...], down_bias[...] = total[6:7, :], total[7:8, :], total[8:9, :]
    for r in range(2):
        up_bias[:, r * depth : (r + 1) * depth] = total[9 + r : 10 + r, :]
    conds = jnp.concatenate([everyone[n, 11:12, : ada.shape[0]] for n in range(1 << EDGES)], axis=0)
    spans = []
    for j in range(ada.shape[1] // width):
        vector, side = divmod(j * width, depth)
        mods = jnp.concatenate([everyone[n, vector : vector + 1, side : side + width] for n in range(1 << EDGES)], axis=0)
        rows = slice(j // 2 * ada.shape[0], (j // 2 + 1) * ada.shape[0])
        spot = (dk, dv)[j % 2].at[rows]
        spot[...] = lax.dot_general(
            conds, mods, (((0,), (0,)), ((), ())), precision=lax.Precision.HIGHEST, preferred_element_type=f32
        )
        spans.append(pltpu.make_async_copy(spot, ada.at[:, j * width : (j + 1) * width], store.at[chunks + j]))
        spans[-1].start()
    until(1000)
    for copy in (*outputs, *spans):
        copy.wait()


def tail(*args):
    ada_shape = args[-1].shape
    hidden, qkv, rows_one, w_qkv, w_out, own_grad, tokens = (args[n] for n in (0, 4, 6, 7, 8, 9, 15))
    known = args[22]
    _, length, width = qkv.shape
    chunks, half, depth = own_grad.shape
    anywhere, near = pl.BlockSpec(memory_space=pl.ANY), pl.BlockSpec(memory_space=pltpu.VMEM)
    shaped, kept = jax.ShapeDtypeStruct, pltpu.VMEM
    in_chunks = (chunks, half, depth)
    scratch = [
        kept(qkv.shape, bf16), kept((length, width), bf16), kept(rows_one.shape, bf16), kept(w_qkv.shape, bf16),
        kept(w_out.shape, bf16), kept((chunks, 2 * half, depth), bf16), kept((length, width), bf16),
        kept((3, length, width), bf16), kept((length, width), f32), kept((length, width), f32),
        kept(in_chunks, bf16), kept(in_chunks, f32), kept(in_chunks, f32), kept(in_chunks, f32),
        kept(in_chunks, bf16), kept(in_chunks, bf16),
        *[kept((depth, depth), bf16)] * 4, kept((width, depth), bf16), kept(in_chunks, bf16),
        kept((8, depth), f32), kept(known.shape, f32), kept(known.shape, f32), kept((1 << EDGES, *known.shape), f32),
        pltpu.SemaphoreType.DMA((30,)), pltpu.SemaphoreType.DMA((chunks + ada_shape[1] // width,)),
        pltpu.SemaphoreType.DMA((4 * chunks + 1,)), pltpu.SemaphoreType.DMA((4 * chunks + 1,)),
        pltpu.SemaphoreType.DMA((EDGES,)), pltpu.SemaphoreType.DMA((EDGES,)),
        *unit_scratch(WIDE, depth) * 2, *unit_scratch(depth, depth) * 3, *unit_scratch(width, depth), *unit_scratch(depth, width) * 3,
    ]
    return pl.pallas_call(
        tail_kernel,
        in_specs=[anywhere] * 17 + [near] * 12,
        out_specs=[anywhere] * 8 + [near] * 7,
        out_shape=[
            shaped((hidden.shape[1], depth), bf16), shaped((depth, hidden.shape[1]), bf16), shaped((width, depth), bf16),
            *[shaped((depth, width), bf16)] * 3, shaped(tokens.shape, bf16),
            shaped(ada_shape, f32), shaped(in_chunks, bf16),
            *[shaped((1, n), f32) for n in (ada_shape[0], ada_shape[1], depth, depth, depth, hidden.shape[1])],
        ],
        scratch_shapes=scratch,
        compiler_params=pltpu.CompilerParams(collective_id=1, has_side_effects=True, vmem_limit_bytes=61 << 20),
        name="tail",
    )(*args)


def body_pair(
    tokens, cond, doc_lengths, w_ada, b_ada, gain_one, w_qkv, w_out, gain_two, w_up, b_up, w_down, b_down, cotangent
):
    own, width = tokens.shape
    length = 2 * own
    chunks = 2

    exponent = jnp.arange(HEAD // 2, dtype=f32) * (2.0 / HEAD)
    frequency = jnp.tile(jnp.power(jnp.float32(rope_base), -exponent), PAIR // (HEAD // 2))[None, :]
    mods = jnp.dot(cond, w_ada, preferred_element_type=f32)
    (
        qkv, mixed, rows_one, full_back, rows_two, hidden, grad_pre, own_grad, send_grad, middle, projected,
        own_branch, send_branch, lse, known, *tables,
    ) = head(
        tokens, cotangent, w_qkv, w_out, w_up, w_down, mods, b_ada[None, :], gain_one[None, :], gain_two[None, :], cond,
        b_up[None, :], frequency, doc_lengths, chunks=chunks,
    )
    *sums, output, grad_w_ada, grad_x, grad_cond, grad_b_ada, grad_gain_one, grad_gain_two, grad_b_down, grad_b_up = tail(
        hidden, full_back, rows_two, grad_pre, qkv, mixed, rows_one, w_qkv, w_out, own_grad, send_grad,
        middle, projected, own_branch, send_branch, tokens, cotangent,
        mods, b_ada[None, :], gain_one[None, :], gain_two[None, :], b_down[None, :], known,
        lse, *tables, w_ada,
    )
    grad_w_down, grad_w_up, grad_w_out, grad_q, grad_k, grad_v = [s.astype(f32) for s in sums]
    grad_w_qkv = jnp.stack([grad_q, grad_k, grad_v])
    grad_x = grad_x.reshape(own, width)
    grad_b_ada, grad_gain_one, grad_gain_two, grad_b_down, grad_b_up = [
        row[0] for row in (grad_b_ada, grad_gain_one, grad_gain_two, grad_b_down, grad_b_up)
    ]
    return (
        output, grad_x, grad_cond, grad_w_ada, grad_b_ada, grad_gain_one, grad_w_qkv, grad_w_out, grad_gain_two,
        grad_w_up, grad_b_up, grad_w_down, grad_b_down,
    )


def body_any(
    tokens, cond, doc_lengths, w_ada, b_ada, gain_one, w_qkv, w_out, gain_two, w_up, b_up, w_down, b_down, cotangent
):
    tensor_size = lax.axis_size("tensor")
    own = tokens.shape[0]
    length = own * tensor_size

    def all_rows(values):
        return lax.all_gather(values, "tensor", axis=0, tiled=True)

    def own_sum(values):
        return lax.psum_scatter(values, "tensor", scatter_dimension=0, tiled=True)

    def sum_over_dp(part):
        return lax.psum(part, "dp")

    places = jnp.arange(length, dtype=jnp.int32)
    segment, doc_first = documents(doc_lengths[0], places)
    cosine, sine = rope_tables(places - doc_first)
    blocks = length // BLOCK
    in_blocks = segment.reshape(blocks, BLOCK)
    least, most = jnp.min(in_blocks, axis=1), jnp.max(in_blocks, axis=1)
    meets = (least[:, None] <= most[None, :]) & (least[None, :] <= most[:, None])
    flags = meets.astype(jnp.int32).reshape(-1)
    seg_rows = in_blocks[:, None, :]
    seg_cols = jnp.broadcast_to(segment[:, None], (length, 128))

    modulation = jnp.dot(cond, w_ada, preferred_element_type=f32)[0] + b_ada
    shift_a, scale_a, gate_a, shift_m, scale_m, gate_m = jnp.split(modulation, 6)
    x_rows = tokens.astype(f32)
    grad_out = cotangent.astype(f32)

    act_one = modulate(x_rows, gain_one, shift_a, scale_a).astype(bf16)
    rows_one = all_rows(act_one)
    grad_branch = (grad_out * gate_m).astype(bf16)
    full_branch = all_rows(grad_branch)
    qkv = project_qkv(rows_one, w_qkv, cosine, sine)
    mixed, lse = attend_forward(flags, qkv, seg_rows, seg_cols)
    projected = own_sum(jnp.dot(mixed, w_out, preferred_element_type=f32))
    middle = x_rows + gate_a * projected
    rows_two = all_rows(modulate(middle, gain_two, shift_m, scale_m).astype(bf16))
    pre_act = jnp.dot(rows_two, w_up, preferred_element_type=f32) + b_up
    hidden = jax.nn.gelu(pre_act, approximate=True).astype(bf16)

    grad_hidden = jnp.einsum("sd,fd->sf", full_branch, w_down, preferred_element_type=f32)
    _, gelu_back = jax.vjp(lambda values: jax.nn.gelu(values, approximate=True), pre_act)
    grad_pre = gelu_back(grad_hidden)[0].astype(bf16)
    grad_act_two = own_sum(jnp.einsum("sf,df->sd", grad_pre, w_up, preferred_element_type=f32))
    grad_w_down = sum_over_dp(jnp.einsum("sf,sd->fd", hidden, full_branch, preferred_element_type=f32))
    grad_w_up = sum_over_dp(jnp.einsum("sd,sf->df", rows_two, grad_pre, preferred_element_type=f32))

    branch = own_sum(jnp.dot(hidden, w_down, preferred_element_type=f32)) + b_down
    output = (middle + gate_m * branch).astype(bf16)
    grad_gate_m = jnp.sum(grad_out * branch, axis=0)
    grad_b_down = jnp.sum(grad_branch.astype(f32), axis=0)
    grad_b_up = jnp.sum(grad_pre.astype(f32), axis=0)

    _, second_back = jax.vjp(modulate, middle, gain_two, shift_m, scale_m)
    grad_middle, grad_gain_two, grad_shift_m, grad_scale_m = second_back(grad_act_two)
    grad_middle = grad_middle + grad_out
    full_proj = all_rows((grad_middle * gate_a).astype(bf16))
    grad_gate_a = jnp.sum(grad_middle * projected, axis=0)
    grad_mixed = jnp.einsum("sd,ed->se", full_proj, w_out, preferred_element_type=f32).astype(bf16)
    grad_w_out = sum_over_dp(jnp.einsum("se,sd->ed", mixed, full_proj, preferred_element_type=f32))
    grad_qkv = attend_backward(flags, qkv, grad_mixed, mixed, lse, seg_rows, seg_cols, cosine, sine)
    grad_act_one = own_sum(jnp.einsum("tse,tde->sd", grad_qkv, w_qkv, preferred_element_type=f32))
    grad_w_qkv = jnp.einsum("sd,tse->tde", rows_one, grad_qkv, preferred_element_type=f32)
    grad_w_qkv = sum_over_dp(grad_w_qkv.reshape(-1, grad_w_qkv.shape[2])).reshape(grad_w_qkv.shape)

    _, first_back = jax.vjp(modulate, x_rows, gain_one, shift_a, scale_a)
    grad_x, grad_gain_one, grad_shift_a, grad_scale_a = first_back(grad_act_one)
    grad_x = (grad_x + grad_middle).astype(bf16)

    small = jnp.concatenate(
        [
            grad_shift_a, grad_scale_a, grad_gate_a, grad_shift_m, grad_scale_m, grad_gate_m,
            grad_gain_one, grad_gain_two, grad_b_down,
        ]
    )
    small = lax.psum(small, "tensor")
    mod_size = modulation.shape[0]
    grad_mod = small[:mod_size]
    grad_cond = jnp.dot(w_ada.astype(f32), grad_mod, precision=lax.Precision.HIGHEST)[None, :]
    everyone = lax.all_gather(
        jnp.concatenate([small, grad_b_up, cond[0].astype(f32)])[None, :], "dp", axis=0, tiled=True
    )
    conds = everyone[:, -cond.shape[1] :]
    mods = everyone[:, :mod_size]
    grad_w_ada = jnp.einsum("nc,nm->cm", conds, mods, precision=lax.Precision.HIGHEST, preferred_element_type=f32)
    sums = jnp.sum(everyone, axis=0)
    width = tokens.shape[1]
    grad_b_ada = sums[:mod_size]
    grad_gain_one, grad_gain_two, grad_b_down = jnp.split(sums[mod_size : mod_size + 3 * width], 3)
    grad_b_up = sums[mod_size + 3 * width : -cond.shape[1]]
    return (
        output, grad_x, grad_cond, grad_w_ada, grad_b_ada, grad_gain_one, grad_w_qkv, grad_w_out, grad_gain_two,
        grad_w_up, grad_b_up, grad_w_down, grad_b_down,
    )


def solution(mesh):
    swaps = mesh.shape["tensor"] == 2 and mesh.shape["dp"] == 16
    placed = (
        P(("dp", "tensor"), None), P("dp", None), P("dp", None), P(), P(), P(), P(None, None, "tensor"),
        P("tensor", None), P(), P(None, "tensor"), P("tensor"), P("tensor", None), P(), P(("dp", "tensor"), None),
    )
    return jax.shard_map(
        body_pair if swaps else body_any,
        mesh=mesh,
        in_specs=placed,
        out_specs=(
            P(("dp", "tensor"), None), P(("dp", "tensor"), None), P("dp", None), P(), P(), P(),
            P(None, None, "tensor"), P("tensor", None), P(), P(None, "tensor"), P("tensor"), P("tensor", None), P(),
        ),
        check_vma=False,
    )
```

```python
import functools

import jax
import jax.numpy as jnp
import numpy as np
from jax import lax
from jax.experimental import pallas as pl
from jax.experimental.pallas import tpu as pltpu
from jax.sharding import PartitionSpec as P

HEAD = 64
PAIR = 2 * HEAD
BLOCK = 256
ROWS = 512

norm_eps = 1e-05
rope_base = 10000.0
masked_score = -1e30
f32, bf16 = jnp.float32, jnp.bfloat16


def layer_norm(values, gain):
    center = values - jnp.mean(values, axis=-1, keepdims=True)
    spread = jnp.mean(center * center, axis=-1, keepdims=True)
    return center * lax.rsqrt(spread + norm_eps) * gain


def modulate(values, gain, shift, scale):
    return layer_norm(values, gain) * (1.0 + scale) + shift


def documents(lengths, places):
    numbers = jnp.arange(lengths.shape[0], dtype=jnp.int32)
    earlier = (numbers[None, :] < numbers[:, None]).astype(jnp.int32)
    starts = jnp.sum(earlier * lengths[None, :], axis=1)
    ends = starts + lengths
    inside = ((places[:, None] >= starts[None, :]) & (places[:, None] < ends[None, :])).astype(
        jnp.int32
    )
    segment = jnp.sum(inside * numbers[None, :], axis=1)
    doc_first = jnp.sum(inside * starts[None, :], axis=1)
    return segment, doc_first


def rope_tables(offsets):
    exponent = jnp.arange(HEAD // 2, dtype=f32) * (2.0 / HEAD)
    frequency = jnp.power(jnp.float32(rope_base), -exponent)
    angles = offsets.astype(f32)[:, None] * frequency[None, :]
    cosine, sine = jnp.cos(angles), jnp.sin(angles)
    repeat = PAIR // (HEAD // 2)
    return jnp.concatenate([cosine] * repeat, axis=-1), jnp.concatenate([sine] * repeat, axis=-1)


def turned(values):
    lane = lax.broadcasted_iota(jnp.int32, values.shape, 1)
    half = HEAD // 2
    from_right = pltpu.roll(values, PAIR - half, axis=1)
    from_left = pltpu.roll(values, half, axis=1)
    return jnp.where(lane % HEAD < half, -from_right, from_left)


def mm(a, b, da, db):
    return lax.dot_general(a, b, (((da,), (db,)), ((), ())), preferred_element_type=f32)


def qkv_kernel(x_ref, w_ref, cos_ref, sin_ref, o_ref):
    which = pl.program_id(1)
    y = mm(x_ref[...], w_ref[...], 1, 0)

    @pl.when(which < 2)
    def _():
        factor = jnp.where(which == 0, HEAD**-0.5, 1.0)
        for p in range(y.shape[1] // PAIR):
            u = y[:, p * PAIR : (p + 1) * PAIR]
            r = u * cos_ref[...] + turned(u) * sin_ref[...]
            o_ref[:, p * PAIR : (p + 1) * PAIR] = (r.astype(bf16) * factor.astype(bf16)).astype(bf16)

    @pl.when(which == 2)
    def _():
        o_ref[...] = y.astype(bf16)


def project_qkv(rows, w_qkv, cosine, sine):
    count, depth = rows.shape
    width = w_qkv.shape[2]
    return pl.pallas_call(
        qkv_kernel,
        grid=(count // ROWS, 3),
        in_specs=[
            pl.BlockSpec((ROWS, depth), lambda r, t: (r, 0)),
            pl.BlockSpec((None, depth, width), lambda r, t: (t, 0, 0)),
            pl.BlockSpec((ROWS, PAIR), lambda r, t: (r, 0)),
            pl.BlockSpec((ROWS, PAIR), lambda r, t: (r, 0)),
        ],
        out_specs=pl.BlockSpec((None, ROWS, width), lambda r, t: (t, r, 0)),
        out_shape=jax.ShapeDtypeStruct((3, count, width), bf16),
        compiler_params=pltpu.CompilerParams(vmem_limit_bytes=32 << 20),
        cost_estimate=pl.CostEstimate(
            flops=6 * count * depth * width, bytes_accessed=8 * count * width, transcendentals=0
        ),
        name="qkv",
    )(rows, w_qkv, cosine, sine)


def head_lanes(block, h):
    lane = lax.broadcasted_iota(jnp.int32, block.shape, 1)
    return jnp.where(lane // HEAD == h, block, jnp.zeros_like(block))


def transposed(block):
    return block.astype(f32).T


def forward_kernel(flag_ref, q_ref, k_ref, v_ref, segr_ref, segc_ref, o_ref, lse_ref, vt, m, l, acc):
    blocks = q_ref.shape[0] // BLOCK
    for b in range(blocks):
        vt[b] = transposed(v_ref[b * BLOCK : (b + 1) * BLOCK, :]).astype(bf16)

    @pl.loop(0, blocks)
    def _(qi):
        rows = pl.ds(pl.multiple_of(qi * BLOCK, BLOCK), BLOCK)
        q = q_ref[rows, :]
        m[...] = jnp.full(m.shape, masked_score, f32)
        l[...] = jnp.zeros(l.shape, f32)
        acc[...] = jnp.zeros(acc.shape, f32)

        @pl.loop(0, blocks)
        def _(ki):
            @pl.when(flag_ref[qi * blocks + ki] > 0)
            def _():
                cols = pl.ds(pl.multiple_of(ki * BLOCK, BLOCK), BLOCK)
                k = k_ref[cols, :]
                docs = segc_ref[cols, :]
                same = jnp.concatenate([docs] * (BLOCK // 128), axis=1) == segr_ref[qi]
                for h in range(2):
                    lo, hi = h * HEAD, (h + 1) * HEAD
                    s = jnp.where(same, mm(k, head_lanes(q, h), 1, 1), masked_score)
                    top = jnp.maximum(m[h], jnp.max(s, axis=0, keepdims=True))
                    p = jnp.exp(s - top)
                    shrink = jnp.exp(m[h] - top)
                    m[h] = top
                    l[h] = l[h] * shrink + jnp.sum(p, axis=0, keepdims=True)
                    acc[lo:hi, :] = acc[lo:hi, :] * shrink + mm(vt[ki, lo:hi, :], p.astype(bf16), 1, 0)

        for h in range(2):
            lo, hi = h * HEAD, (h + 1) * HEAD
            lse_ref[h, qi] = m[h] + jnp.log(l[h])
            acc[lo:hi, :] = acc[lo:hi, :] / l[h]
        o_ref[rows, :] = acc[...].T.astype(bf16)


def backward_kernel(
    flag_ref, q_ref, k_ref, v_ref, g_ref, o_ref, lse_ref, segr_ref, segc_ref, cos_ref, sin_ref,
    out_ref, kt, dk, dv, dq,
):
    blocks = q_ref.shape[0] // BLOCK
    for b in range(blocks):
        kt[b] = transposed(k_ref[b * BLOCK : (b + 1) * BLOCK, :]).astype(bf16)
    dk[...] = jnp.zeros(dk.shape, f32)
    dv[...] = jnp.zeros(dv.shape, f32)

    def turn_back(u, rows):
        return (u * cos_ref[rows, :] - turned(u) * sin_ref[rows, :]).astype(bf16)

    @pl.loop(0, blocks)
    def _(qi):
        rows = pl.ds(pl.multiple_of(qi * BLOCK, BLOCK), BLOCK)
        q, g = q_ref[rows, :], g_ref[rows, :]
        both = (g.astype(f32) * o_ref[rows, :].astype(f32)).T
        dq[...] = jnp.zeros(dq.shape, f32)

        @pl.loop(0, blocks)
        def _(ki):
            @pl.when(flag_ref[qi * blocks + ki] > 0)
            def _():
                cols = pl.ds(pl.multiple_of(ki * BLOCK, BLOCK), BLOCK)
                k, v = k_ref[cols, :], v_ref[cols, :]
                docs = segc_ref[cols, :]
                same = jnp.concatenate([docs] * (BLOCK // 128), axis=1) == segr_ref[qi]
                dk_sum, dv_sum = dk[cols, :], dv[cols, :]
                for h in range(2):
                    lo, hi = h * HEAD, (h + 1) * HEAD
                    delta = jnp.sum(both[lo:hi, :], axis=0, keepdims=True)
                    qh, gh = head_lanes(q, h), head_lanes(g, h)
                    s = jnp.where(same, mm(k, qh, 1, 1), masked_score)
                    p = jnp.exp(s - lse_ref[h, qi])
                    ds = (p * (mm(v, gh, 1, 1) - delta)).astype(bf16)
                    dv_sum = dv_sum + mm(p.astype(bf16), gh, 1, 0)
                    dk_sum = dk_sum + mm(ds, qh, 1, 0)
                    dq[lo:hi, :] = dq[lo:hi, :] + mm(kt[ki, lo:hi, :], ds, 1, 0)
                dk[cols, :] = dk_sum
                dv[cols, :] = dv_sum

        out_ref[0, rows, :] = turn_back(dq[...].T * (HEAD**-0.5), rows)

    @pl.loop(0, blocks)
    def _(b):
        rows = pl.ds(pl.multiple_of(b * BLOCK, BLOCK), BLOCK)
        out_ref[1, rows, :] = turn_back(dk[rows, :], rows)
        out_ref[2, rows, :] = dv[rows, :].astype(bf16)


def pieces_of(qkv, length):
    return [pl.BlockSpec((None, length, PAIR), functools.partial(lambda t, p, *_: (t, 0, p), t)) for t in range(3)]


def attend_forward(flags, qkv, seg_rows, seg_cols):
    _, length, width = qkv.shape
    blocks, pairs = length // BLOCK, width // PAIR
    return pl.pallas_call(
        forward_kernel,
        grid_spec=pltpu.PrefetchScalarGridSpec(
            num_scalar_prefetch=1,
            grid=(pairs,),
            in_specs=[
                *pieces_of(qkv, length),
                pl.BlockSpec((blocks, 1, BLOCK), lambda p, *_: (0, 0, 0)),
                pl.BlockSpec((length, 128), lambda p, *_: (0, 0)),
            ],
            out_specs=[
                pl.BlockSpec((length, PAIR), lambda p, *_: (0, p)),
                pl.BlockSpec((2, blocks, 1, BLOCK), lambda p, *_: (p, 0, 0, 0)),
            ],
            scratch_shapes=[
                pltpu.VMEM((blocks, PAIR, BLOCK), bf16),
                pltpu.VMEM((2, 1, BLOCK), f32),
                pltpu.VMEM((2, 1, BLOCK), f32),
                pltpu.VMEM((PAIR, BLOCK), f32),
            ],
        ),
        out_shape=[
            jax.ShapeDtypeStruct((length, width), bf16),
            jax.ShapeDtypeStruct((2 * pairs, blocks, 1, BLOCK), f32),
        ],
        compiler_params=pltpu.CompilerParams(vmem_limit_bytes=48 << 20),
        cost_estimate=pl.CostEstimate(
            flops=4 * length * length * width, bytes_accessed=8 * length * width, transcendentals=length * length * width // HEAD
        ),
        name="attend",
    )(flags, qkv, qkv, qkv, seg_rows, seg_cols)


def attend_backward(flags, qkv, grad, mixed, lse, seg_rows, seg_cols, cosine, sine):
    _, length, width = qkv.shape
    blocks, pairs = length // BLOCK, width // PAIR
    whole = pl.BlockSpec((length, PAIR), lambda p, *_: (0, p))
    table = pl.BlockSpec((length, PAIR), lambda p, *_: (0, 0))
    return pl.pallas_call(
        backward_kernel,
        grid_spec=pltpu.PrefetchScalarGridSpec(
            num_scalar_prefetch=1,
            grid=(pairs,),
            in_specs=[
                *pieces_of(qkv, length),
                whole,
                whole,
                pl.BlockSpec((2, blocks, 1, BLOCK), lambda p, *_: (p, 0, 0, 0)),
                pl.BlockSpec((blocks, 1, BLOCK), lambda p, *_: (0, 0, 0)),
                table,
                table,
                table,
            ],
            out_specs=pl.BlockSpec((3, length, PAIR), lambda p, *_: (0, 0, p)),
            scratch_shapes=[
                pltpu.VMEM((blocks, PAIR, BLOCK), bf16),
                pltpu.VMEM((length, PAIR), f32),
                pltpu.VMEM((length, PAIR), f32),
                pltpu.VMEM((PAIR, BLOCK), f32),
            ],
        ),
        out_shape=jax.ShapeDtypeStruct((3, length, width), bf16),
        compiler_params=pltpu.CompilerParams(vmem_limit_bytes=56 << 20),
        cost_estimate=pl.CostEstimate(
            flops=10 * length * length * width, bytes_accessed=16 * length * width, transcendentals=length * length * width // HEAD
        ),
        name="attend_back",
    )(flags, qkv, qkv, qkv, grad, mixed, lse, seg_rows, seg_cols, cosine, sine)


MESH = pl.DeviceIdType.MESH
ADD_ROWS = 32
STEPS = 9
EDGES = 4


def add_low(a, a_at, b, rows):
    @pl.loop(0, rows // ADD_ROWS)
    def _(i):
        at = pl.ds(pl.multiple_of(i * ADD_ROWS, ADD_ROWS), ADD_ROWS)
        kept = a[pl.ds(pl.multiple_of(a_at + i * ADD_ROWS, ADD_ROWS), ADD_ROWS), :].astype(f32)
        b[at, :] = (kept + b[at, :].astype(f32)).astype(bf16)


class Unit:
    def __init__(self, part, out, column, got, send, recv, local, place, bits=(0, 1, 2, 3)):
        self.part, self.out, self.got = part, out, got
        self.send, self.recv, self.local = send, recv, local
        self.rows, columns = 2 * got[0].shape[0], got[0].shape[1]
        self.columns = pl.ds(column, columns)
        self.bit = [(place // (1 << b)) % 2 for b in bits]
        self.partner = [place + (1 - 2 * bit) * (1 << b) for bit, b in zip(self.bit, bits, strict=True)]
        self.base = [0]
        for b in range(EDGES):
            self.base.append(self.base[-1] + self.bit[b] * (self.rows >> (b + 1)))

    def remote(self, src, dst, stage, b):
        return pltpu.make_async_remote_copy(
            src_ref=src,
            dst_ref=dst,
            send_sem=self.send.at[stage],
            recv_sem=self.recv.at[stage],
            device_id={"dp": self.partner[b]},
            device_id_type=MESH,
        )

    def halving(self, b):
        half = self.rows >> (b + 1)
        source = self.part if b == 0 else self.got[b - 1]
        away = pl.ds(pl.multiple_of((1 - self.bit[b]) * half, ADD_ROWS), half)
        return self.remote(source.at[away], self.got[b], b, b)

    def spot(self, b):
        size = self.rows >> (b + 1)
        return self.out.at[pl.ds(pl.multiple_of(self.base[b + 1], ADD_ROWS), size), self.columns]

    def own(self):
        return pltpu.make_async_copy(self.got[3], self.spot(3), self.local.at[0])

    def gathering(self, b):
        return self.remote(self.got[3] if b == 3 else self.spot(b), self.spot(b), 7 - b, b)

    def step(self, k):
        if k == 0:
            self.halving(0).start()
        elif k < 5:
            b = k - 1
            self.halving(b).wait()
            half = self.rows >> (b + 1)
            add_low(self.part if b == 0 else self.got[b - 1], self.bit[b] * half, self.got[b], half)
            if b < 3:
                self.halving(b + 1).start()
            else:
                self.own().start()
                self.gathering(3).start()
        elif k == 5:
            self.own().wait()
            self.gathering(3).wait()
            self.gathering(2).start()
        elif k < 8:
            self.gathering(8 - k).wait()
            self.gathering(7 - k).start()
        else:
            self.gathering(0).wait()


def unit_scratch(rows, columns):
    return [
        *[pltpu.VMEM((rows >> (b + 1), columns), bf16) for b in range(EDGES)],
        pltpu.SemaphoreType.DMA((2 * EDGES,)),
        pltpu.SemaphoreType.DMA((2 * EDGES,)),
        pltpu.SemaphoreType.DMA((1,)),
    ]


def greet(targets):
    barrier = pltpu.get_barrier_semaphore()
    for target in targets:
        pl.semaphore_signal(barrier, inc=1, device_id=target, device_id_type=MESH)
    pl.semaphore_wait(barrier, len(targets))


ORDER = (
    (3, 0, 1), (6, 1, 1), (7, 0, 2), (8, 2, 1), (8, 0, 3), (8, 1, 2), (9, 1, 3), (10, 0, 4), (10, 3, 1), (10, 1, 4),
    (10, 2, 2), (10, 4, 1), (11, 0, 5), (13, 1, 5), (13, 2, 3), (15, 2, 4), (15, 0, 6), (15, 3, 2), (15, 1, 6),
    (18, 2, 5), (19, 5, 1), (19, 3, 3), (20, 4, 2), (20, 2, 6), (21, 3, 4), (22, 4, 3), (23, 5, 2), (24, 6, 1),
    (24, 3, 5), (26, 7, 1), (26, 2, 7), (26, 4, 4), (28, 6, 2), (28, 8, 1), (28, 1, 7), (29, 5, 3), (29, 2, 8),
    (29, 4, 5), (29, 3, 6), (29, 6, 3), (29, 0, 7), (29, 1, 8), (30, 7, 2), (32, 5, 4), (32, 8, 2), (32, 4, 6),
    (32, 7, 3), (32, 5, 5), (32, 6, 4), (32, 7, 4), (33, 8, 3), (33, 3, 7), (33, 5, 6), (33, 6, 5), (34, 4, 7),
    (34, 7, 5), (34, 0, 8), (34, 8, 4), (35, 4, 8), (35, 6, 6), (35, 8, 5), (35, 7, 6), (36, 8, 6), (36, 6, 7),
    (36, 5, 7), (37, 8, 7), (38, 7, 7), (99, 6, 8), (99, 5, 8), (99, 7, 8), (99, 3, 8), (99, 8, 8),
)
WIDE = 512
STEP_ROWS = 64


def vectors_of(product, bias, depth):
    return [product[:, r * depth : (r + 1) * depth] + bias[:, r * depth : (r + 1) * depth] for r in range(6)]


def fetcher(sems):
    count = [0]

    def fetch(src, dst):
        copy = pltpu.make_async_copy(src, dst, sems.at[count[0]])
        copy.start()
        count[0] += 1
        return copy

    return fetch


def head_kernel(
    tokens_hbm, cot_hbm, w_qkv_hbm, w_out_hbm, w_up_hbm, w_down_hbm,
    mods, b_ada, gain_one, gain_two, cond, b_up, frequency, lengths,
    qkv_out, mixed_out, one_out, back_out, two_out, hidden_out, pre_out, own_grad, send_grad, middle_out,
    projected_out, own_branch, send_branch, lse, known, segr, segc, cosine, sine,
    tokens, cot, w_qkv, w_out, w_up, w_down, rows_one, full_back, rows_two, qkv, mixed, from_sum, send_sum, projected,
    middle, hidden, pre, grads, branch, low_grads, low_branch, bias, bias_down, load, x_send, x_recv,
):
    me = lax.axis_index("tensor")
    length, depth = rows_one.shape
    chunks, half, _ = from_sum.shape
    chunk = 2 * half
    width = mixed.shape[1]
    pairs = width // PAIR
    across = {"tensor": 1 - me}
    each = range(chunks)
    own = [slice(c * chunk, c * chunk + half) for c in each]
    got = [slice(c * chunk + half, (c + 1) * chunk) for c in each]
    whole = [slice(c * chunk, (c + 1) * chunk) for c in each]
    fetch = fetcher(load)

    def x_copy(src, dst, i):
        return pltpu.make_async_remote_copy(
            src_ref=src, dst_ref=dst, send_sem=x_send.at[i], recv_sem=x_recv.at[i],
            device_id=across, device_id_type=MESH,
        )

    ones = [x_copy(rows_one.at[own[c]], rows_one.at[got[c]], c) for c in each]
    backs = [x_copy(full_back.at[own[c]], full_back.at[got[c]], chunks + c) for c in each]
    shares = [x_copy(send_sum.at[c], from_sum.at[c], 2 * chunks + c) for c in each]
    twos = [x_copy(rows_two.at[own[c]], rows_two.at[got[c]], 3 * chunks + c) for c in each]

    shift_a, scale_a, gate_a, shift_m, scale_m, gate_m = vectors_of(mods, b_ada, depth)
    gain_one, gain_two = gain_one[...], gain_two[...]
    reads = [fetch(tokens_hbm, tokens), fetch(w_qkv_hbm, w_qkv), fetch(cot_hbm, cot)]
    reads += [fetch(w_out_hbm, w_out), fetch(w_up_hbm, w_up), fetch(w_down_hbm, w_down)]
    writes = []
    greet([across])

    def normal_of(values):
        center = values - jnp.mean(values, axis=1, keepdims=True)
        return center * lax.rsqrt(jnp.mean(center * center, axis=1, keepdims=True) + norm_eps)

    def by_rows(work):
        @pl.loop(0, half // STEP_ROWS)
        def _(i):
            work(pl.multiple_of(i * STEP_ROWS, STEP_ROWS))

    reads[0].wait()
    for c in each:

        def first_norm(at, c=c):
            values = tokens[pl.ds(c * half + at, STEP_ROWS), :].astype(f32)
            out = normal_of(values) * gain_one * (1.0 + scale_a) + shift_a
            rows_one[pl.ds(c * chunk + at, STEP_ROWS), :] = out.astype(bf16)

        by_rows(first_norm)
        if c == 0:
            ones[c].start()
    reads[2].wait()
    bias_down[...] = jnp.zeros(bias_down.shape, f32)
    for c in each:

        def weigh(at, c=c):
            low = (cot[pl.ds(c * half + at, STEP_ROWS), :].astype(f32) * gate_m).astype(bf16)
            full_back[pl.ds(c * chunk + at, STEP_ROWS), :] = low
            bias_down[...] += jnp.sum(low.astype(f32), axis=0, keepdims=True)

        by_rows(weigh)

    starts = [0]
    for n in range(lengths.shape[1] - 1):
        starts.append(starts[-1] + lengths[0, n])

    def place_of(step):
        at = step % chunk
        return jnp.where(at < half, me, 1 - me) * (chunks * half) + (step // chunk) * half + at % half

    def document_of(place):
        return sum((place >= start).astype(jnp.int32) for start in starts[1:])

    segr[...] = document_of(place_of(lax.broadcasted_iota(jnp.int32, segr.shape, 1)))

    @pl.loop(0, length // STEP_ROWS)
    def _(i):
        at = pl.multiple_of(i * STEP_ROWS, STEP_ROWS)
        place = place_of(at + lax.broadcasted_iota(jnp.int32, (STEP_ROWS, PAIR), 0))
        first = functools.reduce(jnp.maximum, [jnp.where(place >= start, start, 0) for start in starts])
        angles = (place - first).astype(f32) * frequency[...]
        rows = pl.ds(at, STEP_ROWS)
        segc[rows, :] = document_of(place)
        cosine[rows, :] = jnp.cos(angles)
        sine[rows, :] = jnp.sin(angles)

    reads[1].wait()

    def project(c):
        rows = whole[c]
        for t in range(3):
            y = mm(rows_one[rows, :], w_qkv[t], 1, 0)
            if t == 2:
                qkv[t, rows, :] = y.astype(bf16)
                continue
            for p in range(pairs):
                lanes = slice(p * PAIR, (p + 1) * PAIR)
                u = y[:, lanes]
                low = (u * cosine[rows, :] + turned(u) * sine[rows, :]).astype(bf16)
                qkv[t, rows, lanes] = low * jnp.asarray(HEAD**-0.5 if t == 0 else 1.0, bf16)

    ones[0].wait()
    ones[1].start()
    project(0)
    ones[1].wait()
    backs[0].start()
    project(1)
    writes.append(fetch(rows_one, one_out))
    writes.append(fetch(qkv, qkv_out))

    def attend(p, c):
        lanes = pl.ds(pl.multiple_of(p * PAIR, PAIR), PAIR)
        q = qkv[0, whole[c], lanes]
        docs = segr[:, whole[c]]
        outs = []
        for h in range(2):
            qh = head_lanes(q, h)
            scores = []
            for b in range(0, length, BLOCK):
                same = jnp.concatenate([segc[b : b + BLOCK, :]] * (chunk // 128), axis=1) == docs
                scores.append(jnp.where(same, mm(qkv[1, b : b + BLOCK, lanes], qh, 1, 1), masked_score))
            top = functools.reduce(jnp.maximum, [jnp.max(s, axis=0, keepdims=True) for s in scores])
            total, summed = 0.0, 0.0
            for i, s in enumerate(scores):
                pr = jnp.exp(s - top)
                total = total + jnp.sum(pr, axis=0, keepdims=True)
                v = transposed(qkv[2, i * BLOCK : (i + 1) * BLOCK, lanes]).astype(bf16)
                summed = summed + mm(v[h * HEAD : (h + 1) * HEAD, :], pr.astype(bf16), 1, 0)
            lse[c, 2 * p + h] = top + jnp.log(total)
            outs.append(summed / total)
        mixed[whole[c], lanes] = jnp.concatenate(outs, axis=0).T.astype(bf16)

    for c in each:

        @pl.loop(0, pairs)
        def _(p):
            attend(p, c)

        if c == 0:
            reads[3].wait()
        send_sum[c] = mm(mixed[got[c], :], w_out[...], 1, 0).astype(bf16)
        shares[c].start()
        projected[c] = mm(mixed[own[c], :], w_out[...], 1, 0)
    writes.append(fetch(mixed, mixed_out))

    def second_norm(c):
        shares[c].wait()

        def work(at):
            rows = pl.ds(at, STEP_ROWS)
            share = projected[c, rows, :] + from_sum[c, rows, :].astype(f32)
            projected[c, rows, :] = share
            values = tokens[pl.ds(c * half + at, STEP_ROWS), :].astype(f32) + gate_a * share
            middle[c, rows, :] = values
            out = normal_of(values) * gain_two * (1.0 + scale_m) + shift_m
            rows_two[pl.ds(c * chunk + at, STEP_ROWS), :] = out.astype(bf16)

        by_rows(work)
        twos[c].start()

    cubic, root = 0.044715, (2.0 / jnp.pi) ** 0.5
    tile = 2 * WIDE
    bias[...] = jnp.zeros(bias.shape, f32)
    held = [[], []]

    def feed_forward(slot, rows):
        for copy in held[slot]:
            copy.wait()

        @pl.loop(0, w_up.shape[1] // tile)
        def _(t):
            at = pl.ds(pl.multiple_of(t * tile, tile), tile)
            u = mm(rows_two[rows, :], w_up[:, at], 1, 0) + b_up[:, at]
            square = u * u
            t_h = jnp.tanh(u * (root + (root * cubic) * square))
            rising = 0.5 * (1.0 + t_h)
            low_hidden = (u * rising).astype(bf16)
            slope = rising + (0.5 * u) * (1.0 - t_h * t_h) * (root + (3.0 * cubic * root) * square)
            low = (mm(full_back[rows, :], w_down[at, :], 1, 1) * slope).astype(bf16)
            hidden[slot, :, at] = low_hidden
            pre[slot, :, at] = low
            bias[:, at] += jnp.sum(low.astype(f32), axis=0, keepdims=True)
            more, more_branch = mm(low, w_up[:, at], 1, 1), mm(low_hidden, w_down[at, :], 1, 0)

            @pl.when(t == 0)
            def _():
                grads[slot] = more
                branch[slot] = more_branch

            @pl.when(t > 0)
            def _():
                grads[slot] += more
                branch[slot] += more_branch

        held[slot] = [fetch(hidden.at[slot], hidden_out.at[rows]), fetch(pre.at[slot], pre_out.at[rows])]

    second_norm(0)
    for read in reads[4:]:
        read.wait()
    for c in each:
        if c:
            second_norm(c)
        feed_forward(c, own[c])
        held[c] += [fetch(grads.at[c], own_grad.at[c]), fetch(branch.at[c], own_branch.at[c])]
    writes.append(fetch(middle, middle_out))
    writes.append(fetch(projected, projected_out))
    for c in each:
        twos[c].wait()
        backs[c].wait()
        if c == 0:
            backs[1].start()
        feed_forward(c, got[c])
        low_grads[c] = grads[c].astype(bf16)
        low_branch[c] = branch[c].astype(bf16)
        writes += [fetch(low_grads.at[c], send_grad.at[c]), fetch(low_branch.at[c], send_branch.at[c]), *held[c]]
    writes += [fetch(full_back, back_out), fetch(rows_two, two_out)]
    known[...] = jnp.concatenate(
        [
            jnp.zeros((8, depth), f32), bias_down[...], bias[:, :depth], bias[:, depth:],
            jnp.concatenate([cond[...].astype(f32), jnp.zeros((1, depth - cond.shape[1]), f32)], axis=1),
            jnp.zeros((4, depth), f32),
        ],
        axis=0,
    )
    for copy in writes:
        copy.wait()


def head(tokens, cot, w_qkv, w_out, w_up, w_down, *near_args, chunks):
    own, depth = tokens.shape
    length, width, wide = 2 * own, w_qkv.shape[2], w_up.shape[1]
    half = own // chunks
    anywhere, near = pl.BlockSpec(memory_space=pl.ANY), pl.BlockSpec(memory_space=pltpu.VMEM)
    shaped, kept = jax.ShapeDtypeStruct, pltpu.VMEM
    parts, rows = (chunks, half, depth), (length, depth)
    return pl.pallas_call(
        head_kernel,
        in_specs=[anywhere] * 6 + [near] * (len(near_args) - 1) + [pl.BlockSpec(memory_space=pltpu.SMEM)],
        out_specs=[anywhere] * 13 + [near] * 6,
        out_shape=[
            shaped((3, length, width), bf16), shaped((length, width), bf16), *[shaped(rows, bf16)] * 3,
            *[shaped((length, wide), bf16)] * 2, shaped(parts, f32), shaped(parts, bf16),
            shaped(parts, f32), shaped(parts, f32), shaped(parts, f32), shaped(parts, bf16),
            shaped((chunks, width // HEAD, 1, length // chunks), f32), shaped((16, depth), f32),
            shaped((1, length), jnp.int32), shaped((length, PAIR), jnp.int32), *[shaped((length, PAIR), f32)] * 2,
        ],
        scratch_shapes=[
            kept(tokens.shape, bf16), kept(tokens.shape, bf16), kept(w_qkv.shape, bf16), kept(w_out.shape, bf16),
            kept(w_up.shape, bf16), kept(w_down.shape, bf16), *[kept(rows, bf16)] * 3, kept((3, length, width), bf16),
            kept((length, width), bf16), kept(parts, bf16), kept(parts, bf16), kept(parts, f32), kept(parts, f32),
            *[kept((chunks, half, wide), bf16)] * 2, *[kept(parts, f32)] * 2,
            kept(parts, bf16), kept(parts, bf16), kept((1, wide), f32), kept((1, depth), f32),
            pltpu.SemaphoreType.DMA((32,)),
            pltpu.SemaphoreType.DMA((4 * chunks,)), pltpu.SemaphoreType.DMA((4 * chunks,)),
        ],
        compiler_params=pltpu.CompilerParams(collective_id=2, has_side_effects=True, vmem_limit_bytes=61 << 20),
        name="head",
    )(tokens, cot, w_qkv, w_out, w_up, w_down, *near_args)


def tail_kernel(
    hidden, full_back, rows_two, grad_pre, qkv_hbm, mixed_hbm, rows_hbm, w_qkv_hbm, w_out_hbm,
    own_grad, send_grad, mid_hbm, proj_hbm, own_branch, send_branch, tokens_hbm, cot_hbm,
    mods, b_ada, gain_one, gain_two, b_down, known, lse, segr, segc, cosine, sine,
    down_sum, up_sum, out_sum, q_sum, k_sum, v_sum, output, grad_x, everyone,
    qkv, mixed, rows_one, w_qkv, w_out, proj, mix_grad, d_qkv, dk, dv, from_x, grads, middle, projected, tokens, cot,
    part_a, part_b, part_c, part_d, part_e, branch_got, col_sums, small, small_got,
    load, store, x_send, x_recv, all_send, all_recv, *more,
):
    place, me = lax.axis_index("dp"), lax.axis_index("tensor")
    length, depth = rows_one.shape
    chunks, half, _ = from_x.shape
    chunk = 2 * half
    width = mixed.shape[1]
    pairs = width // PAIR
    across = {"tensor": 1 - me}

    specs = [
        (part_a.at[pl.ds(0, WIDE)], down_sum.at[pl.ds(0, WIDE)], 0),
        (part_a.at[pl.ds(WIDE, WIDE)], down_sum.at[pl.ds(WIDE, WIDE)], 0),
        (part_b, down_sum.at[pl.ds(depth, depth)], 0),
        (part_c, up_sum, 0), (part_d, up_sum, depth), (part_e, out_sum, 0),
        (qkv.at[2], v_sum, 0), (qkv.at[1], k_sum, 0), (qkv.at[0], q_sum, 0),
    ]
    units = []
    for i, (part, out, column) in enumerate(specs):
        *got, send, recv, local = more[7 * i : 7 * (i + 1)]
        units.append(Unit(part, out, column, got, send, recv, local, place))

    def x_copy(src, dst, i):
        return pltpu.make_async_remote_copy(
            src_ref=src, dst_ref=dst, send_sem=x_send.at[i], recv_sem=x_recv.at[i],
            device_id=across, device_id_type=MESH,
        )

    each = range(chunks)
    grads_in = [x_copy(send_grad.at[c], from_x.at[c], c) for c in each]
    projs = [x_copy(proj.at[c, :half], proj.at[c, half:], chunks + c) for c in each]
    ones = [x_copy(proj.at[c, :half], from_x.at[c], 2 * chunks + c) for c in each]
    branches = [x_copy(send_branch.at[c], branch_got.at[c], 3 * chunks + c) for c in each]
    smalls = x_copy(small, small_got, 4 * chunks)
    outputs = [
        pltpu.make_async_copy(branch_got.at[c], output.at[c * half : (c + 1) * half], store.at[c]) for c in each
    ]
    partner = units[0].partner

    fetch = fetcher(load)
    done = [0]

    def until(place_now):
        while done[0] < len(ORDER) and ORDER[done[0]][0] <= place_now:
            _, i, k = ORDER[done[0]]
            units[i].step(k)
            done[0] += 1

    greet([*[{"dp": p} for p in partner], across])
    grads_in[0].start()
    slots = [w_qkv.at[0], w_qkv.at[1], w_qkv.at[2], d_qkv.at[2]]
    cut = lambda t: slice(t * WIDE, (t + 1) * WIDE)
    backs = fetch(full_back, rows_one)
    hiddens = [fetch(hidden.at[:, cut(t)], slots[t]) for t in range(4)]
    norms = [
        [fetch(src, dst.at[c]) for src, dst in (
            (own_grad.at[c], grads), (mid_hbm.at[c], middle), (proj_hbm.at[c], projected),
            (tokens_hbm.at[c * half : (c + 1) * half], tokens), (cot_hbm.at[c * half : (c + 1) * half], cot),
        )]
        for c in each
    ]
    twos = [fetch(rows_two.at[:, cut(t)], d_qkv.at[t]) for t in range(2)]
    col_sums[...] = jnp.zeros(col_sums.shape, f32)

    backs.wait()
    pres = []
    for t in range(4):
        until(1 + t)
        hiddens[t].wait()
        part = (part_a, part_b)[t // 2]

        @pl.loop(0, WIDE // 256)
        def _(r):
            at = pl.ds(pl.multiple_of(r * 256, 256), 256)
            to = pl.ds(pl.multiple_of((t % 2) * WIDE + r * 256, 256), 256)
            part[to, :] = mm(slots[t][:, at], rows_one[...], 0, 0).astype(bf16)

        pres.append(fetch(grad_pre.at[:, cut(t)], slots[t]))
        if t != 2:
            units[min(t, 2)].step(0)
    main = [
        fetch(w_out_hbm, w_out), fetch(mixed_hbm, mixed), fetch(qkv_hbm, qkv), fetch(rows_hbm, rows_one),
    ]

    def up_part(t):
        pres[t].wait()
        part = (part_c, part_d)[t // 2]

        @pl.loop(0, depth // 256)
        def _(r):
            to = pl.ds(pl.multiple_of(r * 256, 256), 256)
            at = pl.ds(pl.multiple_of((r % 2) * 256, 256), 256)
            part[to, cut(t % 2)] = mm(d_qkv[r // 2, :, at], slots[t][...], 0, 0).astype(bf16)

    def fold(row, values):
        col_sums[row : row + 1, :] += jnp.sum(values, axis=0, keepdims=True)

    def norm_back(grad, values, weight):
        center = values - jnp.mean(values, axis=1, keepdims=True)
        root = lax.rsqrt(jnp.mean(center * center, axis=1, keepdims=True) + norm_eps)
        normal = center * root
        inner = grad * weight
        back = inner - jnp.mean(inner, axis=1, keepdims=True) - normal * jnp.mean(inner * normal, axis=1, keepdims=True)
        return root * back, normal

    _, scale_a, gate_a, _, scale_m, gate_m = vectors_of(mods, b_ada, depth)
    gain_one, gain_two, b_down = gain_one[...], gain_two[...], b_down[...]

    def second_norm(c):
        for copy in norms[c]:
            copy.wait()

        @pl.loop(0, half // STEP_ROWS)
        def _(i):
            at = pl.ds(pl.multiple_of(i * STEP_ROWS, STEP_ROWS), STEP_ROWS)
            grad = grads[c, at, :] + from_x[c, at, :].astype(f32)
            back, normal = norm_back(grad, middle[c, at, :], gain_two * (1.0 + scale_m))
            total = back + cot[c, at, :].astype(f32)
            grads[c, at, :] = total
            proj[c, at, :] = (total * gate_a).astype(bf16)
            fold(0, grad)
            fold(1, grad * normal)
            fold(2, total * projected[c, at, :])

        projs[c].start()

    for copy in twos:
        copy.wait()
    until(5)
    up_part(0)
    until(6)
    up_part(1)
    units[3].step(0)
    until(7)
    grads_in[0].wait()
    grads_in[1].start()
    second_norm(0)
    owns = [fetch(own_branch.at[0], projected.at[0])]
    until(8)
    up_part(2)
    until(9)
    up_part(3)
    units[4].step(0)
    weights = fetch(w_qkv_hbm, w_qkv)
    until(10)
    grads_in[1].wait()
    second_norm(1)
    owns.append(fetch(own_branch.at[1], projected.at[1]))

    def turn_back(u, rows):
        return (u * cosine[rows, :] - turned(u) * sine[rows, :]).astype(bf16)

    def attend_back(p, c):
        lanes = pl.ds(pl.multiple_of(p * PAIR, PAIR), PAIR)
        rows = slice(c * chunk, (c + 1) * chunk)
        q, g = qkv[0, rows, lanes], mix_grad[rows, lanes]
        both = (g.astype(f32) * mixed[rows, lanes].astype(f32)).T
        qh = [head_lanes(q, h) for h in range(2)]
        gh = [head_lanes(g, h) for h in range(2)]
        delta = [jnp.sum(both[h * HEAD : (h + 1) * HEAD, :], axis=0, keepdims=True) for h in range(2)]
        q_two, g_two = jnp.concatenate(qh, axis=0), jnp.concatenate(gh, axis=0)
        docs = segr[:, rows]
        dq = [0.0, 0.0]
        for b in range(0, length, BLOCK):
            cols = slice(b, b + BLOCK)
            k, v = qkv[1, cols, lanes], qkv[2, cols, lanes]
            turned_k = transposed(k).astype(bf16)
            same = jnp.concatenate([segc[cols, :]] * (chunk // 128), axis=1) == docs
            ps, ds = [], []
            for h in range(2):
                s = jnp.where(same, mm(k, qh[h], 1, 1), masked_score)
                pr = jnp.exp(s - lse[c, 2 * p + h])
                d = (pr * (mm(v, gh[h], 1, 1) - delta[h])).astype(bf16)
                ps.append(pr.astype(bf16))
                ds.append(d)
                dq[h] = dq[h] + mm(turned_k[h * HEAD : (h + 1) * HEAD, :], d, 1, 0)
            add_v = mm(jnp.concatenate(ps, axis=1), g_two, 1, 0)
            add_k = mm(jnp.concatenate(ds, axis=1), q_two, 1, 0)
            if c < chunks - 1:
                dv[cols, lanes] = add_v if c == 0 else dv[cols, lanes] + add_v
                dk[cols, lanes] = add_k if c == 0 else dk[cols, lanes] + add_k
            else:
                d_qkv[1, cols, lanes] = turn_back(dk[cols, lanes] + add_k, cols)
                d_qkv[2, cols, lanes] = (dv[cols, lanes] + add_v).astype(bf16)
        d_qkv[0, rows, lanes] = turn_back(jnp.concatenate(dq, axis=0).T * (HEAD**-0.5), rows)

    for copy in main:
        copy.wait()
    now = 11
    for c in each:
        until(now)
        projs[c].wait()
        if c == chunks - 1:
            for copy in branches:
                copy.start()
        mix_grad[c * chunk : (c + 1) * chunk, :] = mm(proj[c], w_out[...], 1, 1).astype(bf16)
        now += 1
        if c == chunks - 1:
            until(now)

            @pl.loop(0, width // 256)
            def _(r):
                at = pl.ds(pl.multiple_of(r * 256, 256), 256)
                part_e[at, :] = sum(
                    mm(mixed[n * chunk : (n + 1) * chunk, at], proj[n], 0, 0) for n in each
                ).astype(bf16)

            units[5].step(0)
            now += 1

        @pl.loop(0, pairs)
        def _(p):
            for n in range(pairs):

                @pl.when(p == n)
                def _():
                    until(now + n)

            attend_back(p, c)

        now += pairs

    def rows_back(start):
        at = slice(start, start + half)
        return sum(mm(d_qkv[t, at, :], w_qkv[t], 1, 1) for t in range(3))

    for i in range(3):
        until(now + i)

        @pl.loop(0, depth // 256)
        def _(r):
            at = pl.ds(pl.multiple_of(r * 256, 256), 256)
            qkv[2 - i, at, :] = mm(rows_one[:, at], d_qkv[2 - i], 0, 0).astype(bf16)

        units[6 + i].step(0)
    now += 3
    weights.wait()
    for c in each:
        until(now + c)
        proj[c, :half] = rows_back(c * chunk + half).astype(bf16)
        if c == 0:
            ones[c].start()
    now += chunks
    for c in each:
        until(now + c)
        branches[c].wait()
        owns[c].wait()

        @pl.loop(0, half // STEP_ROWS)
        def _(i):
            at = pl.ds(pl.multiple_of(i * STEP_ROWS, STEP_ROWS), STEP_ROWS)
            branch = projected[c, at, :] + branch_got[c, at, :].astype(f32) + b_down
            branch_got[c, at, :] = (middle[c, at, :] + gate_m * branch).astype(bf16)
            fold(5, cot[c, at, :].astype(f32) * branch)

        outputs[c].start()
    now += chunks
    for c in each:
        until(now + c)
        projected[c] = rows_back(c * chunk)
    now += chunks
    for c in each:
        until(now + c)
        ones[c].wait()
        if c < chunks - 1:
            ones[c + 1].start()

        @pl.loop(0, half // STEP_ROWS)
        def _(i):
            at = pl.ds(pl.multiple_of(i * STEP_ROWS, STEP_ROWS), STEP_ROWS)
            grad = projected[c, at, :] + from_x[c, at, :].astype(f32)
            back, normal = norm_back(grad, tokens[c, at, :].astype(f32), gain_one * (1.0 + scale_a))
            grad_x[c, at, :] = (back + grads[c, at, :]).astype(bf16)
            fold(3, grad)
            fold(4, grad * normal)

    now += chunks
    shift, scaled, gated, shift_one, scaled_one, gated_m = [col_sums[r : r + 1, :] for r in range(6)]
    small[...] = known[...] + jnp.concatenate(
        [
            shift_one, gain_one * scaled_one, gated, shift, gain_two * scaled, gated_m,
            (1.0 + scale_a) * scaled_one, (1.0 + scale_m) * scaled, jnp.zeros((8, depth), f32),
        ],
        axis=0,
    )
    smalls.start()
    until(now)
    smalls.wait()
    number = lax.broadcasted_iota(jnp.int32, small.shape, 0)
    everyone[0] = small[...] + jnp.where(number < 9, small_got[...], 0.0)
    for n, b in enumerate((1, 3, 2, 0)):
        copy = pltpu.make_async_remote_copy(
            src_ref=everyone.at[pl.ds(0, 1 << n)], dst_ref=everyone.at[pl.ds(1 << n, 1 << n)],
            send_sem=all_send.at[n], recv_sem=all_recv.at[n],
            device_id={"dp": partner[b]}, device_id_type=MESH,
        )
        copy.start()
        until(now + 1 + n)
        copy.wait()
    until(1000)
    for copy in outputs:
        copy.wait()


def tail(*args):
    hidden, qkv, rows_one, w_qkv, w_out, own_grad, tokens = (args[n] for n in (0, 4, 6, 7, 8, 9, 15))
    known = args[22]
    _, length, width = qkv.shape
    chunks, half, depth = own_grad.shape
    anywhere, near = pl.BlockSpec(memory_space=pl.ANY), pl.BlockSpec(memory_space=pltpu.VMEM)
    shaped, kept = jax.ShapeDtypeStruct, pltpu.VMEM
    in_chunks = (chunks, half, depth)
    scratch = [
        kept(qkv.shape, bf16), kept((length, width), bf16), kept(rows_one.shape, bf16), kept(w_qkv.shape, bf16),
        kept(w_out.shape, bf16), kept((chunks, 2 * half, depth), bf16), kept((length, width), bf16),
        kept((3, length, width), bf16), kept((length, width), f32), kept((length, width), f32),
        kept(in_chunks, bf16), kept(in_chunks, f32), kept(in_chunks, f32), kept(in_chunks, f32),
        kept(in_chunks, bf16), kept(in_chunks, bf16),
        *[kept((depth, depth), bf16)] * 4, kept((width, depth), bf16), kept(in_chunks, bf16),
        kept((8, depth), f32), kept(known.shape, f32), kept(known.shape, f32),
        pltpu.SemaphoreType.DMA((30,)), pltpu.SemaphoreType.DMA((chunks,)),
        pltpu.SemaphoreType.DMA((4 * chunks + 1,)), pltpu.SemaphoreType.DMA((4 * chunks + 1,)),
        pltpu.SemaphoreType.DMA((EDGES,)), pltpu.SemaphoreType.DMA((EDGES,)),
        *unit_scratch(WIDE, depth) * 2, *unit_scratch(depth, depth) * 3, *unit_scratch(width, depth), *unit_scratch(depth, width) * 3,
    ]
    return pl.pallas_call(
        tail_kernel,
        in_specs=[anywhere] * 17 + [near] * 11,
        out_specs=[anywhere] * 7 + [near] * 2,
        out_shape=[
            shaped((hidden.shape[1], depth), bf16), shaped((depth, hidden.shape[1]), bf16), shaped((width, depth), bf16),
            *[shaped((depth, width), bf16)] * 3, shaped(tokens.shape, bf16),
            shaped(in_chunks, bf16), shaped((1 << EDGES, *known.shape), f32),
        ],
        scratch_shapes=scratch,
        compiler_params=pltpu.CompilerParams(collective_id=1, has_side_effects=True, vmem_limit_bytes=61 << 20),
        name="tail",
    )(*args)


def finish_kernel(
    down, up, out, q, k, v, output, grad_x, everyone, w_ada,
    down_sum, up_sum, out_sum, qkv_sum, output_out, grad_x_out, ada, cond_grad, ada_bias, one_gain, two_gain, down_bias,
    up_bias, mods, conds,
):
    depth = everyone.shape[2]

    @pl.when(pl.program_id(0) == 0)
    def _():
        total = sum(everyone[n] for n in range(everyone.shape[0]))
        lanes = 0.0
        for r in range(6):
            span = slice(r * depth, (r + 1) * depth)
            mods[:, span] = jnp.concatenate([everyone[n, r : r + 1, :] for n in range(everyone.shape[0])], axis=0)
            ada_bias[:, span] = total[r : r + 1, :]
            for t in range(0, depth, 128):
                at = r * depth + t
                lanes = lanes + w_ada[:, at : at + 128].astype(f32) * everyone[0, r : r + 1, t : t + 128]
        cond_grad[...] = jnp.sum(lanes.T, axis=0, keepdims=True)
        one_gain[...], two_gain[...], down_bias[...] = total[6:7, :], total[7:8, :], total[8:9, :]
        up_bias[...] = jnp.concatenate([total[9:10, :], total[10:11, :]], axis=1)
        conds[...] = jnp.concatenate(
            [everyone[n, 11:12, : conds.shape[0]] for n in range(everyone.shape[0])], axis=0
        ).T

    down_sum[...] = down[...].astype(f32)
    up_sum[...] = up[...].astype(f32)
    out_sum[...] = out[...].astype(f32)
    for t, part in enumerate((q, k, v)):
        qkv_sum[t] = part[...].astype(f32)
    output_out[...] = output[...]
    grad_x_out[...] = grad_x[...]
    rows = ada.shape[0]
    some = conds[pl.ds(pl.multiple_of(pl.program_id(0) * rows, rows), rows), :]
    ada[...] = lax.dot_general(
        some, mods[...], (((1,), (0,)), ((), ())), precision=lax.Precision.HIGHEST, preferred_element_type=f32
    )


def finish(sums, output, grad_x, everyone, w_ada):
    steps = 8
    down, up, out, q, _, _ = sums
    shaped = jax.ShapeDtypeStruct
    devices, _, depth = everyone.shape

    def rows_of(array):
        return pl.BlockSpec((array.shape[0] // steps, array.shape[1]), lambda i: (i, 0))

    def whole(shape):
        return pl.BlockSpec(shape, lambda i: (0,) * len(shape))

    ones = [(1, n) for n in (w_ada.shape[0], w_ada.shape[1], depth, depth, depth, up.shape[1])]
    return pl.pallas_call(
        finish_kernel,
        grid=(steps,),
        in_specs=[
            *[rows_of(a) for a in (*sums, output, grad_x)], whole(everyone.shape), whole(w_ada.shape),
        ],
        out_specs=[
            rows_of(down), rows_of(up), rows_of(out),
            pl.BlockSpec((3, q.shape[0] // steps, q.shape[1]), lambda i: (0, i, 0)),
            rows_of(output), rows_of(grad_x), rows_of(w_ada), *[whole(s) for s in ones],
        ],
        out_shape=[
            shaped(down.shape, f32), shaped(up.shape, f32), shaped(out.shape, f32), shaped((3, *q.shape), f32),
            shaped(output.shape, bf16), shaped(grad_x.shape, bf16), shaped(w_ada.shape, f32),
            *[shaped(s, f32) for s in ones],
        ],
        scratch_shapes=[pltpu.VMEM((devices, w_ada.shape[1]), f32), pltpu.VMEM((w_ada.shape[0], devices), f32)],
        compiler_params=pltpu.CompilerParams(vmem_limit_bytes=61 << 20),
        name="finish",
    )(*sums, output, grad_x, everyone, w_ada)


def body_pair(
    tokens, cond, doc_lengths, w_ada, b_ada, gain_one, w_qkv, w_out, gain_two, w_up, b_up, w_down, b_down, cotangent
):
    own, width = tokens.shape
    length = 2 * own
    chunks = 2

    exponent = np.arange(HEAD // 2) * (2.0 / HEAD)
    frequency = np.tile(rope_base**-exponent, PAIR // (HEAD // 2))[None, :].astype(np.float32)
    mods = jnp.dot(cond, w_ada, preferred_element_type=f32)
    (
        qkv, mixed, rows_one, full_back, rows_two, hidden, grad_pre, own_grad, send_grad, middle, projected,
        own_branch, send_branch, lse, known, *tables,
    ) = head(
        tokens, cotangent, w_qkv, w_out, w_up, w_down, mods, b_ada[None, :], gain_one[None, :], gain_two[None, :], cond,
        b_up[None, :], frequency, doc_lengths, chunks=chunks,
    )
    *sums, output, grad_x, everyone = tail(
        hidden, full_back, rows_two, grad_pre, qkv, mixed, rows_one, w_qkv, w_out, own_grad, send_grad,
        middle, projected, own_branch, send_branch, tokens, cotangent,
        mods, b_ada[None, :], gain_one[None, :], gain_two[None, :], b_down[None, :], known,
        lse, *tables,
    )
    (
        grad_w_down, grad_w_up, grad_w_out, grad_w_qkv, output, grad_x, grad_w_ada, grad_cond, *rows,
    ) = finish(sums, output, grad_x.reshape(own, width), everyone, w_ada)
    grad_b_ada, grad_gain_one, grad_gain_two, grad_b_down, grad_b_up = [
        row[0] for row in rows
    ]
    return (
        output, grad_x, grad_cond, grad_w_ada, grad_b_ada, grad_gain_one, grad_w_qkv, grad_w_out, grad_gain_two,
        grad_w_up, grad_b_up, grad_w_down, grad_b_down,
    )


def body_any(
    tokens, cond, doc_lengths, w_ada, b_ada, gain_one, w_qkv, w_out, gain_two, w_up, b_up, w_down, b_down, cotangent
):
    tensor_size = lax.axis_size("tensor")
    own = tokens.shape[0]
    length = own * tensor_size

    def all_rows(values):
        return lax.all_gather(values, "tensor", axis=0, tiled=True)

    def own_sum(values):
        return lax.psum_scatter(values, "tensor", scatter_dimension=0, tiled=True)

    def sum_over_dp(part):
        return lax.psum(part, "dp")

    places = jnp.arange(length, dtype=jnp.int32)
    segment, doc_first = documents(doc_lengths[0], places)
    cosine, sine = rope_tables(places - doc_first)
    blocks = length // BLOCK
    in_blocks = segment.reshape(blocks, BLOCK)
    least, most = jnp.min(in_blocks, axis=1), jnp.max(in_blocks, axis=1)
    meets = (least[:, None] <= most[None, :]) & (least[None, :] <= most[:, None])
    flags = meets.astype(jnp.int32).reshape(-1)
    seg_rows = in_blocks[:, None, :]
    seg_cols = jnp.broadcast_to(segment[:, None], (length, 128))

    modulation = jnp.dot(cond, w_ada, preferred_element_type=f32)[0] + b_ada
    shift_a, scale_a, gate_a, shift_m, scale_m, gate_m = jnp.split(modulation, 6)
    x_rows = tokens.astype(f32)
    grad_out = cotangent.astype(f32)

    act_one = modulate(x_rows, gain_one, shift_a, scale_a).astype(bf16)
    rows_one = all_rows(act_one)
    grad_branch = (grad_out * gate_m).astype(bf16)
    full_branch = all_rows(grad_branch)
    qkv = project_qkv(rows_one, w_qkv, cosine, sine)
    mixed, lse = attend_forward(flags, qkv, seg_rows, seg_cols)
    projected = own_sum(jnp.dot(mixed, w_out, preferred_element_type=f32))
    middle = x_rows + gate_a * projected
    rows_two = all_rows(modulate(middle, gain_two, shift_m, scale_m).astype(bf16))
    pre_act = jnp.dot(rows_two, w_up, preferred_element_type=f32) + b_up
    hidden = jax.nn.gelu(pre_act, approximate=True).astype(bf16)

    grad_hidden = jnp.einsum("sd,fd->sf", full_branch, w_down, preferred_element_type=f32)
    _, gelu_back = jax.vjp(lambda values: jax.nn.gelu(values, approximate=True), pre_act)
    grad_pre = gelu_back(grad_hidden)[0].astype(bf16)
    grad_act_two = own_sum(jnp.einsum("sf,df->sd", grad_pre, w_up, preferred_element_type=f32))
    grad_w_down = sum_over_dp(jnp.einsum("sf,sd->fd", hidden, full_branch, preferred_element_type=f32))
    grad_w_up = sum_over_dp(jnp.einsum("sd,sf->df", rows_two, grad_pre, preferred_element_type=f32))

    branch = own_sum(jnp.dot(hidden, w_down, preferred_element_type=f32)) + b_down
    output = (middle + gate_m * branch).astype(bf16)
    grad_gate_m = jnp.sum(grad_out * branch, axis=0)
    grad_b_down = jnp.sum(grad_branch.astype(f32), axis=0)
    grad_b_up = jnp.sum(grad_pre.astype(f32), axis=0)

    _, second_back = jax.vjp(modulate, middle, gain_two, shift_m, scale_m)
    grad_middle, grad_gain_two, grad_shift_m, grad_scale_m = second_back(grad_act_two)
    grad_middle = grad_middle + grad_out
    full_proj = all_rows((grad_middle * gate_a).astype(bf16))
    grad_gate_a = jnp.sum(grad_middle * projected, axis=0)
    grad_mixed = jnp.einsum("sd,ed->se", full_proj, w_out, preferred_element_type=f32).astype(bf16)
    grad_w_out = sum_over_dp(jnp.einsum("se,sd->ed", mixed, full_proj, preferred_element_type=f32))
    grad_qkv = attend_backward(flags, qkv, grad_mixed, mixed, lse, seg_rows, seg_cols, cosine, sine)
    grad_act_one = own_sum(jnp.einsum("tse,tde->sd", grad_qkv, w_qkv, preferred_element_type=f32))
    grad_w_qkv = jnp.einsum("sd,tse->tde", rows_one, grad_qkv, preferred_element_type=f32)
    grad_w_qkv = sum_over_dp(grad_w_qkv.reshape(-1, grad_w_qkv.shape[2])).reshape(grad_w_qkv.shape)

    _, first_back = jax.vjp(modulate, x_rows, gain_one, shift_a, scale_a)
    grad_x, grad_gain_one, grad_shift_a, grad_scale_a = first_back(grad_act_one)
    grad_x = (grad_x + grad_middle).astype(bf16)

    small = jnp.concatenate(
        [
            grad_shift_a, grad_scale_a, grad_gate_a, grad_shift_m, grad_scale_m, grad_gate_m,
            grad_gain_one, grad_gain_two, grad_b_down,
        ]
    )
    small = lax.psum(small, "tensor")
    mod_size = modulation.shape[0]
    grad_mod = small[:mod_size]
    grad_cond = jnp.dot(w_ada.astype(f32), grad_mod, precision=lax.Precision.HIGHEST)[None, :]
    everyone = lax.all_gather(
        jnp.concatenate([small, grad_b_up, cond[0].astype(f32)])[None, :], "dp", axis=0, tiled=True
    )
    conds = everyone[:, -cond.shape[1] :]
    mods = everyone[:, :mod_size]
    grad_w_ada = jnp.einsum("nc,nm->cm", conds, mods, precision=lax.Precision.HIGHEST, preferred_element_type=f32)
    sums = jnp.sum(everyone, axis=0)
    width = tokens.shape[1]
    grad_b_ada = sums[:mod_size]
    grad_gain_one, grad_gain_two, grad_b_down = jnp.split(sums[mod_size : mod_size + 3 * width], 3)
    grad_b_up = sums[mod_size + 3 * width : -cond.shape[1]]
    return (
        output, grad_x, grad_cond, grad_w_ada, grad_b_ada, grad_gain_one, grad_w_qkv, grad_w_out, grad_gain_two,
        grad_w_up, grad_b_up, grad_w_down, grad_b_down,
    )


def solution(mesh):
    swaps = mesh.shape["tensor"] == 2 and mesh.shape["dp"] == 16
    placed = (
        P(("dp", "tensor"), None), P("dp", None), P("dp", None), P(), P(), P(), P(None, None, "tensor"),
        P("tensor", None), P(), P(None, "tensor"), P("tensor"), P("tensor", None), P(), P(("dp", "tensor"), None),
    )
    return jax.shard_map(
        body_pair if swaps else body_any,
        mesh=mesh,
        in_specs=placed,
        out_specs=(
            P(("dp", "tensor"), None), P(("dp", "tensor"), None), P("dp", None), P(), P(), P(),
            P(None, None, "tensor"), P("tensor", None), P(), P(None, "tensor"), P("tensor"), P("tensor", None), P(),
        ),
        check_vma=False,
    )
```

```python
import functools

import jax
import jax.numpy as jnp
import numpy as np
from jax import lax
from jax.experimental import pallas as pl
from jax.experimental.pallas import tpu as pltpu
from jax.sharding import PartitionSpec as P

HEAD = 64
PAIR = 2 * HEAD
BLOCK = 256
ROWS = 512

norm_eps = 1e-05
rope_base = 10000.0
masked_score = -1e30
f32, bf16 = jnp.float32, jnp.bfloat16


def layer_norm(values, gain):
    center = values - jnp.mean(values, axis=-1, keepdims=True)
    spread = jnp.mean(center * center, axis=-1, keepdims=True)
    return center * lax.rsqrt(spread + norm_eps) * gain


def modulate(values, gain, shift, scale):
    return layer_norm(values, gain) * (1.0 + scale) + shift


def documents(lengths, places):
    numbers = jnp.arange(lengths.shape[0], dtype=jnp.int32)
    earlier = (numbers[None, :] < numbers[:, None]).astype(jnp.int32)
    starts = jnp.sum(earlier * lengths[None, :], axis=1)
    ends = starts + lengths
    inside = ((places[:, None] >= starts[None, :]) & (places[:, None] < ends[None, :])).astype(
        jnp.int32
    )
    segment = jnp.sum(inside * numbers[None, :], axis=1)
    doc_first = jnp.sum(inside * starts[None, :], axis=1)
    return segment, doc_first


def rope_tables(offsets):
    exponent = jnp.arange(HEAD // 2, dtype=f32) * (2.0 / HEAD)
    frequency = jnp.power(jnp.float32(rope_base), -exponent)
    angles = offsets.astype(f32)[:, None] * frequency[None, :]
    cosine, sine = jnp.cos(angles), jnp.sin(angles)
    repeat = PAIR // (HEAD // 2)
    return jnp.concatenate([cosine] * repeat, axis=-1), jnp.concatenate([sine] * repeat, axis=-1)


def turned(values):
    lane = lax.broadcasted_iota(jnp.int32, values.shape, 1)
    half = HEAD // 2
    from_right = pltpu.roll(values, PAIR - half, axis=1)
    from_left = pltpu.roll(values, half, axis=1)
    return jnp.where(lane % HEAD < half, -from_right, from_left)


def mm(a, b, da, db):
    return lax.dot_general(a, b, (((da,), (db,)), ((), ())), preferred_element_type=f32)


def qkv_kernel(x_ref, w_ref, cos_ref, sin_ref, o_ref):
    which = pl.program_id(1)
    y = mm(x_ref[...], w_ref[...], 1, 0)

    @pl.when(which < 2)
    def _():
        factor = jnp.where(which == 0, HEAD**-0.5, 1.0)
        for p in range(y.shape[1] // PAIR):
            u = y[:, p * PAIR : (p + 1) * PAIR]
            r = u * cos_ref[...] + turned(u) * sin_ref[...]
            o_ref[:, p * PAIR : (p + 1) * PAIR] = (r.astype(bf16) * factor.astype(bf16)).astype(bf16)

    @pl.when(which == 2)
    def _():
        o_ref[...] = y.astype(bf16)


def project_qkv(rows, w_qkv, cosine, sine):
    count, depth = rows.shape
    width = w_qkv.shape[2]
    return pl.pallas_call(
        qkv_kernel,
        grid=(count // ROWS, 3),
        in_specs=[
            pl.BlockSpec((ROWS, depth), lambda r, t: (r, 0)),
            pl.BlockSpec((None, depth, width), lambda r, t: (t, 0, 0)),
            pl.BlockSpec((ROWS, PAIR), lambda r, t: (r, 0)),
            pl.BlockSpec((ROWS, PAIR), lambda r, t: (r, 0)),
        ],
        out_specs=pl.BlockSpec((None, ROWS, width), lambda r, t: (t, r, 0)),
        out_shape=jax.ShapeDtypeStruct((3, count, width), bf16),
        compiler_params=pltpu.CompilerParams(vmem_limit_bytes=32 << 20),
        cost_estimate=pl.CostEstimate(
            flops=6 * count * depth * width, bytes_accessed=8 * count * width, transcendentals=0
        ),
        name="qkv",
    )(rows, w_qkv, cosine, sine)


def head_lanes(block, h):
    lane = lax.broadcasted_iota(jnp.int32, block.shape, 1)
    return jnp.where(lane // HEAD == h, block, jnp.zeros_like(block))


def transposed(block):
    return block.astype(f32).T


def forward_kernel(flag_ref, q_ref, k_ref, v_ref, segr_ref, segc_ref, o_ref, lse_ref, vt, m, l, acc):
    blocks = q_ref.shape[0] // BLOCK
    for b in range(blocks):
        vt[b] = transposed(v_ref[b * BLOCK : (b + 1) * BLOCK, :]).astype(bf16)

    @pl.loop(0, blocks)
    def _(qi):
        rows = pl.ds(pl.multiple_of(qi * BLOCK, BLOCK), BLOCK)
        q = q_ref[rows, :]
        m[...] = jnp.full(m.shape, masked_score, f32)
        l[...] = jnp.zeros(l.shape, f32)
        acc[...] = jnp.zeros(acc.shape, f32)

        @pl.loop(0, blocks)
        def _(ki):
            @pl.when(flag_ref[qi * blocks + ki] > 0)
            def _():
                cols = pl.ds(pl.multiple_of(ki * BLOCK, BLOCK), BLOCK)
                k = k_ref[cols, :]
                docs = segc_ref[cols, :]
                same = jnp.concatenate([docs] * (BLOCK // 128), axis=1) == segr_ref[qi]
                for h in range(2):
                    lo, hi = h * HEAD, (h + 1) * HEAD
                    s = jnp.where(same, mm(k, head_lanes(q, h), 1, 1), masked_score)
                    top = jnp.maximum(m[h], jnp.max(s, axis=0, keepdims=True))
                    p = jnp.exp(s - top)
                    shrink = jnp.exp(m[h] - top)
                    m[h] = top
                    l[h] = l[h] * shrink + jnp.sum(p, axis=0, keepdims=True)
                    acc[lo:hi, :] = acc[lo:hi, :] * shrink + mm(vt[ki, lo:hi, :], p.astype(bf16), 1, 0)

        for h in range(2):
            lo, hi = h * HEAD, (h + 1) * HEAD
            lse_ref[h, qi] = m[h] + jnp.log(l[h])
            acc[lo:hi, :] = acc[lo:hi, :] / l[h]
        o_ref[rows, :] = acc[...].T.astype(bf16)


def backward_kernel(
    flag_ref, q_ref, k_ref, v_ref, g_ref, o_ref, lse_ref, segr_ref, segc_ref, cos_ref, sin_ref,
    out_ref, kt, dk, dv, dq,
):
    blocks = q_ref.shape[0] // BLOCK
    for b in range(blocks):
        kt[b] = transposed(k_ref[b * BLOCK : (b + 1) * BLOCK, :]).astype(bf16)
    dk[...] = jnp.zeros(dk.shape, f32)
    dv[...] = jnp.zeros(dv.shape, f32)

    def turn_back(u, rows):
        return (u * cos_ref[rows, :] - turned(u) * sin_ref[rows, :]).astype(bf16)

    @pl.loop(0, blocks)
    def _(qi):
        rows = pl.ds(pl.multiple_of(qi * BLOCK, BLOCK), BLOCK)
        q, g = q_ref[rows, :], g_ref[rows, :]
        both = (g.astype(f32) * o_ref[rows, :].astype(f32)).T
        dq[...] = jnp.zeros(dq.shape, f32)

        @pl.loop(0, blocks)
        def _(ki):
            @pl.when(flag_ref[qi * blocks + ki] > 0)
            def _():
                cols = pl.ds(pl.multiple_of(ki * BLOCK, BLOCK), BLOCK)
                k, v = k_ref[cols, :], v_ref[cols, :]
                docs = segc_ref[cols, :]
                same = jnp.concatenate([docs] * (BLOCK // 128), axis=1) == segr_ref[qi]
                dk_sum, dv_sum = dk[cols, :], dv[cols, :]
                for h in range(2):
                    lo, hi = h * HEAD, (h + 1) * HEAD
                    delta = jnp.sum(both[lo:hi, :], axis=0, keepdims=True)
                    qh, gh = head_lanes(q, h), head_lanes(g, h)
                    s = jnp.where(same, mm(k, qh, 1, 1), masked_score)
                    p = jnp.exp(s - lse_ref[h, qi])
                    ds = (p * (mm(v, gh, 1, 1) - delta)).astype(bf16)
                    dv_sum = dv_sum + mm(p.astype(bf16), gh, 1, 0)
                    dk_sum = dk_sum + mm(ds, qh, 1, 0)
                    dq[lo:hi, :] = dq[lo:hi, :] + mm(kt[ki, lo:hi, :], ds, 1, 0)
                dk[cols, :] = dk_sum
                dv[cols, :] = dv_sum

        out_ref[0, rows, :] = turn_back(dq[...].T * (HEAD**-0.5), rows)

    @pl.loop(0, blocks)
    def _(b):
        rows = pl.ds(pl.multiple_of(b * BLOCK, BLOCK), BLOCK)
        out_ref[1, rows, :] = turn_back(dk[rows, :], rows)
        out_ref[2, rows, :] = dv[rows, :].astype(bf16)


def pieces_of(qkv, length):
    return [pl.BlockSpec((None, length, PAIR), functools.partial(lambda t, p, *_: (t, 0, p), t)) for t in range(3)]


def attend_forward(flags, qkv, seg_rows, seg_cols):
    _, length, width = qkv.shape
    blocks, pairs = length // BLOCK, width // PAIR
    return pl.pallas_call(
        forward_kernel,
        grid_spec=pltpu.PrefetchScalarGridSpec(
            num_scalar_prefetch=1,
            grid=(pairs,),
            in_specs=[
                *pieces_of(qkv, length),
                pl.BlockSpec((blocks, 1, BLOCK), lambda p, *_: (0, 0, 0)),
                pl.BlockSpec((length, 128), lambda p, *_: (0, 0)),
            ],
            out_specs=[
                pl.BlockSpec((length, PAIR), lambda p, *_: (0, p)),
                pl.BlockSpec((2, blocks, 1, BLOCK), lambda p, *_: (p, 0, 0, 0)),
            ],
            scratch_shapes=[
                pltpu.VMEM((blocks, PAIR, BLOCK), bf16),
                pltpu.VMEM((2, 1, BLOCK), f32),
                pltpu.VMEM((2, 1, BLOCK), f32),
                pltpu.VMEM((PAIR, BLOCK), f32),
            ],
        ),
        out_shape=[
            jax.ShapeDtypeStruct((length, width), bf16),
            jax.ShapeDtypeStruct((2 * pairs, blocks, 1, BLOCK), f32),
        ],
        compiler_params=pltpu.CompilerParams(vmem_limit_bytes=48 << 20),
        cost_estimate=pl.CostEstimate(
            flops=4 * length * length * width, bytes_accessed=8 * length * width, transcendentals=length * length * width // HEAD
        ),
        name="attend",
    )(flags, qkv, qkv, qkv, seg_rows, seg_cols)


def attend_backward(flags, qkv, grad, mixed, lse, seg_rows, seg_cols, cosine, sine):
    _, length, width = qkv.shape
    blocks, pairs = length // BLOCK, width // PAIR
    whole = pl.BlockSpec((length, PAIR), lambda p, *_: (0, p))
    table = pl.BlockSpec((length, PAIR), lambda p, *_: (0, 0))
    return pl.pallas_call(
        backward_kernel,
        grid_spec=pltpu.PrefetchScalarGridSpec(
            num_scalar_prefetch=1,
            grid=(pairs,),
            in_specs=[
                *pieces_of(qkv, length),
                whole,
                whole,
                pl.BlockSpec((2, blocks, 1, BLOCK), lambda p, *_: (p, 0, 0, 0)),
                pl.BlockSpec((blocks, 1, BLOCK), lambda p, *_: (0, 0, 0)),
                table,
                table,
                table,
            ],
            out_specs=pl.BlockSpec((3, length, PAIR), lambda p, *_: (0, 0, p)),
            scratch_shapes=[
                pltpu.VMEM((blocks, PAIR, BLOCK), bf16),
                pltpu.VMEM((length, PAIR), f32),
                pltpu.VMEM((length, PAIR), f32),
                pltpu.VMEM((PAIR, BLOCK), f32),
            ],
        ),
        out_shape=jax.ShapeDtypeStruct((3, length, width), bf16),
        compiler_params=pltpu.CompilerParams(vmem_limit_bytes=56 << 20),
        cost_estimate=pl.CostEstimate(
            flops=10 * length * length * width, bytes_accessed=16 * length * width, transcendentals=length * length * width // HEAD
        ),
        name="attend_back",
    )(flags, qkv, qkv, qkv, grad, mixed, lse, seg_rows, seg_cols, cosine, sine)


MESH = pl.DeviceIdType.MESH
ADD_ROWS = 32
STEPS = 9
EDGES = 4


def add_low(a, a_at, b, rows):
    @pl.loop(0, rows // ADD_ROWS)
    def _(i):
        at = pl.ds(pl.multiple_of(i * ADD_ROWS, ADD_ROWS), ADD_ROWS)
        kept = a[pl.ds(pl.multiple_of(a_at + i * ADD_ROWS, ADD_ROWS), ADD_ROWS), :].astype(f32)
        b[at, :] = (kept + b[at, :].astype(f32)).astype(bf16)


class Unit:
    def __init__(self, part, out, column, got, send, recv, local, place, bits=(0, 1, 2, 3)):
        self.part, self.out, self.got = part, out, got
        self.send, self.recv, self.local = send, recv, local
        self.rows, columns = 2 * got[0].shape[0], got[0].shape[1]
        self.columns = pl.ds(column, columns)
        self.bit = [(place // (1 << b)) % 2 for b in bits]
        self.partner = [place + (1 - 2 * bit) * (1 << b) for bit, b in zip(self.bit, bits, strict=True)]
        self.base = [0]
        for b in range(EDGES):
            self.base.append(self.base[-1] + self.bit[b] * (self.rows >> (b + 1)))

    def remote(self, src, dst, stage, b):
        return pltpu.make_async_remote_copy(
            src_ref=src,
            dst_ref=dst,
            send_sem=self.send.at[stage],
            recv_sem=self.recv.at[stage],
            device_id={"dp": self.partner[b]},
            device_id_type=MESH,
        )

    def halving(self, b):
        half = self.rows >> (b + 1)
        source = self.part if b == 0 else self.got[b - 1]
        away = pl.ds(pl.multiple_of((1 - self.bit[b]) * half, ADD_ROWS), half)
        return self.remote(source.at[away], self.got[b], b, b)

    def spot(self, b):
        size = self.rows >> (b + 1)
        return self.out.at[pl.ds(pl.multiple_of(self.base[b + 1], ADD_ROWS), size), self.columns]

    def own(self):
        return pltpu.make_async_copy(self.got[3], self.spot(3), self.local.at[0])

    def gathering(self, b):
        return self.remote(self.got[3] if b == 3 else self.spot(b), self.spot(b), 7 - b, b)

    def step(self, k):
        if k == 0:
            self.halving(0).start()
        elif k < 5:
            b = k - 1
            self.halving(b).wait()
            half = self.rows >> (b + 1)
            add_low(self.part if b == 0 else self.got[b - 1], self.bit[b] * half, self.got[b], half)
            if b < 3:
                self.halving(b + 1).start()
            else:
                self.own().start()
                self.gathering(3).start()
        elif k == 5:
            self.own().wait()
            self.gathering(3).wait()
            self.gathering(2).start()
        elif k < 8:
            self.gathering(8 - k).wait()
            self.gathering(7 - k).start()
        else:
            self.gathering(0).wait()


def unit_scratch(rows, columns):
    return [
        *[pltpu.VMEM((rows >> (b + 1), columns), bf16) for b in range(EDGES)],
        pltpu.SemaphoreType.DMA((2 * EDGES,)),
        pltpu.SemaphoreType.DMA((2 * EDGES,)),
        pltpu.SemaphoreType.DMA((1,)),
    ]


def greet(targets):
    barrier = pltpu.get_barrier_semaphore()
    for target in targets:
        pl.semaphore_signal(barrier, inc=1, device_id=target, device_id_type=MESH)
    pl.semaphore_wait(barrier, len(targets))


ORDER = (
    (3, 0, 1), (6, 1, 1), (7, 0, 2), (8, 2, 1), (8, 0, 3), (8, 1, 2), (9, 1, 3), (10, 0, 4), (10, 3, 1), (10, 1, 4),
    (10, 2, 2), (10, 4, 1), (11, 0, 5), (13, 1, 5), (13, 2, 3), (15, 2, 4), (15, 0, 6), (15, 3, 2), (15, 1, 6),
    (18, 2, 5), (19, 5, 1), (19, 3, 3), (20, 4, 2), (20, 2, 6), (21, 3, 4), (22, 4, 3), (23, 5, 2), (24, 6, 1),
    (24, 3, 5), (26, 7, 1), (26, 2, 7), (26, 4, 4), (28, 6, 2), (28, 8, 1), (28, 1, 7), (29, 5, 3), (29, 2, 8),
    (29, 4, 5), (29, 3, 6), (29, 6, 3), (29, 0, 7), (29, 1, 8), (30, 7, 2), (32, 5, 4), (32, 8, 2), (32, 4, 6),
    (32, 7, 3), (32, 5, 5), (32, 6, 4), (32, 7, 4), (33, 8, 3), (33, 3, 7), (33, 5, 6), (33, 6, 5), (34, 4, 7),
    (34, 7, 5), (34, 0, 8), (34, 8, 4), (35, 4, 8), (35, 6, 6), (35, 8, 5), (35, 7, 6), (36, 8, 6), (36, 6, 7),
    (36, 5, 7), (37, 8, 7), (38, 7, 7), (99, 6, 8), (99, 5, 8), (99, 7, 8), (99, 3, 8), (99, 8, 8),
)
WIDE = 512
STEP_ROWS = 64


def vectors_of(product, bias, depth):
    return [product[:, r * depth : (r + 1) * depth] + bias[:, r * depth : (r + 1) * depth] for r in range(6)]


def fetcher(sems):
    count = [0]

    def fetch(src, dst):
        copy = pltpu.make_async_copy(src, dst, sems.at[count[0]])
        copy.start()
        count[0] += 1
        return copy

    return fetch


def head_kernel(
    tokens_hbm, cot_hbm, w_qkv_hbm, w_out_hbm, w_up_hbm, w_down_hbm,
    mods, b_ada, gain_one, gain_two, cond, b_up, frequency, lengths,
    qkv_out, mixed_out, one_out, back_out, two_out, hidden_out, pre_out, own_grad, send_grad, middle_out,
    projected_out, own_branch, send_branch, lse, known, segr, segc, cosine, sine,
    tokens, cot, w_qkv, w_out, w_up, w_down, rows_one, full_back, rows_two, qkv, mixed, from_sum, send_sum, projected,
    middle, hidden, pre, grads, branch, low_grads, low_branch, slope, bias, bias_down, load, x_send, x_recv,
):
    me = lax.axis_index("tensor")
    length, depth = rows_one.shape
    chunks, half, _ = from_sum.shape
    chunk = 2 * half
    width = mixed.shape[1]
    pairs = width // PAIR
    across = {"tensor": 1 - me}
    each = range(chunks)
    own = [slice(c * chunk, c * chunk + half) for c in each]
    got = [slice(c * chunk + half, (c + 1) * chunk) for c in each]
    whole = [slice(c * chunk, (c + 1) * chunk) for c in each]
    fetch = fetcher(load)

    def x_copy(src, dst, i):
        return pltpu.make_async_remote_copy(
            src_ref=src, dst_ref=dst, send_sem=x_send.at[i], recv_sem=x_recv.at[i],
            device_id=across, device_id_type=MESH,
        )

    ones = [x_copy(rows_one.at[own[c]], rows_one.at[got[c]], c) for c in each]
    backs = [x_copy(full_back.at[own[c]], full_back.at[got[c]], chunks + c) for c in each]
    shares = [x_copy(send_sum.at[c], from_sum.at[c], 2 * chunks + c) for c in each]
    twos = [x_copy(rows_two.at[own[c]], rows_two.at[got[c]], 3 * chunks + c) for c in each]

    shift_a, scale_a, gate_a, shift_m, scale_m, gate_m = vectors_of(mods, b_ada, depth)
    gain_one, gain_two = gain_one[...], gain_two[...]
    reads = [fetch(tokens_hbm, tokens), fetch(w_qkv_hbm, w_qkv), fetch(cot_hbm, cot)]
    reads += [fetch(w_out_hbm, w_out), fetch(w_up_hbm, w_up), fetch(w_down_hbm, w_down)]
    writes = []
    greet([across])

    def normal_of(values):
        center = values - jnp.mean(values, axis=1, keepdims=True)
        return center * lax.rsqrt(jnp.mean(center * center, axis=1, keepdims=True) + norm_eps)

    def by_rows(work):
        @pl.loop(0, half // STEP_ROWS)
        def _(i):
            work(pl.multiple_of(i * STEP_ROWS, STEP_ROWS))

    reads[0].wait()
    for c in each:

        def first_norm(at, c=c):
            values = tokens[pl.ds(c * half + at, STEP_ROWS), :].astype(f32)
            out = normal_of(values) * gain_one * (1.0 + scale_a) + shift_a
            rows_one[pl.ds(c * chunk + at, STEP_ROWS), :] = out.astype(bf16)

        by_rows(first_norm)
        ones[c].start()
    reads[2].wait()
    bias_down[...] = jnp.zeros(bias_down.shape, f32)
    for c in each:

        def weigh(at, c=c):
            low = (cot[pl.ds(c * half + at, STEP_ROWS), :].astype(f32) * gate_m).astype(bf16)
            full_back[pl.ds(c * chunk + at, STEP_ROWS), :] = low
            bias_down[...] += jnp.sum(low.astype(f32), axis=0, keepdims=True)

        by_rows(weigh)

    starts = [0]
    for n in range(lengths.shape[1] - 1):
        starts.append(starts[-1] + lengths[0, n])

    def place_of(step):
        at = step % chunk
        return jnp.where(at < half, me, 1 - me) * (chunks * half) + (step // chunk) * half + at % half

    def document_of(place):
        return sum((place >= start).astype(jnp.int32) for start in starts[1:])

    segr[...] = document_of(place_of(lax.broadcasted_iota(jnp.int32, segr.shape, 1)))

    @pl.loop(0, length // STEP_ROWS)
    def _(i):
        at = pl.multiple_of(i * STEP_ROWS, STEP_ROWS)
        place = place_of(at + lax.broadcasted_iota(jnp.int32, (STEP_ROWS, PAIR), 0))
        first = functools.reduce(jnp.maximum, [jnp.where(place >= start, start, 0) for start in starts])
        angles = (place - first).astype(f32) * frequency[...]
        rows = pl.ds(at, STEP_ROWS)
        segc[rows, :] = document_of(place)
        cosine[rows, :] = jnp.cos(angles)
        sine[rows, :] = jnp.sin(angles)

    reads[1].wait()

    def project(c):
        rows = whole[c]
        for t in range(3):
            y = mm(rows_one[rows, :], w_qkv[t], 1, 0)
            if t == 2:
                qkv[t, rows, :] = y.astype(bf16)
                continue
            for p in range(pairs):
                lanes = slice(p * PAIR, (p + 1) * PAIR)
                u = y[:, lanes]
                low = (u * cosine[rows, :] + turned(u) * sine[rows, :]).astype(bf16)
                qkv[t, rows, lanes] = low * jnp.asarray(HEAD**-0.5 if t == 0 else 1.0, bf16)

    ones[0].wait()
    project(0)
    ones[1].wait()
    backs[0].start()
    project(1)
    writes.append(fetch(rows_one, one_out))
    writes.append(fetch(qkv, qkv_out))

    def attend(p, c):
        lanes = pl.ds(pl.multiple_of(p * PAIR, PAIR), PAIR)
        q = qkv[0, whole[c], lanes]
        docs = segr[:, whole[c]]
        outs = []
        for h in range(2):
            qh = head_lanes(q, h)
            scores = []
            for b in range(0, length, BLOCK):
                same = jnp.concatenate([segc[b : b + BLOCK, :]] * (chunk // 128), axis=1) == docs
                scores.append(jnp.where(same, mm(qkv[1, b : b + BLOCK, lanes], qh, 1, 1), masked_score))
            top = functools.reduce(jnp.maximum, [jnp.max(s, axis=0, keepdims=True) for s in scores])
            total, summed = 0.0, 0.0
            for i, s in enumerate(scores):
                pr = jnp.exp(s - top)
                total = total + jnp.sum(pr, axis=0, keepdims=True)
                v = transposed(qkv[2, i * BLOCK : (i + 1) * BLOCK, lanes]).astype(bf16)
                summed = summed + mm(v[h * HEAD : (h + 1) * HEAD, :], pr.astype(bf16), 1, 0)
            lse[c, 2 * p + h] = top + jnp.log(total)
            outs.append(summed / total)
        mixed[whole[c], lanes] = jnp.concatenate(outs, axis=0).T.astype(bf16)

    for c in each:

        @pl.loop(0, pairs)
        def _(p):
            attend(p, c)

        if c == 0:
            reads[3].wait()
        send_sum[c] = mm(mixed[got[c], :], w_out[...], 1, 0).astype(bf16)
        shares[c].start()
        projected[c] = mm(mixed[own[c], :], w_out[...], 1, 0)
    writes.append(fetch(mixed, mixed_out))

    def second_norm(c):
        shares[c].wait()

        def work(at):
            rows = pl.ds(at, STEP_ROWS)
            share = projected[c, rows, :] + from_sum[c, rows, :].astype(f32)
            projected[c, rows, :] = share
            values = tokens[pl.ds(c * half + at, STEP_ROWS), :].astype(f32) + gate_a * share
            middle[c, rows, :] = values
            out = normal_of(values) * gain_two * (1.0 + scale_m) + shift_m
            rows_two[pl.ds(c * chunk + at, STEP_ROWS), :] = out.astype(bf16)

        by_rows(work)
        twos[c].start()

    cubic, root = 0.044715, (2.0 / jnp.pi) ** 0.5
    tile = 2 * WIDE
    bias[...] = jnp.zeros(bias.shape, f32)
    held = [[], []]

    def feed(slot, rows):
        for copy in held[slot]:
            copy.wait()

        @pl.loop(0, w_up.shape[1] // tile)
        def _(t):
            at = pl.ds(pl.multiple_of(t * tile, tile), tile)
            u = mm(rows_two[rows, :], w_up[:, at], 1, 0) + b_up[:, at]
            square = u * u
            t_h = jnp.tanh(u * (root + (root * cubic) * square))
            rising = 0.5 * (1.0 + t_h)
            low_hidden = (u * rising).astype(bf16)
            slope[:, at] = rising + (0.5 * u) * (1.0 - t_h * t_h) * (root + (3.0 * cubic * root) * square)
            hidden[slot, :, at] = low_hidden
            more = mm(low_hidden, w_down[at, :], 1, 0)

            @pl.when(t == 0)
            def _():
                branch[slot] = more

            @pl.when(t > 0)
            def _():
                branch[slot] += more

        held[slot] = [fetch(hidden.at[slot], hidden_out.at[rows])]

    def feed_back(slot, rows):
        @pl.loop(0, w_up.shape[1] // tile)
        def _(t):
            at = pl.ds(pl.multiple_of(t * tile, tile), tile)
            low = (mm(full_back[rows, :], w_down[at, :], 1, 1) * slope[:, at]).astype(bf16)
            pre[slot, :, at] = low
            bias[:, at] += jnp.sum(low.astype(f32), axis=0, keepdims=True)
            more = mm(low, w_up[:, at], 1, 1)

            @pl.when(t == 0)
            def _():
                grads[slot] = more

            @pl.when(t > 0)
            def _():
                grads[slot] += more

        held[slot].append(fetch(pre.at[slot], pre_out.at[rows]))

    second_norm(0)
    for read in reads[4:]:
        read.wait()
    for c in each:
        if c:
            second_norm(c)
        feed(c, own[c])
        feed_back(c, own[c])
        held[c] += [fetch(grads.at[c], own_grad.at[c]), fetch(branch.at[c], own_branch.at[c])]
    writes.append(fetch(middle, middle_out))
    writes.append(fetch(projected, projected_out))
    for c in each:
        twos[c].wait()
        if c == 0:
            backs[0].wait()
            backs[1].start()
        feed(c, got[c])
        low_branch[c] = branch[c].astype(bf16)
        if c:
            backs[c].wait()
        feed_back(c, got[c])
        low_grads[c] = grads[c].astype(bf16)
        writes += [fetch(low_grads.at[c], send_grad.at[c]), fetch(low_branch.at[c], send_branch.at[c]), *held[c]]
    writes += [fetch(full_back, back_out), fetch(rows_two, two_out)]
    known[...] = jnp.concatenate(
        [
            jnp.zeros((8, depth), f32), bias_down[...], bias[:, :depth], bias[:, depth:],
            jnp.concatenate([cond[...].astype(f32), jnp.zeros((1, depth - cond.shape[1]), f32)], axis=1),
            jnp.zeros((4, depth), f32),
        ],
        axis=0,
    )
    for copy in writes:
        copy.wait()


def head(tokens, cot, w_qkv, w_out, w_up, w_down, *near_args, chunks):
    own, depth = tokens.shape
    length, width, wide = 2 * own, w_qkv.shape[2], w_up.shape[1]
    half = own // chunks
    anywhere, near = pl.BlockSpec(memory_space=pl.ANY), pl.BlockSpec(memory_space=pltpu.VMEM)
    shaped, kept = jax.ShapeDtypeStruct, pltpu.VMEM
    parts, rows = (chunks, half, depth), (length, depth)
    return pl.pallas_call(
        head_kernel,
        in_specs=[anywhere] * 6 + [near] * (len(near_args) - 1) + [pl.BlockSpec(memory_space=pltpu.SMEM)],
        out_specs=[anywhere] * 13 + [near] * 6,
        out_shape=[
            shaped((3, length, width), bf16), shaped((length, width), bf16), *[shaped(rows, bf16)] * 3,
            *[shaped((length, wide), bf16)] * 2, shaped(parts, f32), shaped(parts, bf16),
            shaped(parts, f32), shaped(parts, f32), shaped(parts, f32), shaped(parts, bf16),
            shaped((chunks, width // HEAD, 1, length // chunks), f32), shaped((16, depth), f32),
            shaped((1, length), jnp.int32), shaped((length, PAIR), jnp.int32), *[shaped((length, PAIR), f32)] * 2,
        ],
        scratch_shapes=[
            kept(tokens.shape, bf16), kept(tokens.shape, bf16), kept(w_qkv.shape, bf16), kept(w_out.shape, bf16),
            kept(w_up.shape, bf16), kept(w_down.shape, bf16), *[kept(rows, bf16)] * 3, kept((3, length, width), bf16),
            kept((length, width), bf16), kept(parts, bf16), kept(parts, bf16), kept(parts, f32), kept(parts, f32),
            *[kept((chunks, half, wide), bf16)] * 2, *[kept(parts, f32)] * 2,
            kept(parts, bf16), kept(parts, bf16), kept((half, wide), f32), kept((1, wide), f32), kept((1, depth), f32),
            pltpu.SemaphoreType.DMA((32,)),
            pltpu.SemaphoreType.DMA((4 * chunks,)), pltpu.SemaphoreType.DMA((4 * chunks,)),
        ],
        compiler_params=pltpu.CompilerParams(collective_id=2, has_side_effects=True, vmem_limit_bytes=61 << 20),
        name="head",
    )(tokens, cot, w_qkv, w_out, w_up, w_down, *near_args)


def tail_kernel(
    hidden, full_back, rows_two, grad_pre, qkv_hbm, mixed_hbm, rows_hbm, w_qkv_hbm, w_out_hbm,
    own_grad, send_grad, mid_hbm, proj_hbm, own_branch, send_branch, tokens_hbm, cot_hbm,
    mods, b_ada, gain_one, gain_two, b_down, known, lse, segr, segc, cosine, sine,
    down_sum, up_sum, out_sum, q_sum, k_sum, v_sum, output, grad_x, everyone,
    qkv, mixed, rows_one, w_qkv, w_out, proj, mix_grad, d_qkv, dk, dv, from_x, grads, middle, projected, tokens, cot,
    part_a, part_b, part_c, part_d, part_e, branch_got, col_sums, small, small_got,
    load, store, x_send, x_recv, all_send, all_recv, *more,
):
    place, me = lax.axis_index("dp"), lax.axis_index("tensor")
    length, depth = rows_one.shape
    chunks, half, _ = from_x.shape
    chunk = 2 * half
    width = mixed.shape[1]
    pairs = width // PAIR
    across = {"tensor": 1 - me}

    specs = [
        (part_a.at[pl.ds(0, WIDE)], down_sum.at[pl.ds(0, WIDE)], 0),
        (part_a.at[pl.ds(WIDE, WIDE)], down_sum.at[pl.ds(WIDE, WIDE)], 0),
        (part_b, down_sum.at[pl.ds(depth, depth)], 0),
        (part_c, up_sum, 0), (part_d, up_sum, depth), (part_e, out_sum, 0),
        (qkv.at[2], v_sum, 0), (qkv.at[1], k_sum, 0), (qkv.at[0], q_sum, 0),
    ]
    units = []
    for i, (part, out, column) in enumerate(specs):
        *got, send, recv, local = more[7 * i : 7 * (i + 1)]
        units.append(Unit(part, out, column, got, send, recv, local, place))

    def x_copy(src, dst, i):
        return pltpu.make_async_remote_copy(
            src_ref=src, dst_ref=dst, send_sem=x_send.at[i], recv_sem=x_recv.at[i],
            device_id=across, device_id_type=MESH,
        )

    each = range(chunks)
    grads_in = [x_copy(send_grad.at[c], from_x.at[c], c) for c in each]
    projs = [x_copy(proj.at[c, :half], proj.at[c, half:], chunks + c) for c in each]
    ones = [x_copy(proj.at[c, :half], from_x.at[c], 2 * chunks + c) for c in each]
    branches = [x_copy(send_branch.at[c], branch_got.at[c], 3 * chunks + c) for c in each]
    smalls = x_copy(small, small_got, 4 * chunks)
    outputs = [
        pltpu.make_async_copy(branch_got.at[c], output.at[c * half : (c + 1) * half], store.at[c]) for c in each
    ]
    partner = units[0].partner

    fetch = fetcher(load)
    done = [0]

    def until(place_now):
        while done[0] < len(ORDER) and ORDER[done[0]][0] <= place_now:
            _, i, k = ORDER[done[0]]
            units[i].step(k)
            done[0] += 1

    greet([*[{"dp": p} for p in partner], across])
    grads_in[0].start()
    slots = [w_qkv.at[0], w_qkv.at[1], w_qkv.at[2], d_qkv.at[2]]
    cut = lambda t: slice(t * WIDE, (t + 1) * WIDE)
    backs = fetch(full_back, rows_one)
    hiddens = [fetch(hidden.at[:, cut(t)], slots[t]) for t in range(4)]
    norms = [
        [fetch(src, dst.at[c]) for src, dst in (
            (own_grad.at[c], grads), (mid_hbm.at[c], middle), (proj_hbm.at[c], projected),
            (tokens_hbm.at[c * half : (c + 1) * half], tokens), (cot_hbm.at[c * half : (c + 1) * half], cot),
        )]
        for c in each
    ]
    twos = [fetch(rows_two.at[:, cut(t)], d_qkv.at[t]) for t in range(2)]
    col_sums[...] = jnp.zeros(col_sums.shape, f32)

    backs.wait()
    pres = []
    for t in range(4):
        until(1 + t)
        hiddens[t].wait()
        part = (part_a, part_b)[t // 2]

        @pl.loop(0, WIDE // 256)
        def _(r):
            at = pl.ds(pl.multiple_of(r * 256, 256), 256)
            to = pl.ds(pl.multiple_of((t % 2) * WIDE + r * 256, 256), 256)
            part[to, :] = mm(slots[t][:, at], rows_one[...], 0, 0).astype(bf16)

        pres.append(fetch(grad_pre.at[:, cut(t)], slots[t]))
        if t != 2:
            units[min(t, 2)].step(0)
    main = [
        fetch(w_out_hbm, w_out), fetch(mixed_hbm, mixed), fetch(qkv_hbm, qkv), fetch(rows_hbm, rows_one),
    ]

    def up_part(t):
        pres[t].wait()
        part = (part_c, part_d)[t // 2]

        @pl.loop(0, depth // 256)
        def _(r):
            to = pl.ds(pl.multiple_of(r * 256, 256), 256)
            at = pl.ds(pl.multiple_of((r % 2) * 256, 256), 256)
            part[to, cut(t % 2)] = mm(d_qkv[r // 2, :, at], slots[t][...], 0, 0).astype(bf16)

    def fold(row, values):
        col_sums[row : row + 1, :] += jnp.sum(values, axis=0, keepdims=True)

    def norm_back(grad, values, weight):
        center = values - jnp.mean(values, axis=1, keepdims=True)
        root = lax.rsqrt(jnp.mean(center * center, axis=1, keepdims=True) + norm_eps)
        normal = center * root
        inner = grad * weight
        back = inner - jnp.mean(inner, axis=1, keepdims=True) - normal * jnp.mean(inner * normal, axis=1, keepdims=True)
        return root * back, normal

    _, scale_a, gate_a, _, scale_m, gate_m = vectors_of(mods, b_ada, depth)
    gain_one, gain_two, b_down = gain_one[...], gain_two[...], b_down[...]

    def second_norm(c):
        for copy in norms[c]:
            copy.wait()

        @pl.loop(0, half // STEP_ROWS)
        def _(i):
            at = pl.ds(pl.multiple_of(i * STEP_ROWS, STEP_ROWS), STEP_ROWS)
            grad = grads[c, at, :] + from_x[c, at, :].astype(f32)
            back, normal = norm_back(grad, middle[c, at, :], gain_two * (1.0 + scale_m))
            total = back + cot[c, at, :].astype(f32)
            grads[c, at, :] = total
            proj[c, at, :] = (total * gate_a).astype(bf16)
            fold(0, grad)
            fold(1, grad * normal)
            fold(2, total * projected[c, at, :])

        projs[c].start()

    for copy in twos:
        copy.wait()
    until(5)
    up_part(0)
    until(6)
    up_part(1)
    units[3].step(0)
    until(7)
    grads_in[0].wait()
    grads_in[1].start()
    second_norm(0)
    owns = [fetch(own_branch.at[0], projected.at[0])]
    until(8)
    up_part(2)
    until(9)
    up_part(3)
    units[4].step(0)
    weights = fetch(w_qkv_hbm, w_qkv)
    until(10)
    grads_in[1].wait()
    second_norm(1)
    owns.append(fetch(own_branch.at[1], projected.at[1]))

    def turn_back(u, rows):
        return (u * cosine[rows, :] - turned(u) * sine[rows, :]).astype(bf16)

    def attend_back(p, c):
        lanes = pl.ds(pl.multiple_of(p * PAIR, PAIR), PAIR)
        rows = slice(c * chunk, (c + 1) * chunk)
        q, g = qkv[0, rows, lanes], mix_grad[rows, lanes]
        both = (g.astype(f32) * mixed[rows, lanes].astype(f32)).T
        qh = [head_lanes(q, h) for h in range(2)]
        gh = [head_lanes(g, h) for h in range(2)]
        delta = [jnp.sum(both[h * HEAD : (h + 1) * HEAD, :], axis=0, keepdims=True) for h in range(2)]
        q_two, g_two = jnp.concatenate(qh, axis=0), jnp.concatenate(gh, axis=0)
        docs = segr[:, rows]
        dq = [0.0, 0.0]
        for b in range(0, length, BLOCK):
            cols = slice(b, b + BLOCK)
            k, v = qkv[1, cols, lanes], qkv[2, cols, lanes]
            turned_k = transposed(k).astype(bf16)
            same = jnp.concatenate([segc[cols, :]] * (chunk // 128), axis=1) == docs
            ps, ds = [], []
            for h in range(2):
                s = jnp.where(same, mm(k, qh[h], 1, 1), masked_score)
                pr = jnp.exp(s - lse[c, 2 * p + h])
                d = (pr * (mm(v, gh[h], 1, 1) - delta[h])).astype(bf16)
                ps.append(pr.astype(bf16))
                ds.append(d)
                dq[h] = dq[h] + mm(turned_k[h * HEAD : (h + 1) * HEAD, :], d, 1, 0)
            add_v = mm(jnp.concatenate(ps, axis=1), g_two, 1, 0)
            add_k = mm(jnp.concatenate(ds, axis=1), q_two, 1, 0)
            if c < chunks - 1:
                dv[cols, lanes] = add_v if c == 0 else dv[cols, lanes] + add_v
                dk[cols, lanes] = add_k if c == 0 else dk[cols, lanes] + add_k
            else:
                d_qkv[1, cols, lanes] = turn_back(dk[cols, lanes] + add_k, cols)
                d_qkv[2, cols, lanes] = (dv[cols, lanes] + add_v).astype(bf16)
        d_qkv[0, rows, lanes] = turn_back(jnp.concatenate(dq, axis=0).T * (HEAD**-0.5), rows)

    for copy in main:
        copy.wait()
    now = 11
    for c in each:
        until(now)
        projs[c].wait()
        if c == chunks - 1:
            for copy in branches:
                copy.start()
        mix_grad[c * chunk : (c + 1) * chunk, :] = mm(proj[c], w_out[...], 1, 1).astype(bf16)
        now += 1
        if c == chunks - 1:
            until(now)

            @pl.loop(0, width // 256)
            def _(r):
                at = pl.ds(pl.multiple_of(r * 256, 256), 256)
                part_e[at, :] = sum(
                    mm(mixed[n * chunk : (n + 1) * chunk, at], proj[n], 0, 0) for n in each
                ).astype(bf16)

            units[5].step(0)
            now += 1

        @pl.loop(0, pairs)
        def _(p):
            for n in range(pairs):

                @pl.when(p == n)
                def _():
                    until(now + n)

            attend_back(p, c)

        now += pairs

    def rows_back(start):
        at = slice(start, start + half)
        return sum(mm(d_qkv[t, at, :], w_qkv[t], 1, 1) for t in range(3))

    for i in range(3):
        until(now + i)

        @pl.loop(0, depth // 256)
        def _(r):
            at = pl.ds(pl.multiple_of(r * 256, 256), 256)
            qkv[2 - i, at, :] = mm(rows_one[:, at], d_qkv[2 - i], 0, 0).astype(bf16)

        units[6 + i].step(0)
    now += 3
    weights.wait()
    for c in each:
        until(now + c)
        proj[c, :half] = rows_back(c * chunk + half).astype(bf16)
        if c == 0:
            ones[c].start()
    now += chunks
    for c in each:
        until(now + c)
        branches[c].wait()
        owns[c].wait()

        @pl.loop(0, half // STEP_ROWS)
        def _(i):
            at = pl.ds(pl.multiple_of(i * STEP_ROWS, STEP_ROWS), STEP_ROWS)
            branch = projected[c, at, :] + branch_got[c, at, :].astype(f32) + b_down
            branch_got[c, at, :] = (middle[c, at, :] + gate_m * branch).astype(bf16)
            fold(5, cot[c, at, :].astype(f32) * branch)

        outputs[c].start()
    now += chunks
    for c in each:
        until(now + c)
        projected[c] = rows_back(c * chunk)
    now += chunks
    for c in each:
        until(now + c)
        ones[c].wait()
        if c < chunks - 1:
            ones[c + 1].start()

        @pl.loop(0, half // STEP_ROWS)
        def _(i):
            at = pl.ds(pl.multiple_of(i * STEP_ROWS, STEP_ROWS), STEP_ROWS)
            grad = projected[c, at, :] + from_x[c, at, :].astype(f32)
            back, normal = norm_back(grad, tokens[c, at, :].astype(f32), gain_one * (1.0 + scale_a))
            grad_x[c, at, :] = (back + grads[c, at, :]).astype(bf16)
            fold(3, grad)
            fold(4, grad * normal)

    now += chunks
    shift, scaled, gated, shift_one, scaled_one, gated_m = [col_sums[r : r + 1, :] for r in range(6)]
    small[...] = known[...] + jnp.concatenate(
        [
            shift_one, gain_one * scaled_one, gated, shift, gain_two * scaled, gated_m,
            (1.0 + scale_a) * scaled_one, (1.0 + scale_m) * scaled, jnp.zeros((8, depth), f32),
        ],
        axis=0,
    )
    smalls.start()
    until(now)
    smalls.wait()
    number = lax.broadcasted_iota(jnp.int32, small.shape, 0)
    everyone[0] = small[...] + jnp.where(number < 9, small_got[...], 0.0)
    for n, b in enumerate((1, 3, 2, 0)):
        copy = pltpu.make_async_remote_copy(
            src_ref=everyone.at[pl.ds(0, 1 << n)], dst_ref=everyone.at[pl.ds(1 << n, 1 << n)],
            send_sem=all_send.at[n], recv_sem=all_recv.at[n],
            device_id={"dp": partner[b]}, device_id_type=MESH,
        )
        copy.start()
        until(now + 1 + n)
        copy.wait()
    until(1000)
    for copy in outputs:
        copy.wait()


def tail(*args):
    hidden, qkv, rows_one, w_qkv, w_out, own_grad, tokens = (args[n] for n in (0, 4, 6, 7, 8, 9, 15))
    known = args[22]
    _, length, width = qkv.shape
    chunks, half, depth = own_grad.shape
    anywhere, near = pl.BlockSpec(memory_space=pl.ANY), pl.BlockSpec(memory_space=pltpu.VMEM)
    shaped, kept = jax.ShapeDtypeStruct, pltpu.VMEM
    in_chunks = (chunks, half, depth)
    scratch = [
        kept(qkv.shape, bf16), kept((length, width), bf16), kept(rows_one.shape, bf16), kept(w_qkv.shape, bf16),
        kept(w_out.shape, bf16), kept((chunks, 2 * half, depth), bf16), kept((length, width), bf16),
        kept((3, length, width), bf16), kept((length, width), f32), kept((length, width), f32),
        kept(in_chunks, bf16), kept(in_chunks, f32), kept(in_chunks, f32), kept(in_chunks, f32),
        kept(in_chunks, bf16), kept(in_chunks, bf16),
        *[kept((depth, depth), bf16)] * 4, kept((width, depth), bf16), kept(in_chunks, bf16),
        kept((8, depth), f32), kept(known.shape, f32), kept(known.shape, f32),
        pltpu.SemaphoreType.DMA((30,)), pltpu.SemaphoreType.DMA((chunks,)),
        pltpu.SemaphoreType.DMA((4 * chunks + 1,)), pltpu.SemaphoreType.DMA((4 * chunks + 1,)),
        pltpu.SemaphoreType.DMA((EDGES,)), pltpu.SemaphoreType.DMA((EDGES,)),
        *unit_scratch(WIDE, depth) * 2, *unit_scratch(depth, depth) * 3, *unit_scratch(width, depth), *unit_scratch(depth, width) * 3,
    ]
    return pl.pallas_call(
        tail_kernel,
        in_specs=[anywhere] * 17 + [near] * 11,
        out_specs=[anywhere] * 7 + [near] * 2,
        out_shape=[
            shaped((hidden.shape[1], depth), bf16), shaped((depth, hidden.shape[1]), bf16), shaped((width, depth), bf16),
            *[shaped((depth, width), bf16)] * 3, shaped(tokens.shape, bf16),
            shaped(in_chunks, bf16), shaped((1 << EDGES, *known.shape), f32),
        ],
        scratch_shapes=scratch,
        compiler_params=pltpu.CompilerParams(collective_id=1, has_side_effects=True, vmem_limit_bytes=61 << 20),
        name="tail",
    )(*args)


def finish_kernel(
    down, up, out, q, k, v, output, grad_x, everyone, w_ada,
    down_sum, up_sum, out_sum, qkv_sum, output_out, grad_x_out, ada, cond_grad, ada_bias, one_gain, two_gain, down_bias,
    up_bias, mods, conds,
):
    depth = everyone.shape[2]

    @pl.when(pl.program_id(0) == 0)
    def _():
        total = sum(everyone[n] for n in range(everyone.shape[0]))
        lanes = 0.0
        for r in range(6):
            span = slice(r * depth, (r + 1) * depth)
            mods[:, span] = jnp.concatenate([everyone[n, r : r + 1, :] for n in range(everyone.shape[0])], axis=0)
            ada_bias[:, span] = total[r : r + 1, :]
            for t in range(0, depth, 128):
                at = r * depth + t
                lanes = lanes + w_ada[:, at : at + 128].astype(f32) * everyone[0, r : r + 1, t : t + 128]
        cond_grad[...] = jnp.sum(lanes.T, axis=0, keepdims=True)
        one_gain[...], two_gain[...], down_bias[...] = total[6:7, :], total[7:8, :], total[8:9, :]
        up_bias[...] = jnp.concatenate([total[9:10, :], total[10:11, :]], axis=1)
        conds[...] = jnp.concatenate(
            [everyone[n, 11:12, : conds.shape[0]] for n in range(everyone.shape[0])], axis=0
        ).T

    down_sum[...] = down[...].astype(f32)
    up_sum[...] = up[...].astype(f32)
    out_sum[...] = out[...].astype(f32)
    for t, part in enumerate((q, k, v)):
        qkv_sum[t] = part[...].astype(f32)
    output_out[...] = output[...]
    grad_x_out[...] = grad_x[...]
    rows = ada.shape[0]
    some = conds[pl.ds(pl.multiple_of(pl.program_id(0) * rows, rows), rows), :]
    ada[...] = lax.dot_general(
        some, mods[...], (((1,), (0,)), ((), ())), precision=lax.Precision.HIGHEST, preferred_element_type=f32
    )


def finish(sums, output, grad_x, everyone, w_ada):
    steps = 8
    down, up, out, q, _, _ = sums
    shaped = jax.ShapeDtypeStruct
    devices, _, depth = everyone.shape

    def rows_of(array):
        return pl.BlockSpec((array.shape[0] // steps, array.shape[1]), lambda i: (i, 0))

    def whole(shape):
        return pl.BlockSpec(shape, lambda i: (0,) * len(shape))

    ones = [(1, n) for n in (w_ada.shape[0], w_ada.shape[1], depth, depth, depth, up.shape[1])]
    return pl.pallas_call(
        finish_kernel,
        grid=(steps,),
        in_specs=[
            *[rows_of(a) for a in (*sums, output, grad_x)], whole(everyone.shape), whole(w_ada.shape),
        ],
        out_specs=[
            rows_of(down), rows_of(up), rows_of(out),
            pl.BlockSpec((3, q.shape[0] // steps, q.shape[1]), lambda i: (0, i, 0)),
            rows_of(output), rows_of(grad_x), rows_of(w_ada), *[whole(s) for s in ones],
        ],
        out_shape=[
            shaped(down.shape, f32), shaped(up.shape, f32), shaped(out.shape, f32), shaped((3, *q.shape), f32),
            shaped(output.shape, bf16), shaped(grad_x.shape, bf16), shaped(w_ada.shape, f32),
            *[shaped(s, f32) for s in ones],
        ],
        scratch_shapes=[pltpu.VMEM((devices, w_ada.shape[1]), f32), pltpu.VMEM((w_ada.shape[0], devices), f32)],
        compiler_params=pltpu.CompilerParams(vmem_limit_bytes=61 << 20),
        name="finish",
    )(*sums, output, grad_x, everyone, w_ada)


def body_pair(
    tokens, cond, doc_lengths, w_ada, b_ada, gain_one, w_qkv, w_out, gain_two, w_up, b_up, w_down, b_down, cotangent
):
    own, width = tokens.shape
    length = 2 * own
    chunks = 2

    exponent = np.arange(HEAD // 2) * (2.0 / HEAD)
    frequency = np.tile(rope_base**-exponent, PAIR // (HEAD // 2))[None, :].astype(np.float32)
    mods = jnp.dot(cond, w_ada, preferred_element_type=f32)
    (
        qkv, mixed, rows_one, full_back, rows_two, hidden, grad_pre, own_grad, send_grad, middle, projected,
        own_branch, send_branch, lse, known, *tables,
    ) = head(
        tokens, cotangent, w_qkv, w_out, w_up, w_down, mods, b_ada[None, :], gain_one[None, :], gain_two[None, :], cond,
        b_up[None, :], frequency, doc_lengths, chunks=chunks,
    )
    *sums, output, grad_x, everyone = tail(
        hidden, full_back, rows_two, grad_pre, qkv, mixed, rows_one, w_qkv, w_out, own_grad, send_grad,
        middle, projected, own_branch, send_branch, tokens, cotangent,
        mods, b_ada[None, :], gain_one[None, :], gain_two[None, :], b_down[None, :], known,
        lse, *tables,
    )
    (
        grad_w_down, grad_w_up, grad_w_out, grad_w_qkv, output, grad_x, grad_w_ada, grad_cond, *rows,
    ) = finish(sums, output, grad_x.reshape(own, width), everyone, w_ada)
    grad_b_ada, grad_gain_one, grad_gain_two, grad_b_down, grad_b_up = [
        row[0] for row in rows
    ]
    return (
        output, grad_x, grad_cond, grad_w_ada, grad_b_ada, grad_gain_one, grad_w_qkv, grad_w_out, grad_gain_two,
        grad_w_up, grad_b_up, grad_w_down, grad_b_down,
    )


def body_any(
    tokens, cond, doc_lengths, w_ada, b_ada, gain_one, w_qkv, w_out, gain_two, w_up, b_up, w_down, b_down, cotangent
):
    tensor_size = lax.axis_size("tensor")
    own = tokens.shape[0]
    length = own * tensor_size

    def all_rows(values):
        return lax.all_gather(values, "tensor", axis=0, tiled=True)

    def own_sum(values):
        return lax.psum_scatter(values, "tensor", scatter_dimension=0, tiled=True)

    def sum_over_dp(part):
        return lax.psum(part, "dp")

    places = jnp.arange(length, dtype=jnp.int32)
    segment, doc_first = documents(doc_lengths[0], places)
    cosine, sine = rope_tables(places - doc_first)
    blocks = length // BLOCK
    in_blocks = segment.reshape(blocks, BLOCK)
    least, most = jnp.min(in_blocks, axis=1), jnp.max(in_blocks, axis=1)
    meets = (least[:, None] <= most[None, :]) & (least[None, :] <= most[:, None])
    flags = meets.astype(jnp.int32).reshape(-1)
    seg_rows = in_blocks[:, None, :]
    seg_cols = jnp.broadcast_to(segment[:, None], (length, 128))

    modulation = jnp.dot(cond, w_ada, preferred_element_type=f32)[0] + b_ada
    shift_a, scale_a, gate_a, shift_m, scale_m, gate_m = jnp.split(modulation, 6)
    x_rows = tokens.astype(f32)
    grad_out = cotangent.astype(f32)

    act_one = modulate(x_rows, gain_one, shift_a, scale_a).astype(bf16)
    rows_one = all_rows(act_one)
    grad_branch = (grad_out * gate_m).astype(bf16)
    full_branch = all_rows(grad_branch)
    qkv = project_qkv(rows_one, w_qkv, cosine, sine)
    mixed, lse = attend_forward(flags, qkv, seg_rows, seg_cols)
    projected = own_sum(jnp.dot(mixed, w_out, preferred_element_type=f32))
    middle = x_rows + gate_a * projected
    rows_two = all_rows(modulate(middle, gain_two, shift_m, scale_m).astype(bf16))
    pre_act = jnp.dot(rows_two, w_up, preferred_element_type=f32) + b_up
    hidden = jax.nn.gelu(pre_act, approximate=True).astype(bf16)

    grad_hidden = jnp.einsum("sd,fd->sf", full_branch, w_down, preferred_element_type=f32)
    _, gelu_back = jax.vjp(lambda values: jax.nn.gelu(values, approximate=True), pre_act)
    grad_pre = gelu_back(grad_hidden)[0].astype(bf16)
    grad_act_two = own_sum(jnp.einsum("sf,df->sd", grad_pre, w_up, preferred_element_type=f32))
    grad_w_down = sum_over_dp(jnp.einsum("sf,sd->fd", hidden, full_branch, preferred_element_type=f32))
    grad_w_up = sum_over_dp(jnp.einsum("sd,sf->df", rows_two, grad_pre, preferred_element_type=f32))

    branch = own_sum(jnp.dot(hidden, w_down, preferred_element_type=f32)) + b_down
    output = (middle + gate_m * branch).astype(bf16)
    grad_gate_m = jnp.sum(grad_out * branch, axis=0)
    grad_b_down = jnp.sum(grad_branch.astype(f32), axis=0)
    grad_b_up = jnp.sum(grad_pre.astype(f32), axis=0)

    _, second_back = jax.vjp(modulate, middle, gain_two, shift_m, scale_m)
    grad_middle, grad_gain_two, grad_shift_m, grad_scale_m = second_back(grad_act_two)
    grad_middle = grad_middle + grad_out
    full_proj = all_rows((grad_middle * gate_a).astype(bf16))
    grad_gate_a = jnp.sum(grad_middle * projected, axis=0)
    grad_mixed = jnp.einsum("sd,ed->se", full_proj, w_out, preferred_element_type=f32).astype(bf16)
    grad_w_out = sum_over_dp(jnp.einsum("se,sd->ed", mixed, full_proj, preferred_element_type=f32))
    grad_qkv = attend_backward(flags, qkv, grad_mixed, mixed, lse, seg_rows, seg_cols, cosine, sine)
    grad_act_one = own_sum(jnp.einsum("tse,tde->sd", grad_qkv, w_qkv, preferred_element_type=f32))
    grad_w_qkv = jnp.einsum("sd,tse->tde", rows_one, grad_qkv, preferred_element_type=f32)
    grad_w_qkv = sum_over_dp(grad_w_qkv.reshape(-1, grad_w_qkv.shape[2])).reshape(grad_w_qkv.shape)

    _, first_back = jax.vjp(modulate, x_rows, gain_one, shift_a, scale_a)
    grad_x, grad_gain_one, grad_shift_a, grad_scale_a = first_back(grad_act_one)
    grad_x = (grad_x + grad_middle).astype(bf16)

    small = jnp.concatenate(
        [
            grad_shift_a, grad_scale_a, grad_gate_a, grad_shift_m, grad_scale_m, grad_gate_m,
            grad_gain_one, grad_gain_two, grad_b_down,
        ]
    )
    small = lax.psum(small, "tensor")
    mod_size = modulation.shape[0]
    grad_mod = small[:mod_size]
    grad_cond = jnp.dot(w_ada.astype(f32), grad_mod, precision=lax.Precision.HIGHEST)[None, :]
    everyone = lax.all_gather(
        jnp.concatenate([small, grad_b_up, cond[0].astype(f32)])[None, :], "dp", axis=0, tiled=True
    )
    conds = everyone[:, -cond.shape[1] :]
    mods = everyone[:, :mod_size]
    grad_w_ada = jnp.einsum("nc,nm->cm", conds, mods, precision=lax.Precision.HIGHEST, preferred_element_type=f32)
    sums = jnp.sum(everyone, axis=0)
    width = tokens.shape[1]
    grad_b_ada = sums[:mod_size]
    grad_gain_one, grad_gain_two, grad_b_down = jnp.split(sums[mod_size : mod_size + 3 * width], 3)
    grad_b_up = sums[mod_size + 3 * width : -cond.shape[1]]
    return (
        output, grad_x, grad_cond, grad_w_ada, grad_b_ada, grad_gain_one, grad_w_qkv, grad_w_out, grad_gain_two,
        grad_w_up, grad_b_up, grad_w_down, grad_b_down,
    )


def solution(mesh):
    swaps = mesh.shape["tensor"] == 2 and mesh.shape["dp"] == 16
    placed = (
        P(("dp", "tensor"), None), P("dp", None), P("dp", None), P(), P(), P(), P(None, None, "tensor"),
        P("tensor", None), P(), P(None, "tensor"), P("tensor"), P("tensor", None), P(), P(("dp", "tensor"), None),
    )
    return jax.shard_map(
        body_pair if swaps else body_any,
        mesh=mesh,
        in_specs=placed,
        out_specs=(
            P(("dp", "tensor"), None), P(("dp", "tensor"), None), P("dp", None), P(), P(), P(),
            P(None, None, "tensor"), P("tensor", None), P(), P(None, "tensor"), P("tensor"), P("tensor", None), P(),
        ),
        check_vma=False,
    )
```

```python
import functools

import jax
import jax.numpy as jnp
import numpy as np
from jax import lax
from jax.experimental import pallas as pl
from jax.experimental.pallas import tpu as pltpu
from jax.sharding import PartitionSpec as P

HEAD = 64
PAIR = 2 * HEAD
BLOCK = 256
ROWS = 512

norm_eps = 1e-05
rope_base = 10000.0
masked_score = -1e30
f32, bf16 = jnp.float32, jnp.bfloat16


def layer_norm(values, gain):
    center = values - jnp.mean(values, axis=-1, keepdims=True)
    spread = jnp.mean(center * center, axis=-1, keepdims=True)
    return center * lax.rsqrt(spread + norm_eps) * gain


def modulate(values, gain, shift, scale):
    return layer_norm(values, gain) * (1.0 + scale) + shift


def documents(lengths, places):
    numbers = jnp.arange(lengths.shape[0], dtype=jnp.int32)
    earlier = (numbers[None, :] < numbers[:, None]).astype(jnp.int32)
    starts = jnp.sum(earlier * lengths[None, :], axis=1)
    ends = starts + lengths
    inside = ((places[:, None] >= starts[None, :]) & (places[:, None] < ends[None, :])).astype(
        jnp.int32
    )
    segment = jnp.sum(inside * numbers[None, :], axis=1)
    doc_first = jnp.sum(inside * starts[None, :], axis=1)
    return segment, doc_first


def rope_tables(offsets):
    exponent = jnp.arange(HEAD // 2, dtype=f32) * (2.0 / HEAD)
    frequency = jnp.power(jnp.float32(rope_base), -exponent)
    angles = offsets.astype(f32)[:, None] * frequency[None, :]
    cosine, sine = jnp.cos(angles), jnp.sin(angles)
    repeat = PAIR // (HEAD // 2)
    return jnp.concatenate([cosine] * repeat, axis=-1), jnp.concatenate([sine] * repeat, axis=-1)


def turned(values):
    lane = lax.broadcasted_iota(jnp.int32, values.shape, 1)
    half = HEAD // 2
    from_right = pltpu.roll(values, PAIR - half, axis=1)
    from_left = pltpu.roll(values, half, axis=1)
    return jnp.where(lane % HEAD < half, -from_right, from_left)


def mm(a, b, da, db):
    return lax.dot_general(a, b, (((da,), (db,)), ((), ())), preferred_element_type=f32)


def qkv_kernel(x_ref, w_ref, cos_ref, sin_ref, o_ref):
    which = pl.program_id(1)
    y = mm(x_ref[...], w_ref[...], 1, 0)

    @pl.when(which < 2)
    def _():
        factor = jnp.where(which == 0, HEAD**-0.5, 1.0)
        for p in range(y.shape[1] // PAIR):
            u = y[:, p * PAIR : (p + 1) * PAIR]
            r = u * cos_ref[...] + turned(u) * sin_ref[...]
            o_ref[:, p * PAIR : (p + 1) * PAIR] = (r.astype(bf16) * factor.astype(bf16)).astype(bf16)

    @pl.when(which == 2)
    def _():
        o_ref[...] = y.astype(bf16)


def project_qkv(rows, w_qkv, cosine, sine):
    count, depth = rows.shape
    width = w_qkv.shape[2]
    return pl.pallas_call(
        qkv_kernel,
        grid=(count // ROWS, 3),
        in_specs=[
            pl.BlockSpec((ROWS, depth), lambda r, t: (r, 0)),
            pl.BlockSpec((None, depth, width), lambda r, t: (t, 0, 0)),
            pl.BlockSpec((ROWS, PAIR), lambda r, t: (r, 0)),
            pl.BlockSpec((ROWS, PAIR), lambda r, t: (r, 0)),
        ],
        out_specs=pl.BlockSpec((None, ROWS, width), lambda r, t: (t, r, 0)),
        out_shape=jax.ShapeDtypeStruct((3, count, width), bf16),
        compiler_params=pltpu.CompilerParams(vmem_limit_bytes=32 << 20),
        cost_estimate=pl.CostEstimate(
            flops=6 * count * depth * width, bytes_accessed=8 * count * width, transcendentals=0
        ),
        name="qkv",
    )(rows, w_qkv, cosine, sine)


def head_lanes(block, h):
    lane = lax.broadcasted_iota(jnp.int32, block.shape, 1)
    return jnp.where(lane // HEAD == h, block, jnp.zeros_like(block))


def transposed(block):
    return block.astype(f32).T


def forward_kernel(flag_ref, q_ref, k_ref, v_ref, segr_ref, segc_ref, o_ref, lse_ref, vt, m, l, acc):
    blocks = q_ref.shape[0] // BLOCK
    for b in range(blocks):
        vt[b] = transposed(v_ref[b * BLOCK : (b + 1) * BLOCK, :]).astype(bf16)

    @pl.loop(0, blocks)
    def _(qi):
        rows = pl.ds(pl.multiple_of(qi * BLOCK, BLOCK), BLOCK)
        q = q_ref[rows, :]
        m[...] = jnp.full(m.shape, masked_score, f32)
        l[...] = jnp.zeros(l.shape, f32)
        acc[...] = jnp.zeros(acc.shape, f32)

        @pl.loop(0, blocks)
        def _(ki):
            @pl.when(flag_ref[qi * blocks + ki] > 0)
            def _():
                cols = pl.ds(pl.multiple_of(ki * BLOCK, BLOCK), BLOCK)
                k = k_ref[cols, :]
                docs = segc_ref[cols, :]
                same = jnp.concatenate([docs] * (BLOCK // 128), axis=1) == segr_ref[qi]
                for h in range(2):
                    lo, hi = h * HEAD, (h + 1) * HEAD
                    s = jnp.where(same, mm(k, head_lanes(q, h), 1, 1), masked_score)
                    top = jnp.maximum(m[h], jnp.max(s, axis=0, keepdims=True))
                    p = jnp.exp(s - top)
                    shrink = jnp.exp(m[h] - top)
                    m[h] = top
                    l[h] = l[h] * shrink + jnp.sum(p, axis=0, keepdims=True)
                    acc[lo:hi, :] = acc[lo:hi, :] * shrink + mm(vt[ki, lo:hi, :], p.astype(bf16), 1, 0)

        for h in range(2):
            lo, hi = h * HEAD, (h + 1) * HEAD
            lse_ref[h, qi] = m[h] + jnp.log(l[h])
            acc[lo:hi, :] = acc[lo:hi, :] / l[h]
        o_ref[rows, :] = acc[...].T.astype(bf16)


def backward_kernel(
    flag_ref, q_ref, k_ref, v_ref, g_ref, o_ref, lse_ref, segr_ref, segc_ref, cos_ref, sin_ref,
    out_ref, kt, dk, dv, dq,
):
    blocks = q_ref.shape[0] // BLOCK
    for b in range(blocks):
        kt[b] = transposed(k_ref[b * BLOCK : (b + 1) * BLOCK, :]).astype(bf16)
    dk[...] = jnp.zeros(dk.shape, f32)
    dv[...] = jnp.zeros(dv.shape, f32)

    def turn_back(u, rows):
        return (u * cos_ref[rows, :] - turned(u) * sin_ref[rows, :]).astype(bf16)

    @pl.loop(0, blocks)
    def _(qi):
        rows = pl.ds(pl.multiple_of(qi * BLOCK, BLOCK), BLOCK)
        q, g = q_ref[rows, :], g_ref[rows, :]
        both = (g.astype(f32) * o_ref[rows, :].astype(f32)).T
        dq[...] = jnp.zeros(dq.shape, f32)

        @pl.loop(0, blocks)
        def _(ki):
            @pl.when(flag_ref[qi * blocks + ki] > 0)
            def _():
                cols = pl.ds(pl.multiple_of(ki * BLOCK, BLOCK), BLOCK)
                k, v = k_ref[cols, :], v_ref[cols, :]
                docs = segc_ref[cols, :]
                same = jnp.concatenate([docs] * (BLOCK // 128), axis=1) == segr_ref[qi]
                dk_sum, dv_sum = dk[cols, :], dv[cols, :]
                for h in range(2):
                    lo, hi = h * HEAD, (h + 1) * HEAD
                    delta = jnp.sum(both[lo:hi, :], axis=0, keepdims=True)
                    qh, gh = head_lanes(q, h), head_lanes(g, h)
                    s = jnp.where(same, mm(k, qh, 1, 1), masked_score)
                    p = jnp.exp(s - lse_ref[h, qi])
                    ds = (p * (mm(v, gh, 1, 1) - delta)).astype(bf16)
                    dv_sum = dv_sum + mm(p.astype(bf16), gh, 1, 0)
                    dk_sum = dk_sum + mm(ds, qh, 1, 0)
                    dq[lo:hi, :] = dq[lo:hi, :] + mm(kt[ki, lo:hi, :], ds, 1, 0)
                dk[cols, :] = dk_sum
                dv[cols, :] = dv_sum

        out_ref[0, rows, :] = turn_back(dq[...].T * (HEAD**-0.5), rows)

    @pl.loop(0, blocks)
    def _(b):
        rows = pl.ds(pl.multiple_of(b * BLOCK, BLOCK), BLOCK)
        out_ref[1, rows, :] = turn_back(dk[rows, :], rows)
        out_ref[2, rows, :] = dv[rows, :].astype(bf16)


def pieces_of(qkv, length):
    return [pl.BlockSpec((None, length, PAIR), functools.partial(lambda t, p, *_: (t, 0, p), t)) for t in range(3)]


def attend_forward(flags, qkv, seg_rows, seg_cols):
    _, length, width = qkv.shape
    blocks, pairs = length // BLOCK, width // PAIR
    return pl.pallas_call(
        forward_kernel,
        grid_spec=pltpu.PrefetchScalarGridSpec(
            num_scalar_prefetch=1,
            grid=(pairs,),
            in_specs=[
                *pieces_of(qkv, length),
                pl.BlockSpec((blocks, 1, BLOCK), lambda p, *_: (0, 0, 0)),
                pl.BlockSpec((length, 128), lambda p, *_: (0, 0)),
            ],
            out_specs=[
                pl.BlockSpec((length, PAIR), lambda p, *_: (0, p)),
                pl.BlockSpec((2, blocks, 1, BLOCK), lambda p, *_: (p, 0, 0, 0)),
            ],
            scratch_shapes=[
                pltpu.VMEM((blocks, PAIR, BLOCK), bf16),
                pltpu.VMEM((2, 1, BLOCK), f32),
                pltpu.VMEM((2, 1, BLOCK), f32),
                pltpu.VMEM((PAIR, BLOCK), f32),
            ],
        ),
        out_shape=[
            jax.ShapeDtypeStruct((length, width), bf16),
            jax.ShapeDtypeStruct((2 * pairs, blocks, 1, BLOCK), f32),
        ],
        compiler_params=pltpu.CompilerParams(vmem_limit_bytes=48 << 20),
        cost_estimate=pl.CostEstimate(
            flops=4 * length * length * width, bytes_accessed=8 * length * width, transcendentals=length * length * width // HEAD
        ),
        name="attend",
    )(flags, qkv, qkv, qkv, seg_rows, seg_cols)


def attend_backward(flags, qkv, grad, mixed, lse, seg_rows, seg_cols, cosine, sine):
    _, length, width = qkv.shape
    blocks, pairs = length // BLOCK, width // PAIR
    whole = pl.BlockSpec((length, PAIR), lambda p, *_: (0, p))
    table = pl.BlockSpec((length, PAIR), lambda p, *_: (0, 0))
    return pl.pallas_call(
        backward_kernel,
        grid_spec=pltpu.PrefetchScalarGridSpec(
            num_scalar_prefetch=1,
            grid=(pairs,),
            in_specs=[
                *pieces_of(qkv, length),
                whole,
                whole,
                pl.BlockSpec((2, blocks, 1, BLOCK), lambda p, *_: (p, 0, 0, 0)),
                pl.BlockSpec((blocks, 1, BLOCK), lambda p, *_: (0, 0, 0)),
                table,
                table,
                table,
            ],
            out_specs=pl.BlockSpec((3, length, PAIR), lambda p, *_: (0, 0, p)),
            scratch_shapes=[
                pltpu.VMEM((blocks, PAIR, BLOCK), bf16),
                pltpu.VMEM((length, PAIR), f32),
                pltpu.VMEM((length, PAIR), f32),
                pltpu.VMEM((PAIR, BLOCK), f32),
            ],
        ),
        out_shape=jax.ShapeDtypeStruct((3, length, width), bf16),
        compiler_params=pltpu.CompilerParams(vmem_limit_bytes=56 << 20),
        cost_estimate=pl.CostEstimate(
            flops=10 * length * length * width, bytes_accessed=16 * length * width, transcendentals=length * length * width // HEAD
        ),
        name="attend_back",
    )(flags, qkv, qkv, qkv, grad, mixed, lse, seg_rows, seg_cols, cosine, sine)


MESH = pl.DeviceIdType.MESH
ADD_ROWS = 32
STEPS = 9
EDGES = 4


def add_low(a, a_at, b, rows):
    @pl.loop(0, rows // ADD_ROWS)
    def _(i):
        at = pl.ds(pl.multiple_of(i * ADD_ROWS, ADD_ROWS), ADD_ROWS)
        kept = a[pl.ds(pl.multiple_of(a_at + i * ADD_ROWS, ADD_ROWS), ADD_ROWS), :].astype(f32)
        b[at, :] = (kept + b[at, :].astype(f32)).astype(bf16)


class Unit:
    def __init__(self, part, out, column, got, send, recv, local, place, bits=(0, 1, 2, 3)):
        self.part, self.out, self.got = part, out, got
        self.send, self.recv, self.local = send, recv, local
        self.rows, columns = 2 * got[0].shape[0], got[0].shape[1]
        self.columns = pl.ds(column, columns)
        self.bit = [(place // (1 << b)) % 2 for b in bits]
        self.partner = [place + (1 - 2 * bit) * (1 << b) for bit, b in zip(self.bit, bits, strict=True)]
        self.base = [0]
        for b in range(EDGES):
            self.base.append(self.base[-1] + self.bit[b] * (self.rows >> (b + 1)))

    def remote(self, src, dst, stage, b):
        return pltpu.make_async_remote_copy(
            src_ref=src,
            dst_ref=dst,
            send_sem=self.send.at[stage],
            recv_sem=self.recv.at[stage],
            device_id={"dp": self.partner[b]},
            device_id_type=MESH,
        )

    def halving(self, b):
        half = self.rows >> (b + 1)
        source = self.part if b == 0 else self.got[b - 1]
        away = pl.ds(pl.multiple_of((1 - self.bit[b]) * half, ADD_ROWS), half)
        return self.remote(source.at[away], self.got[b], b, b)

    def spot(self, b):
        size = self.rows >> (b + 1)
        return self.out.at[pl.ds(pl.multiple_of(self.base[b + 1], ADD_ROWS), size), self.columns]

    def own(self):
        return pltpu.make_async_copy(self.got[3], self.spot(3), self.local.at[0])

    def gathering(self, b):
        return self.remote(self.got[3] if b == 3 else self.spot(b), self.spot(b), 7 - b, b)

    def step(self, k):
        if k == 0:
            self.halving(0).start()
        elif k < 5:
            b = k - 1
            self.halving(b).wait()
            half = self.rows >> (b + 1)
            add_low(self.part if b == 0 else self.got[b - 1], self.bit[b] * half, self.got[b], half)
            if b < 3:
                self.halving(b + 1).start()
            else:
                self.own().start()
                self.gathering(3).start()
        elif k == 5:
            self.own().wait()
            self.gathering(3).wait()
            self.gathering(2).start()
        elif k < 8:
            self.gathering(8 - k).wait()
            self.gathering(7 - k).start()
        else:
            self.gathering(0).wait()


def unit_scratch(rows, columns):
    return [
        *[pltpu.VMEM((rows >> (b + 1), columns), bf16) for b in range(EDGES)],
        pltpu.SemaphoreType.DMA((2 * EDGES,)),
        pltpu.SemaphoreType.DMA((2 * EDGES,)),
        pltpu.SemaphoreType.DMA((1,)),
    ]


def greet(targets):
    barrier = pltpu.get_barrier_semaphore()
    for target in targets:
        pl.semaphore_signal(barrier, inc=1, device_id=target, device_id_type=MESH)
    pl.semaphore_wait(barrier, len(targets))


ORDER = (
    (3, 0, 1), (4, 1, 1), (8, 0, 2), (8, 2, 1), (10, 0, 3), (10, 1, 2), (10, 0, 4), (10, 1, 3), (10, 3, 1),
    (10, 2, 2), (10, 4, 1), (11, 1, 4), (12, 0, 5), (12, 2, 3), (14, 0, 6), (14, 2, 4), (14, 1, 5), (15, 3, 2),
    (16, 2, 5), (17, 1, 6), (19, 5, 1), (19, 4, 2), (19, 3, 3), (20, 2, 6), (21, 3, 4), (21, 5, 2), (23, 4, 3),
    (24, 6, 1), (24, 1, 7), (24, 3, 5), (24, 7, 1), (24, 5, 3), (24, 4, 4), (26, 6, 2), (26, 8, 1), (26, 7, 2),
    (27, 5, 4), (27, 3, 6), (28, 4, 5), (29, 7, 3), (31, 6, 3), (31, 2, 7), (31, 5, 5), (32, 4, 6), (32, 8, 2),
    (32, 6, 4), (32, 7, 4), (32, 7, 5), (32, 8, 3), (32, 5, 6), (32, 3, 7), (33, 8, 4), (33, 0, 7), (34, 6, 5),
    (34, 4, 7), (34, 0, 8), (34, 3, 8), (34, 7, 6), (34, 2, 8), (34, 8, 5), (35, 6, 6), (36, 7, 7), (36, 8, 6),
    (36, 6, 7), (36, 5, 7), (36, 1, 8), (37, 8, 7), (99, 6, 8), (99, 7, 8), (99, 8, 8), (99, 4, 8), (99, 5, 8),
)
WIDE = 512
STEP_ROWS = 64


def vectors_of(product, bias, depth):
    return [product[:, r * depth : (r + 1) * depth] + bias[:, r * depth : (r + 1) * depth] for r in range(6)]


def fetcher(sems):
    count = [0]

    def fetch(src, dst):
        copy = pltpu.make_async_copy(src, dst, sems.at[count[0]])
        copy.start()
        count[0] += 1
        return copy

    return fetch


def head_kernel(
    tokens_hbm, cot_hbm, w_qkv_hbm, w_out_hbm, w_up_hbm, w_down_hbm,
    mods, b_ada, gain_one, gain_two, cond, b_up, frequency, lengths,
    qkv_out, mixed_out, one_out, back_out, two_out, hidden_out, pre_out, own_grad, send_grad, middle_out,
    projected_out, own_branch, send_branch, lse, known, segr, segc, cosine, sine,
    tokens, cot, w_qkv, w_out, w_up, w_down, rows_one, full_back, rows_two, qkv, mixed, from_sum, send_sum, projected,
    middle, hidden, pre, grads, branch, low_grads, low_branch, slope, bias, bias_down, load, x_send, x_recv,
):
    me = lax.axis_index("tensor")
    length, depth = rows_one.shape
    chunks, half, _ = from_sum.shape
    chunk = 2 * half
    width = mixed.shape[1]
    pairs = width // PAIR
    across = {"tensor": 1 - me}
    each = range(chunks)
    own = [slice(c * chunk, c * chunk + half) for c in each]
    got = [slice(c * chunk + half, (c + 1) * chunk) for c in each]
    whole = [slice(c * chunk, (c + 1) * chunk) for c in each]
    fetch = fetcher(load)

    def x_copy(src, dst, i):
        return pltpu.make_async_remote_copy(
            src_ref=src, dst_ref=dst, send_sem=x_send.at[i], recv_sem=x_recv.at[i],
            device_id=across, device_id_type=MESH,
        )

    ones = [x_copy(rows_one.at[own[c]], rows_one.at[got[c]], c) for c in each]
    backs = [x_copy(full_back.at[own[c]], full_back.at[got[c]], chunks + c) for c in each]
    shares = [x_copy(send_sum.at[c], from_sum.at[c], 2 * chunks + c) for c in each]
    twos = [x_copy(rows_two.at[own[c]], rows_two.at[got[c]], 3 * chunks + c) for c in each]

    shift_a, scale_a, gate_a, shift_m, scale_m, gate_m = vectors_of(mods, b_ada, depth)
    gain_one, gain_two = gain_one[...], gain_two[...]
    reads = [fetch(tokens_hbm, tokens), fetch(w_qkv_hbm, w_qkv), fetch(cot_hbm, cot)]
    reads += [fetch(w_out_hbm, w_out), fetch(w_up_hbm, w_up), fetch(w_down_hbm, w_down)]
    writes = []
    greet([across])

    def normal_of(values):
        center = values - jnp.mean(values, axis=1, keepdims=True)
        return center * lax.rsqrt(jnp.mean(center * center, axis=1, keepdims=True) + norm_eps)

    def by_rows(work):
        @pl.loop(0, half // STEP_ROWS)
        def _(i):
            work(pl.multiple_of(i * STEP_ROWS, STEP_ROWS))

    reads[0].wait()
    for c in each:

        def first_norm(at, c=c):
            values = tokens[pl.ds(c * half + at, STEP_ROWS), :].astype(f32)
            out = normal_of(values) * gain_one * (1.0 + scale_a) + shift_a
            rows_one[pl.ds(c * chunk + at, STEP_ROWS), :] = out.astype(bf16)

        by_rows(first_norm)
        ones[c].start()
    reads[2].wait()
    bias_down[...] = jnp.zeros(bias_down.shape, f32)
    for c in each:

        def weigh(at, c=c):
            low = (cot[pl.ds(c * half + at, STEP_ROWS), :].astype(f32) * gate_m).astype(bf16)
            full_back[pl.ds(c * chunk + at, STEP_ROWS), :] = low
            bias_down[...] += jnp.sum(low.astype(f32), axis=0, keepdims=True)

        by_rows(weigh)

    starts = [0]
    for n in range(lengths.shape[1] - 1):
        starts.append(starts[-1] + lengths[0, n])

    def place_of(step):
        at = step % chunk
        return jnp.where(at < half, me, 1 - me) * (chunks * half) + (step // chunk) * half + at % half

    def document_of(place):
        return sum((place >= start).astype(jnp.int32) for start in starts[1:])

    segr[...] = document_of(place_of(lax.broadcasted_iota(jnp.int32, segr.shape, 1)))

    @pl.loop(0, length // STEP_ROWS)
    def _(i):
        at = pl.multiple_of(i * STEP_ROWS, STEP_ROWS)
        place = place_of(at + lax.broadcasted_iota(jnp.int32, (STEP_ROWS, PAIR), 0))
        first = functools.reduce(jnp.maximum, [jnp.where(place >= start, start, 0) for start in starts])
        angles = (place - first).astype(f32) * frequency[...]
        rows = pl.ds(at, STEP_ROWS)
        segc[rows, :] = document_of(place)
        cosine[rows, :] = jnp.cos(angles)
        sine[rows, :] = jnp.sin(angles)

    reads[1].wait()

    def project(c):
        rows = whole[c]
        for t in range(3):
            y = mm(rows_one[rows, :], w_qkv[t], 1, 0)
            if t == 2:
                qkv[t, rows, :] = y.astype(bf16)
                continue
            for p in range(pairs):
                lanes = slice(p * PAIR, (p + 1) * PAIR)
                u = y[:, lanes]
                low = (u * cosine[rows, :] + turned(u) * sine[rows, :]).astype(bf16)
                qkv[t, rows, lanes] = low * jnp.asarray(HEAD**-0.5 if t == 0 else 1.0, bf16)

    ones[0].wait()
    project(0)
    ones[1].wait()
    backs[0].start()
    project(1)
    writes.append(fetch(rows_one, one_out))
    writes.append(fetch(qkv, qkv_out))

    def attend(p, c):
        lanes = pl.ds(pl.multiple_of(p * PAIR, PAIR), PAIR)
        q = qkv[0, whole[c], lanes]
        docs = segr[:, whole[c]]
        outs = []
        for h in range(2):
            qh = head_lanes(q, h)
            scores = []
            for b in range(0, length, BLOCK):
                same = jnp.concatenate([segc[b : b + BLOCK, :]] * (chunk // 128), axis=1) == docs
                scores.append(jnp.where(same, mm(qkv[1, b : b + BLOCK, lanes], qh, 1, 1), masked_score))
            top = functools.reduce(jnp.maximum, [jnp.max(s, axis=0, keepdims=True) for s in scores])
            total, summed = 0.0, 0.0
            for i, s in enumerate(scores):
                pr = jnp.exp(s - top)
                total = total + jnp.sum(pr, axis=0, keepdims=True)
                v = transposed(qkv[2, i * BLOCK : (i + 1) * BLOCK, lanes]).astype(bf16)
                summed = summed + mm(v[h * HEAD : (h + 1) * HEAD, :], pr.astype(bf16), 1, 0)
            lse[c, 2 * p + h] = top + jnp.log(total)
            outs.append(summed / total)
        mixed[whole[c], lanes] = jnp.concatenate(outs, axis=0).T.astype(bf16)

    for c in each:

        @pl.loop(0, pairs)
        def _(p):
            attend(p, c)

        if c == 0:
            reads[3].wait()
        send_sum[c] = mm(mixed[got[c], :], w_out[...], 1, 0).astype(bf16)
        shares[c].start()
        projected[c] = mm(mixed[own[c], :], w_out[...], 1, 0)
    writes.append(fetch(mixed, mixed_out))

    def second_norm(c):
        shares[c].wait()

        def work(at):
            rows = pl.ds(at, STEP_ROWS)
            share = projected[c, rows, :] + from_sum[c, rows, :].astype(f32)
            projected[c, rows, :] = share
            values = tokens[pl.ds(c * half + at, STEP_ROWS), :].astype(f32) + gate_a * share
            middle[c, rows, :] = values
            out = normal_of(values) * gain_two * (1.0 + scale_m) + shift_m
            rows_two[pl.ds(c * chunk + at, STEP_ROWS), :] = out.astype(bf16)

        by_rows(work)
        twos[c].start()

    cubic, root = 0.044715, (2.0 / jnp.pi) ** 0.5
    tile = 2 * WIDE
    bias[...] = jnp.zeros(bias.shape, f32)
    held = [[], []]

    def feed(slot, rows):
        for copy in held[slot]:
            copy.wait()

        @pl.loop(0, w_up.shape[1] // tile)
        def _(t):
            at = pl.ds(pl.multiple_of(t * tile, tile), tile)
            u = mm(rows_two[rows, :], w_up[:, at], 1, 0) + b_up[:, at]
            square = u * u
            t_h = jnp.tanh(u * (root + (root * cubic) * square))
            rising = 0.5 * (1.0 + t_h)
            low_hidden = (u * rising).astype(bf16)
            slope[:, at] = rising + (0.5 * u) * (1.0 - t_h * t_h) * (root + (3.0 * cubic * root) * square)
            hidden[slot, :, at] = low_hidden
            more = mm(low_hidden, w_down[at, :], 1, 0)

            @pl.when(t == 0)
            def _():
                branch[slot] = more

            @pl.when(t > 0)
            def _():
                branch[slot] += more

        held[slot] = [fetch(hidden.at[slot], hidden_out.at[rows])]

    def feed_back(slot, rows):
        @pl.loop(0, w_up.shape[1] // tile)
        def _(t):
            at = pl.ds(pl.multiple_of(t * tile, tile), tile)
            low = (mm(full_back[rows, :], w_down[at, :], 1, 1) * slope[:, at]).astype(bf16)
            pre[slot, :, at] = low
            bias[:, at] += jnp.sum(low.astype(f32), axis=0, keepdims=True)
            more = mm(low, w_up[:, at], 1, 1)

            @pl.when(t == 0)
            def _():
                grads[slot] = more

            @pl.when(t > 0)
            def _():
                grads[slot] += more

        held[slot].append(fetch(pre.at[slot], pre_out.at[rows]))

    second_norm(0)
    for read in reads[4:]:
        read.wait()
    for c in each:
        if c:
            second_norm(c)
        feed(c, own[c])
        feed_back(c, own[c])
        held[c] += [fetch(grads.at[c], own_grad.at[c]), fetch(branch.at[c], own_branch.at[c])]
    writes.append(fetch(middle, middle_out))
    writes.append(fetch(projected, projected_out))
    for c in each:
        twos[c].wait()
        if c == 0:
            backs[0].wait()
            backs[1].start()
        feed(c, got[c])
        low_branch[c] = branch[c].astype(bf16)
        if c:
            backs[c].wait()
        feed_back(c, got[c])
        low_grads[c] = grads[c].astype(bf16)
        writes += [fetch(low_grads.at[c], send_grad.at[c]), fetch(low_branch.at[c], send_branch.at[c]), *held[c]]
    writes += [fetch(full_back, back_out), fetch(rows_two, two_out)]
    known[...] = jnp.concatenate(
        [
            jnp.zeros((8, depth), f32), bias_down[...], bias[:, :depth], bias[:, depth:],
            jnp.concatenate([cond[...].astype(f32), jnp.zeros((1, depth - cond.shape[1]), f32)], axis=1),
            jnp.zeros((4, depth), f32),
        ],
        axis=0,
    )
    for copy in writes:
        copy.wait()


def head(tokens, cot, w_qkv, w_out, w_up, w_down, *near_args, chunks):
    own, depth = tokens.shape
    length, width, wide = 2 * own, w_qkv.shape[2], w_up.shape[1]
    half = own // chunks
    anywhere, near = pl.BlockSpec(memory_space=pl.ANY), pl.BlockSpec(memory_space=pltpu.VMEM)
    shaped, kept = jax.ShapeDtypeStruct, pltpu.VMEM
    parts, rows = (chunks, half, depth), (length, depth)
    return pl.pallas_call(
        head_kernel,
        in_specs=[anywhere] * 6 + [near] * (len(near_args) - 1) + [pl.BlockSpec(memory_space=pltpu.SMEM)],
        out_specs=[anywhere] * 13 + [near] * 6,
        out_shape=[
            shaped((3, length, width), bf16), shaped((length, width), bf16), *[shaped(rows, bf16)] * 3,
            *[shaped((length, wide), bf16)] * 2, shaped(parts, f32), shaped(parts, bf16),
            shaped(parts, f32), shaped(parts, f32), shaped(parts, f32), shaped(parts, bf16),
            shaped((chunks, width // HEAD, 1, length // chunks), f32), shaped((16, depth), f32),
            shaped((1, length), jnp.int32), shaped((length, PAIR), jnp.int32), *[shaped((length, PAIR), f32)] * 2,
        ],
        scratch_shapes=[
            kept(tokens.shape, bf16), kept(tokens.shape, bf16), kept(w_qkv.shape, bf16), kept(w_out.shape, bf16),
            kept(w_up.shape, bf16), kept(w_down.shape, bf16), *[kept(rows, bf16)] * 3, kept((3, length, width), bf16),
            kept((length, width), bf16), kept(parts, bf16), kept(parts, bf16), kept(parts, f32), kept(parts, f32),
            *[kept((chunks, half, wide), bf16)] * 2, *[kept(parts, f32)] * 2,
            kept(parts, bf16), kept(parts, bf16), kept((half, wide), f32), kept((1, wide), f32), kept((1, depth), f32),
            pltpu.SemaphoreType.DMA((32,)),
            pltpu.SemaphoreType.DMA((4 * chunks,)), pltpu.SemaphoreType.DMA((4 * chunks,)),
        ],
        compiler_params=pltpu.CompilerParams(collective_id=2, has_side_effects=True, vmem_limit_bytes=61 << 20),
        name="head",
    )(tokens, cot, w_qkv, w_out, w_up, w_down, *near_args)


def tail_kernel(
    hidden, full_back, rows_two, grad_pre, qkv_hbm, mixed_hbm, rows_hbm, w_qkv_hbm, w_out_hbm,
    own_grad, send_grad, mid_hbm, proj_hbm, own_branch, send_branch, tokens_hbm, cot_hbm,
    mods, b_ada, gain_one, gain_two, b_down, known, lse, segr, segc, cosine, sine,
    down_sum, up_sum, out_sum, q_sum, k_sum, v_sum, output, grad_x, everyone,
    qkv, mixed, rows_one, w_qkv, w_out, proj, mix_grad, d_qkv, dk, dv, from_x, grads, middle, projected, tokens, cot,
    part_a, part_b, part_c, part_d, part_e, branch_got, col_sums, small, small_got,
    load, store, x_send, x_recv, all_send, all_recv, *more,
):
    place, me = lax.axis_index("dp"), lax.axis_index("tensor")
    length, depth = rows_one.shape
    chunks, half, _ = from_x.shape
    chunk = 2 * half
    width = mixed.shape[1]
    pairs = width // PAIR
    across = {"tensor": 1 - me}

    specs = [
        (part_a.at[pl.ds(0, WIDE)], down_sum.at[pl.ds(0, WIDE)], 0),
        (part_a.at[pl.ds(WIDE, WIDE)], down_sum.at[pl.ds(WIDE, WIDE)], 0),
        (part_b, down_sum.at[pl.ds(depth, depth)], 0),
        (part_c, up_sum, 0), (part_d, up_sum, depth), (part_e, out_sum, 0),
        (qkv.at[2], v_sum, 0), (qkv.at[1], k_sum, 0), (qkv.at[0], q_sum, 0),
    ]
    units = []
    for i, (part, out, column) in enumerate(specs):
        *got, send, recv, local = more[7 * i : 7 * (i + 1)]
        units.append(Unit(part, out, column, got, send, recv, local, place))

    def x_copy(src, dst, i):
        return pltpu.make_async_remote_copy(
            src_ref=src, dst_ref=dst, send_sem=x_send.at[i], recv_sem=x_recv.at[i],
            device_id=across, device_id_type=MESH,
        )

    each = range(chunks)
    grads_in = [x_copy(send_grad.at[c], from_x.at[c], c) for c in each]
    projs = [x_copy(proj.at[c, :half], proj.at[c, half:], chunks + c) for c in each]
    ones = [x_copy(proj.at[c, :half], from_x.at[c], 2 * chunks + c) for c in each]
    branches = [x_copy(send_branch.at[c], branch_got.at[c], 3 * chunks + c) for c in each]
    smalls = x_copy(small, small_got, 4 * chunks)
    outputs = [
        pltpu.make_async_copy(branch_got.at[c], output.at[c * half : (c + 1) * half], store.at[c]) for c in each
    ]
    partner = units[0].partner

    fetch = fetcher(load)
    done = [0]

    def until(place_now):
        while done[0] < len(ORDER) and ORDER[done[0]][0] <= place_now:
            _, i, k = ORDER[done[0]]
            units[i].step(k)
            done[0] += 1

    greet([*[{"dp": p} for p in partner], across])
    grads_in[0].start()
    slots = [w_qkv.at[0], w_qkv.at[1], w_qkv.at[2], d_qkv.at[2]]
    cut = lambda t: slice(t * WIDE, (t + 1) * WIDE)
    backs = fetch(full_back, rows_one)
    hiddens = [fetch(hidden.at[:, cut(t)], slots[t]) for t in range(4)]
    norms = [
        [fetch(src, dst.at[c]) for src, dst in (
            (own_grad.at[c], grads), (mid_hbm.at[c], middle), (proj_hbm.at[c], projected),
            (tokens_hbm.at[c * half : (c + 1) * half], tokens), (cot_hbm.at[c * half : (c + 1) * half], cot),
        )]
        for c in each
    ]
    twos = [fetch(rows_two.at[:, cut(t)], d_qkv.at[t]) for t in range(2)]
    col_sums[...] = jnp.zeros(col_sums.shape, f32)

    backs.wait()
    pres = []
    for t in range(4):
        until(1 + t)
        hiddens[t].wait()
        part = (part_a, part_b)[t // 2]

        @pl.loop(0, WIDE // 256)
        def _(r):
            at = pl.ds(pl.multiple_of(r * 256, 256), 256)
            to = pl.ds(pl.multiple_of((t % 2) * WIDE + r * 256, 256), 256)
            part[to, :] = mm(slots[t][:, at], rows_one[...], 0, 0).astype(bf16)

        pres.append(fetch(grad_pre.at[:, cut(t)], slots[t]))
        if t != 2:
            units[min(t, 2)].step(0)
    main = [
        fetch(w_out_hbm, w_out), fetch(mixed_hbm, mixed), fetch(qkv_hbm, qkv), fetch(rows_hbm, rows_one),
    ]

    def up_part(t):
        pres[t].wait()
        part = (part_c, part_d)[t // 2]

        @pl.loop(0, depth // 256)
        def _(r):
            to = pl.ds(pl.multiple_of(r * 256, 256), 256)
            at = pl.ds(pl.multiple_of((r % 2) * 256, 256), 256)
            part[to, cut(t % 2)] = mm(d_qkv[r // 2, :, at], slots[t][...], 0, 0).astype(bf16)

    def fold(row, values):
        col_sums[row : row + 1, :] += jnp.sum(values, axis=0, keepdims=True)

    def norm_back(grad, values, weight):
        center = values - jnp.mean(values, axis=1, keepdims=True)
        root = lax.rsqrt(jnp.mean(center * center, axis=1, keepdims=True) + norm_eps)
        normal = center * root
        inner = grad * weight
        back = inner - jnp.mean(inner, axis=1, keepdims=True) - normal * jnp.mean(inner * normal, axis=1, keepdims=True)
        return root * back, normal

    _, scale_a, gate_a, _, scale_m, gate_m = vectors_of(mods, b_ada, depth)
    gain_one, gain_two, b_down = gain_one[...], gain_two[...], b_down[...]

    def second_norm(c):
        for copy in norms[c]:
            copy.wait()

        @pl.loop(0, half // STEP_ROWS)
        def _(i):
            at = pl.ds(pl.multiple_of(i * STEP_ROWS, STEP_ROWS), STEP_ROWS)
            grad = grads[c, at, :] + from_x[c, at, :].astype(f32)
            back, normal = norm_back(grad, middle[c, at, :], gain_two * (1.0 + scale_m))
            total = back + cot[c, at, :].astype(f32)
            grads[c, at, :] = total
            proj[c, at, :] = (total * gate_a).astype(bf16)
            fold(0, grad)
            fold(1, grad * normal)
            fold(2, total * projected[c, at, :])

        projs[c].start()

    for copy in twos:
        copy.wait()
    until(5)
    up_part(0)
    until(6)
    up_part(1)
    units[3].step(0)
    until(7)
    grads_in[0].wait()
    grads_in[1].start()
    second_norm(0)
    owns = [fetch(own_branch.at[0], projected.at[0])]
    until(8)
    up_part(2)
    until(9)
    up_part(3)
    units[4].step(0)
    weights = fetch(w_qkv_hbm, w_qkv)
    until(10)
    grads_in[1].wait()
    second_norm(1)
    owns.append(fetch(own_branch.at[1], projected.at[1]))

    def turn_back(u, rows):
        return (u * cosine[rows, :] - turned(u) * sine[rows, :]).astype(bf16)

    def attend_back(p, c):
        lanes = pl.ds(pl.multiple_of(p * PAIR, PAIR), PAIR)
        rows = slice(c * chunk, (c + 1) * chunk)
        q, g = qkv[0, rows, lanes], mix_grad[rows, lanes]
        both = (g.astype(f32) * mixed[rows, lanes].astype(f32)).T
        qh = [head_lanes(q, h) for h in range(2)]
        gh = [head_lanes(g, h) for h in range(2)]
        delta = [jnp.sum(both[h * HEAD : (h + 1) * HEAD, :], axis=0, keepdims=True) for h in range(2)]
        q_two, g_two = jnp.concatenate(qh, axis=0), jnp.concatenate(gh, axis=0)
        docs = segr[:, rows]
        dq = [0.0, 0.0]
        for b in range(0, length, BLOCK):
            cols = slice(b, b + BLOCK)
            k, v = qkv[1, cols, lanes], qkv[2, cols, lanes]
            turned_k = transposed(k).astype(bf16)
            same = jnp.concatenate([segc[cols, :]] * (chunk // 128), axis=1) == docs
            ps, ds = [], []
            for h in range(2):
                s = jnp.where(same, mm(k, qh[h], 1, 1), masked_score)
                pr = jnp.exp(s - lse[c, 2 * p + h])
                d = (pr * (mm(v, gh[h], 1, 1) - delta[h])).astype(bf16)
                ps.append(pr.astype(bf16))
                ds.append(d)
                dq[h] = dq[h] + mm(turned_k[h * HEAD : (h + 1) * HEAD, :], d, 1, 0)
            add_v = mm(jnp.concatenate(ps, axis=1), g_two, 1, 0)
            add_k = mm(jnp.concatenate(ds, axis=1), q_two, 1, 0)
            if c < chunks - 1:
                dv[cols, lanes] = add_v if c == 0 else dv[cols, lanes] + add_v
                dk[cols, lanes] = add_k if c == 0 else dk[cols, lanes] + add_k
            else:
                d_qkv[1, cols, lanes] = turn_back(dk[cols, lanes] + add_k, cols)
                d_qkv[2, cols, lanes] = (dv[cols, lanes] + add_v).astype(bf16)
        d_qkv[0, rows, lanes] = turn_back(jnp.concatenate(dq, axis=0).T * (HEAD**-0.5), rows)

    for copy in main:
        copy.wait()
    now = 11
    for c in each:
        until(now)
        projs[c].wait()
        if c == chunks - 1:
            for copy in branches:
                copy.start()
        mix_grad[c * chunk : (c + 1) * chunk, :] = mm(proj[c], w_out[...], 1, 1).astype(bf16)
        now += 1
        if c == chunks - 1:
            until(now)

            @pl.loop(0, width // 256)
            def _(r):
                at = pl.ds(pl.multiple_of(r * 256, 256), 256)
                part_e[at, :] = sum(
                    mm(mixed[n * chunk : (n + 1) * chunk, at], proj[n], 0, 0) for n in each
                ).astype(bf16)

            units[5].step(0)
            now += 1

        @pl.loop(0, pairs)
        def _(p):
            for n in range(pairs):

                @pl.when(p == n)
                def _():
                    until(now + n)

            attend_back(p, c)

        now += pairs

    def rows_back(start):
        at = slice(start, start + half)
        return sum(mm(d_qkv[t, at, :], w_qkv[t], 1, 1) for t in range(3))

    for i in range(3):
        until(now + i)

        @pl.loop(0, depth // 256)
        def _(r):
            at = pl.ds(pl.multiple_of(r * 256, 256), 256)
            qkv[2 - i, at, :] = mm(rows_one[:, at], d_qkv[2 - i], 0, 0).astype(bf16)

        units[6 + i].step(0)
    now += 3
    weights.wait()
    for c in each:
        until(now + c)
        proj[c, :half] = rows_back(c * chunk + half).astype(bf16)
        if c == 0:
            ones[c].start()
    now += chunks
    for c in each:
        until(now + c)
        branches[c].wait()
        owns[c].wait()

        @pl.loop(0, half // STEP_ROWS)
        def _(i):
            at = pl.ds(pl.multiple_of(i * STEP_ROWS, STEP_ROWS), STEP_ROWS)
            branch = projected[c, at, :] + branch_got[c, at, :].astype(f32) + b_down
            branch_got[c, at, :] = (middle[c, at, :] + gate_m * branch).astype(bf16)
            fold(5, cot[c, at, :].astype(f32) * branch)

        outputs[c].start()
    now += chunks
    for c in each:
        until(now + c)
        projected[c] = rows_back(c * chunk)
    now += chunks
    for c in each:
        until(now + c)
        ones[c].wait()
        if c < chunks - 1:
            ones[c + 1].start()

        @pl.loop(0, half // STEP_ROWS)
        def _(i):
            at = pl.ds(pl.multiple_of(i * STEP_ROWS, STEP_ROWS), STEP_ROWS)
            grad = projected[c, at, :] + from_x[c, at, :].astype(f32)
            back, normal = norm_back(grad, tokens[c, at, :].astype(f32), gain_one * (1.0 + scale_a))
            grad_x[c, at, :] = (back + grads[c, at, :]).astype(bf16)
            fold(3, grad)
            fold(4, grad * normal)

    now += chunks
    shift, scaled, gated, shift_one, scaled_one, gated_m = [col_sums[r : r + 1, :] for r in range(6)]
    small[...] = known[...] + jnp.concatenate(
        [
            shift_one, gain_one * scaled_one, gated, shift, gain_two * scaled, gated_m,
            (1.0 + scale_a) * scaled_one, (1.0 + scale_m) * scaled, jnp.zeros((8, depth), f32),
        ],
        axis=0,
    )
    smalls.start()
    until(now)
    smalls.wait()
    number = lax.broadcasted_iota(jnp.int32, small.shape, 0)
    everyone[0] = small[...] + jnp.where(number < 9, small_got[...], 0.0)
    for n, b in enumerate((1, 3, 2, 0)):
        copy = pltpu.make_async_remote_copy(
            src_ref=everyone.at[pl.ds(0, 1 << n)], dst_ref=everyone.at[pl.ds(1 << n, 1 << n)],
            send_sem=all_send.at[n], recv_sem=all_recv.at[n],
            device_id={"dp": partner[b]}, device_id_type=MESH,
        )
        copy.start()
        until(now + 1 + n)
        copy.wait()
    until(1000)
    for copy in outputs:
        copy.wait()


def tail(*args):
    hidden, qkv, rows_one, w_qkv, w_out, own_grad, tokens = (args[n] for n in (0, 4, 6, 7, 8, 9, 15))
    known = args[22]
    _, length, width = qkv.shape
    chunks, half, depth = own_grad.shape
    anywhere, near = pl.BlockSpec(memory_space=pl.ANY), pl.BlockSpec(memory_space=pltpu.VMEM)
    shaped, kept = jax.ShapeDtypeStruct, pltpu.VMEM
    in_chunks = (chunks, half, depth)
    scratch = [
        kept(qkv.shape, bf16), kept((length, width), bf16), kept(rows_one.shape, bf16), kept(w_qkv.shape, bf16),
        kept(w_out.shape, bf16), kept((chunks, 2 * half, depth), bf16), kept((length, width), bf16),
        kept((3, length, width), bf16), kept((length, width), f32), kept((length, width), f32),
        kept(in_chunks, bf16), kept(in_chunks, f32), kept(in_chunks, f32), kept(in_chunks, f32),
        kept(in_chunks, bf16), kept(in_chunks, bf16),
        *[kept((depth, depth), bf16)] * 4, kept((width, depth), bf16), kept(in_chunks, bf16),
        kept((8, depth), f32), kept(known.shape, f32), kept(known.shape, f32),
        pltpu.SemaphoreType.DMA((30,)), pltpu.SemaphoreType.DMA((chunks,)),
        pltpu.SemaphoreType.DMA((4 * chunks + 1,)), pltpu.SemaphoreType.DMA((4 * chunks + 1,)),
        pltpu.SemaphoreType.DMA((EDGES,)), pltpu.SemaphoreType.DMA((EDGES,)),
        *unit_scratch(WIDE, depth) * 2, *unit_scratch(depth, depth) * 3, *unit_scratch(width, depth), *unit_scratch(depth, width) * 3,
    ]
    return pl.pallas_call(
        tail_kernel,
        in_specs=[anywhere] * 17 + [near] * 11,
        out_specs=[anywhere] * 7 + [near] * 2,
        out_shape=[
            shaped((hidden.shape[1], depth), bf16), shaped((depth, hidden.shape[1]), bf16), shaped((width, depth), bf16),
            *[shaped((depth, width), bf16)] * 3, shaped(tokens.shape, bf16),
            shaped(in_chunks, bf16), shaped((1 << EDGES, *known.shape), f32),
        ],
        scratch_shapes=scratch,
        compiler_params=pltpu.CompilerParams(collective_id=1, has_side_effects=True, vmem_limit_bytes=61 << 20),
        name="tail",
    )(*args)


def finish_kernel(
    down, up, out, q, k, v, output, grad_x, everyone, w_ada,
    down_sum, up_sum, out_sum, qkv_sum, output_out, grad_x_out, ada, cond_grad, ada_bias, one_gain, two_gain, down_bias,
    up_bias, mods, conds,
):
    depth = everyone.shape[2]

    @pl.when(pl.program_id(0) == 0)
    def _():
        total = sum(everyone[n] for n in range(everyone.shape[0]))
        lanes = 0.0
        for r in range(6):
            span = slice(r * depth, (r + 1) * depth)
            mods[:, span] = jnp.concatenate([everyone[n, r : r + 1, :] for n in range(everyone.shape[0])], axis=0)
            ada_bias[:, span] = total[r : r + 1, :]
            for t in range(0, depth, 128):
                at = r * depth + t
                lanes = lanes + w_ada[:, at : at + 128].astype(f32) * everyone[0, r : r + 1, t : t + 128]
        cond_grad[...] = jnp.sum(lanes.T, axis=0, keepdims=True)
        one_gain[...], two_gain[...], down_bias[...] = total[6:7, :], total[7:8, :], total[8:9, :]
        up_bias[...] = jnp.concatenate([total[9:10, :], total[10:11, :]], axis=1)
        conds[...] = jnp.concatenate(
            [everyone[n, 11:12, : conds.shape[0]] for n in range(everyone.shape[0])], axis=0
        ).T

    down_sum[...] = down[...].astype(f32)
    up_sum[...] = up[...].astype(f32)
    out_sum[...] = out[...].astype(f32)
    for t, part in enumerate((q, k, v)):
        qkv_sum[t] = part[...].astype(f32)
    output_out[...] = output[...]
    grad_x_out[...] = grad_x[...]
    rows = ada.shape[0]
    some = conds[pl.ds(pl.multiple_of(pl.program_id(0) * rows, rows), rows), :]
    ada[...] = lax.dot_general(
        some, mods[...], (((1,), (0,)), ((), ())), precision=lax.Precision.HIGHEST, preferred_element_type=f32
    )


def finish(sums, output, grad_x, everyone, w_ada):
    steps = 4
    down, up, out, q, _, _ = sums
    shaped = jax.ShapeDtypeStruct
    devices, _, depth = everyone.shape

    def rows_of(array):
        return pl.BlockSpec((array.shape[0] // steps, array.shape[1]), lambda i: (i, 0))

    def whole(shape):
        return pl.BlockSpec(shape, lambda i: (0,) * len(shape))

    ones = [(1, n) for n in (w_ada.shape[0], w_ada.shape[1], depth, depth, depth, up.shape[1])]
    return pl.pallas_call(
        finish_kernel,
        grid=(steps,),
        in_specs=[
            *[rows_of(a) for a in (*sums, output, grad_x)], whole(everyone.shape), whole(w_ada.shape),
        ],
        out_specs=[
            rows_of(down), rows_of(up), rows_of(out),
            pl.BlockSpec((3, q.shape[0] // steps, q.shape[1]), lambda i: (0, i, 0)),
            rows_of(output), rows_of(grad_x), rows_of(w_ada), *[whole(s) for s in ones],
        ],
        out_shape=[
            shaped(down.shape, f32), shaped(up.shape, f32), shaped(out.shape, f32), shaped((3, *q.shape), f32),
            shaped(output.shape, bf16), shaped(grad_x.shape, bf16), shaped(w_ada.shape, f32),
            *[shaped(s, f32) for s in ones],
        ],
        scratch_shapes=[pltpu.VMEM((devices, w_ada.shape[1]), f32), pltpu.VMEM((w_ada.shape[0], devices), f32)],
        compiler_params=pltpu.CompilerParams(vmem_limit_bytes=61 << 20),
        name="finish",
    )(*sums, output, grad_x, everyone, w_ada)


def body_pair(
    tokens, cond, doc_lengths, w_ada, b_ada, gain_one, w_qkv, w_out, gain_two, w_up, b_up, w_down, b_down, cotangent
):
    own, width = tokens.shape
    length = 2 * own
    chunks = 2

    exponent = np.arange(HEAD // 2) * (2.0 / HEAD)
    frequency = np.tile(rope_base**-exponent, PAIR // (HEAD // 2))[None, :].astype(np.float32)
    mods = jnp.dot(cond, w_ada, preferred_element_type=f32)
    (
        qkv, mixed, rows_one, full_back, rows_two, hidden, grad_pre, own_grad, send_grad, middle, projected,
        own_branch, send_branch, lse, known, *tables,
    ) = head(
        tokens, cotangent, w_qkv, w_out, w_up, w_down, mods, b_ada[None, :], gain_one[None, :], gain_two[None, :], cond,
        b_up[None, :], frequency, doc_lengths, chunks=chunks,
    )
    *sums, output, grad_x, everyone = tail(
        hidden, full_back, rows_two, grad_pre, qkv, mixed, rows_one, w_qkv, w_out, own_grad, send_grad,
        middle, projected, own_branch, send_branch, tokens, cotangent,
        mods, b_ada[None, :], gain_one[None, :], gain_two[None, :], b_down[None, :], known,
        lse, *tables,
    )
    (
        grad_w_down, grad_w_up, grad_w_out, grad_w_qkv, output, grad_x, grad_w_ada, grad_cond, *rows,
    ) = finish(sums, output, grad_x.reshape(own, width), everyone, w_ada)
    grad_b_ada, grad_gain_one, grad_gain_two, grad_b_down, grad_b_up = [
        row[0] for row in rows
    ]
    return (
        output, grad_x, grad_cond, grad_w_ada, grad_b_ada, grad_gain_one, grad_w_qkv, grad_w_out, grad_gain_two,
        grad_w_up, grad_b_up, grad_w_down, grad_b_down,
    )


def body_any(
    tokens, cond, doc_lengths, w_ada, b_ada, gain_one, w_qkv, w_out, gain_two, w_up, b_up, w_down, b_down, cotangent
):
    tensor_size = lax.axis_size("tensor")
    own = tokens.shape[0]
    length = own * tensor_size

    def all_rows(values):
        return lax.all_gather(values, "tensor", axis=0, tiled=True)

    def own_sum(values):
        return lax.psum_scatter(values, "tensor", scatter_dimension=0, tiled=True)

    def sum_over_dp(part):
        return lax.psum(part, "dp")

    places = jnp.arange(length, dtype=jnp.int32)
    segment, doc_first = documents(doc_lengths[0], places)
    cosine, sine = rope_tables(places - doc_first)
    blocks = length // BLOCK
    in_blocks = segment.reshape(blocks, BLOCK)
    least, most = jnp.min(in_blocks, axis=1), jnp.max(in_blocks, axis=1)
    meets = (least[:, None] <= most[None, :]) & (least[None, :] <= most[:, None])
    flags = meets.astype(jnp.int32).reshape(-1)
    seg_rows = in_blocks[:, None, :]
    seg_cols = jnp.broadcast_to(segment[:, None], (length, 128))

    modulation = jnp.dot(cond, w_ada, preferred_element_type=f32)[0] + b_ada
    shift_a, scale_a, gate_a, shift_m, scale_m, gate_m = jnp.split(modulation, 6)
    x_rows = tokens.astype(f32)
    grad_out = cotangent.astype(f32)

    act_one = modulate(x_rows, gain_one, shift_a, scale_a).astype(bf16)
    rows_one = all_rows(act_one)
    grad_branch = (grad_out * gate_m).astype(bf16)
    full_branch = all_rows(grad_branch)
    qkv = project_qkv(rows_one, w_qkv, cosine, sine)
    mixed, lse = attend_forward(flags, qkv, seg_rows, seg_cols)
    projected = own_sum(jnp.dot(mixed, w_out, preferred_element_type=f32))
    middle = x_rows + gate_a * projected
    rows_two = all_rows(modulate(middle, gain_two, shift_m, scale_m).astype(bf16))
    pre_act = jnp.dot(rows_two, w_up, preferred_element_type=f32) + b_up
    hidden = jax.nn.gelu(pre_act, approximate=True).astype(bf16)

    grad_hidden = jnp.einsum("sd,fd->sf", full_branch, w_down, preferred_element_type=f32)
    _, gelu_back = jax.vjp(lambda values: jax.nn.gelu(values, approximate=True), pre_act)
    grad_pre = gelu_back(grad_hidden)[0].astype(bf16)
    grad_act_two = own_sum(jnp.einsum("sf,df->sd", grad_pre, w_up, preferred_element_type=f32))
    grad_w_down = sum_over_dp(jnp.einsum("sf,sd->fd", hidden, full_branch, preferred_element_type=f32))
    grad_w_up = sum_over_dp(jnp.einsum("sd,sf->df", rows_two, grad_pre, preferred_element_type=f32))

    branch = own_sum(jnp.dot(hidden, w_down, preferred_element_type=f32)) + b_down
    output = (middle + gate_m * branch).astype(bf16)
    grad_gate_m = jnp.sum(grad_out * branch, axis=0)
    grad_b_down = jnp.sum(grad_branch.astype(f32), axis=0)
    grad_b_up = jnp.sum(grad_pre.astype(f32), axis=0)

    _, second_back = jax.vjp(modulate, middle, gain_two, shift_m, scale_m)
    grad_middle, grad_gain_two, grad_shift_m, grad_scale_m = second_back(grad_act_two)
    grad_middle = grad_middle + grad_out
    full_proj = all_rows((grad_middle * gate_a).astype(bf16))
    grad_gate_a = jnp.sum(grad_middle * projected, axis=0)
    grad_mixed = jnp.einsum("sd,ed->se", full_proj, w_out, preferred_element_type=f32).astype(bf16)
    grad_w_out = sum_over_dp(jnp.einsum("se,sd->ed", mixed, full_proj, preferred_element_type=f32))
    grad_qkv = attend_backward(flags, qkv, grad_mixed, mixed, lse, seg_rows, seg_cols, cosine, sine)
    grad_act_one = own_sum(jnp.einsum("tse,tde->sd", grad_qkv, w_qkv, preferred_element_type=f32))
    grad_w_qkv = jnp.einsum("sd,tse->tde", rows_one, grad_qkv, preferred_element_type=f32)
    grad_w_qkv = sum_over_dp(grad_w_qkv.reshape(-1, grad_w_qkv.shape[2])).reshape(grad_w_qkv.shape)

    _, first_back = jax.vjp(modulate, x_rows, gain_one, shift_a, scale_a)
    grad_x, grad_gain_one, grad_shift_a, grad_scale_a = first_back(grad_act_one)
    grad_x = (grad_x + grad_middle).astype(bf16)

    small = jnp.concatenate(
        [
            grad_shift_a, grad_scale_a, grad_gate_a, grad_shift_m, grad_scale_m, grad_gate_m,
            grad_gain_one, grad_gain_two, grad_b_down,
        ]
    )
    small = lax.psum(small, "tensor")
    mod_size = modulation.shape[0]
    grad_mod = small[:mod_size]
    grad_cond = jnp.dot(w_ada.astype(f32), grad_mod, precision=lax.Precision.HIGHEST)[None, :]
    everyone = lax.all_gather(
        jnp.concatenate([small, grad_b_up, cond[0].astype(f32)])[None, :], "dp", axis=0, tiled=True
    )
    conds = everyone[:, -cond.shape[1] :]
    mods = everyone[:, :mod_size]
    grad_w_ada = jnp.einsum("nc,nm->cm", conds, mods, precision=lax.Precision.HIGHEST, preferred_element_type=f32)
    sums = jnp.sum(everyone, axis=0)
    width = tokens.shape[1]
    grad_b_ada = sums[:mod_size]
    grad_gain_one, grad_gain_two, grad_b_down = jnp.split(sums[mod_size : mod_size + 3 * width], 3)
    grad_b_up = sums[mod_size + 3 * width : -cond.shape[1]]
    return (
        output, grad_x, grad_cond, grad_w_ada, grad_b_ada, grad_gain_one, grad_w_qkv, grad_w_out, grad_gain_two,
        grad_w_up, grad_b_up, grad_w_down, grad_b_down,
    )


def solution(mesh):
    swaps = mesh.shape["tensor"] == 2 and mesh.shape["dp"] == 16
    placed = (
        P(("dp", "tensor"), None), P("dp", None), P("dp", None), P(), P(), P(), P(None, None, "tensor"),
        P("tensor", None), P(), P(None, "tensor"), P("tensor"), P("tensor", None), P(), P(("dp", "tensor"), None),
    )
    return jax.shard_map(
        body_pair if swaps else body_any,
        mesh=mesh,
        in_specs=placed,
        out_specs=(
            P(("dp", "tensor"), None), P(("dp", "tensor"), None), P("dp", None), P(), P(), P(),
            P(None, None, "tensor"), P("tensor", None), P(), P(None, "tensor"), P("tensor"), P("tensor", None), P(),
        ),
        check_vma=False,
    )
```
